32 devices in a mesh: tm: 2 (over x), lon: 4 (over y, core), lat: 4 (over z).
Axes of the slice: x: 2, y: 2, z: 4, core: 2. Of those that a mesh axis runs over, the one named last changes fastest.
Arguments:
- iterate: float32 [2, 64, 64, 512], P('tm', None, 'lat', 'lon'), may hold values from -6 to 6
- heating: float32 [2, 64, 64, 512], P('tm', None, 'lat', 'lon'), may hold values from -6 to 6
- initial: float32 [64, 64, 512], P(None, 'lat', 'lon'), may hold values from -6 to 6
- region: int32 [64, 64, 512], P(None, 'lat', 'lon'), may hold values from 0 to 7
- cond_table: float32 [8], replicated, may hold values from 0.3 to 3
Outputs:
- updated: float32 [2, 64, 64, 512], P('tm', None, 'lat', 'lon')
The draws below stay inside these ranges and needn't reach their ends.
Inputs may be any that keep to these rules, and one draw needn't show every extreme that they name: `region`: class index of each cell.
All inputs are finite; a program needn't handle non-finite values.
Results may differ from the reference program's by a relative error of at most 0.0003.
Values sent between devices are 32-bit elements; how exact they have to be, the bound alone decides.
No kernel may reach another device: no remote copies, remote signals or barrier semaphores. Data moves between devices by JAX's collectives and lax.ppermute only.
A program may use at most 128 MiB of HBM per device.

```python
import math
import jax
import jax.numpy as jnp
from jax import lax

LEV = 64
CLASSES = 8
SWEEPS = 4
STEPS = 2
NLAT = 64
NLON = 512


def set_ends(array, own_key, smallest, largest):
    place = [jax.random.randint(jax.random.fold_in(own_key, axis), (), 0, length) for axis, length in enumerate(array.shape)]
    main_axis = array.shape.index(max(array.shape))
    beside = place[:main_axis] + [(place[main_axis] + 1) % array.shape[main_axis]] + place[main_axis + 1:]
    return array.at[tuple(place)].set(smallest).at[tuple(beside)].set(largest)


def block_scale(key, extent, shards, smallest, top_value):
    gain = 1.0
    for position, blocks in shards:
        draws = jax.random.uniform(jax.random.fold_in(jax.random.fold_in(key, 6), position), (blocks,), jnp.float32, smallest / len(shards), top_value / len(shards))
        gain = gain * jnp.repeat(jnp.exp(draws), extent[position] // blocks).reshape((-1,) + (1,) * (len(extent) - 1 - position))
    return gain


def centred(own_key, dims, width, bound, shards=(), kind=jnp.bfloat16):
    array = jax.random.normal(own_key, dims, jnp.float32) * width
    if len(shards) > 0:
        array = block_scale(own_key, dims, shards, -0.22, 0.18) * array
    return jnp.clip(array, min=-bound, max=bound).astype(kind)


def setup_inputs(seed: int = 0) -> dict:
    seeds = jax.random.split(jax.random.key(seed), 6)
    iterate = centred(seeds[0], (STEPS, LEV, NLAT, NLON), 1.0, 6.0, ((0, 2), (2, 4), (3, 4)), jnp.float32)
    heating = centred(seeds[1], (STEPS, LEV, NLAT, NLON), 1.0, 6.0, ((0, 2), (2, 4), (3, 4)), jnp.float32)
    initial = centred(seeds[2], (LEV, NLAT, NLON), 1.0, 6.0, ((1, 4), (2, 4)), jnp.float32)
    region = set_ends(jax.random.randint(seeds[3], (LEV, NLAT, NLON), 0, CLASSES), jax.random.fold_in(seeds[3], 1), 0, CLASSES - 1).astype(jnp.int32)
    cond_table = jnp.clip(jnp.exp(jax.random.uniform(seeds[4], (CLASSES,), jnp.float32, math.log(0.3), math.log(3.0))), 0.3, 3.0)
    return {"iterate": iterate, "heating": heating, "initial": initial, "region": region, "cond_table": cond_table}


corner_weight = 0.1


def harmonic(first, second):
    return 2.0 * first * second / (first + second)


def conductivity(region, cond_table):
    classes = jnp.arange(cond_table.shape[0], dtype=jnp.int32)
    onehot = (region[..., None] == classes).astype(jnp.float32)
    return jnp.sum(onehot * cond_table.astype(jnp.float32), axis=-1)


def extend(field):
    lead = field.ndim - 3
    wrapped = jnp.concatenate([field[..., -1:], field, field[..., :1]], axis=-1)
    pads = [(0, 0)] * lead + [(1, 1), (1, 1), (0, 0)]
    return jnp.pad(wrapped, pads)


def face_weights(kext):
    centre = kext[1:-1, 1:-1, 1:-1]
    return (harmonic(centre, kext[:-2, 1:-1, 1:-1]), harmonic(centre, kext[2:, 1:-1, 1:-1]),
            harmonic(centre, kext[1:-1, :-2, 1:-1]), harmonic(centre, kext[1:-1, 2:, 1:-1]),
            harmonic(centre, kext[1:-1, 1:-1, :-2]), harmonic(centre, kext[1:-1, 1:-1, 2:]))


def neighbours(weights, ext):
    near = weights[0] * ext[..., :-2, 1:-1, 1:-1] + weights[1] * ext[..., 2:, 1:-1, 1:-1]
    near = near + weights[2] * ext[..., 1:-1, :-2, 1:-1] + weights[3] * ext[..., 1:-1, 2:, 1:-1]
    near = near + weights[4] * ext[..., 1:-1, 1:-1, :-2] + weights[5] * ext[..., 1:-1, 1:-1, 2:]
    return near


def reference(iterate, heating, initial, region, cond_table):
    steps = iterate.shape[0]
    weights = face_weights(extend(conductivity(region, cond_table)))
    total = weights[0] + weights[1] + weights[2] + weights[3] + weights[4] + weights[5]
    previous = jnp.concatenate([initial[None], iterate[:-1]], axis=0)
    residual = heating + previous - ((1.0 + total) * iterate - neighbours(weights, extend(iterate)))
    index = jnp.arange(steps, dtype=jnp.int32)
    scales = corner_weight ** (index.astype(jnp.float32) / steps)
    beta = corner_weight ** (1.0 / steps)
    scaled = residual * scales[:, None, None, None]
    angle = (2.0 * jnp.pi / steps) * ((index[:, None] * index[None, :]) % steps).astype(jnp.float32)
    cosine = jnp.cos(angle)
    sine = jnp.sin(angle)
    high = lax.Precision.HIGHEST
    spec_re = jnp.einsum("kn,nabc->kabc", cosine, scaled, precision=high)
    spec_im = -jnp.einsum("kn,nabc->kabc", sine, scaled, precision=high)
    shift_re = 1.0 - beta * cosine[:, 1]
    shift_im = beta * sine[:, 1]
    diag_re = shift_re[:, None, None, None] + total[None]
    diag_im = shift_im[:, None, None, None] + jnp.zeros_like(total)[None]
    denom = diag_re * diag_re + diag_im * diag_im
    inv_re = diag_re / denom
    inv_im = -diag_im / denom
    sol_re = spec_re * inv_re - spec_im * inv_im
    sol_im = spec_re * inv_im + spec_im * inv_re
    for sweep in range(SWEEPS - 1):
        rhs_re = spec_re + neighbours(weights, extend(sol_re))
        rhs_im = spec_im + neighbours(weights, extend(sol_im))
        sol_re = rhs_re * inv_re - rhs_im * inv_im
        sol_im = rhs_re * inv_im + rhs_im * inv_re
    back = (jnp.einsum("kn,kabc->nabc", cosine, sol_re, precision=high)
            - jnp.einsum("kn,kabc->nabc", sine, sol_im, precision=high)) / steps
    return iterate + back / scales[:, None, None, None]
```

```python
import jax
import jax.numpy as jnp
from jax import lax
from jax.experimental import pallas as pl
from jax.experimental.pallas import tpu as pltpu
from jax.sharding import PartitionSpec as P

SWEEPS = 4


corner_weight = 0.1


def padded(value, sides, width, wrap):
    for axis, dim in sides:
        peers, length = (lax.axis_size(axis), value.shape[dim])
        up = [(i, (i + 1) % peers) for i in range(peers if wrap else peers - 1)]
        down = [(j, i) for i, j in up]
        last = lax.slice_in_dim(value, length - width, length, axis=dim)
        initial = lax.slice_in_dim(value, 0, width, axis=dim)
        before = lax.ppermute(last, axis, up)
        after = lax.ppermute(initial, axis, down)
        value = jnp.concatenate([before, value, after], axis=dim)
    return value


def passed_along(block, axis, distance):
    devices = range(lax.axis_size(axis))
    route = [(i - distance, i) for i in devices if i - distance in devices]
    return lax.ppermute(block, axis, route)


def harmonic(first, second):
    return 2.0 * first * second / (first + second)


def conductivity(region, cond_table):
    classes = jnp.arange(cond_table.shape[0], dtype=jnp.int32)
    onehot = (region[..., None] == classes).astype(jnp.float32)
    return jnp.sum(onehot * cond_table, axis=-1)


def extend(stack):
    lat_ext = padded(stack, (("lat", 2),), 1, False)
    both = padded(lat_ext, (("lon", 3),), 1, True)
    return jnp.pad(both, ((0, 0), (1, 1), (0, 0), (0, 0)))


def face_weights(kext):
    centre = kext[1:-1, 1:-1, 1:-1]
    return (
        harmonic(centre, kext[:-2, 1:-1, 1:-1]),
        harmonic(centre, kext[2:, 1:-1, 1:-1]),
        harmonic(centre, kext[1:-1, :-2, 1:-1]),
        harmonic(centre, kext[1:-1, 2:, 1:-1]),
        harmonic(centre, kext[1:-1, 1:-1, :-2]),
        harmonic(centre, kext[1:-1, 1:-1, 2:]),
    )


def neighbours(weights, ext):
    near = weights[0] * ext[..., :-2, 1:-1, 1:-1] + weights[1] * ext[..., 2:, 1:-1, 1:-1]
    near = near + weights[2] * ext[..., 1:-1, :-2, 1:-1] + weights[3] * ext[..., 1:-1, 2:, 1:-1]
    near = near + weights[4] * ext[..., 1:-1, 1:-1, :-2] + weights[5] * ext[..., 1:-1, 1:-1, 2:]
    return near


def on_device(iterate, heating, initial, region, cond_table):
    steps = lax.axis_size("tm")
    own = lax.axis_index("tm")
    high = lax.Precision.HIGHEST
    kfield = conductivity(region, cond_table)
    ext = extend(jnp.stack([kfield, iterate[0]]))
    weights = face_weights(ext[0])
    total = weights[0] + weights[1] + weights[2] + weights[3] + weights[4] + weights[5]
    shifted = passed_along(iterate, "tm", 1)[0]
    previous = jnp.where(own == 0, initial, shifted)
    residual = heating[0] + previous - ((1.0 + total) * iterate[0] - neighbours(weights, ext[1]))
    scale_own = corner_weight ** (own.astype(jnp.float32) / steps)
    scaled = residual * scale_own
    zeros = jnp.zeros_like(residual)
    piece = lax.all_gather(scaled[None], "tm", axis=0, tiled=True)
    order = jnp.arange(piece.shape[0], dtype=jnp.int32)
    angle = 2.0 * jnp.pi / steps * (own * order % steps).astype(jnp.float32)
    real_part = jnp.einsum("n,nabc->abc", jnp.cos(angle), piece, precision=high)
    imag_part = (zeros, zeros)[1] - jnp.einsum("n,nabc->abc", jnp.sin(angle), piece, precision=high)
    beta = corner_weight ** (1.0 / steps)
    freq_angle = 2.0 * jnp.pi / steps * (own % steps).astype(jnp.float32)
    diag_re = 1.0 - beta * jnp.cos(freq_angle) + total
    diag_im = beta * jnp.sin(freq_angle) + zeros
    denom = diag_re * diag_re + diag_im * diag_im
    inv_re = diag_re / denom
    inv_im = -diag_im / denom
    sol_re = real_part * inv_re - imag_part * inv_im
    sol_im = real_part * inv_im + imag_part * inv_re
    for sweep in range(SWEEPS - 1):
        near = neighbours(weights, extend(jnp.stack([sol_re, sol_im])))
        rhs_re = real_part + near[0]
        rhs_im = imag_part + near[1]
        sol_re = rhs_re * inv_re - rhs_im * inv_im
        sol_im = rhs_re * inv_im + rhs_im * inv_re
    pieces = (
        lax.all_gather(sol_re[None], "tm", axis=0, tiled=True),
        lax.all_gather(sol_im[None], "tm", axis=0, tiled=True),
    )
    order = jnp.arange(pieces[0].shape[0], dtype=jnp.int32)
    angle = 2.0 * jnp.pi / steps * (order * own % steps).astype(jnp.float32)
    summed = jnp.einsum("k,kabc->abc", jnp.cos(angle), pieces[0], precision=high) - jnp.einsum(
        "k,kabc->abc", jnp.sin(angle), pieces[1], precision=high
    )
    back = summed / steps
    return iterate + (back / scale_own)[None]


HALO = 4
TILE = 8
UNROLL = 4


def vmem(count):
    return [pl.BlockSpec(memory_space=pltpu.VMEM)] * count


def call(body, outs, ins, scratch=(), limit=8, smem=0):
    moved = sum(x.size * 4 for x in ins) + sum(x.size * 4 for x in outs)
    return pl.pallas_call(
        body,
        out_shape=outs,
        in_specs=vmem(len(ins) - smem) + [pl.BlockSpec(memory_space=pltpu.SMEM)] * smem,
        out_specs=vmem(len(outs)),
        scratch_shapes=scratch,
        compiler_params=pltpu.CompilerParams(vmem_limit_bytes=limit << 20),
        cost_estimate=pl.CostEstimate(flops=moved * 4, bytes_accessed=moved, transcendentals=0),
    )(*ins)


def shape(*dims):
    return jax.ShapeDtypeStruct(dims, jnp.float32)


def ids(rows, dim, lanes=128):
    return lax.broadcasted_iota(jnp.int32, (rows, lanes), dim)


def other_half(lane, t):
    return ((lane + 64 * t) & 127) >= 64


def loop(count, step, unroll=UNROLL):
    def body(i, carry):
        for u in range(unroll):
            step(i * unroll + u)
        return carry

    lax.fori_loop(0, count // unroll, body, 0)


def pack_halves(read, out, base, half, mask):
    def step(l):
        out[base + l] = jnp.where(mask, read(l), pltpu.roll(read(l + half), 64, 1))

    loop(half, step)


def pack_strip(read, out, base, levels, first, rows):
    group = ids(rows, 1) // HALO
    for G in range(levels // 32):
        acc = jnp.zeros((rows, 128), jnp.float32)
        for g in range(32):
            moved = pltpu.roll(read(32 * G + g), (HALO * g + 128 - first) & 127, 1)
            acc = jnp.where(group == g, moved, acc)
        out[base + G] = acc


def send_own(it, h, xm, down, up):
    t = lax.axis_index("tm")
    levels = it.shape[0]
    half = levels // 2
    rows = it.shape[1]
    mask = other_half(ids(rows, 1), t)
    for f, ref in enumerate((it, h)):
        pack_halves(lambda l: ref[l], xm, f * half, half, mask)
    for f, ref in enumerate((it, h)):
        pack_strip(lambda l: ref[l], xm, 2 * half + f * (levels // 32), levels, 60 + 4 * t, rows)
    edge_rows(it, h, down, up)


def edge_rows(first, second, down, up):
    top = ids(TILE, 0) < HALO
    rows = first.shape[1]

    def step(l):
        down[l] = jnp.where(top, first[l, :TILE], pltpu.roll(second[l, :TILE], HALO, 0))
        up[l] = jnp.where(top, pltpu.roll(first[l, rows - TILE :], HALO, 0), second[l, rows - TILE :])

    loop(first.shape[0], step)


def send_fixed(region, initial, table, kap, down, up):
    def step(l):
        classes = region[l]
        value = jnp.full(classes.shape, table[0], jnp.float32)
        for c in range(1, table.shape[0]):
            value = jnp.where(classes == c, table[c], value)
        kap[l] = value

    loop(region.shape[0], step)
    edge_rows(kap, initial, down, up)


def halo_tiles(after, before):
    top = ids(TILE, 0) < HALO
    return (
        jnp.where(top, after, pltpu.roll(before, HALO, 0)),
        jnp.where(top, pltpu.roll(after, HALO, 0), before),
    )


def send_halo(after, before, xe, hit, hh):
    t = lax.axis_index("tm")
    levels = after.shape[0]
    half = levels // 2

    def step(l):
        hit[l], hh[l] = halo_tiles(after[l], before[l])

    loop(levels, step)
    mask = other_half(ids(TILE, 1), t)
    for f, ref in enumerate((hit, hh)):
        pack_halves(lambda l: ref[l], xe, f * half, half, mask)
        pack_strip(lambda l: ref[l], xe, 2 * half + f * (levels // 32), levels, 60 + 4 * t, TILE)


def send_sides(it, h, hit, hh, same, cross):
    t = lax.axis_index("tm")
    levels = it.shape[0]
    for f, (own, halo) in enumerate(((it, hit), (h, hh))):
        def read(l):
            return jnp.concatenate([own[l], halo[l]], axis=0)

        base = f * (levels // 32)
        pack_strip(read, same, base, levels, 124 * (1 - t), own.shape[1] + TILE)
        pack_strip(read, cross, base, levels, 124 * t, own.shape[1] + TILE)


def send_fixed_sides(kap, initial, after, before, same):
    t = lax.axis_index("tm")
    levels = kap.shape[0]
    for f, own in enumerate((kap, initial)):
        def read(l):
            return jnp.concatenate([own[l], halo_tiles(after[l], before[l])[f]], axis=0)

        pack_strip(read, same, f * (levels // 32), levels, 124 * (1 - t), own.shape[1] + TILE)


def face(a, b):
    return 2.0 * a * b / jnp.maximum(a + b, 1e-30)


def iterate_block(
    it, h, hit, hh, kap, initial, after, before, xm, xe, same, cross, fixed,
    w_own, w_send,
    K, it0, it1, s0, s1, wl, wy, wyp, wx, wxp, inv0, inv1, x0, x1, y0, y1,
):
    t = lax.axis_index("tm")
    levels, own_rows = it.shape[0], it.shape[1]
    half, groups = levels // 2, levels // 32
    rows = own_rows + TILE
    lane = ids(rows, 1)
    outer_at = 124 * (1 - t)
    inner_at = 64 - 4 * t
    outer = ((lane + 128 - outer_at) & 127) < HALO
    inner = ((lane + 128 - inner_at) & 127) < HALO
    first = t == 0
    zero = jnp.zeros((rows, 128), jnp.float32)

    def cat(a, b):
        return jnp.concatenate([a, b], axis=0)

    def strip(value, g, at):
        return pltpu.roll(value, (at + 256 - HALO * g) & 127, 1)

    def assemble(g):
        for part in range(groups):
            l = 32 * part + g
            halo_k, halo_i = halo_tiles(after[l], before[l])
            K[l + 1] = jnp.where(outer, strip(fixed[part], g, outer_at), cat(kap[l], halo_k))
            start = jnp.where(outer, strip(fixed[groups + part], g, outer_at), cat(initial[l], halo_i))
            fields = []
            for f, (own, halo) in enumerate(((it, hit), (h, hh))):
                mine = jnp.where(outer, strip(same[f * groups + part], g, outer_at), cat(own[l], halo[l]))
                at = f * half + (l if part < groups // 2 else l - half)
                theirs = cat(xm[at], xe[at])
                if part >= groups // 2:
                    theirs = pltpu.roll(theirs, 64, 1)
                at = 2 * half + f * groups + part
                theirs = jnp.where(inner, strip(cat(xm[at], xe[at]), g, inner_at), theirs)
                theirs = jnp.where(outer, strip(cross[f * groups + part], g, outer_at), theirs)
                fields.append((jnp.where(first, mine, theirs), jnp.where(first, theirs, mine)))
            (i0, i1), (h0, h1) = fields
            it0[l + 1] = i0
            it1[l + 1] = i1
            s0[l] = h0 + start
            s1[l] = h1 + i0

    for ref in (K, it0, it1, x0, x1, y0, y1):
        ref[0] = zero
        ref[levels + 1] = zero
    loop(32, assemble, 2)

    def near(ref, l, w):
        mid = ref[l + 1]
        total = w[0] * ref[l] + w[1] * ref[l + 2]
        total = total + (w[2] * pltpu.roll(mid, 1, 0) + w[3] * pltpu.roll(mid, rows - 1, 0))
        return total + (w[4] * pltpu.roll(mid, 1, 1) + w[5] * pltpu.roll(mid, 127, 1))

    beta = corner_weight ** 0.5

    wl[0] = zero

    def weigh(l):
        here = K[l + 1]
        high = face(here, K[l + 2])
        next_row = face(here, pltpu.roll(here, rows - 1, 0))
        next_lane = face(here, pltpu.roll(here, 127, 1))
        last_row = pltpu.roll(next_row, 1, 0)
        last_lane = pltpu.roll(next_lane, 1, 1)
        low = wl[l]
        wl[l + 1] = high
        wy[l] = next_row
        wyp[l] = last_row
        wx[l] = next_lane
        wxp[l] = last_lane
        w = (low, high, last_row, next_row, last_lane, next_lane)
        total = w[0] + w[1] + w[2] + w[3] + w[4] + w[5]
        r0 = s0[l] - ((1.0 + total) * it0[l + 1] - near(it0, l, w))
        r1 = s1[l] - ((1.0 + total) * it1[l + 1] - near(it1, l, w))
        r1 = r1 * beta
        spec0 = r0 + r1
        spec1 = r0 - r1
        i0 = 1.0 / ((1.0 - beta) + total)
        i1 = 1.0 / ((1.0 + beta) + total)
        s0[l] = spec0
        s1[l] = spec1
        inv0[l] = i0
        inv1[l] = i1
        x0[l + 1] = spec0 * i0
        x1[l + 1] = spec1 * i1

    loop(levels, weigh, 2)

    def sweep(l, a0, a1):
        w = (wl[l], wl[l + 1], wyp[l], wy[l], wxp[l], wx[l])
        return (s0[l] + near(a0, l, w)) * inv0[l], (s1[l] + near(a1, l, w)) * inv1[l]

    def plain(a0, a1, b0, b1):
        def step(l):
            b0[l + 1], b1[l + 1] = sweep(l, a0, a1)

        loop(levels, step)

    plain(x0, x1, y0, y1)
    plain(y0, y1, x0, x1)
    handled = jnp.logical_not(other_half(ids(own_rows, 1), t))

    def last(l):
        theirs = []
        for at in (l, l + half):
            a, b = sweep(at, x0, x1)
            w0 = (a + b)[:own_rows] * 0.5
            w1 = (a - b)[:own_rows] * (0.5 / beta)
            w_own[at] = jnp.where(first, w0, w1)
            theirs.append(jnp.where(first, w1, w0))
        w_send[l] = jnp.where(handled, theirs[0], pltpu.roll(theirs[1], 64, 1))

    loop(half, last, 2)


def finish(it, w_own, got, out):
    t = lax.axis_index("tm")
    levels, rows = it.shape[0], it.shape[1]
    half = levels // 2
    handled = jnp.logical_not(other_half(ids(rows, 1), t))

    def step(l):
        theirs = got[l]
        out[l] = it[l] + jnp.where(handled, w_own[l], theirs)
        out[l + half] = it[l + half] + jnp.where(handled, w_own[l + half], pltpu.roll(theirs, 64, 1))

    loop(half, step)


def two_steps(iterate, heating, initial, region, cond_table):
    it, h = iterate[0], heating[0]
    levels, rows, lanes = it.shape
    half, groups = levels // 2, levels // 32
    lats, lons = lax.axis_size("lat"), lax.axis_size("lon")
    swap = [(0, 1), (1, 0)]
    rise = [(i, i + 1) for i in range(lats - 1)]
    fall = [(i + 1, i) for i in range(lats - 1)]
    after_lon = [(j + 1) % lons for j in range(lons)]
    straight = [(j, after_lon[j]) for j in range(lons)] + [(lons + after_lon[j], lons + j) for j in range(lons)]
    crossing = [(lons + j, after_lon[j]) for j in range(lons)] + [(after_lon[j], lons + j) for j in range(lons)]
    both = ("tm", "lon")
    sides = shape(2 * groups, rows + TILE, lanes)

    xm, down, up = call(
        send_own,
        [shape(levels + 2 * groups, rows, lanes), shape(levels, TILE, lanes), shape(levels, TILE, lanes)],
        [it, h],
    )
    xm = lax.ppermute(xm, "tm", swap)
    after = lax.ppermute(down, "lat", fall)
    before = lax.ppermute(up, "lat", rise)
    kap, fixed_down, fixed_up = call(
        send_fixed,
        [shape(levels, rows, lanes), shape(levels, TILE, lanes), shape(levels, TILE, lanes)],
        [region, initial, cond_table],
        smem=1,
    )
    fixed_after = lax.ppermute(fixed_down, "lat", fall)
    fixed_before = lax.ppermute(fixed_up, "lat", rise)
    xe, hit, hh = call(
        send_halo,
        [shape(levels + 2 * groups, TILE, lanes), shape(levels, TILE, lanes), shape(levels, TILE, lanes)],
        [after, before],
    )
    xe = lax.ppermute(xe, "tm", swap)
    same, cross = call(send_sides, [sides, sides], [it, h, hit, hh])
    same = lax.ppermute(same, both, straight)
    cross = lax.ppermute(cross, both, crossing)
    (fixed,) = call(send_fixed_sides, [sides], [kap, initial, fixed_after, fixed_before])
    fixed = lax.ppermute(fixed, both, straight)
    deep = pltpu.VMEM((levels + 2, rows + TILE, lanes), jnp.float32)
    flat = pltpu.VMEM((levels, rows + TILE, lanes), jnp.float32)
    w_own, w_send = call(
        iterate_block,
        [shape(levels, rows, lanes), shape(half, rows, lanes)],
        [it, h, hit, hh, kap, initial, fixed_after, fixed_before, xm, xe, same, cross, fixed],
        scratch=[deep] * 3 + [flat] * 2 + [deep] + [flat] * 6 + [deep] * 4,
        limit=32,
    )
    got = lax.ppermute(w_send, "tm", swap)
    (out,) = call(finish, [shape(levels, rows, lanes)], [it, w_own, got])
    return out[None]


def solution(mesh):
    return jax.shard_map(
        two_steps if mesh.shape["tm"] == 2 else on_device,
        mesh=mesh,
        in_specs=(
            P("tm", None, "lat", "lon"),
            P("tm", None, "lat", "lon"),
            P(None, "lat", "lon"),
            P(None, "lat", "lon"),
            P(),
        ),
        out_specs=P("tm", None, "lat", "lon"),
        check_vma=False,
    )
```

```python
import jax
import jax.numpy as jnp
from jax import lax
from jax.experimental import pallas as pl
from jax.experimental.pallas import tpu as pltpu
from jax.sharding import PartitionSpec as P

SWEEPS = 4


corner_weight = 0.1


def padded(value, sides, width, wrap):
    for axis, dim in sides:
        peers, length = (lax.axis_size(axis), value.shape[dim])
        up = [(i, (i + 1) % peers) for i in range(peers if wrap else peers - 1)]
        down = [(j, i) for i, j in up]
        last = lax.slice_in_dim(value, length - width, length, axis=dim)
        initial = lax.slice_in_dim(value, 0, width, axis=dim)
        before = lax.ppermute(last, axis, up)
        after = lax.ppermute(initial, axis, down)
        value = jnp.concatenate([before, value, after], axis=dim)
    return value


def passed_along(block, axis, distance):
    devices = range(lax.axis_size(axis))
    route = [(i - distance, i) for i in devices if i - distance in devices]
    return lax.ppermute(block, axis, route)


def harmonic(first, second):
    return 2.0 * first * second / (first + second)


def conductivity(region, cond_table):
    classes = jnp.arange(cond_table.shape[0], dtype=jnp.int32)
    onehot = (region[..., None] == classes).astype(jnp.float32)
    return jnp.sum(onehot * cond_table, axis=-1)


def extend(stack):
    lat_ext = padded(stack, (("lat", 2),), 1, False)
    both = padded(lat_ext, (("lon", 3),), 1, True)
    return jnp.pad(both, ((0, 0), (1, 1), (0, 0), (0, 0)))


def face_weights(kext):
    centre = kext[1:-1, 1:-1, 1:-1]
    return (
        harmonic(centre, kext[:-2, 1:-1, 1:-1]),
        harmonic(centre, kext[2:, 1:-1, 1:-1]),
        harmonic(centre, kext[1:-1, :-2, 1:-1]),
        harmonic(centre, kext[1:-1, 2:, 1:-1]),
        harmonic(centre, kext[1:-1, 1:-1, :-2]),
        harmonic(centre, kext[1:-1, 1:-1, 2:]),
    )


def neighbours(weights, ext):
    near = weights[0] * ext[..., :-2, 1:-1, 1:-1] + weights[1] * ext[..., 2:, 1:-1, 1:-1]
    near = near + weights[2] * ext[..., 1:-1, :-2, 1:-1] + weights[3] * ext[..., 1:-1, 2:, 1:-1]
    near = near + weights[4] * ext[..., 1:-1, 1:-1, :-2] + weights[5] * ext[..., 1:-1, 1:-1, 2:]
    return near


def on_device(iterate, heating, initial, region, cond_table):
    steps = lax.axis_size("tm")
    own = lax.axis_index("tm")
    high = lax.Precision.HIGHEST
    kfield = conductivity(region, cond_table)
    ext = extend(jnp.stack([kfield, iterate[0]]))
    weights = face_weights(ext[0])
    total = weights[0] + weights[1] + weights[2] + weights[3] + weights[4] + weights[5]
    shifted = passed_along(iterate, "tm", 1)[0]
    previous = jnp.where(own == 0, initial, shifted)
    residual = heating[0] + previous - ((1.0 + total) * iterate[0] - neighbours(weights, ext[1]))
    scale_own = corner_weight ** (own.astype(jnp.float32) / steps)
    scaled = residual * scale_own
    zeros = jnp.zeros_like(residual)
    piece = lax.all_gather(scaled[None], "tm", axis=0, tiled=True)
    order = jnp.arange(piece.shape[0], dtype=jnp.int32)
    angle = 2.0 * jnp.pi / steps * (own * order % steps).astype(jnp.float32)
    real_part = jnp.einsum("n,nabc->abc", jnp.cos(angle), piece, precision=high)
    imag_part = (zeros, zeros)[1] - jnp.einsum("n,nabc->abc", jnp.sin(angle), piece, precision=high)
    beta = corner_weight ** (1.0 / steps)
    freq_angle = 2.0 * jnp.pi / steps * (own % steps).astype(jnp.float32)
    diag_re = 1.0 - beta * jnp.cos(freq_angle) + total
    diag_im = beta * jnp.sin(freq_angle) + zeros
    denom = diag_re * diag_re + diag_im * diag_im
    inv_re = diag_re / denom
    inv_im = -diag_im / denom
    sol_re = real_part * inv_re - imag_part * inv_im
    sol_im = real_part * inv_im + imag_part * inv_re
    for sweep in range(SWEEPS - 1):
        near = neighbours(weights, extend(jnp.stack([sol_re, sol_im])))
        rhs_re = real_part + near[0]
        rhs_im = imag_part + near[1]
        sol_re = rhs_re * inv_re - rhs_im * inv_im
        sol_im = rhs_re * inv_im + rhs_im * inv_re
    pieces = (
        lax.all_gather(sol_re[None], "tm", axis=0, tiled=True),
        lax.all_gather(sol_im[None], "tm", axis=0, tiled=True),
    )
    order = jnp.arange(pieces[0].shape[0], dtype=jnp.int32)
    angle = 2.0 * jnp.pi / steps * (order * own % steps).astype(jnp.float32)
    summed = jnp.einsum("k,kabc->abc", jnp.cos(angle), pieces[0], precision=high) - jnp.einsum(
        "k,kabc->abc", jnp.sin(angle), pieces[1], precision=high
    )
    back = summed / steps
    return iterate + (back / scale_own)[None]


HALO = 4
TILE = 8


def vmem(count):
    return [pl.BlockSpec(memory_space=pltpu.VMEM)] * count


def call(body, outs, ins, scratch=(), limit=8, smem=0):
    moved = sum(x.size * 4 for x in ins) + sum(x.size * 4 for x in outs)
    return pl.pallas_call(
        body,
        out_shape=outs,
        in_specs=vmem(len(ins) - smem) + [pl.BlockSpec(memory_space=pltpu.SMEM)] * smem,
        out_specs=vmem(len(outs)),
        scratch_shapes=scratch,
        compiler_params=pltpu.CompilerParams(vmem_limit_bytes=limit << 20),
        cost_estimate=pl.CostEstimate(flops=moved * 4, bytes_accessed=moved, transcendentals=0),
    )(*ins)


def shape(*dims):
    return jax.ShapeDtypeStruct(dims, jnp.float32)


def ids(rows, dim, lanes=128):
    return lax.broadcasted_iota(jnp.int32, (rows, lanes), dim)


def other_half(lane, t):
    return ((lane + 64 * t) & 127) >= 64


def cat(a, b):
    return jnp.concatenate([a, b], axis=0)


def blocks(count, width, read, write):
    def body(i, carry):
        levels = [i * width + u for u in range(width)]
        values = [read(l) for l in levels]
        for l, value in zip(levels, values):
            write(l, value)
        return carry

    lax.fori_loop(0, count // width, body, 0)


def put(*refs, at=0):
    def write(l, values):
        for ref, value in zip(refs, values):
            ref[l + at] = value

    return write


def pack_halves(read, out, base, half, mask):
    blocks(half, 8, lambda l: (jnp.where(mask, read(l), pltpu.roll(read(l + half), 64, 1)),), put(out, at=base))


def pack_strip(read, out, base, levels, first, rows):
    group = ids(rows, 1) // HALO
    for G in range(levels // 32):
        acc = jnp.zeros((rows, 128), jnp.float32)
        for g in range(32):
            moved = pltpu.roll(read(32 * G + g), (HALO * g + 128 - first) & 127, 1)
            acc = jnp.where(group == g, moved, acc)
        out[base + G] = acc


def send_main(it, h, xm):
    t = lax.axis_index("tm")
    levels, rows = it.shape[:2]
    half = levels // 2
    mask = other_half(ids(rows, 1), t)
    for f, ref in enumerate((it, h)):
        pack_halves(lambda l: ref[l], xm, f * half, half, mask)
    for f, ref in enumerate((it, h)):
        pack_strip(lambda l: ref[l], xm, 2 * half + f * (levels // 32), levels, 60 + 4 * t, rows)


def even_lat():
    return lax.rem(lax.axis_index("lat"), 2) == 0


def edge_rows(first, second, near_pair, far_pair):
    top = ids(TILE, 0) < HALO
    rows = first.shape[1]
    even = even_lat()

    def read(l):
        down = jnp.where(top, first[l, :TILE], pltpu.roll(second[l, :TILE], HALO, 0))
        up = jnp.where(top, pltpu.roll(first[l, rows - TILE :], HALO, 0), second[l, rows - TILE :])
        return jnp.where(even, up, down), jnp.where(even, down, up)

    blocks(first.shape[0], 8, read, put(near_pair, far_pair))


def send_fixed(region, initial, table, kap, near_pair, far_pair):
    def read(l):
        classes = region[l]
        value = jnp.full(classes.shape, table[0], jnp.float32)
        for c in range(1, table.shape[0]):
            value = jnp.where(classes == c, table[c], value)
        return (value,)

    blocks(region.shape[0], 8, read, put(kap))
    edge_rows(kap, initial, near_pair, far_pair)


def halo_tiles(near_pair, far_pair):
    even = even_lat()
    after = jnp.where(even, near_pair, far_pair)
    before = jnp.where(even, far_pair, near_pair)
    top = ids(TILE, 0) < HALO
    return (
        jnp.where(top, after, pltpu.roll(before, HALO, 0)),
        jnp.where(top, pltpu.roll(after, HALO, 0), before),
    )


def send_halo(near_pair, far_pair, xe, hit, hh):
    t = lax.axis_index("tm")
    levels = near_pair.shape[0]
    half = levels // 2
    blocks(levels, 8, lambda l: halo_tiles(near_pair[l], far_pair[l]), put(hit, hh))
    mask = other_half(ids(TILE, 1), t)
    for f, ref in enumerate((hit, hh)):
        pack_halves(lambda l: ref[l], xe, f * half, half, mask)
        pack_strip(lambda l: ref[l], xe, 2 * half + f * (levels // 32), levels, 60 + 4 * t, TILE)


def send_sides(it, h, hit, hh, kap, initial, near_pair, far_pair, same, cross, hk, hi):
    t = lax.axis_index("tm")
    levels = it.shape[0]
    blocks(levels, 8, lambda l: halo_tiles(near_pair[l], far_pair[l]), put(hk, hi))
    for f, (own, halo) in enumerate(((it, hit), (h, hh), (kap, hk), (initial, hi))):
        def read(l):
            return cat(own[l], halo[l])

        base = f * (levels // 32)
        if f < 2:
            pack_strip(read, same, base, levels, 124 * (1 - t), own.shape[1] + TILE)
        pack_strip(read, cross, base, levels, 124 * t, own.shape[1] + TILE)


def face(a, b):
    return 2.0 * a * b / jnp.maximum(a + b, 1e-30)


def strip(value, g, at):
    return pltpu.roll(value, (at + 256 - HALO * g) & 127, 1)


def lanes_from(lane, at):
    return ((lane + 128 - at) & 127) < HALO


def near(low, mid, high, wl, wh, wy, wx):
    rows = mid.shape[0]
    total = wl * low + wh * high
    total = total + (wy * pltpu.roll(mid, rows - 1, 0) + pltpu.roll(wy * mid, 1, 0))
    return total + (wx * pltpu.roll(mid, 127, 1) + pltpu.roll(wx * mid, 1, 1))


def prepare(
    it, h, hit, hh, kap, initial, hk, hi, same, cross,
    wl, wy, wx, total, inv0, inv1, part, extra,
    K, own_it,
):
    t = lax.axis_index("tm")
    levels, own_rows = it.shape[:2]
    groups = levels // 32
    rows = own_rows + TILE
    outer_at = 124 * (1 - t)
    outer = lanes_from(ids(rows, 1), outer_at)
    first = t == 0
    zero = jnp.zeros((rows, 128), jnp.float32)
    beta = corner_weight ** 0.5
    for ref in (K, own_it):
        ref[0] = zero
        ref[levels + 1] = zero
    wl[0] = zero

    def assemble(g):
        found = []
        for G in range(groups):
            l = 32 * G + g
            k = jnp.where(outer, strip(cross[2 * groups + G], g, outer_at), cat(kap[l], hk[l]))
            start = jnp.where(outer, strip(cross[3 * groups + G], g, outer_at), cat(initial[l], hi[l]))
            mine = jnp.where(outer, strip(same[G], g, outer_at), cat(it[l], hit[l]))
            heat = jnp.where(outer, strip(same[groups + G], g, outer_at), cat(h[l], hh[l]))
            found.append((k, mine, jnp.where(first, heat + start, heat), jnp.where(first, mine, start)))
        return found

    def store(g, found):
        for G in range(groups):
            k, mine, source, other = found[G]
            l = 32 * G + g
            K[l + 1] = k
            own_it[l + 1] = mine
            part[l] = source
            extra[l] = other

    blocks(32, 4, assemble, store)

    def weigh(l):
        here = K[l + 1]
        high = face(here, K[l + 2])
        low = face(K[l], here)
        row = face(here, pltpu.roll(here, rows - 1, 0))
        lane = face(here, pltpu.roll(here, 127, 1))
        sums = low + high + (row + pltpu.roll(row, 1, 0)) + (lane + pltpu.roll(lane, 1, 1))
        mid = own_it[l + 1]
        left = part[l] - ((1.0 + sums) * mid - near(own_it[l], mid, own_it[l + 2], low, high, row, lane))
        return high, row, lane, sums, 1.0 / ((1.0 - beta) + sums), 1.0 / ((1.0 + beta) + sums), left

    def keep(l, values):
        wl[l + 1] = values[0]
        put(wy, wx, total, inv0, inv1, part)(l, values[1:])

    blocks(levels, 4, weigh, keep)


def iterate_block(
    wl, wy, wx, total, inv0, inv1, part, extra, xm, xe, cross,
    w_own, w_send,
    it, s0, s1, x0, x1, y0, y1,
):
    t = lax.axis_index("tm")
    levels, rows = wy.shape[:2]
    own_rows = rows - TILE
    half, groups = levels // 2, levels // 32
    lane = ids(rows, 1)
    outer_at = 124 * (1 - t)
    inner_at = 64 - 4 * t
    outer = lanes_from(lane, outer_at)
    inner = lanes_from(lane, inner_at)
    first = t == 0
    zero = jnp.zeros((rows, 128), jnp.float32)
    beta = corner_weight ** 0.5
    for ref in (it, x0, x1, y0, y1):
        ref[0] = zero
        ref[levels + 1] = zero

    def assemble(g):
        found = []
        for G in range(groups):
            l = 32 * G + g
            for f in range(2):
                high = G >= groups // 2
                at = f * half + (l - half if high else l)
                theirs = cat(xm[at], xe[at])
                if high:
                    theirs = pltpu.roll(theirs, 64, 1)
                at = 2 * half + f * groups + G
                theirs = jnp.where(inner, strip(cat(xm[at], xe[at]), g, inner_at), theirs)
                found.append(jnp.where(outer, strip(cross[f * groups + G], g, outer_at), theirs))
        return found

    def store(g, found):
        for G in range(groups):
            it[32 * G + g + 1] = found[2 * G]
            s0[32 * G + g] = found[2 * G + 1]

    blocks(32, 4, assemble, store)

    def residual(l):
        mid = it[l + 1]
        theirs = s0[l] + extra[l] - (
            (1.0 + total[l]) * mid - near(it[l], mid, it[l + 2], wl[l], wl[l + 1], wy[l], wx[l])
        )
        mine = part[l] + jnp.where(first, 0.0, 1.0) * mid
        r0 = jnp.where(first, mine, theirs)
        r1 = jnp.where(first, theirs, mine) * beta
        a, b = r0 + r1, r0 - r1
        return a, b, a * inv0[l], b * inv1[l]

    def keep(l, values):
        put(s0, s1)(l, values)
        put(x0, x1, at=1)(l, values[2:])

    blocks(levels, 4, residual, keep)

    def sweep(l, a, spec, inv):
        return (spec[l] + near(a[l], a[l + 1], a[l + 2], wl[l], wl[l + 1], wy[l], wx[l])) * inv[l]

    def both(l, a0, a1):
        return sweep(l, a0, s0, inv0), sweep(l, a1, s1, inv1)

    blocks(levels, 4, lambda l: both(l, x0, x1), put(y0, y1, at=1))
    blocks(levels, 4, lambda l: both(l, y0, y1), put(x0, x1, at=1))
    handled = jnp.logical_not(other_half(ids(own_rows, 1), t))

    def last(l):
        mine, theirs = [], []
        for at in (l, l + half):
            a, b = both(at, x0, x1)
            w0 = (a + b)[:own_rows] * 0.5
            w1 = (a - b)[:own_rows] * (0.5 / beta)
            mine.append(jnp.where(first, w0, w1))
            theirs.append(jnp.where(first, w1, w0))
        return mine[0], mine[1], jnp.where(handled, theirs[0], pltpu.roll(theirs[1], 64, 1))

    def give(l, values):
        w_own[l], w_own[l + half], w_send[l] = values

    blocks(half, 2, last, give)


def finish(it, w_own, got, out):
    t = lax.axis_index("tm")
    levels, rows = it.shape[:2]
    half = levels // 2
    handled = jnp.logical_not(other_half(ids(rows, 1), t))

    def read(l):
        theirs = got[l]
        return (
            it[l] + jnp.where(handled, w_own[l], theirs),
            it[l + half] + jnp.where(handled, w_own[l + half], pltpu.roll(theirs, 64, 1)),
        )

    def write(l, values):
        out[l], out[l + half] = values

    blocks(half, 4, read, write)


def two_steps(iterate, heating, initial, region, cond_table):
    it, h = iterate[0], heating[0]
    levels, rows, lanes = it.shape
    half, groups = levels // 2, levels // 32
    lats, lons = lax.axis_size("lat"), lax.axis_size("lon")
    swap = [(0, 1), (1, 0)]
    pairs = [[(i, i + 1) for i in range(start, lats - 1, 2)] for start in (0, 1)]
    pairs = [p + [(j, i) for i, j in p] for p in pairs]
    after_lon = [(j + 1) % lons for j in range(lons)]
    straight = [(j, after_lon[j]) for j in range(lons)] + [(lons + after_lon[j], lons + j) for j in range(lons)]
    crossing = [(lons + j, after_lon[j]) for j in range(lons)] + [(after_lon[j], lons + j) for j in range(lons)]
    both = ("tm", "lon")
    full = shape(levels, rows, lanes)
    tile = shape(levels, TILE, lanes)
    wide = shape(levels, rows + TILE, lanes)

    (xm,) = call(send_main, [shape(levels + 2 * groups, rows, lanes)], [it, h])
    xm = lax.ppermute(xm, "tm", swap)
    near_rows, far_rows = call(edge_rows, [tile, tile], [it, h])
    near_rows = lax.ppermute(near_rows, "lat", pairs[0])
    far_rows = lax.ppermute(far_rows, "lat", pairs[1])
    kap, near_fixed, far_fixed = call(send_fixed, [full, tile, tile], [region, initial, cond_table], smem=1)
    near_fixed = lax.ppermute(near_fixed, "lat", pairs[0])
    far_fixed = lax.ppermute(far_fixed, "lat", pairs[1])
    xe, hit, hh = call(send_halo, [shape(levels + 2 * groups, TILE, lanes), tile, tile], [near_rows, far_rows])
    xe = lax.ppermute(xe, "tm", swap)
    same, cross, hk, hi = call(
        send_sides,
        [shape(2 * groups, rows + TILE, lanes), shape(4 * groups, rows + TILE, lanes), tile, tile],
        [it, h, hit, hh, kap, initial, near_fixed, far_fixed],
    )
    same = lax.ppermute(same, both, straight)
    cross = lax.ppermute(cross, both, crossing)
    deep = pltpu.VMEM((levels + 2, rows + TILE, lanes), jnp.float32)
    flat = pltpu.VMEM((levels, rows + TILE, lanes), jnp.float32)
    ready = call(
        prepare,
        [shape(levels + 1, rows + TILE, lanes)] + [wide] * 7,
        [it, h, hit, hh, kap, initial, hk, hi, same, cross],
        scratch=[deep] * 2,
        limit=16,
    )
    w_own, w_send = call(
        iterate_block,
        [full, shape(half, rows, lanes)],
        [*ready, xm, xe, cross],
        scratch=[deep] + [flat] * 2 + [deep] * 4,
        limit=24,
    )
    got = lax.ppermute(w_send, "tm", swap)
    (out,) = call(finish, [full], [it, w_own, got])
    return out[None]


def solution(mesh):
    return jax.shard_map(
        two_steps if mesh.shape["tm"] == 2 else on_device,
        mesh=mesh,
        in_specs=(
            P("tm", None, "lat", "lon"),
            P("tm", None, "lat", "lon"),
            P(None, "lat", "lon"),
            P(None, "lat", "lon"),
            P(),
        ),
        out_specs=P("tm", None, "lat", "lon"),
        check_vma=False,
    )
```

```python
import jax
import jax.numpy as jnp
from jax import lax
from jax.experimental import pallas as pl
from jax.experimental.pallas import tpu as pltpu
from jax.sharding import PartitionSpec as P

SWEEPS = 4


corner_weight = 0.1


def padded(value, sides, width, wrap):
    for axis, dim in sides:
        peers, length = (lax.axis_size(axis), value.shape[dim])
        up = [(i, (i + 1) % peers) for i in range(peers if wrap else peers - 1)]
        down = [(j, i) for i, j in up]
        last = lax.slice_in_dim(value, length - width, length, axis=dim)
        initial = lax.slice_in_dim(value, 0, width, axis=dim)
        before = lax.ppermute(last, axis, up)
        after = lax.ppermute(initial, axis, down)
        value = jnp.concatenate([before, value, after], axis=dim)
    return value


def passed_along(block, axis, distance):
    devices = range(lax.axis_size(axis))
    route = [(i - distance, i) for i in devices if i - distance in devices]
    return lax.ppermute(block, axis, route)


def harmonic(first, second):
    return 2.0 * first * second / (first + second)


def conductivity(region, cond_table):
    classes = jnp.arange(cond_table.shape[0], dtype=jnp.int32)
    onehot = (region[..., None] == classes).astype(jnp.float32)
    return jnp.sum(onehot * cond_table, axis=-1)


def extend(stack):
    lat_ext = padded(stack, (("lat", 2),), 1, False)
    both = padded(lat_ext, (("lon", 3),), 1, True)
    return jnp.pad(both, ((0, 0), (1, 1), (0, 0), (0, 0)))


def face_weights(kext):
    centre = kext[1:-1, 1:-1, 1:-1]
    return (
        harmonic(centre, kext[:-2, 1:-1, 1:-1]),
        harmonic(centre, kext[2:, 1:-1, 1:-1]),
        harmonic(centre, kext[1:-1, :-2, 1:-1]),
        harmonic(centre, kext[1:-1, 2:, 1:-1]),
        harmonic(centre, kext[1:-1, 1:-1, :-2]),
        harmonic(centre, kext[1:-1, 1:-1, 2:]),
    )


def neighbours(weights, ext):
    near = weights[0] * ext[..., :-2, 1:-1, 1:-1] + weights[1] * ext[..., 2:, 1:-1, 1:-1]
    near = near + weights[2] * ext[..., 1:-1, :-2, 1:-1] + weights[3] * ext[..., 1:-1, 2:, 1:-1]
    near = near + weights[4] * ext[..., 1:-1, 1:-1, :-2] + weights[5] * ext[..., 1:-1, 1:-1, 2:]
    return near


def on_device(iterate, heating, initial, region, cond_table):
    steps = lax.axis_size("tm")
    own = lax.axis_index("tm")
    high = lax.Precision.HIGHEST
    kfield = conductivity(region, cond_table)
    ext = extend(jnp.stack([kfield, iterate[0]]))
    weights = face_weights(ext[0])
    total = weights[0] + weights[1] + weights[2] + weights[3] + weights[4] + weights[5]
    shifted = passed_along(iterate, "tm", 1)[0]
    previous = jnp.where(own == 0, initial, shifted)
    residual = heating[0] + previous - ((1.0 + total) * iterate[0] - neighbours(weights, ext[1]))
    scale_own = corner_weight ** (own.astype(jnp.float32) / steps)
    scaled = residual * scale_own
    zeros = jnp.zeros_like(residual)
    piece = lax.all_gather(scaled[None], "tm", axis=0, tiled=True)
    order = jnp.arange(piece.shape[0], dtype=jnp.int32)
    angle = 2.0 * jnp.pi / steps * (own * order % steps).astype(jnp.float32)
    real_part = jnp.einsum("n,nabc->abc", jnp.cos(angle), piece, precision=high)
    imag_part = (zeros, zeros)[1] - jnp.einsum("n,nabc->abc", jnp.sin(angle), piece, precision=high)
    beta = corner_weight ** (1.0 / steps)
    freq_angle = 2.0 * jnp.pi / steps * (own % steps).astype(jnp.float32)
    diag_re = 1.0 - beta * jnp.cos(freq_angle) + total
    diag_im = beta * jnp.sin(freq_angle) + zeros
    denom = diag_re * diag_re + diag_im * diag_im
    inv_re = diag_re / denom
    inv_im = -diag_im / denom
    sol_re = real_part * inv_re - imag_part * inv_im
    sol_im = real_part * inv_im + imag_part * inv_re
    for sweep in range(SWEEPS - 1):
        near = neighbours(weights, extend(jnp.stack([sol_re, sol_im])))
        rhs_re = real_part + near[0]
        rhs_im = imag_part + near[1]
        sol_re = rhs_re * inv_re - rhs_im * inv_im
        sol_im = rhs_re * inv_im + rhs_im * inv_re
    pieces = (
        lax.all_gather(sol_re[None], "tm", axis=0, tiled=True),
        lax.all_gather(sol_im[None], "tm", axis=0, tiled=True),
    )
    order = jnp.arange(pieces[0].shape[0], dtype=jnp.int32)
    angle = 2.0 * jnp.pi / steps * (order * own % steps).astype(jnp.float32)
    summed = jnp.einsum("k,kabc->abc", jnp.cos(angle), pieces[0], precision=high) - jnp.einsum(
        "k,kabc->abc", jnp.sin(angle), pieces[1], precision=high
    )
    back = summed / steps
    return iterate + (back / scale_own)[None]


HALO = 4
TILE = 8


def specs(count, hbm):
    return [pl.BlockSpec(memory_space=pltpu.HBM if hbm else pltpu.VMEM)] * count


def call(body, outs, ins, scratch=(), limit=8, smem=0, hbm_ins=False, hbm_outs=False):
    moved = sum(x.size * 4 for x in ins) + sum(x.size * 4 for x in outs)
    return pl.pallas_call(
        body,
        out_shape=outs,
        in_specs=specs(len(ins) - smem, hbm_ins) + [pl.BlockSpec(memory_space=pltpu.SMEM)] * smem,
        out_specs=specs(len(outs), hbm_outs),
        scratch_shapes=scratch,
        compiler_params=pltpu.CompilerParams(vmem_limit_bytes=limit << 20),
        cost_estimate=pl.CostEstimate(flops=moved * 4, bytes_accessed=moved, transcendentals=0),
    )(*ins)


def shape(*dims):
    return jax.ShapeDtypeStruct(dims, jnp.float32)


def ids(rows, dim, lanes=128):
    return lax.broadcasted_iota(jnp.int32, (rows, lanes), dim)


def other_half(lane, t):
    return ((lane + 64 * t) & 127) >= 64


def cat(a, b):
    return jnp.concatenate([a, b], axis=0)


def blocks(count, width, read, write):
    def body(i, carry):
        levels = [i * width + u for u in range(width)]
        values = [read(l) for l in levels]
        for l, value in zip(levels, values):
            write(l, value)
        return carry

    lax.fori_loop(0, count // width, body, 0)


def put(*refs, at=0):
    def write(l, values):
        for ref, value in zip(refs, values):
            ref[l + at] = value

    return write


def pack_halves(ref, out, base, lo, hi, mask):
    half = ref.shape[0] // 2

    def read(i):
        l = lo + i
        return (jnp.where(mask, ref[l], pltpu.roll(ref[l + half], 64, 1)),)

    blocks(hi - lo, 8, read, put(out, at=base + lo))


def pack_strips(jobs, width=4):
    rows = jobs[0][1].shape[1]
    group = ids(rows, 1) // HALO

    def body(i, accs):
        for u in range(width):
            g = i * width + u
            here = group == g
            accs = tuple(
                jnp.where(here, pltpu.roll(read(g), (HALO * g + 128 - first) & 127, 1), acc)
                for acc, (read, _, _, first) in zip(accs, jobs)
            )
        return accs

    accs = lax.fori_loop(0, 32 // width, body, (jnp.zeros((rows, 128), jnp.float32),) * len(jobs))
    for acc, (_, out, place, _) in zip(accs, jobs):
        out[place] = acc


def levels_of(*refs, G=0):
    def read(g):
        found = [ref[32 * G + g] for ref in refs]
        return found[0] if len(found) == 1 else cat(*found)

    return read


CHUNKS = 4


def send_first(it_hbm, h_hbm, xm, near_pair, far_pair, it, h, sems):
    t = lax.axis_index("tm")
    levels, rows = it.shape[:2]
    half, groups = levels // 2, levels // 32
    part = half // CHUNKS
    copies = []
    for c in range(CHUNKS):
        for f, (source, target) in enumerate(((it_hbm, it), (h_hbm, h))):
            for s in range(2):
                span = pl.ds(s * half + c * part, part)
                copy = pltpu.make_async_copy(source.at[span], target.at[span], sems.at[c, f, s])
                copy.start()
                copies.append(copy)
    mask = other_half(ids(rows, 1), t)
    for c in range(CHUNKS):
        for f, ref in enumerate((it, h)):
            for s in range(2):
                copies[4 * c + 2 * f + s].wait()
            pack_halves(ref, xm, f * half, c * part, (c + 1) * part, mask)
    inner_at = 60 + 4 * t
    pack_strips(
        [(levels_of(ref, G=G), xm, 2 * half + f * groups + G, inner_at) for f, ref in enumerate((it, h)) for G in range(groups)]
    )
    edge_rows(it, h, near_pair, far_pair)


def even_lat():
    return lax.rem(lax.axis_index("lat"), 2) == 0


def edge_pair(first, second):
    top = ids(TILE, 0) < HALO
    even = even_lat()
    down = jnp.where(top, first[:TILE], pltpu.roll(second[:TILE], HALO, 0))
    up = jnp.where(top, pltpu.roll(first[-TILE:], HALO, 0), second[-TILE:])
    return jnp.where(even, up, down), jnp.where(even, down, up)


def edge_rows(first, second, near_pair, far_pair):
    blocks(first.shape[0], 8, lambda l: edge_pair(first[l], second[l]), put(near_pair, far_pair))


def send_fixed(region, initial, table, kap, cross):
    t = lax.axis_index("tm")
    groups = region.shape[0] // 32

    def read(l):
        classes = region[l]
        value = jnp.full(classes.shape, table[0], jnp.float32)
        for c in range(1, table.shape[0]):
            value = jnp.where(classes == c, table[c], value)
        return (value,)

    blocks(region.shape[0], 8, read, put(kap))
    pack_strips(
        [(levels_of(ref, G=G), cross, f * groups + G, 124 * t) for f, ref in enumerate((kap, initial)) for G in range(groups)]
    )


def fixed_rows(kap, initial, cross, near_pair, far_pair):
    levels = kap.shape[0]
    groups = levels // 32
    edge_rows(kap, initial, near_pair, far_pair)
    found = [edge_pair(cross[G], cross[groups + G]) for G in range(groups)]
    for G in range(groups):
        put(near_pair, far_pair)(levels + G, found[G])


def halo_tiles(near_pair, far_pair):
    even = even_lat()
    after = jnp.where(even, near_pair, far_pair)
    before = jnp.where(even, far_pair, near_pair)
    top = ids(TILE, 0) < HALO
    return (
        jnp.where(top, after, pltpu.roll(before, HALO, 0)),
        jnp.where(top, pltpu.roll(after, HALO, 0), before),
    )


def send_halo(near_pair, far_pair, xe, hit, hh):
    t = lax.axis_index("tm")
    levels = near_pair.shape[0]
    half, groups = levels // 2, levels // 32
    blocks(levels, 8, lambda l: halo_tiles(near_pair[l], far_pair[l]), put(hit, hh))
    mask = other_half(ids(TILE, 1), t)
    for f, ref in enumerate((hit, hh)):
        pack_halves(ref, xe, f * half, 0, half, mask)
    inner_at = 60 + 4 * t
    pack_strips(
        [(levels_of(ref, G=G), xe, 2 * half + f * groups + G, inner_at) for f, ref in enumerate((hit, hh)) for G in range(groups)]
    )


def send_sides(it, h, hit, hh, same, cross):
    t = lax.axis_index("tm")
    groups = it.shape[0] // 32
    for out, first in ((cross, 124 * t), (same, 124 * (1 - t))):
        pack_strips(
            [
                (levels_of(own, halo, G=G), out, f * groups + G, first)
                for f, (own, halo) in enumerate(((it, hit), (h, hh)))
                for G in range(groups)
            ]
        )


def reciprocal(d):
    y = pl.reciprocal(d, approx=True)
    return y * (2.0 - d * y)


def face(a, b):
    return 2.0 * a * b * reciprocal(jnp.maximum(a + b, 1e-30))


def strip(value, g, at):
    return pltpu.roll(value, (at + 256 - HALO * g) & 127, 1)


def lanes_from(lane, at):
    return ((lane + 128 - at) & 127) < HALO


def near(low, mid, high, wl, wh, wy, wx):
    rows = mid.shape[0]
    total = wl * low + wh * high
    total = total + (wy * pltpu.roll(mid, rows - 1, 0) + pltpu.roll(wy * mid, 1, 0))
    return total + (wx * pltpu.roll(mid, 127, 1) + pltpu.roll(wx * mid, 1, 1))


def weights(kap, cross, near_pair, far_pair, wl, wy, wx, total, inv0, inv1, K):
    t = lax.axis_index("tm")
    levels, own_rows = kap.shape[:2]
    groups = levels // 32
    rows = own_rows + TILE
    outer_at = 124 * (1 - t)
    outer = lanes_from(ids(rows, 1), outer_at)
    zero = jnp.zeros((rows, 128), jnp.float32)
    beta = corner_weight ** 0.5
    K[0] = zero
    K[levels + 1] = zero
    wl[0] = zero

    def halo(l):
        return halo_tiles(near_pair[l], far_pair[l])[0]

    for G in range(groups):
        side = cat(cross[G], halo(levels + G))
        blocks(
            32,
            4,
            lambda g: (jnp.where(outer, strip(side, g, outer_at), cat(kap[32 * G + g], halo(32 * G + g))),),
            put(K, at=32 * G + 1),
        )

    def weigh(l):
        here = K[l + 1]
        high = face(here, K[l + 2])
        row = face(here, pltpu.roll(here, rows - 1, 0))
        lane = face(here, pltpu.roll(here, 127, 1))
        return high, row, lane, (row + pltpu.roll(row, 1, 0)) + (lane + pltpu.roll(lane, 1, 1))

    def keep(l, values):
        wl[l + 1] = values[0]
        put(wy, wx, total)(l, values[1:])

    blocks(levels, 4, weigh, keep)

    def invert(l):
        sums = total[l] + (wl[l] + wl[l + 1])
        d0 = (1.0 - beta) + sums
        d1 = (1.0 + beta) + sums
        r = reciprocal(d0 * d1)
        return sums, d1 * r, d0 * r

    blocks(levels, 4, invert, put(total, inv0, inv1))


def own_step(it, h, hit, hh, initial, near_pair, far_pair, same, cross, wl, wy, wx, total, part, extra, own_it):
    t = lax.axis_index("tm")
    levels, own_rows = it.shape[:2]
    groups = levels // 32
    rows = own_rows + TILE
    outer_at = 124 * (1 - t)
    outer = lanes_from(ids(rows, 1), outer_at)
    first = t == 0
    zero = jnp.zeros((rows, 128), jnp.float32)
    own_it[0] = zero
    own_it[levels + 1] = zero

    def halo(l):
        return halo_tiles(near_pair[l], far_pair[l])[1]

    for G in range(groups):
        sides = (same[G], same[groups + G], cat(cross[groups + G], halo(levels + G)))

        def assemble(g):
            l = 32 * G + g
            fields = (cat(it[l], hit[l]), cat(h[l], hh[l]), cat(initial[l], halo(l)))
            mine, heat, start = [
                jnp.where(outer, strip(side, g, outer_at), field) for side, field in zip(sides, fields)
            ]
            return mine, jnp.where(first, heat + start, heat), jnp.where(first, mine, start)

        def store(g, values):
            l = 32 * G + g
            own_it[l + 1], part[l], extra[l] = values

        blocks(32, 4, assemble, store)

    def residual(l):
        mid = own_it[l + 1]
        around = near(own_it[l], mid, own_it[l + 2], wl[l], wl[l + 1], wy[l], wx[l])
        return (part[l] - ((1.0 + total[l]) * mid - around),)

    blocks(levels, 4, residual, put(part))


def place(packed, sides, out, at):
    t = lax.axis_index("tm")
    rows = packed.shape[1]
    levels = out[0].shape[0] - 2 * at
    half, groups = levels // 2, levels // 32
    lane = ids(rows, 1)
    outer_at = 124 * (1 - t)
    inner_at = 64 - 4 * t
    outer = lanes_from(lane, outer_at)
    inner = lanes_from(lane, inner_at)
    for G in range(groups):
        upper = G >= groups // 2
        within = [packed[2 * half + f * groups + G] for f in range(2)]
        beside = [sides[f * groups + G] for f in range(2)]

        def read(g):
            found = []
            for f in range(2):
                value = packed[f * half + 32 * G + g - (half if upper else 0)]
                if upper:
                    value = pltpu.roll(value, 64, 1)
                value = jnp.where(inner, strip(within[f], g, inner_at), value)
                found.append(jnp.where(outer, strip(beside[f], g, outer_at), value))
            return found

        blocks(32, 4, read, put(*out, at=32 * G + at))


def unpack(xm, cross, it, h):
    rows = it.shape[1]
    place(xm, [cross[i, :rows] for i in range(cross.shape[0])], (it, h), 0)


def iterate_block(
    wl, wy, wx, total, inv0, inv1, part, extra, main_it, main_h, xe, cross,
    w_own, w_send,
    it, halo_it, halo_h, s0, s1, x0, x1, y0, y1,
):
    t = lax.axis_index("tm")
    levels, rows = wy.shape[:2]
    own_rows = rows - TILE
    half = levels // 2
    first = t == 0
    zero = jnp.zeros((rows, 128), jnp.float32)
    beta = corner_weight ** 0.5
    for ref in (it, x0, x1, y0, y1):
        ref[0] = zero
        ref[levels + 1] = zero
    place(xe, [cross[i, own_rows:] for i in range(cross.shape[0])], (halo_it, halo_h), 0)
    blocks(levels, 8, lambda l: (cat(main_it[l], halo_it[l]),), put(it, at=1))

    def residual(l):
        mid = it[l + 1]
        around = near(it[l], mid, it[l + 2], wl[l], wl[l + 1], wy[l], wx[l])
        theirs = cat(main_h[l], halo_h[l]) + extra[l] - ((1.0 + total[l]) * mid - around)
        mine = part[l] + jnp.where(first, 0.0, 1.0) * mid
        r0 = jnp.where(first, mine, theirs)
        r1 = jnp.where(first, theirs, mine) * beta
        a, b = r0 + r1, r0 - r1
        return a, b, a * inv0[l], b * inv1[l]

    def keep(l, values):
        put(s0, s1)(l, values)
        put(x0, x1, at=1)(l, values[2:])

    blocks(levels, 4, residual, keep)

    def sweep(l, a, spec, inv):
        return (spec[l] + near(a[l], a[l + 1], a[l + 2], wl[l], wl[l + 1], wy[l], wx[l])) * inv[l]

    def both(l, a0, a1):
        return sweep(l, a0, s0, inv0), sweep(l, a1, s1, inv1)

    blocks(levels, 4, lambda l: both(l, x0, x1), put(y0, y1, at=1))
    blocks(levels, 4, lambda l: both(l, y0, y1), put(x0, x1, at=1))
    handled = jnp.logical_not(other_half(ids(own_rows, 1), t))

    def last(l):
        mine, theirs = [], []
        for at in (l, l + half):
            a, b = both(at, x0, x1)
            w0 = (a + b)[:own_rows] * 0.5
            w1 = (a - b)[:own_rows] * (0.5 / beta)
            mine.append(jnp.where(first, w0, w1))
            theirs.append(jnp.where(first, w1, w0))
        return mine[0], mine[1], jnp.where(handled, theirs[0], pltpu.roll(theirs[1], 64, 1))

    def give(l, values):
        w_own[l], w_own[l + half], w_send[l] = values

    blocks(half, 2, last, give)


def finish(it, w_own, got, out_hbm, out, sems):
    t = lax.axis_index("tm")
    levels, rows = it.shape[:2]
    half = levels // 2
    part = half // CHUNKS
    handled = jnp.logical_not(other_half(ids(rows, 1), t))
    copies = []
    for c in range(CHUNKS):
        def read(i):
            l = c * part + i
            theirs = got[l]
            return (
                it[l] + jnp.where(handled, w_own[l], theirs),
                it[l + half] + jnp.where(handled, w_own[l + half], pltpu.roll(theirs, 64, 1)),
            )

        def write(i, values):
            l = c * part + i
            out[l], out[l + half] = values

        blocks(part, 4, read, write)
        for s in range(2):
            span = pl.ds(s * half + c * part, part)
            copy = pltpu.make_async_copy(out.at[span], out_hbm.at[span], sems.at[c, s])
            copy.start()
            copies.append(copy)
    for copy in copies:
        copy.wait()


def two_steps(iterate, heating, initial, region, cond_table):
    it, h = iterate[0], heating[0]
    levels, rows, lanes = it.shape
    half, groups = levels // 2, levels // 32
    lats, lons = lax.axis_size("lat"), lax.axis_size("lon")
    swap = [(0, 1), (1, 0)]
    pairs = [[(i, i + 1) for i in range(start, lats - 1, 2)] for start in (0, 1)]
    pairs = [p + [(j, i) for i, j in p] for p in pairs]
    after_lon = [(j + 1) % lons for j in range(lons)]
    straight = [(j, after_lon[j]) for j in range(lons)] + [(lons + after_lon[j], lons + j) for j in range(lons)]
    crossing = [(lons + j, after_lon[j]) for j in range(lons)] + [(after_lon[j], lons + j) for j in range(lons)]
    both = ("tm", "lon")
    full = shape(levels, rows, lanes)
    tile = shape(levels, TILE, lanes)
    wide = shape(levels, rows + TILE, lanes)

    xm, near_rows, far_rows = call(
        send_first,
        [shape(levels + 2 * groups, rows, lanes), tile, tile],
        [pltpu.with_memory_space_constraint(it, pltpu.HBM), pltpu.with_memory_space_constraint(h, pltpu.HBM)],
        scratch=[pltpu.VMEM(it.shape, jnp.float32)] * 2 + [pltpu.SemaphoreType.DMA((CHUNKS, 2, 2))],
        hbm_ins=True,
    )
    xm = lax.ppermute(xm, "tm", swap)
    near_rows = lax.ppermute(near_rows, "lat", pairs[0])
    far_rows = lax.ppermute(far_rows, "lat", pairs[1])
    kap, fixed = call(send_fixed, [full, shape(2 * groups, rows, lanes)], [region, initial, cond_table], smem=1)
    fixed = lax.ppermute(fixed, both, crossing)
    rimmed = shape(levels + groups, TILE, lanes)
    near_fixed, far_fixed = call(fixed_rows, [rimmed, rimmed], [kap, initial, fixed])
    near_fixed = lax.ppermute(near_fixed, "lat", pairs[0])
    far_fixed = lax.ppermute(far_fixed, "lat", pairs[1])
    xe, hit, hh = call(send_halo, [shape(levels + 2 * groups, TILE, lanes), tile, tile], [near_rows, far_rows])
    xe = lax.ppermute(xe, "tm", swap)
    sides = shape(2 * groups, rows + TILE, lanes)
    same, cross = call(send_sides, [sides, sides], [it, h, hit, hh])
    cross = lax.ppermute(cross, both, crossing)
    same = lax.ppermute(same, both, straight)
    deep = pltpu.VMEM((levels + 2, rows + TILE, lanes), jnp.float32)
    flat = pltpu.VMEM((levels, rows + TILE, lanes), jnp.float32)
    small = pltpu.VMEM((levels, TILE, lanes), jnp.float32)
    wl, wy, wx, total, inv0, inv1 = call(
        weights,
        [shape(levels + 1, rows + TILE, lanes)] + [wide] * 5,
        [kap, fixed, near_fixed, far_fixed],
        scratch=[deep],
        limit=16,
    )
    part, extra = call(
        own_step,
        [wide, wide],
        [it, h, hit, hh, initial, near_fixed, far_fixed, same, fixed, wl, wy, wx, total],
        scratch=[deep],
        limit=16,
    )
    main_it, main_h = call(unpack, [full, full], [xm, cross])
    w_own, w_send = call(
        iterate_block,
        [full, shape(half, rows, lanes)],
        [wl, wy, wx, total, inv0, inv1, part, extra, main_it, main_h, xe, cross],
        scratch=[deep] + [small] * 2 + [flat] * 2 + [deep] * 4,
        limit=24,
    )
    got = lax.ppermute(w_send, "tm", swap)
    (out,) = call(
        finish,
        [full],
        [it, w_own, got],
        scratch=[pltpu.VMEM(it.shape, jnp.float32), pltpu.SemaphoreType.DMA((CHUNKS, 2))],
        hbm_outs=True,
    )
    return out[None]


def solution(mesh):
    return jax.shard_map(
        two_steps if mesh.shape["tm"] == 2 else on_device,
        mesh=mesh,
        in_specs=(
            P("tm", None, "lat", "lon"),
            P("tm", None, "lat", "lon"),
            P(None, "lat", "lon"),
            P(None, "lat", "lon"),
            P(),
        ),
        out_specs=P("tm", None, "lat", "lon"),
        check_vma=False,
    )
```

```python
import jax
import jax.numpy as jnp
from jax import lax
from jax.experimental import pallas as pl
from jax.experimental.pallas import tpu as pltpu
from jax.sharding import PartitionSpec as P

SWEEPS = 4


corner_weight = 0.1


def padded(value, sides, width, wrap):
    for axis, dim in sides:
        peers, length = (lax.axis_size(axis), value.shape[dim])
        up = [(i, (i + 1) % peers) for i in range(peers if wrap else peers - 1)]
        down = [(j, i) for i, j in up]
        last = lax.slice_in_dim(value, length - width, length, axis=dim)
        initial = lax.slice_in_dim(value, 0, width, axis=dim)
        before = lax.ppermute(last, axis, up)
        after = lax.ppermute(initial, axis, down)
        value = jnp.concatenate([before, value, after], axis=dim)
    return value


def passed_along(block, axis, distance):
    devices = range(lax.axis_size(axis))
    route = [(i - distance, i) for i in devices if i - distance in devices]
    return lax.ppermute(block, axis, route)


def harmonic(first, second):
    return 2.0 * first * second / (first + second)


def conductivity(region, cond_table):
    classes = jnp.arange(cond_table.shape[0], dtype=jnp.int32)
    onehot = (region[..., None] == classes).astype(jnp.float32)
    return jnp.sum(onehot * cond_table, axis=-1)


def extend(stack):
    lat_ext = padded(stack, (("lat", 2),), 1, False)
    both = padded(lat_ext, (("lon", 3),), 1, True)
    return jnp.pad(both, ((0, 0), (1, 1), (0, 0), (0, 0)))


def face_weights(kext):
    centre = kext[1:-1, 1:-1, 1:-1]
    return (
        harmonic(centre, kext[:-2, 1:-1, 1:-1]),
        harmonic(centre, kext[2:, 1:-1, 1:-1]),
        harmonic(centre, kext[1:-1, :-2, 1:-1]),
        harmonic(centre, kext[1:-1, 2:, 1:-1]),
        harmonic(centre, kext[1:-1, 1:-1, :-2]),
        harmonic(centre, kext[1:-1, 1:-1, 2:]),
    )


def neighbours(weights, ext):
    near = weights[0] * ext[..., :-2, 1:-1, 1:-1] + weights[1] * ext[..., 2:, 1:-1, 1:-1]
    near = near + weights[2] * ext[..., 1:-1, :-2, 1:-1] + weights[3] * ext[..., 1:-1, 2:, 1:-1]
    near = near + weights[4] * ext[..., 1:-1, 1:-1, :-2] + weights[5] * ext[..., 1:-1, 1:-1, 2:]
    return near


def on_device(iterate, heating, initial, region, cond_table):
    steps = lax.axis_size("tm")
    own = lax.axis_index("tm")
    high = lax.Precision.HIGHEST
    kfield = conductivity(region, cond_table)
    ext = extend(jnp.stack([kfield, iterate[0]]))
    weights = face_weights(ext[0])
    total = weights[0] + weights[1] + weights[2] + weights[3] + weights[4] + weights[5]
    shifted = passed_along(iterate, "tm", 1)[0]
    previous = jnp.where(own == 0, initial, shifted)
    residual = heating[0] + previous - ((1.0 + total) * iterate[0] - neighbours(weights, ext[1]))
    scale_own = corner_weight ** (own.astype(jnp.float32) / steps)
    scaled = residual * scale_own
    zeros = jnp.zeros_like(residual)
    piece = lax.all_gather(scaled[None], "tm", axis=0, tiled=True)
    order = jnp.arange(piece.shape[0], dtype=jnp.int32)
    angle = 2.0 * jnp.pi / steps * (own * order % steps).astype(jnp.float32)
    real_part = jnp.einsum("n,nabc->abc", jnp.cos(angle), piece, precision=high)
    imag_part = (zeros, zeros)[1] - jnp.einsum("n,nabc->abc", jnp.sin(angle), piece, precision=high)
    beta = corner_weight ** (1.0 / steps)
    freq_angle = 2.0 * jnp.pi / steps * (own % steps).astype(jnp.float32)
    diag_re = 1.0 - beta * jnp.cos(freq_angle) + total
    diag_im = beta * jnp.sin(freq_angle) + zeros
    denom = diag_re * diag_re + diag_im * diag_im
    inv_re = diag_re / denom
    inv_im = -diag_im / denom
    sol_re = real_part * inv_re - imag_part * inv_im
    sol_im = real_part * inv_im + imag_part * inv_re
    for sweep in range(SWEEPS - 1):
        near = neighbours(weights, extend(jnp.stack([sol_re, sol_im])))
        rhs_re = real_part + near[0]
        rhs_im = imag_part + near[1]
        sol_re = rhs_re * inv_re - rhs_im * inv_im
        sol_im = rhs_re * inv_im + rhs_im * inv_re
    pieces = (
        lax.all_gather(sol_re[None], "tm", axis=0, tiled=True),
        lax.all_gather(sol_im[None], "tm", axis=0, tiled=True),
    )
    order = jnp.arange(pieces[0].shape[0], dtype=jnp.int32)
    angle = 2.0 * jnp.pi / steps * (order * own % steps).astype(jnp.float32)
    summed = jnp.einsum("k,kabc->abc", jnp.cos(angle), pieces[0], precision=high) - jnp.einsum(
        "k,kabc->abc", jnp.sin(angle), pieces[1], precision=high
    )
    back = summed / steps
    return iterate + (back / scale_own)[None]


HALO = 4
TILE = 8


def specs(count, hbm):
    return [pl.BlockSpec(memory_space=pltpu.HBM if hbm else pltpu.VMEM)] * count


def call(body, outs, ins, scratch=(), limit=8, smem=0, hbm_ins=False, hbm_outs=False):
    moved = sum(x.size * 4 for x in ins) + sum(x.size * 4 for x in outs)
    return pl.pallas_call(
        body,
        out_shape=outs,
        in_specs=specs(len(ins) - smem, hbm_ins) + [pl.BlockSpec(memory_space=pltpu.SMEM)] * smem,
        out_specs=specs(len(outs), hbm_outs),
        scratch_shapes=scratch,
        compiler_params=pltpu.CompilerParams(vmem_limit_bytes=limit << 20),
        cost_estimate=pl.CostEstimate(flops=moved * 4, bytes_accessed=moved, transcendentals=0),
    )(*ins)


def shape(*dims):
    return jax.ShapeDtypeStruct(dims, jnp.float32)


def ids(rows, dim, lanes=128):
    return lax.broadcasted_iota(jnp.int32, (rows, lanes), dim)


def other_half(lane, t):
    return ((lane + 64 * t) & 127) >= 64


def cat(a, b):
    return jnp.concatenate([a, b], axis=0)


def blocks(count, width, read, write):
    def body(i, carry):
        for u in range(width):
            write(i * width + u, read(i * width + u))
        return carry

    lax.fori_loop(0, count // width, body, 0)


def put(*refs, at=0):
    def write(l, values):
        for ref, value in zip(refs, values):
            ref[l + at] = value

    return write


def pack_halves(ref, out, base, lo, hi, mask):
    half = ref.shape[0] // 2

    def read(i):
        l = lo + i
        return (jnp.where(mask, ref[l], pltpu.roll(ref[l + half], 64, 1)),)

    blocks(hi - lo, 8, read, put(out, at=base + lo))


def pack_strips(jobs):
    rows = jobs[0][1].shape[1]
    group = ids(rows, 1) // HALO
    accs = [jnp.zeros((rows, 128), jnp.float32) for _ in jobs]
    for g in range(32):
        for i, (read, _, _, first) in enumerate(jobs):
            accs[i] = jnp.where(group == g, pltpu.roll(read(g), (HALO * g + 128 - first) & 127, 1), accs[i])
    for acc, (_, out, place, _) in zip(accs, jobs):
        out[place] = acc


def levels_of(ref, G):
    return lambda g: ref[32 * G + g]


CHUNKS = 4


def send_first(it_hbm, h_hbm, xm, it, h, sems):
    t = lax.axis_index("tm")
    levels, rows = it.shape[:2]
    half, groups = levels // 2, levels // 32
    part = half // CHUNKS
    copies = []
    for c in range(CHUNKS):
        for f, (source, target) in enumerate(((it_hbm, it), (h_hbm, h))):
            for s in range(2):
                span = pl.ds(s * half + c * part, part)
                copy = pltpu.make_async_copy(source.at[span], target.at[span], sems.at[c, f, s])
                copy.start()
                copies.append(copy)
    mask = other_half(ids(rows, 1), t)
    for c in range(CHUNKS):
        for f, ref in enumerate((it, h)):
            for s in range(2):
                copies[4 * c + 2 * f + s].wait()
            pack_halves(ref, xm, f * half, c * part, (c + 1) * part, mask)
    pack_strips(
        [
            (levels_of(ref, G), xm, 2 * half + f * groups + G, 60 + 4 * t)
            for f, ref in enumerate((it, h))
            for G in range(groups)
        ]
    )


def send_sides(it, h, region, initial, table, kap, right, left):
    groups = it.shape[0] // 32

    def read(l):
        classes = region[l]
        value = jnp.full(classes.shape, table[0], jnp.float32)
        for c in range(1, table.shape[0]):
            value = jnp.where(classes == c, table[c], value)
        return (value,)

    blocks(region.shape[0], 8, read, put(kap))
    for f, ref in enumerate((it, h, kap, initial)):
        pack_strips(
            [
                (levels_of(ref, G), out, f * groups + G, first)
                for out, first in ((right, 124), (left, 0))
                for G in range(groups)
            ]
        )


def even_lat():
    return lax.rem(lax.axis_index("lat"), 2) == 0


def edge_pair(first, second):
    top = ids(TILE, 0) < HALO
    even = even_lat()
    down = jnp.where(top, first[:TILE], pltpu.roll(second[:TILE], HALO, 0))
    up = jnp.where(top, pltpu.roll(first[-TILE:], HALO, 0), second[-TILE:])
    return jnp.where(even, up, down), jnp.where(even, down, up)


def send_rows(it, h, kap, initial, from_left, from_right, near_lat, far_lat, near_diag, far_diag, near_e, far_e):
    t = lax.axis_index("tm")
    levels = it.shape[0]
    half, groups = levels // 2, levels // 32
    other = other_half(ids(TILE, 1), t)
    own = jnp.logical_not(other)
    for f, (a, b) in enumerate(((it, h), (kap, initial))):
        def read(l):
            found = []
            for low, high in zip(edge_pair(a[l], b[l]), edge_pair(a[l + half], b[l + half])):
                high_moved = pltpu.roll(high, 64, 1)
                found += [low, high, jnp.where(own, low, high_moved), jnp.where(other, low, high_moved)]
            return found

        def write(l, values):
            for at, (edges, lat, diag) in enumerate(((near_e, near_lat, near_diag), (far_e, far_lat, far_diag))):
                edges[l], edges[l + half], lat[f * half + l] = values[4 * at : 4 * at + 3]
                if f == 0:
                    diag[l] = values[4 * at + 3]

        blocks(half, 4, read, write)
        jobs = []
        for edges, lat, diag in ((near_e, near_lat, near_diag), (far_e, far_lat, far_diag)):
            for G in range(groups):
                jobs.append((levels_of(edges, G), lat, 2 * half + (2 + f) * groups + G, 64 - 4 * t))
                if f == 0:
                    jobs.append((levels_of(edges, G), diag, half + groups + G, 60 + 4 * t))
        pack_strips(jobs)
    low = t == 0
    strips = [(jnp.where(low, from_left[i], from_right[i]), jnp.where(low, from_right[i], from_left[i])) for i in range(4 * groups)]
    for G in range(groups):
        for f in range(2):
            a, b = strips[2 * f * groups + G], strips[(2 * f + 1) * groups + G]
            put(near_lat, far_lat)(2 * half + f * groups + G, edge_pair(a[0], b[0]))
            if f == 0:
                put(near_diag, far_diag)(half + G, edge_pair(a[1], b[1]))


def forward(from_left, from_right, xs):
    low = lax.axis_index("tm") == 0
    for i in range(xs.shape[0]):
        xs[i] = jnp.where(low, from_right[i], from_left[i])


def halo_tiles(near_pair, far_pair):
    even = even_lat()
    after = jnp.where(even, near_pair, far_pair)
    before = jnp.where(even, far_pair, near_pair)
    top = ids(TILE, 0) < HALO
    return (
        jnp.where(top, after, pltpu.roll(before, HALO, 0)),
        jnp.where(top, pltpu.roll(after, HALO, 0), before),
    )


def reciprocal(d):
    y = pl.reciprocal(d, approx=True)
    return y * (2.0 - d * y)


def face(a, b):
    return 2.0 * a * b * reciprocal(jnp.maximum(a + b, 1e-30))


def strip(value, g, at):
    return pltpu.roll(value, (at + 256 - HALO * g) & 127, 1)


def lanes_from(lane, at):
    return ((lane + 128 - at) & 127) < HALO


def wrap(*refs):
    def write(l, values):
        for ref, value in zip(refs, values):
            ref[l + 1, TILE:-TILE] = value
            ref[l + 1, :TILE] = value[-TILE:]
            ref[l + 1, -TILE:] = value[:TILE]

    return write


def clear_ends(*refs):
    for ref in refs:
        zero = jnp.zeros(ref.shape[1:], jnp.float32)
        ref[0] = zero
        ref[ref.shape[0] - 1] = zero


def rows_of(ref, l, shift=0):
    return ref[l, TILE + shift : ref.shape[1] - TILE + shift]


def near(ref, l, wl, wy, wyp, wx):
    mid = rows_of(ref, l + 1)
    total = wl[l] * rows_of(ref, l) + wl[l + 1] * rows_of(ref, l + 2)
    total = total + (wy[l] * rows_of(ref, l + 1, 1) + wyp[l] * rows_of(ref, l + 1, -1))
    w = wx[l]
    return total + (w * pltpu.roll(mid, 127, 1) + pltpu.roll(w * mid, 1, 1))


def packed(read, within, beside, G, half):
    t = lax.axis_index("tm")
    lane = ids(within[0].shape[0], 1)
    outer_at = 124 * (1 - t)
    inner_at = 64 - 4 * t
    outer = lanes_from(lane, outer_at)
    inner = lanes_from(lane, inner_at)
    upper = 32 * G >= half

    def read_level(g):
        found = []
        for f, value in enumerate(read(32 * G + g - (half if upper else 0))):
            if upper:
                value = pltpu.roll(value, 64, 1)
            value = jnp.where(inner, strip(within[f], g, inner_at), value)
            if beside is not None:
                value = jnp.where(outer, strip(beside[f], g, outer_at), value)
            found.append(value)
        return found

    return read_level


def halo_of(near_pair, far_pair, base, within, beside, G, half):
    def tiles(i):
        return halo_tiles(near_pair[i], far_pair[i])

    return packed(lambda l: tiles(base + l), tiles(within + G), tiles(beside + G), G, half)


def prepare(
    it, h, kap, initial, from_left, from_right, near_lat, far_lat,
    wl, wy, wyp, wx, total, inv0, inv1, part, extra,
    K, own_it,
):
    t = lax.axis_index("tm")
    levels, own_rows = it.shape[:2]
    half, groups = levels // 2, levels // 32
    rows = own_rows + TILE
    outer_at = 124 * (1 - t)
    outer = lanes_from(ids(own_rows, 1), outer_at)
    first = t == 0
    beta = corner_weight ** 0.5
    clear_ends(K, own_it)
    wl[0] = jnp.zeros((rows, 128), jnp.float32)

    for G in range(groups):
        sides = [jnp.where(first, from_left[f * groups + G], from_right[f * groups + G]) for f in range(4)]
        moving = halo_of(near_lat, far_lat, 0, 2 * half + 2 * groups, 2 * half, G, half)
        fixed = halo_of(near_lat, far_lat, half, 2 * half + 3 * groups, 2 * half + groups, G, half)

        def assemble(g):
            l = 32 * G + g
            halos = moving(g) + fixed(g)
            mine, heat, k, start = [
                cat(jnp.where(outer, strip(side, g, outer_at), ref[l]), halo)
                for side, ref, halo in zip(sides, (it, h, kap, initial), halos)
            ]
            return mine, k, jnp.where(first, heat + start, heat), jnp.where(first, mine, start)

        def store(g, values):
            l = 32 * G + g
            wrap(own_it, K)(l, values[:2])
            part[l], extra[l] = values[2:]

        blocks(32, 4, assemble, store)

    def weigh(l):
        here = rows_of(K, l + 1)
        high = face(here, rows_of(K, l + 2))
        row = face(here, rows_of(K, l + 1, 1))
        lane = face(here, pltpu.roll(here, 127, 1))
        last_row = pltpu.roll(row, 1, 0)
        return high, row, last_row, lane, (row + last_row) + (lane + pltpu.roll(lane, 1, 1))

    def keep(l, values):
        wl[l + 1] = values[0]
        put(wy, wyp, wx, total)(l, values[1:])

    blocks(levels, 8, weigh, keep)

    def residual(l):
        sums = total[l] + (wl[l] + wl[l + 1])
        d0 = (1.0 - beta) + sums
        d1 = (1.0 + beta) + sums
        r = reciprocal(d0 * d1)
        mid = rows_of(own_it, l + 1)
        left = part[l] - ((1.0 + sums) * mid - near(own_it, l, wl, wy, wyp, wx))
        return sums, d1 * r, d0 * r, left

    blocks(levels, 8, residual, put(total, inv0, inv1, part))


def unpack(xm, it, h):
    levels = it.shape[0]
    half, groups = levels // 2, levels // 32
    for G in range(groups):
        within = [xm[2 * half + f * groups + G] for f in range(2)]
        blocks(32, 4, packed(lambda l: (xm[l], xm[half + l]), within, None, G, half), put(it, h, at=32 * G))


def iterate_block(
    wl, wy, wyp, wx, total, inv0, inv1, part, extra, main_it, main_h, xs, near_diag, far_diag,
    w_own, w_send,
    it, s0, s1, x0, x1, y0, y1,
):
    t = lax.axis_index("tm")
    levels, rows = wy.shape[:2]
    own_rows = rows - TILE
    half, groups = levels // 2, levels // 32
    first = t == 0
    beta = corner_weight ** 0.5
    outer_at = 124 * (1 - t)
    outer = lanes_from(ids(own_rows, 1), outer_at)
    clear_ends(it, x0, x1, y0, y1)
    for G in range(groups):
        halo = halo_of(near_diag, far_diag, 0, half + groups, half, G, half)

        def assemble(g):
            l = 32 * G + g
            return [
                cat(jnp.where(outer, strip(xs[f * groups + G], g, outer_at), main[l]), tile)
                for f, (main, tile) in enumerate(zip((main_it, main_h), halo(g)))
            ]

        def store(g, values):
            wrap(it)(32 * G + g, values[:1])
            s0[32 * G + g] = values[1]

        blocks(32, 4, assemble, store)

    def residual(l):
        mid = rows_of(it, l + 1)
        theirs = s0[l] + extra[l] - ((1.0 + total[l]) * mid - near(it, l, wl, wy, wyp, wx))
        mine = part[l] + jnp.where(first, 0.0, 1.0) * mid
        r0 = jnp.where(first, mine, theirs)
        r1 = jnp.where(first, theirs, mine) * beta
        a, b = r0 + r1, r0 - r1
        return a, b, a * inv0[l], b * inv1[l]

    def keep(l, values):
        put(s0, s1)(l, values)
        wrap(x0, x1)(l, values[2:])

    blocks(levels, 8, residual, keep)

    def both(l, a0, a1):
        return (
            (s0[l] + near(a0, l, wl, wy, wyp, wx)) * inv0[l],
            (s1[l] + near(a1, l, wl, wy, wyp, wx)) * inv1[l],
        )

    blocks(levels, 8, lambda l: both(l, x0, x1), wrap(y0, y1))
    blocks(levels, 8, lambda l: both(l, y0, y1), wrap(x0, x1))
    handled = jnp.logical_not(other_half(ids(own_rows, 1), t))

    def last(l):
        mine, theirs = [], []
        for at in (l, l + half):
            a, b = both(at, x0, x1)
            w0 = (a + b)[:own_rows] * 0.5
            w1 = (a - b)[:own_rows] * (0.5 / beta)
            mine.append(jnp.where(first, w0, w1))
            theirs.append(jnp.where(first, w1, w0))
        return mine[0], mine[1], jnp.where(handled, theirs[0], pltpu.roll(theirs[1], 64, 1))

    def give(l, values):
        w_own[l], w_own[l + half], w_send[l] = values

    blocks(half, 4, last, give)


def finish(it, w_own, got, out_hbm, out, sems):
    t = lax.axis_index("tm")
    levels, rows = it.shape[:2]
    half = levels // 2
    part = half // CHUNKS
    handled = jnp.logical_not(other_half(ids(rows, 1), t))
    copies = []
    for c in range(CHUNKS):
        def read(i):
            l = c * part + i
            theirs = got[l]
            return (
                it[l] + jnp.where(handled, w_own[l], theirs),
                it[l + half] + jnp.where(handled, w_own[l + half], pltpu.roll(theirs, 64, 1)),
            )

        def write(i, values):
            l = c * part + i
            out[l], out[l + half] = values

        blocks(part, 4, read, write)
        for s in range(2):
            span = pl.ds(s * half + c * part, part)
            copy = pltpu.make_async_copy(out.at[span], out_hbm.at[span], sems.at[c, s])
            copy.start()
            copies.append(copy)
    for copy in copies:
        copy.wait()


def two_steps(iterate, heating, initial, region, cond_table):
    it, h = iterate[0], heating[0]
    levels, rows, lanes = it.shape
    half, groups = levels // 2, levels // 32
    lats, lons = lax.axis_size("lat"), lax.axis_size("lon")
    swap = [(0, 1), (1, 0)]
    pairs = [[(i, i + 1) for i in range(start, lats - 1, 2)] for start in (0, 1)]
    pairs = [p + [(j, i) for i, j in p] for p in pairs]
    diagonals = [[(t * lats + i, (1 - t) * lats + j) for t in range(2) for i, j in p] for p in pairs]
    ring = [(j, (j + 1) % lons) for j in range(lons)]
    full = shape(levels, rows, lanes)
    wide = shape(levels, rows + TILE, lanes)

    (xm,) = call(
        send_first,
        [shape(levels + 2 * groups, rows, lanes)],
        [pltpu.with_memory_space_constraint(it, pltpu.HBM), pltpu.with_memory_space_constraint(h, pltpu.HBM)],
        scratch=[pltpu.VMEM(it.shape, jnp.float32)] * 2 + [pltpu.SemaphoreType.DMA((CHUNKS, 2, 2))],
        hbm_ins=True,
    )
    xm = lax.ppermute(xm, "tm", swap)
    sides = shape(4 * groups, rows, lanes)
    kap, right, left = call(send_sides, [full, sides, sides], [it, h, region, initial, cond_table], smem=1)
    from_left = lax.ppermute(right, "lon", ring)
    from_right = lax.ppermute(left, "lon", [(j, i) for i, j in ring])
    (xs,) = call(forward, [shape(2 * groups, rows, lanes)], [from_left, from_right])
    xs = lax.ppermute(xs, "tm", swap)
    lat = shape(levels + 4 * groups, TILE, lanes)
    diag = shape(half + 2 * groups, TILE, lanes)
    near_lat, far_lat, near_diag, far_diag = call(
        send_rows,
        [lat, lat, diag, diag],
        [it, h, kap, initial, from_left, from_right],
        scratch=[pltpu.VMEM((levels, TILE, lanes), jnp.float32)] * 2,
    )
    near_lat = lax.ppermute(near_lat, "lat", pairs[0])
    far_lat = lax.ppermute(far_lat, "lat", pairs[1])
    near_diag = lax.ppermute(near_diag, ("tm", "lat"), diagonals[0])
    far_diag = lax.ppermute(far_diag, ("tm", "lat"), diagonals[1])
    deep = pltpu.VMEM((levels + 2, rows + 3 * TILE, lanes), jnp.float32)
    flat = pltpu.VMEM((levels, rows + TILE, lanes), jnp.float32)
    ready = call(
        prepare,
        [shape(levels + 1, rows + TILE, lanes)] + [wide] * 8,
        [it, h, kap, initial, from_left, from_right, near_lat, far_lat],
        scratch=[deep] * 2,
        limit=16,
    )
    main_it, main_h = call(unpack, [full, full], [xm])
    w_own, w_send = call(
        iterate_block,
        [full, shape(half, rows, lanes)],
        [*ready, main_it, main_h, xs, near_diag, far_diag],
        scratch=[deep] + [flat] * 2 + [deep] * 4,
        limit=24,
    )
    got = lax.ppermute(w_send, "tm", swap)
    (out,) = call(
        finish,
        [full],
        [it, w_own, got],
        scratch=[pltpu.VMEM(it.shape, jnp.float32), pltpu.SemaphoreType.DMA((CHUNKS, 2))],
        hbm_outs=True,
    )
    return out[None]


def solution(mesh):
    return jax.shard_map(
        two_steps if mesh.shape["tm"] == 2 else on_device,
        mesh=mesh,
        in_specs=(
            P("tm", None, "lat", "lon"),
            P("tm", None, "lat", "lon"),
            P(None, "lat", "lon"),
            P(None, "lat", "lon"),
            P(),
        ),
        out_specs=P("tm", None, "lat", "lon"),
        check_vma=False,
    )
```

```python
import jax
import jax.numpy as jnp
from jax import lax
from jax.experimental import pallas as pl
from jax.experimental.pallas import tpu as pltpu
from jax.sharding import PartitionSpec as P

SWEEPS = 4


corner_weight = 0.1


def padded(value, sides, width, wrap):
    for axis, dim in sides:
        peers, length = (lax.axis_size(axis), value.shape[dim])
        up = [(i, (i + 1) % peers) for i in range(peers if wrap else peers - 1)]
        down = [(j, i) for i, j in up]
        last = lax.slice_in_dim(value, length - width, length, axis=dim)
        initial = lax.slice_in_dim(value, 0, width, axis=dim)
        before = lax.ppermute(last, axis, up)
        after = lax.ppermute(initial, axis, down)
        value = jnp.concatenate([before, value, after], axis=dim)
    return value


def passed_along(block, axis, distance):
    devices = range(lax.axis_size(axis))
    route = [(i - distance, i) for i in devices if i - distance in devices]
    return lax.ppermute(block, axis, route)


def harmonic(first, second):
    return 2.0 * first * second / (first + second)


def conductivity(region, cond_table):
    classes = jnp.arange(cond_table.shape[0], dtype=jnp.int32)
    onehot = (region[..., None] == classes).astype(jnp.float32)
    return jnp.sum(onehot * cond_table, axis=-1)


def extend(stack):
    lat_ext = padded(stack, (("lat", 2),), 1, False)
    both = padded(lat_ext, (("lon", 3),), 1, True)
    return jnp.pad(both, ((0, 0), (1, 1), (0, 0), (0, 0)))


def face_weights(kext):
    centre = kext[1:-1, 1:-1, 1:-1]
    return (
        harmonic(centre, kext[:-2, 1:-1, 1:-1]),
        harmonic(centre, kext[2:, 1:-1, 1:-1]),
        harmonic(centre, kext[1:-1, :-2, 1:-1]),
        harmonic(centre, kext[1:-1, 2:, 1:-1]),
        harmonic(centre, kext[1:-1, 1:-1, :-2]),
        harmonic(centre, kext[1:-1, 1:-1, 2:]),
    )


def neighbours(weights, ext):
    near = weights[0] * ext[..., :-2, 1:-1, 1:-1] + weights[1] * ext[..., 2:, 1:-1, 1:-1]
    near = near + weights[2] * ext[..., 1:-1, :-2, 1:-1] + weights[3] * ext[..., 1:-1, 2:, 1:-1]
    near = near + weights[4] * ext[..., 1:-1, 1:-1, :-2] + weights[5] * ext[..., 1:-1, 1:-1, 2:]
    return near


def on_device(iterate, heating, initial, region, cond_table):
    steps = lax.axis_size("tm")
    own = lax.axis_index("tm")
    high = lax.Precision.HIGHEST
    kfield = conductivity(region, cond_table)
    ext = extend(jnp.stack([kfield, iterate[0]]))
    weights = face_weights(ext[0])
    total = weights[0] + weights[1] + weights[2] + weights[3] + weights[4] + weights[5]
    shifted = passed_along(iterate, "tm", 1)[0]
    previous = jnp.where(own == 0, initial, shifted)
    residual = heating[0] + previous - ((1.0 + total) * iterate[0] - neighbours(weights, ext[1]))
    scale_own = corner_weight ** (own.astype(jnp.float32) / steps)
    scaled = residual * scale_own
    zeros = jnp.zeros_like(residual)
    piece = lax.all_gather(scaled[None], "tm", axis=0, tiled=True)
    order = jnp.arange(piece.shape[0], dtype=jnp.int32)
    angle = 2.0 * jnp.pi / steps * (own * order % steps).astype(jnp.float32)
    real_part = jnp.einsum("n,nabc->abc", jnp.cos(angle), piece, precision=high)
    imag_part = (zeros, zeros)[1] - jnp.einsum("n,nabc->abc", jnp.sin(angle), piece, precision=high)
    beta = corner_weight ** (1.0 / steps)
    freq_angle = 2.0 * jnp.pi / steps * (own % steps).astype(jnp.float32)
    diag_re = 1.0 - beta * jnp.cos(freq_angle) + total
    diag_im = beta * jnp.sin(freq_angle) + zeros
    denom = diag_re * diag_re + diag_im * diag_im
    inv_re = diag_re / denom
    inv_im = -diag_im / denom
    sol_re = real_part * inv_re - imag_part * inv_im
    sol_im = real_part * inv_im + imag_part * inv_re
    for sweep in range(SWEEPS - 1):
        near = neighbours(weights, extend(jnp.stack([sol_re, sol_im])))
        rhs_re = real_part + near[0]
        rhs_im = imag_part + near[1]
        sol_re = rhs_re * inv_re - rhs_im * inv_im
        sol_im = rhs_re * inv_im + rhs_im * inv_re
    pieces = (
        lax.all_gather(sol_re[None], "tm", axis=0, tiled=True),
        lax.all_gather(sol_im[None], "tm", axis=0, tiled=True),
    )
    order = jnp.arange(pieces[0].shape[0], dtype=jnp.int32)
    angle = 2.0 * jnp.pi / steps * (order * own % steps).astype(jnp.float32)
    summed = jnp.einsum("k,kabc->abc", jnp.cos(angle), pieces[0], precision=high) - jnp.einsum(
        "k,kabc->abc", jnp.sin(angle), pieces[1], precision=high
    )
    back = summed / steps
    return iterate + (back / scale_own)[None]


HALO = 4
TILE = 8


def specs(count, hbm):
    return [pl.BlockSpec(memory_space=pltpu.HBM if i in hbm else pltpu.VMEM) for i in range(count)]


def call(body, outs, ins, scratch=(), limit=8, smem=0, hbm_ins=(), hbm_outs=(), aliases={}):
    moved = sum(x.size * 4 for x in ins) + sum(x.size * 4 for x in outs)
    return pl.pallas_call(
        body,
        out_shape=outs,
        in_specs=specs(len(ins) - smem, hbm_ins) + [pl.BlockSpec(memory_space=pltpu.SMEM)] * smem,
        out_specs=specs(len(outs), hbm_outs),
        scratch_shapes=scratch,
        input_output_aliases=aliases,
        compiler_params=pltpu.CompilerParams(vmem_limit_bytes=limit << 20),
        cost_estimate=pl.CostEstimate(flops=moved * 4, bytes_accessed=moved, transcendentals=0),
    )(*ins)


def shape(*dims):
    return jax.ShapeDtypeStruct(dims, jnp.float32)


def ids(rows, dim, lanes=128):
    return lax.broadcasted_iota(jnp.int32, (rows, lanes), dim)


def other_half(lane, t):
    return ((lane + 64 * t) & 127) >= 64


def cat(a, b):
    return jnp.concatenate([a, b], axis=0)


def blocks(count, width, read, write):
    def body(i, carry):
        for u in range(width):
            write(i * width + u, read(i * width + u))
        return carry

    lax.fori_loop(0, count // width, body, 0)


def put(*refs, at=0):
    def write(l, values):
        for ref, value in zip(refs, values):
            ref[l + at] = value

    return write


def pack_halves(ref, out, base, lo, hi, mask):
    half = ref.shape[0] // 2

    def read(i):
        l = lo + i
        return (jnp.where(mask, ref[l], pltpu.roll(ref[l + half], 64, 1)),)

    blocks(hi - lo, 8, read, put(out, at=base + lo))


def pack_strips(jobs):
    rows = jobs[0][1].shape[1]
    group = ids(rows, 1) // HALO
    accs = [jnp.zeros((rows, 128), jnp.float32) for _ in jobs]
    for g in range(32):
        for i, (read, _, _, first) in enumerate(jobs):
            accs[i] = jnp.where(group == g, pltpu.roll(read(g), (HALO * g + 128 - first) & 127, 1), accs[i])
    for acc, (_, out, place, _) in zip(accs, jobs):
        out[place] = acc


def levels_of(ref, G):
    return lambda g: ref[32 * G + g]


CHUNKS = 4


def send_first(it_hbm, h_hbm, xm, it, h, sems):
    t = lax.axis_index("tm")
    levels, rows = it.shape[:2]
    half, groups = levels // 2, levels // 32
    part = half // CHUNKS
    copies = []
    for c in range(CHUNKS):
        for f, (source, target) in enumerate(((it_hbm, it), (h_hbm, h))):
            for s in range(2):
                span = pl.ds(s * half + c * part, part)
                copy = pltpu.make_async_copy(source.at[span], target.at[span], sems.at[c, f, s])
                copy.start()
                copies.append(copy)
    mask = other_half(ids(rows, 1), t)
    for c in range(CHUNKS):
        for f, ref in enumerate((it, h)):
            for s in range(2):
                copies[4 * c + 2 * f + s].wait()
            pack_halves(ref, xm, f * half, c * part, (c + 1) * part, mask)
    pack_strips(
        [
            (levels_of(ref, G), xm, 2 * half + f * groups + G, 60 + 4 * t)
            for f, ref in enumerate((it, h))
            for G in range(groups)
        ]
    )


def even(axis):
    return lax.rem(lax.axis_index(axis), 2) == 0


def send_sides(it, h, region_hbm, initial_hbm, table, kap, near_sides, far_sides, region, initial, sems):
    groups = it.shape[0] // 32
    part = it.shape[0] // CHUNKS
    copies = []
    for c in range(CHUNKS):
        for i, (source, target) in enumerate(((region_hbm, region), (initial_hbm, initial))):
            span = pl.ds(c * part, part)
            copy = pltpu.make_async_copy(source.at[span], target.at[span], sems.at[c, i])
            copy.start()
            copies.append(copy)
    to_near = 124 * jnp.where(even("lon"), 1, 0)

    def pack(f, ref):
        pack_strips(
            [
                (levels_of(ref, G), out, f * groups + G, first)
                for out, first in ((near_sides, to_near), (far_sides, 124 - to_near))
                for G in range(groups)
            ]
        )

    pack(0, it)
    pack(1, h)
    for copy in copies:
        copy.wait()

    def read(l):
        classes = region[l]
        value = jnp.full(classes.shape, table[0], jnp.float32)
        for c in range(1, table.shape[0]):
            value = jnp.where(classes == c, table[c], value)
        return (value,)

    blocks(region.shape[0], 8, read, put(kap))
    pack(2, kap)
    pack(3, initial)


def edge_pair(first, second):
    top = ids(TILE, 0) < HALO
    first_up = even("lat")
    down = jnp.where(top, first[:TILE], pltpu.roll(second[:TILE], HALO, 0))
    up = jnp.where(top, pltpu.roll(first[-TILE:], HALO, 0), second[-TILE:])
    return jnp.where(first_up, up, down), jnp.where(first_up, down, up)


def send_rows(it, h, kap, initial, near_lat, far_lat, near_diag, far_diag, near_e, far_e):
    t = lax.axis_index("tm")
    levels = it.shape[0]
    half, groups = levels // 2, levels // 32
    other = other_half(ids(TILE, 1), t)
    own = jnp.logical_not(other)
    for f, (a, b) in enumerate(((it, h), (kap, initial))):
        def read(l):
            found = []
            for low, high in zip(edge_pair(a[l], b[l]), edge_pair(a[l + half], b[l + half])):
                high_moved = pltpu.roll(high, 64, 1)
                found += [low, high, jnp.where(own, low, high_moved), jnp.where(other, low, high_moved)]
            return found

        def write(l, values):
            for at, (edges, lat, diag) in enumerate(((near_e, near_lat, near_diag), (far_e, far_lat, far_diag))):
                edges[l], edges[l + half], lat[f * half + l] = values[4 * at : 4 * at + 3]
                if f == 0:
                    diag[l] = values[4 * at + 3]

        blocks(half, 8, read, write)
        jobs = []
        for edges, lat, diag in ((near_e, near_lat, near_diag), (far_e, far_lat, far_diag)):
            for G in range(groups):
                jobs.append((levels_of(edges, G), lat, 2 * half + (2 + f) * groups + G, 64 - 4 * t))
                if f == 0:
                    jobs.append((levels_of(edges, G), diag, half + groups + G, 60 + 4 * t))
        pack_strips(jobs)


def side_strips(near_sides, far_sides):
    t = lax.axis_index("tm")
    from_near = (t == 0) != even("lon")
    count = near_sides.shape[0]
    own = [jnp.where(from_near, near_sides[i], far_sides[i]) for i in range(count)]
    partner = [jnp.where(from_near, far_sides[i], near_sides[i]) for i in range(count)]
    return own, partner


def add_rows(near_sides, far_sides, near_lat0, far_lat0, near_diag0, far_diag0, near_lat, far_lat, near_diag, far_diag, xs):
    groups = near_sides.shape[0] // 4
    half = 16 * groups
    own, partner = side_strips(near_sides, far_sides)
    for G in range(groups):
        for f in range(2):
            a, b = 2 * f * groups + G, (2 * f + 1) * groups + G
            put(near_lat, far_lat)(2 * half + f * groups + G, edge_pair(own[a], own[b]))
        put(near_diag, far_diag)(half + G, edge_pair(partner[G], partner[groups + G]))
    for i in range(2 * groups):
        xs[i] = partner[i]


def halo_tiles(near_pair, far_pair):
    first_up = even("lat")
    after = jnp.where(first_up, near_pair, far_pair)
    before = jnp.where(first_up, far_pair, near_pair)
    top = ids(TILE, 0) < HALO
    return (
        jnp.where(top, after, pltpu.roll(before, HALO, 0)),
        jnp.where(top, pltpu.roll(after, HALO, 0), before),
    )


def reciprocal(d):
    y = pl.reciprocal(d, approx=True)
    return y * (2.0 - d * y)


def face(a, b):
    return 2.0 * a * b * reciprocal(jnp.maximum(a + b, 1e-30))


def strip(value, g, at):
    return pltpu.roll(value, (at + 256 - HALO * g) & 127, 1)


def lanes_from(lane, at):
    return ((lane + 128 - at) & 127) < HALO


def wrap(*refs):
    def write(l, values):
        for ref, value in zip(refs, values):
            ref[l + 1, TILE:-TILE] = value
            ref[l + 1, :TILE] = value[-TILE:]
            ref[l + 1, -TILE:] = value[:TILE]

    return write


def clear_ends(*refs):
    for ref in refs:
        zero = jnp.zeros(ref.shape[1:], jnp.float32)
        ref[0] = zero
        ref[ref.shape[0] - 1] = zero


def rows_of(ref, l, shift=0):
    return ref[l, TILE + shift : ref.shape[1] - TILE + shift]


def near(ref, l, w, around=None):
    low, mid, high = around or [rows_of(ref, l + i) for i in range(3)]
    wl, wh, wy, wyp, wx = w
    total = wl * low + wh * high
    total = total + (wy * rows_of(ref, l + 1, 1) + wyp * rows_of(ref, l + 1, -1))
    return total + (wx * pltpu.roll(mid, 127, 1) + pltpu.roll(wx * mid, 1, 1))


def packed(read, within, beside, G, half):
    t = lax.axis_index("tm")
    lane = ids(within[0].shape[0], 1)
    outer_at = 124 * (1 - t)
    inner_at = 64 - 4 * t
    outer = lanes_from(lane, outer_at)
    inner = lanes_from(lane, inner_at)
    upper = 32 * G >= half

    def read_level(g):
        found = []
        for f, value in enumerate(read(32 * G + g - (half if upper else 0))):
            if upper:
                value = pltpu.roll(value, 64, 1)
            value = jnp.where(inner, strip(within[f], g, inner_at), value)
            if beside is not None:
                value = jnp.where(outer, strip(beside[f], g, outer_at), value)
            found.append(value)
        return found

    return read_level


def halo_of(near_pair, far_pair, base, within, beside, G, half):
    def tiles(i):
        return halo_tiles(near_pair[i], far_pair[i])

    return packed(lambda l: tiles(base + l), tiles(within + G), tiles(beside + G), G, half)


def prepare_main(it, h, kap, initial, near_sides, far_sides, K, own_it, part, extra, wl, wx, partial):
    t = lax.axis_index("tm")
    levels, rows = it.shape[:2]
    groups = levels // 32
    outer_at = 124 * (1 - t)
    outer = lanes_from(ids(rows, 1), outer_at)
    first = t == 0
    own, _ = side_strips(near_sides, far_sides)
    clear_ends(K)
    for G in range(groups):
        def assemble(g):
            l = 32 * G + g
            mine, heat, k, start = [
                jnp.where(outer, strip(own[f * groups + G], g, outer_at), ref[l])
                for f, ref in enumerate((it, h, kap, initial))
            ]
            return mine, jnp.where(first, heat + start, heat), jnp.where(first, mine, start), k

        def store(g, values):
            l = 32 * G + g
            put(own_it, part, extra)(l, values[:3])
            K[l + 1] = values[3]

        blocks(32, 8, assemble, store)
    wl[0] = jnp.zeros((rows, 128), jnp.float32)

    def weigh(l):
        here = K[l + 1]
        high = face(here, K[l + 2])
        lane = face(here, pltpu.roll(here, 127, 1))
        return high, lane, lane + pltpu.roll(lane, 1, 1)

    def keep(l, values):
        wl[l + 1] = values[0]
        put(wx, partial)(l, values[1:])

    blocks(levels, 8, weigh, keep)


def prepare(
    Km, it_m, part_m, extra_m, wl_m, wx_m, partial, near_lat, far_lat, _,
    wl, wy, wyp, wx, total, inv0, inv1, part, extra,
    Kh, own_it,
):
    t = lax.axis_index("tm")
    levels, own_rows = it_m.shape[:2]
    half, groups = levels // 2, levels // 32
    rows = own_rows + TILE
    first = t == 0
    beta = corner_weight ** 0.5
    clear_ends(Kh, own_it)
    wl[0] = jnp.zeros((rows, 128), jnp.float32)

    for G in range(groups):
        moving = halo_of(near_lat, far_lat, 0, 2 * half + 2 * groups, 2 * half, G, half)
        fixed = halo_of(near_lat, far_lat, half, 2 * half + 3 * groups, 2 * half + groups, G, half)

        def assemble(g):
            l = 32 * G + g
            mine, heat, k, start = moving(g) + fixed(g)
            return (
                k,
                cat(it_m[l], mine),
                cat(part_m[l], jnp.where(first, heat + start, heat)),
                cat(extra_m[l], jnp.where(first, mine, start)),
            )

        def store(g, values):
            l = 32 * G + g
            Kh[l + 1] = values[0]
            wrap(own_it)(l, values[1:2])
            part[l], extra[l] = values[2:]

        blocks(32, 8, assemble, store)

    def weigh(l):
        tile = Kh[l + 1]
        here = cat(Km[l + 1], tile)
        low = cat(wl_m[l], face(Kh[l], tile))
        high = cat(wl_m[l + 1], face(tile, Kh[l + 2]))
        row = face(here, pltpu.roll(here, rows - 1, 0))
        last_row = pltpu.roll(row, 1, 0)
        side = face(tile, pltpu.roll(tile, 127, 1))
        lane = cat(wx_m[l], side)
        sums = (low + high) + (row + last_row) + cat(partial[l], side + pltpu.roll(side, 1, 1))
        d0 = (1.0 - beta) + sums
        d1 = (1.0 + beta) + sums
        r = reciprocal(d0 * d1)
        mid = rows_of(own_it, l + 1)
        left = part[l] - ((1.0 + sums) * mid - near(own_it, l, (low, high, row, last_row, lane)))
        return high, row, last_row, lane, sums, d1 * r, d0 * r, left

    def keep(l, values):
        wl[l + 1] = values[0]
        put(wy, wyp, wx, total, inv0, inv1, part)(l, values[1:])

    blocks(levels, 8, weigh, keep)


def unpack(xm, it, h):
    levels = it.shape[0]
    half, groups = levels // 2, levels // 32
    for G in range(groups):
        within = [xm[2 * half + f * groups + G] for f in range(2)]
        blocks(32, 4, packed(lambda l: (xm[l], xm[half + l]), within, None, G, half), put(it, h, at=32 * G))


def iterate_block(
    wl, wy, wyp, wx, total, inv0, inv1, part, extra, main_it, main_h, xs, near_diag, far_diag,
    w_own, w_send,
    it, s0, s1, x0, x1, y0, y1,
):
    t = lax.axis_index("tm")
    levels, rows = wy.shape[:2]
    own_rows = rows - TILE
    half, groups = levels // 2, levels // 32
    first = t == 0
    beta = corner_weight ** 0.5
    outer_at = 124 * (1 - t)
    outer = lanes_from(ids(own_rows, 1), outer_at)
    clear_ends(it, x0, x1, y0, y1)
    for G in range(groups):
        halo = halo_of(near_diag, far_diag, 0, half + groups, half, G, half)

        def assemble(g):
            l = 32 * G + g
            return [
                cat(jnp.where(outer, strip(xs[f * groups + G], g, outer_at), main[l]), tile)
                for f, (main, tile) in enumerate(zip((main_it, main_h), halo(g)))
            ]

        def store(g, values):
            wrap(it)(32 * G + g, values[:1])
            s0[32 * G + g] = values[1]

        blocks(32, 4, assemble, store)

    def faces(l):
        return wl[l], wl[l + 1], wy[l], wyp[l], wx[l]

    def residual(l):
        mid = rows_of(it, l + 1)
        theirs = s0[l] + extra[l] - ((1.0 + total[l]) * mid - near(it, l, faces(l)))
        mine = part[l] + jnp.where(first, 0.0, 1.0) * mid
        r0 = jnp.where(first, mine, theirs)
        r1 = jnp.where(first, theirs, mine) * beta
        a, b = r0 + r1, r0 - r1
        return a, b, a * inv0[l], b * inv1[l]

    def keep(l, values):
        put(s0, s1)(l, values)
        wrap(x0, x1)(l, values[2:])

    blocks(levels, 8, residual, keep)

    def sweep(count, width, a0, a1, write, bases=(0,)):
        def body(i, carry):
            start = i * width
            around = [[[rows_of(a, base + start + n) for n in range(2)] for a in (a0, a1)] for base in bases]
            for u in range(width):
                found = []
                for base, kept in zip(bases, around):
                    l = base + start + u
                    w = faces(l)
                    for a, levels_kept, spec, inv in zip((a0, a1), kept, (s0, s1), (inv0, inv1)):
                        levels_kept.append(rows_of(a, l + 2))
                        found.append((spec[l] + near(a, l, w, levels_kept)) * inv[l])
                        levels_kept.pop(0)
                write(start + u, found)
            return carry

        lax.fori_loop(0, count // width, body, 0)

    sweep(levels, 8, x0, x1, wrap(y0, y1))
    sweep(levels, 8, y0, y1, wrap(x0, x1))
    handled = jnp.logical_not(other_half(ids(own_rows, 1), t))

    def give(l, found):
        theirs = []
        for at, (a, b) in ((l, found[:2]), (l + half, found[2:])):
            w0 = (a + b)[:own_rows] * 0.5
            w1 = (a - b)[:own_rows] * (0.5 / beta)
            w_own[at] = jnp.where(first, w0, w1)
            theirs.append(jnp.where(first, w1, w0))
        w_send[l] = jnp.where(handled, theirs[0], pltpu.roll(theirs[1], 64, 1))

    sweep(half, 4, x0, x1, give, (0, half))


def finish(it, w_own, got, out_hbm, out, sems):
    t = lax.axis_index("tm")
    levels, rows = it.shape[:2]
    half = levels // 2
    part = half // CHUNKS
    handled = jnp.logical_not(other_half(ids(rows, 1), t))
    copies = []
    for c in range(CHUNKS):
        def read(i):
            l = c * part + i
            theirs = got[l]
            return (
                it[l] + jnp.where(handled, w_own[l], theirs),
                it[l + half] + jnp.where(handled, w_own[l + half], pltpu.roll(theirs, 64, 1)),
            )

        def write(i, values):
            l = c * part + i
            out[l], out[l + half] = values

        blocks(part, 4, read, write)
        for s in range(2):
            span = pl.ds(s * half + c * part, part)
            copy = pltpu.make_async_copy(out.at[span], out_hbm.at[span], sems.at[c, s])
            copy.start()
            copies.append(copy)
    for copy in copies:
        copy.wait()


def two_steps(iterate, heating, initial, region, cond_table):
    it, h = iterate[0], heating[0]
    levels, rows, lanes = it.shape
    half, groups = levels // 2, levels // 32
    lats, lons = lax.axis_size("lat"), lax.axis_size("lon")
    swap = [(0, 1), (1, 0)]
    pairs = [[(i, i + 1) for i in range(start, lats - 1, 2)] for start in (0, 1)]
    pairs = [p + [(j, i) for i, j in p] for p in pairs]
    diagonals = [[(t * lats + i, (1 - t) * lats + j) for t in range(2) for i, j in p] for p in pairs]
    round_lon = [[(i, (i + 1) % lons) for i in range(start, lons, 2)] for start in (0, 1)]
    round_lon = [p + [(j, i) for i, j in p] for p in round_lon]
    full = shape(levels, rows, lanes)
    wide = shape(levels, rows + TILE, lanes)

    (xm,) = call(
        send_first,
        [shape(levels + 2 * groups, rows, lanes)],
        [pltpu.with_memory_space_constraint(it, pltpu.HBM), pltpu.with_memory_space_constraint(h, pltpu.HBM)],
        scratch=[pltpu.VMEM(it.shape, jnp.float32)] * 2 + [pltpu.SemaphoreType.DMA((CHUNKS, 2, 2))],
        hbm_ins=(0, 1),
    )
    xm = lax.ppermute(xm, "tm", swap)
    sides = shape(4 * groups, rows, lanes)
    kap, near_sides, far_sides = call(
        send_sides,
        [full, sides, sides],
        [it, h, pltpu.with_memory_space_constraint(region, pltpu.HBM), pltpu.with_memory_space_constraint(initial, pltpu.HBM), cond_table],
        scratch=[pltpu.VMEM(it.shape, jnp.int32), pltpu.VMEM(it.shape, jnp.float32), pltpu.SemaphoreType.DMA((CHUNKS, 2))],
        smem=1,
        hbm_ins=(2, 3),
    )
    near_sides = lax.ppermute(near_sides, "lon", round_lon[0])
    far_sides = lax.ppermute(far_sides, "lon", round_lon[1])
    lat = shape(levels + 4 * groups, TILE, lanes)
    diag = shape(half + 2 * groups, TILE, lanes)
    messages = call(
        send_rows,
        [lat, lat, diag, diag],
        [it, h, kap, initial],
        scratch=[pltpu.VMEM((levels, TILE, lanes), jnp.float32)] * 2,
    )
    near_lat, far_lat, near_diag, far_diag, xs = call(
        add_rows,
        [lat, lat, diag, diag, shape(2 * groups, rows, lanes)],
        [near_sides, far_sides, *messages],
        aliases={2 + i: i for i in range(4)},
    )
    near_lat = lax.ppermute(near_lat, "lat", pairs[0])
    far_lat = lax.ppermute(far_lat, "lat", pairs[1])
    near_diag = lax.ppermute(near_diag, ("tm", "lat"), diagonals[0])
    far_diag = lax.ppermute(far_diag, ("tm", "lat"), diagonals[1])
    xs = lax.ppermute(xs, "tm", swap)
    main = call(
        prepare_main,
        [shape(levels + 2, rows, lanes)] + [full] * 3 + [shape(levels + 1, rows, lanes)] + [full] * 2,
        [it, h, kap, initial, near_sides, far_sides],
    )
    main_it, main_h = call(unpack, [full, full], [xm])
    deep = pltpu.VMEM((levels + 2, rows + 3 * TILE, lanes), jnp.float32)
    flat = pltpu.VMEM((levels, rows + TILE, lanes), jnp.float32)
    ready = call(
        prepare,
        [shape(levels + 1, rows + TILE, lanes)] + [wide] * 8,
        [*main, near_lat, far_lat, main_it],
        scratch=[pltpu.VMEM((levels + 2, TILE, lanes), jnp.float32), deep],
        limit=16,
    )
    w_own, w_send = call(
        iterate_block,
        [full, shape(half, rows, lanes)],
        [*ready, main_it, main_h, xs, near_diag, far_diag],
        scratch=[deep] + [flat] * 2 + [deep] * 4,
        limit=24,
    )
    got = lax.ppermute(w_send, "tm", swap)
    (out,) = call(
        finish,
        [full],
        [it, w_own, got],
        scratch=[pltpu.VMEM(it.shape, jnp.float32), pltpu.SemaphoreType.DMA((CHUNKS, 2))],
        hbm_outs=(0,),
    )
    return out[None]


def solution(mesh):
    return jax.shard_map(
        two_steps if mesh.shape["tm"] == 2 else on_device,
        mesh=mesh,
        in_specs=(
            P("tm", None, "lat", "lon"),
            P("tm", None, "lat", "lon"),
            P(None, "lat", "lon"),
            P(None, "lat", "lon"),
            P(),
        ),
        out_specs=P("tm", None, "lat", "lon"),
        check_vma=False,
    )
```

```python
import jax
import jax.numpy as jnp
from jax import lax
from jax.experimental import pallas as pl
from jax.experimental.pallas import tpu as pltpu
from jax.sharding import PartitionSpec as P

SWEEPS = 4


corner_weight = 0.1


def padded(value, sides, width, wrap):
    for axis, dim in sides:
        peers, length = (lax.axis_size(axis), value.shape[dim])
        up = [(i, (i + 1) % peers) for i in range(peers if wrap else peers - 1)]
        down = [(j, i) for i, j in up]
        last = lax.slice_in_dim(value, length - width, length, axis=dim)
        initial = lax.slice_in_dim(value, 0, width, axis=dim)
        before = lax.ppermute(last, axis, up)
        after = lax.ppermute(initial, axis, down)
        value = jnp.concatenate([before, value, after], axis=dim)
    return value


def passed_along(block, axis, distance):
    devices = range(lax.axis_size(axis))
    route = [(i - distance, i) for i in devices if i - distance in devices]
    return lax.ppermute(block, axis, route)


def harmonic(first, second):
    return 2.0 * first * second / (first + second)


def conductivity(region, cond_table):
    classes = jnp.arange(cond_table.shape[0], dtype=jnp.int32)
    onehot = (region[..., None] == classes).astype(jnp.float32)
    return jnp.sum(onehot * cond_table, axis=-1)


def extend(stack):
    lat_ext = padded(stack, (("lat", 2),), 1, False)
    both = padded(lat_ext, (("lon", 3),), 1, True)
    return jnp.pad(both, ((0, 0), (1, 1), (0, 0), (0, 0)))


def face_weights(kext):
    centre = kext[1:-1, 1:-1, 1:-1]
    return (
        harmonic(centre, kext[:-2, 1:-1, 1:-1]),
        harmonic(centre, kext[2:, 1:-1, 1:-1]),
        harmonic(centre, kext[1:-1, :-2, 1:-1]),
        harmonic(centre, kext[1:-1, 2:, 1:-1]),
        harmonic(centre, kext[1:-1, 1:-1, :-2]),
        harmonic(centre, kext[1:-1, 1:-1, 2:]),
    )


def neighbours(weights, ext):
    near = weights[0] * ext[..., :-2, 1:-1, 1:-1] + weights[1] * ext[..., 2:, 1:-1, 1:-1]
    near = near + weights[2] * ext[..., 1:-1, :-2, 1:-1] + weights[3] * ext[..., 1:-1, 2:, 1:-1]
    near = near + weights[4] * ext[..., 1:-1, 1:-1, :-2] + weights[5] * ext[..., 1:-1, 1:-1, 2:]
    return near


def on_device(iterate, heating, initial, region, cond_table):
    steps = lax.axis_size("tm")
    own = lax.axis_index("tm")
    high = lax.Precision.HIGHEST
    kfield = conductivity(region, cond_table)
    ext = extend(jnp.stack([kfield, iterate[0]]))
    weights = face_weights(ext[0])
    total = weights[0] + weights[1] + weights[2] + weights[3] + weights[4] + weights[5]
    shifted = passed_along(iterate, "tm", 1)[0]
    previous = jnp.where(own == 0, initial, shifted)
    residual = heating[0] + previous - ((1.0 + total) * iterate[0] - neighbours(weights, ext[1]))
    scale_own = corner_weight ** (own.astype(jnp.float32) / steps)
    scaled = residual * scale_own
    zeros = jnp.zeros_like(residual)
    piece = lax.all_gather(scaled[None], "tm", axis=0, tiled=True)
    order = jnp.arange(piece.shape[0], dtype=jnp.int32)
    angle = 2.0 * jnp.pi / steps * (own * order % steps).astype(jnp.float32)
    real_part = jnp.einsum("n,nabc->abc", jnp.cos(angle), piece, precision=high)
    imag_part = (zeros, zeros)[1] - jnp.einsum("n,nabc->abc", jnp.sin(angle), piece, precision=high)
    beta = corner_weight ** (1.0 / steps)
    freq_angle = 2.0 * jnp.pi / steps * (own % steps).astype(jnp.float32)
    diag_re = 1.0 - beta * jnp.cos(freq_angle) + total
    diag_im = beta * jnp.sin(freq_angle) + zeros
    denom = diag_re * diag_re + diag_im * diag_im
    inv_re = diag_re / denom
    inv_im = -diag_im / denom
    sol_re = real_part * inv_re - imag_part * inv_im
    sol_im = real_part * inv_im + imag_part * inv_re
    for sweep in range(SWEEPS - 1):
        near = neighbours(weights, extend(jnp.stack([sol_re, sol_im])))
        rhs_re = real_part + near[0]
        rhs_im = imag_part + near[1]
        sol_re = rhs_re * inv_re - rhs_im * inv_im
        sol_im = rhs_re * inv_im + rhs_im * inv_re
    pieces = (
        lax.all_gather(sol_re[None], "tm", axis=0, tiled=True),
        lax.all_gather(sol_im[None], "tm", axis=0, tiled=True),
    )
    order = jnp.arange(pieces[0].shape[0], dtype=jnp.int32)
    angle = 2.0 * jnp.pi / steps * (order * own % steps).astype(jnp.float32)
    summed = jnp.einsum("k,kabc->abc", jnp.cos(angle), pieces[0], precision=high) - jnp.einsum(
        "k,kabc->abc", jnp.sin(angle), pieces[1], precision=high
    )
    back = summed / steps
    return iterate + (back / scale_own)[None]


HALO = 4
TILE = 8


def specs(count, hbm):
    return [pl.BlockSpec(memory_space=pltpu.HBM if i in hbm else pltpu.VMEM) for i in range(count)]


def call(body, outs, ins, scratch=(), limit=8, smem=0, hbm_ins=(), hbm_outs=(), aliases={}):
    moved = sum(x.size * 4 for x in ins) + sum(x.size * 4 for x in outs)
    return pl.pallas_call(
        body,
        out_shape=outs,
        in_specs=specs(len(ins) - smem, hbm_ins) + [pl.BlockSpec(memory_space=pltpu.SMEM)] * smem,
        out_specs=specs(len(outs), hbm_outs),
        scratch_shapes=scratch,
        input_output_aliases=aliases,
        compiler_params=pltpu.CompilerParams(vmem_limit_bytes=limit << 20),
        cost_estimate=pl.CostEstimate(flops=moved * 4, bytes_accessed=moved, transcendentals=0),
    )(*ins)


def shape(*dims):
    return jax.ShapeDtypeStruct(dims, jnp.float32)


def ids(rows, dim, lanes=128):
    return lax.broadcasted_iota(jnp.int32, (rows, lanes), dim)


def other_half(lane, t):
    return ((lane + 64 * t) & 127) >= 64


def cat(*values):
    return jnp.concatenate(values, axis=0)


def blocks(count, width, read, write):
    def body(i, carry):
        for u in range(width):
            write(i * width + u, read(i * width + u))
        return carry

    lax.fori_loop(0, count // width, body, 0)


def put(*refs, at=0):
    def write(l, values):
        for ref, value in zip(refs, values):
            ref[l + at] = value

    return write


def pack_halves(ref, out, base, lo, hi, mask):
    half = ref.shape[0] // 2

    def read(i):
        l = lo + i
        return (jnp.where(mask, ref[l], pltpu.roll(ref[l + half], 64, 1)),)

    blocks(hi - lo, 8, read, put(out, at=base + lo))


def pack_strips(jobs):
    rows = jobs[0][1].shape[1]
    group = ids(rows, 1) // HALO
    accs = [jnp.zeros((rows, 128), jnp.float32) for _ in jobs]
    for g in range(32):
        for i, (read, _, _, first) in enumerate(jobs):
            accs[i] = jnp.where(group == g, pltpu.roll(read(g), (HALO * g + 128 - first) & 127, 1), accs[i])
    for acc, (_, out, place, _) in zip(accs, jobs):
        out[place] = acc


def levels_of(ref, G):
    return lambda g: ref[32 * G + g]


CHUNKS = 4


def send_first(it_hbm, h_hbm, xm, it, h, sems):
    t = lax.axis_index("tm")
    levels, rows = it.shape[:2]
    half, groups = levels // 2, levels // 32
    part = half // CHUNKS
    copies = []
    for c in range(CHUNKS):
        for f, (source, target) in enumerate(((it_hbm, it), (h_hbm, h))):
            for s in range(2):
                span = pl.ds(s * half + c * part, part)
                copy = pltpu.make_async_copy(source.at[span], target.at[span], sems.at[c, f, s])
                copy.start()
                copies.append(copy)
    mask = other_half(ids(rows, 1), t)
    for c in range(CHUNKS):
        for f, ref in enumerate((it, h)):
            for s in range(2):
                copies[4 * c + 2 * f + s].wait()
            pack_halves(ref, xm, f * half, c * part, (c + 1) * part, mask)
    pack_strips(
        [
            (levels_of(ref, G), xm, 2 * half + f * groups + G, 60 + 4 * t)
            for f, ref in enumerate((it, h))
            for G in range(groups)
        ]
    )


def even(axis):
    return lax.rem(lax.axis_index(axis), 2) == 0


def send_sides(it, h, region_hbm, initial_hbm, table, kap, near_sides, far_sides, region, initial, right, left, sems):
    groups = it.shape[0] // 32
    part = it.shape[0] // CHUNKS
    copies = []
    for c in range(CHUNKS):
        for i, (source, target) in enumerate(((region_hbm, region), (initial_hbm, initial))):
            span = pl.ds(c * part, part)
            copy = pltpu.make_async_copy(source.at[span], target.at[span], sems.at[c, i])
            copy.start()
            copies.append(copy)
    near_right = even("lon")
    count = near_sides.shape[0]

    def pack(f, ref):
        pack_strips(
            [
                (levels_of(ref, G), out, f * groups + G, first)
                for out, first in ((right, 124), (left, 0))
                for G in range(groups)
            ]
        )

    pack(0, it)
    pack(1, h)
    for copy in copies:
        copy.wait()

    def read(l):
        classes = region[l]
        value = jnp.full(classes.shape, table[0], jnp.float32)
        for c in range(1, table.shape[0]):
            value = jnp.where(classes == c, table[c], value)
        return (value,)

    blocks(region.shape[0], 8, read, put(kap))
    pack(2, kap)
    pack(3, initial)
    for i in range(count):
        near_sides[i] = jnp.where(near_right, right[i], left[i])
        far_sides[i] = jnp.where(near_right, left[i], right[i])


def edge_pair(first, second):
    top = ids(TILE, 0) < HALO
    first_up = even("lat")
    down = jnp.where(top, first[:TILE], pltpu.roll(second[:TILE], HALO, 0))
    up = jnp.where(top, pltpu.roll(first[-TILE:], HALO, 0), second[-TILE:])
    return jnp.where(first_up, up, down), jnp.where(first_up, down, up)


def send_rows(it, h, kap, initial, near_lat, far_lat, near_diag, far_diag, near_e, far_e):
    t = lax.axis_index("tm")
    levels = it.shape[0]
    half, groups = levels // 2, levels // 32
    other = other_half(ids(TILE, 1), t)
    own = jnp.logical_not(other)
    for f, (a, b) in enumerate(((it, h), (kap, initial))):
        def read(l):
            found = []
            for low, high in zip(edge_pair(a[l], b[l]), edge_pair(a[l + half], b[l + half])):
                high_moved = pltpu.roll(high, 64, 1)
                found += [low, high, jnp.where(own, low, high_moved), jnp.where(other, low, high_moved)]
            return found

        def write(l, values):
            for at, (edges, lat, diag) in enumerate(((near_e, near_lat, near_diag), (far_e, far_lat, far_diag))):
                edges[l], edges[l + half], lat[f * half + l] = values[4 * at : 4 * at + 3]
                if f == 0:
                    diag[l] = values[4 * at + 3]

        blocks(half, 8, read, write)
        jobs = []
        for edges, lat, diag in ((near_e, near_lat, near_diag), (far_e, far_lat, far_diag)):
            for G in range(groups):
                jobs.append((levels_of(edges, G), lat, 2 * half + (2 + f) * groups + G, 64 - 4 * t))
                if f == 0:
                    jobs.append((levels_of(edges, G), diag, half + groups + G, 60 + 4 * t))
        pack_strips(jobs)


def side_strips(near_sides, far_sides):
    t = lax.axis_index("tm")
    from_near = (t == 0) != even("lon")
    count = near_sides.shape[0]
    own = [jnp.where(from_near, near_sides[i], far_sides[i]) for i in range(count)]
    partner = [jnp.where(from_near, far_sides[i], near_sides[i]) for i in range(count)]
    return own, partner


def add_rows(near_sides, far_sides, near_lat0, far_lat0, near_lat, far_lat):
    groups = near_sides.shape[0] // 4
    own, _ = side_strips(near_sides, far_sides)
    for G in range(groups):
        for f in range(2):
            a, b = 2 * f * groups + G, (2 * f + 1) * groups + G
            put(near_lat, far_lat)(32 * groups + f * groups + G, edge_pair(own[a], own[b]))


def add_partner_rows(near_sides, far_sides, near_diag0, far_diag0, _, near_diag, far_diag, xs):
    groups = near_sides.shape[0] // 4
    _, partner = side_strips(near_sides, far_sides)
    for G in range(groups):
        put(near_diag, far_diag)(16 * groups + G, edge_pair(partner[G], partner[groups + G]))
    for i in range(2 * groups):
        xs[i] = partner[i]


def halo_tiles(near_pair, far_pair):
    first_up = even("lat")
    after = jnp.where(first_up, near_pair, far_pair)
    before = jnp.where(first_up, far_pair, near_pair)
    top = ids(TILE, 0) < HALO
    return (
        jnp.where(top, after, pltpu.roll(before, HALO, 0)),
        jnp.where(top, pltpu.roll(after, HALO, 0), before),
    )


def reciprocal(d):
    y = pl.reciprocal(d, approx=True)
    return y * (2.0 - d * y)


def face(a, b):
    return 2.0 * a * b * reciprocal(jnp.maximum(a + b, 1e-30))


def strip(value, g, at):
    return pltpu.roll(value, (at + 256 - HALO * g) & 127, 1)


def lanes_from(lane, at):
    return ((lane + 128 - at) & 127) < HALO


def clear_ends(*refs):
    for ref in refs:
        zero = jnp.zeros(ref.shape[1:], jnp.float32)
        ref[0] = zero
        ref[ref.shape[0] - 1] = zero


def woven(ref, l):
    return cat(*[ref[l, pl.ds(j, TILE, stride=3), :] for j in range(3)])


def next_row(x):
    return cat(x[TILE:], pltpu.roll(x[:TILE], TILE - 1, 0))


def last_row(x):
    return cat(pltpu.roll(x[-TILE:], 1, 0), x[:-TILE])


def near(around, w):
    low, mid, high = around
    wl, wh, wy, wyp, wx = w
    total = wl * low + wh * high
    total = total + (wy * next_row(mid) + wyp * last_row(mid))
    return total + (wx * pltpu.roll(mid, 127, 1) + pltpu.roll(wx * mid, 1, 1))


def packed(read, within, beside, G, half):
    t = lax.axis_index("tm")
    lane = ids(within[0].shape[0], 1)
    outer_at = 124 * (1 - t)
    inner_at = 64 - 4 * t
    outer = lanes_from(lane, outer_at)
    inner = lanes_from(lane, inner_at)
    upper = 32 * G >= half

    def read_level(g):
        found = []
        for f, value in enumerate(read(32 * G + g - (half if upper else 0))):
            if upper:
                value = pltpu.roll(value, 64, 1)
            value = jnp.where(inner, strip(within[f], g, inner_at), value)
            if beside is not None:
                value = jnp.where(outer, strip(beside[f], g, outer_at), value)
            found.append(value)
        return found

    return read_level


def halo_of(near_pair, far_pair, base, within, beside, G, half):
    def tiles(i):
        return halo_tiles(near_pair[i], far_pair[i])

    return packed(lambda l: tiles(base + l), tiles(within + G), tiles(beside + G), G, half)


def assemble_main(it, h, kap, initial, near_sides, far_sides, own_it, part, extra, K):
    t = lax.axis_index("tm")
    levels, rows = it.shape[:2]
    groups = levels // 32
    outer_at = 124 * (1 - t)
    outer = lanes_from(ids(rows, 1), outer_at)
    first = t == 0
    own, _ = side_strips(near_sides, far_sides)
    for G in range(groups):
        def assemble(g):
            l = 32 * G + g
            mine, heat, k, start = [
                jnp.where(outer, strip(own[f * groups + G], g, outer_at), ref[l])
                for f, ref in enumerate((it, h, kap, initial))
            ]
            return mine, jnp.where(first, heat + start, heat), jnp.where(first, mine, start), k

        blocks(32, 8, assemble, put(own_it, part, extra, K, at=32 * G))


def prepare(
    it_m, part_m, extra_m, K_m, near_lat, far_lat, _,
    wl, wy, wyp, wx, total, inv0, inv1, part, extra,
    K, own_it, part_n, extra_n,
):
    t = lax.axis_index("tm")
    levels, own_rows = it_m.shape[:2]
    half, groups = levels // 2, levels // 32
    rows = own_rows + TILE
    first = t == 0
    beta = corner_weight ** 0.5
    clear_ends(K, own_it)
    wl[0] = jnp.zeros((rows, 128), jnp.float32)

    for G in range(groups):
        moving = halo_of(near_lat, far_lat, 0, 2 * half + 2 * groups, 2 * half, G, half)
        fixed = halo_of(near_lat, far_lat, half, 2 * half + 3 * groups, 2 * half + groups, G, half)

        def assemble(g):
            l = 32 * G + g
            mine, heat, k, start = moving(g) + fixed(g)
            return (
                cat(K_m[l], k),
                cat(it_m[l], mine),
                cat(part_m[l], jnp.where(first, heat + start, heat)),
                cat(extra_m[l], jnp.where(first, mine, start)),
            )

        def store(g, values):
            l = 32 * G + g
            put(K, own_it, at=1)(l, values[:2])
            put(part_n, extra_n)(l, values[2:])

        blocks(32, 8, assemble, store)

    width = 8

    def weigh(i, carry):
        start = i * width
        ks = [woven(K, start), woven(K, start + 1)]
        its = [woven(own_it, start), woven(own_it, start + 1)]
        low = wl[start]
        for u in range(width):
            l = start + u
            ks = [*ks[-2:], woven(K, l + 2)]
            its = [*its[-2:], woven(own_it, l + 2)]
            here = ks[1]
            high = face(here, ks[2])
            row = face(here, next_row(here))
            before = last_row(row)
            lane = face(here, pltpu.roll(here, 127, 1))
            sums = (low + high) + (row + before) + (lane + pltpu.roll(lane, 1, 1))
            d0 = (1.0 - beta) + sums
            d1 = (1.0 + beta) + sums
            r = reciprocal(d0 * d1)
            left = woven(part_n, l) - ((1.0 + sums) * its[1] - near(its, (low, high, row, before, lane)))
            wl[l + 1] = high
            put(wy, wyp, wx, total, inv0, inv1, part, extra)(
                l, (row, before, lane, sums, d1 * r, d0 * r, left, woven(extra_n, l))
            )
            low = high
        return carry

    lax.fori_loop(0, levels // width, weigh, 0)


def unpack(xm, it, h):
    levels = it.shape[0]
    half, groups = levels // 2, levels // 32
    for G in range(groups):
        within = [xm[2 * half + f * groups + G] for f in range(2)]
        blocks(32, 4, packed(lambda l: (xm[l], xm[half + l]), within, None, G, half), put(it, h, at=32 * G))


def iterate_block(
    wl, wy, wyp, wx, total, inv0, inv1, part, extra, main_it, main_h, xs, near_diag, far_diag,
    w_own, w_send,
    it, h, s0, s1, x0, x1, y0, y1,
):
    t = lax.axis_index("tm")
    levels, rows = wy.shape[:2]
    own_rows = rows - TILE
    half, groups = levels // 2, levels // 32
    first = t == 0
    beta = corner_weight ** 0.5
    outer_at = 124 * (1 - t)
    outer = lanes_from(ids(own_rows, 1), outer_at)
    clear_ends(it, x0, x1, y0, y1)
    for G in range(groups):
        halo = halo_of(near_diag, far_diag, 0, half + groups, half, G, half)

        def assemble(g):
            l = 32 * G + g
            return [
                cat(jnp.where(outer, strip(xs[f * groups + G], g, outer_at), main[l]), tile)
                for f, (main, tile) in enumerate(zip((main_it, main_h), halo(g)))
            ]

        def store(g, values):
            it[32 * G + g + 1], h[32 * G + g] = values

        blocks(32, 8, assemble, store)

    def faces(l):
        return wl[l], wl[l + 1], wy[l], wyp[l], wx[l]

    def over(width, read, fields, step):
        def body(i, carry):
            start = i * width
            around = [[read(a, start), read(a, start + 1)] for a in fields]
            for u in range(width):
                around = [[*kept[-2:], read(a, start + u + 2)] for a, kept in zip(fields, around)]
                step(start + u, *around)
            return carry

        lax.fori_loop(0, levels // width, body, 0)

    def residual(l, around):
        mid = around[1]
        theirs = woven(h, l) + extra[l] - ((1.0 + total[l]) * mid - near(around, faces(l)))
        mine = part[l] + jnp.where(first, 0.0, 1.0) * mid
        r0 = jnp.where(first, mine, theirs)
        r1 = jnp.where(first, theirs, mine) * beta
        a, b = r0 + r1, r0 - r1
        put(s0, s1)(l, (a, b))
        put(x0, x1, at=1)(l, (a * inv0[l], b * inv1[l]))

    over(16, woven, (it,), residual)

    def sweep(l, around0, around1):
        w = faces(l)
        return (s0[l] + near(around0, w)) * inv0[l], (s1[l] + near(around1, w)) * inv1[l]

    def to(*refs):
        return lambda l, a, b: put(*refs, at=1)(l, sweep(l, a, b))

    def plain(ref, l):
        return ref[l]

    over(16, plain, (x0, x1), to(y0, y1))
    over(16, plain, (y0, y1), to(x0, x1))
    theirs = h

    def last(l, around0, around1):
        a, b = sweep(l, around0, around1)
        w0, w1 = (a + b) * 0.5, (a - b) * (0.5 / beta)
        for ref, value in ((w_own, jnp.where(first, w0, w1)), (theirs, jnp.where(first, w1, w0))):
            for j in range(3):
                ref[l, pl.ds(j, TILE, stride=3), :] = value[j * TILE : (j + 1) * TILE]

    over(16, plain, (x0, x1), last)
    handled = jnp.logical_not(other_half(ids(own_rows, 1), t))

    def pair(l):
        return (jnp.where(handled, theirs[l, :own_rows], pltpu.roll(theirs[l + half, :own_rows], 64, 1)),)

    blocks(half, 16, pair, put(w_send))


def finish(it, w_own, got, out_hbm, out, sems):
    t = lax.axis_index("tm")
    levels, rows = it.shape[:2]
    half = levels // 2
    part = half // CHUNKS
    handled = jnp.logical_not(other_half(ids(rows, 1), t))
    copies = []
    for c in range(CHUNKS):
        def read(i):
            l = c * part + i
            theirs = got[l]
            return (
                it[l] + jnp.where(handled, w_own[l, :rows], theirs),
                it[l + half] + jnp.where(handled, w_own[l + half, :rows], pltpu.roll(theirs, 64, 1)),
            )

        def write(i, values):
            l = c * part + i
            out[l], out[l + half] = values

        blocks(part, 4, read, write)
        for s in range(2):
            span = pl.ds(s * half + c * part, part)
            copy = pltpu.make_async_copy(out.at[span], out_hbm.at[span], sems.at[c, s])
            copy.start()
            copies.append(copy)
    for copy in copies:
        copy.wait()


def two_steps(iterate, heating, initial, region, cond_table):
    it, h = iterate[0], heating[0]
    levels, rows, lanes = it.shape
    half, groups = levels // 2, levels // 32
    lats, lons = lax.axis_size("lat"), lax.axis_size("lon")
    swap = [(0, 1), (1, 0)]
    pairs = [[(i, i + 1) for i in range(start, lats - 1, 2)] for start in (0, 1)]
    pairs = [p + [(j, i) for i, j in p] for p in pairs]
    diagonals = [[(t * lats + i, (1 - t) * lats + j) for t in range(2) for i, j in p] for p in pairs]
    round_lon = [[(i, (i + 1) % lons) for i in range(start, lons, 2)] for start in (0, 1)]
    round_lon = [p + [(j, i) for i, j in p] for p in round_lon]
    full = shape(levels, rows, lanes)
    wide = shape(levels, rows + TILE, lanes)

    (xm,) = call(
        send_first,
        [shape(levels + 2 * groups, rows, lanes)],
        [pltpu.with_memory_space_constraint(it, pltpu.HBM), pltpu.with_memory_space_constraint(h, pltpu.HBM)],
        scratch=[pltpu.VMEM(it.shape, jnp.float32)] * 2 + [pltpu.SemaphoreType.DMA((CHUNKS, 2, 2))],
        hbm_ins=(0, 1),
    )
    xm = lax.ppermute(xm, "tm", swap)
    sides = shape(4 * groups, rows, lanes)
    kap, near_sides, far_sides = call(
        send_sides,
        [full, sides, sides],
        [it, h, pltpu.with_memory_space_constraint(region, pltpu.HBM), pltpu.with_memory_space_constraint(initial, pltpu.HBM), cond_table],
        scratch=[pltpu.VMEM(it.shape, jnp.int32), pltpu.VMEM(it.shape, jnp.float32)] + [pltpu.VMEM(sides.shape, jnp.float32)] * 2 + [pltpu.SemaphoreType.DMA((CHUNKS, 2))],
        smem=1,
        hbm_ins=(2, 3),
    )
    near_sides = lax.ppermute(near_sides, "lon", round_lon[0])
    far_sides = lax.ppermute(far_sides, "lon", round_lon[1])
    lat = shape(levels + 4 * groups, TILE, lanes)
    diag = shape(half + 2 * groups, TILE, lanes)
    messages = call(
        send_rows,
        [lat, lat, diag, diag],
        [it, h, kap, initial],
        scratch=[pltpu.VMEM((levels, TILE, lanes), jnp.float32)] * 2,
    )
    near_lat, far_lat = call(add_rows, [lat, lat], [near_sides, far_sides, *messages[:2]], aliases={2: 0, 3: 1})
    near_lat = lax.ppermute(near_lat, "lat", pairs[0])
    far_lat = lax.ppermute(far_lat, "lat", pairs[1])
    main = call(assemble_main, [full] * 4, [it, h, kap, initial, near_sides, far_sides])
    near_diag, far_diag, xs = call(
        add_partner_rows,
        [diag, diag, shape(2 * groups, rows, lanes)],
        [near_sides, far_sides, *messages[2:], main[3]],
        aliases={2: 0, 3: 1},
    )
    near_diag = lax.ppermute(near_diag, ("tm", "lat"), diagonals[0])
    far_diag = lax.ppermute(far_diag, ("tm", "lat"), diagonals[1])
    xs = lax.ppermute(xs, "tm", swap)
    main_it, main_h = call(unpack, [full, full], [xm])
    deep = pltpu.VMEM((levels + 2, rows + TILE, lanes), jnp.float32)
    flat = pltpu.VMEM((levels, rows + TILE, lanes), jnp.float32)
    ready = call(
        prepare,
        [shape(levels + 1, rows + TILE, lanes)] + [wide] * 8,
        [*main, near_lat, far_lat, main_it],
        scratch=[deep] * 2 + [flat] * 2,
        limit=16,
    )
    w_own, w_send = call(
        iterate_block,
        [wide, shape(half, rows, lanes)],
        [*ready, main_it, main_h, xs, near_diag, far_diag],
        scratch=[deep] + [flat] * 3 + [deep] * 4,
        limit=24,
    )
    got = lax.ppermute(w_send, "tm", swap)
    (out,) = call(
        finish,
        [full],
        [it, w_own, got],
        scratch=[pltpu.VMEM(it.shape, jnp.float32), pltpu.SemaphoreType.DMA((CHUNKS, 2))],
        hbm_outs=(0,),
    )
    return out[None]


def solution(mesh):
    return jax.shard_map(
        two_steps if mesh.shape["tm"] == 2 else on_device,
        mesh=mesh,
        in_specs=(
            P("tm", None, "lat", "lon"),
            P("tm", None, "lat", "lon"),
            P(None, "lat", "lon"),
            P(None, "lat", "lon"),
            P(),
        ),
        out_specs=P("tm", None, "lat", "lon"),
        check_vma=False,
    )
```

```python
import jax
import jax.numpy as jnp
from jax import lax
from jax.experimental import pallas as pl
from jax.experimental.pallas import tpu as pltpu
from jax.sharding import PartitionSpec as P

SWEEPS = 4


corner_weight = 0.1


def padded(value, sides, width, wrap):
    for axis, dim in sides:
        peers, length = (lax.axis_size(axis), value.shape[dim])
        up = [(i, (i + 1) % peers) for i in range(peers if wrap else peers - 1)]
        down = [(j, i) for i, j in up]
        last = lax.slice_in_dim(value, length - width, length, axis=dim)
        initial = lax.slice_in_dim(value, 0, width, axis=dim)
        before = lax.ppermute(last, axis, up)
        after = lax.ppermute(initial, axis, down)
        value = jnp.concatenate([before, value, after], axis=dim)
    return value


def passed_along(block, axis, distance):
    devices = range(lax.axis_size(axis))
    route = [(i - distance, i) for i in devices if i - distance in devices]
    return lax.ppermute(block, axis, route)


def harmonic(first, second):
    return 2.0 * first * second / (first + second)


def conductivity(region, cond_table):
    classes = jnp.arange(cond_table.shape[0], dtype=jnp.int32)
    onehot = (region[..., None] == classes).astype(jnp.float32)
    return jnp.sum(onehot * cond_table, axis=-1)


def extend(stack):
    lat_ext = padded(stack, (("lat", 2),), 1, False)
    both = padded(lat_ext, (("lon", 3),), 1, True)
    return jnp.pad(both, ((0, 0), (1, 1), (0, 0), (0, 0)))


def face_weights(kext):
    centre = kext[1:-1, 1:-1, 1:-1]
    return (
        harmonic(centre, kext[:-2, 1:-1, 1:-1]),
        harmonic(centre, kext[2:, 1:-1, 1:-1]),
        harmonic(centre, kext[1:-1, :-2, 1:-1]),
        harmonic(centre, kext[1:-1, 2:, 1:-1]),
        harmonic(centre, kext[1:-1, 1:-1, :-2]),
        harmonic(centre, kext[1:-1, 1:-1, 2:]),
    )


def neighbours(weights, ext):
    near = weights[0] * ext[..., :-2, 1:-1, 1:-1] + weights[1] * ext[..., 2:, 1:-1, 1:-1]
    near = near + weights[2] * ext[..., 1:-1, :-2, 1:-1] + weights[3] * ext[..., 1:-1, 2:, 1:-1]
    near = near + weights[4] * ext[..., 1:-1, 1:-1, :-2] + weights[5] * ext[..., 1:-1, 1:-1, 2:]
    return near


def on_device(iterate, heating, initial, region, cond_table):
    steps = lax.axis_size("tm")
    own = lax.axis_index("tm")
    high = lax.Precision.HIGHEST
    kfield = conductivity(region, cond_table)
    ext = extend(jnp.stack([kfield, iterate[0]]))
    weights = face_weights(ext[0])
    total = weights[0] + weights[1] + weights[2] + weights[3] + weights[4] + weights[5]
    shifted = passed_along(iterate, "tm", 1)[0]
    previous = jnp.where(own == 0, initial, shifted)
    residual = heating[0] + previous - ((1.0 + total) * iterate[0] - neighbours(weights, ext[1]))
    scale_own = corner_weight ** (own.astype(jnp.float32) / steps)
    scaled = residual * scale_own
    zeros = jnp.zeros_like(residual)
    piece = lax.all_gather(scaled[None], "tm", axis=0, tiled=True)
    order = jnp.arange(piece.shape[0], dtype=jnp.int32)
    angle = 2.0 * jnp.pi / steps * (own * order % steps).astype(jnp.float32)
    real_part = jnp.einsum("n,nabc->abc", jnp.cos(angle), piece, precision=high)
    imag_part = (zeros, zeros)[1] - jnp.einsum("n,nabc->abc", jnp.sin(angle), piece, precision=high)
    beta = corner_weight ** (1.0 / steps)
    freq_angle = 2.0 * jnp.pi / steps * (own % steps).astype(jnp.float32)
    diag_re = 1.0 - beta * jnp.cos(freq_angle) + total
    diag_im = beta * jnp.sin(freq_angle) + zeros
    denom = diag_re * diag_re + diag_im * diag_im
    inv_re = diag_re / denom
    inv_im = -diag_im / denom
    sol_re = real_part * inv_re - imag_part * inv_im
    sol_im = real_part * inv_im + imag_part * inv_re
    for sweep in range(SWEEPS - 1):
        near = neighbours(weights, extend(jnp.stack([sol_re, sol_im])))
        rhs_re = real_part + near[0]
        rhs_im = imag_part + near[1]
        sol_re = rhs_re * inv_re - rhs_im * inv_im
        sol_im = rhs_re * inv_im + rhs_im * inv_re
    pieces = (
        lax.all_gather(sol_re[None], "tm", axis=0, tiled=True),
        lax.all_gather(sol_im[None], "tm", axis=0, tiled=True),
    )
    order = jnp.arange(pieces[0].shape[0], dtype=jnp.int32)
    angle = 2.0 * jnp.pi / steps * (order * own % steps).astype(jnp.float32)
    summed = jnp.einsum("k,kabc->abc", jnp.cos(angle), pieces[0], precision=high) - jnp.einsum(
        "k,kabc->abc", jnp.sin(angle), pieces[1], precision=high
    )
    back = summed / steps
    return iterate + (back / scale_own)[None]


HALO = 4
TILE = 8


def specs(count, hbm):
    return [pl.BlockSpec(memory_space=pltpu.HBM if i in hbm else pltpu.VMEM) for i in range(count)]


def call(body, outs, ins, scratch=(), limit=8, smem=0, hbm_ins=(), hbm_outs=(), aliases={}):
    moved = sum(x.size * 4 for x in ins) + sum(x.size * 4 for x in outs)
    return pl.pallas_call(
        body,
        out_shape=outs,
        in_specs=specs(len(ins) - smem, hbm_ins) + [pl.BlockSpec(memory_space=pltpu.SMEM)] * smem,
        out_specs=specs(len(outs), hbm_outs),
        scratch_shapes=scratch,
        input_output_aliases=aliases,
        compiler_params=pltpu.CompilerParams(vmem_limit_bytes=limit << 20),
        cost_estimate=pl.CostEstimate(flops=moved * 4, bytes_accessed=moved, transcendentals=0),
    )(*ins)


def shape(*dims):
    return jax.ShapeDtypeStruct(dims, jnp.float32)


def ids(rows, dim, lanes=128):
    return lax.broadcasted_iota(jnp.int32, (rows, lanes), dim)


def other_half(lane, t):
    return ((lane + 64 * t) & 127) >= 64


def cat(*values):
    return jnp.concatenate(values, axis=0)


def blocks(count, width, read, write):
    def body(i, carry):
        for u in range(width):
            write(i * width + u, read(i * width + u))
        return carry

    lax.fori_loop(0, count // width, body, 0)


def put(*refs, at=0):
    def write(l, values):
        for ref, value in zip(refs, values):
            ref[l + at] = value

    return write


def pack_halves(ref, out, base, lo, hi, mask):
    half = ref.shape[0] // 2

    def read(i):
        l = lo + i
        return (jnp.where(mask, ref[l], pltpu.roll(ref[l + half], 64, 1)),)

    blocks(hi - lo, 8, read, put(out, at=base + lo))


def pack_strips(jobs):
    rows = jobs[0][1].shape[1]
    group = ids(rows, 1) // HALO
    accs = [jnp.zeros((rows, 128), jnp.float32) for _ in jobs]
    for g in range(32):
        for i, (read, _, _, first) in enumerate(jobs):
            accs[i] = jnp.where(group == g, pltpu.roll(read(g), (HALO * g + 128 - first) & 127, 1), accs[i])
    for acc, (_, out, place, _) in zip(accs, jobs):
        out[place] = acc


def levels_of(ref, G):
    return lambda g: ref[32 * G + g]


CHUNKS = 4
OUTER = 48
INNER = 51
LAT_TILES = 54


def send_first(it_hbm, h_hbm, xm, it, h, sems):
    t = lax.axis_index("tm")
    levels, rows = it.shape[:2]
    half, groups = levels // 2, levels // 32
    part = half // CHUNKS
    copies = []
    for c in range(CHUNKS):
        for f, (source, target) in enumerate(((it_hbm, it), (h_hbm, h))):
            for s in range(2):
                span = pl.ds(s * half + c * part, part)
                copy = pltpu.make_async_copy(source.at[span], target.at[span], sems.at[c, f, s])
                copy.start()
                copies.append(copy)
    mask = other_half(ids(rows, 1), t)
    for c in range(CHUNKS):
        for f, ref in enumerate((it, h)):
            for s in range(2):
                copies[4 * c + 2 * f + s].wait()
            pack_halves(ref, xm, f * half, c * part, (c + 1) * part, mask)
    pack_strips(
        [
            (levels_of(ref, G), xm, 2 * half + f * groups + G, 60 + 4 * t)
            for f, ref in enumerate((it, h))
            for G in range(groups)
        ]
    )


def even(axis):
    return lax.rem(lax.axis_index(axis), 2) == 0


def send_sides(it, h, region_hbm, initial_hbm, table, kap, heat, initial, near_sides, far_sides, region, right, left, sems):
    groups = it.shape[0] // 32
    part = it.shape[0] // CHUNKS
    copies = []
    for c in range(CHUNKS):
        for i, (source, target) in enumerate(((region_hbm, region), (initial_hbm, initial))):
            span = pl.ds(c * part, part)
            copy = pltpu.make_async_copy(source.at[span], target.at[span], sems.at[c, i])
            copy.start()
            copies.append(copy)
    near_right = even("lon")
    count = near_sides.shape[0]

    def pack(f, ref):
        pack_strips(
            [
                (levels_of(ref, G), out, f * groups + G, first)
                for out, first in ((right, 124), (left, 0))
                for G in range(groups)
            ]
        )

    pack(0, it)
    begin = jnp.where(lax.axis_index("tm") == 0, 1.0, 0.0)
    for copy in copies:
        copy.wait()

    def read(l):
        classes = region[l]
        value = jnp.full(classes.shape, table[0], jnp.float32)
        for c in range(1, table.shape[0]):
            value = jnp.where(classes == c, table[c], value)
        return value, h[l] + begin * initial[l]

    blocks(region.shape[0], 8, read, put(kap, heat))
    pack(1, heat)
    pack(2, kap)
    for i in range(count):
        near_sides[i] = jnp.where(near_right, right[i], left[i])
        far_sides[i] = jnp.where(near_right, left[i], right[i])


def edge_pair(first, second):
    top = ids(TILE, 0) < HALO
    first_up = even("lat")
    down = jnp.where(top, first[:TILE], pltpu.roll(second[:TILE], HALO, 0))
    up = jnp.where(top, pltpu.roll(first[-TILE:], HALO, 0), second[-TILE:])
    return jnp.where(first_up, up, down), jnp.where(first_up, down, up)


def send_rows(it, heat, kap, near_lat, far_lat, near_diag, far_diag, near_e, far_e):
    t = lax.axis_index("tm")
    levels = it.shape[0]
    half, groups = levels // 2, levels // 32
    other = other_half(ids(TILE, 1), t)
    own = jnp.logical_not(other)

    def read(l):
        found = []
        for low, high in zip(edge_pair(it[l], heat[l]), edge_pair(it[l + half], heat[l + half])):
            high_moved = pltpu.roll(high, 64, 1)
            found += [low, high, jnp.where(own, low, high_moved), jnp.where(other, low, high_moved)]
        return found

    def write(l, values):
        for at, (edges, lat, diag) in enumerate(((near_e, near_lat, near_diag), (far_e, far_lat, far_diag))):
            edges[l], edges[l + half], lat[l], diag[l] = values[4 * at : 4 * at + 4]

    blocks(half, 8, read, write)
    jobs = []
    inner_at = 64 - 4 * t
    for edges, lat, diag in ((near_e, near_lat, near_diag), (far_e, far_lat, far_diag)):
        for G in range(groups):
            jobs.append((levels_of(edges, G), lat, INNER + G, inner_at))
            jobs.append((levels_of(edges, G), diag, half + groups + G, 60 + 4 * t))
    pack_strips(jobs)
    quarter = half // 2

    def read_fixed(l):
        found = []
        for low, high in zip(
            edge_pair(kap[l], kap[l + half]), edge_pair(kap[l + quarter], kap[l + quarter + half])
        ):
            found += [low, high, jnp.where(own, low, pltpu.roll(high, 64, 1))]
        return found

    def write_fixed(l, values):
        for at, (edges, lat) in enumerate(((near_e, near_lat), (far_e, far_lat))):
            edges[l], edges[l + quarter], lat[half + l] = values[3 * at : 3 * at + 3]

    blocks(quarter, 8, read_fixed, write_fixed)
    pack_strips([(levels_of(edges, 0), lat, INNER + groups, inner_at) for edges, lat in ((near_e, near_lat), (far_e, far_lat))])


def side_strips(near_sides, far_sides):
    t = lax.axis_index("tm")
    from_near = (t == 0) != even("lon")
    count = near_sides.shape[0]
    own = [jnp.where(from_near, near_sides[i], far_sides[i]) for i in range(count)]
    partner = [jnp.where(from_near, far_sides[i], near_sides[i]) for i in range(count)]
    return own, partner


def add_rows(near_sides, far_sides, near_lat0, far_lat0, near_lat, far_lat):
    own, _ = side_strips(near_sides, far_sides)
    for i, (a, b) in enumerate(((0, 2), (1, 3), (4, 5))):
        put(near_lat, far_lat)(OUTER + i, edge_pair(own[a], own[b]))


def add_partner_rows(near_sides, far_sides, near_diag0, far_diag0, _, near_diag, far_diag, xs):
    groups = near_sides.shape[0] // 3
    _, partner = side_strips(near_sides, far_sides)
    for G in range(groups):
        put(near_diag, far_diag)(16 * groups + G, edge_pair(partner[G], partner[groups + G]))
    for i in range(2 * groups):
        xs[i] = partner[i]


def halo_tiles(near_pair, far_pair):
    first_up = even("lat")
    after = jnp.where(first_up, near_pair, far_pair)
    before = jnp.where(first_up, far_pair, near_pair)
    top = ids(TILE, 0) < HALO
    return (
        jnp.where(top, after, pltpu.roll(before, HALO, 0)),
        jnp.where(top, pltpu.roll(after, HALO, 0), before),
    )


def reciprocal(d):
    y = pl.reciprocal(d, approx=True)
    return y * (2.0 - d * y)


def face(a, b):
    return 2.0 * a * b * reciprocal(jnp.maximum(a + b, 1e-30))


def strip(value, g, at):
    return pltpu.roll(value, (at + 256 - HALO * g) & 127, 1)


def lanes_from(lane, at):
    return ((lane + 128 - at) & 127) < HALO


def clear_ends(*refs):
    for ref in refs:
        zero = jnp.zeros(ref.shape[1:], jnp.float32)
        ref[0] = zero
        ref[ref.shape[0] - 1] = zero


def woven(ref, l):
    return cat(*[ref[l, pl.ds(j, TILE, stride=3), :] for j in range(3)])


def next_row(x):
    return cat(x[TILE:], pltpu.roll(x[:TILE], TILE - 1, 0))


def last_row(x):
    return cat(pltpu.roll(x[-TILE:], 1, 0), x[:-TILE])


def near(around, w):
    low, mid, high = around
    wl, wh, wy, wyp, wx = w
    total = wl * low + wh * high
    total = total + (wy * next_row(mid) + wyp * last_row(mid))
    return total + (wx * pltpu.roll(mid, 127, 1) + pltpu.roll(wx * mid, 1, 1))


def packed(read, within, beside, G, half, upper=None):
    t = lax.axis_index("tm")
    lane = ids(within[0].shape[0], 1)
    outer_at = 124 * (1 - t)
    inner_at = 64 - 4 * t
    outer = lanes_from(lane, outer_at)
    inner = lanes_from(lane, inner_at)
    shift_levels = upper is None and 32 * G >= half
    upper = 32 * G >= half if upper is None else upper

    def read_level(g):
        found = []
        for f, value in enumerate(read(32 * G + g - (half if shift_levels else 0))):
            if upper:
                value = pltpu.roll(value, 64, 1)
            value = jnp.where(inner, strip(within[f], g, inner_at), value)
            if beside is not None:
                value = jnp.where(outer, strip(beside[f], g, outer_at), value)
            found.append(value)
        return found

    return read_level


def halo_of(near_pair, far_pair, base, within, beside, G, half, upper=None):
    def tiles(i):
        return halo_tiles(near_pair[i], far_pair[i])

    return packed(lambda l: tiles(base + l), tiles(within + G), tiles(beside + G), G, half, upper)


def assemble_main(it, heat, kap, near_sides, far_sides, own_it, part, K):
    levels, rows = it.shape[:2]
    groups = levels // 32
    outer_at = 124 * (1 - lax.axis_index("tm"))
    outer = lanes_from(ids(rows, 1), outer_at)
    own, _ = side_strips(near_sides, far_sides)
    for G in range(groups):
        def assemble(g):
            return [
                jnp.where(outer, strip(own[f * groups + G], g, outer_at), ref[32 * G + g])
                for f, ref in enumerate((it, heat, kap))
            ]

        blocks(32, 8, assemble, put(own_it, part, K, at=32 * G))


def prepare(
    it_m, part_m, K_m, near_lat, far_lat, _,
    wl, wy, wyp, wx, total, inv0, inv1, part, extra,
    K, own_it, part_n,
):
    t = lax.axis_index("tm")
    levels, own_rows = it_m.shape[:2]
    half, groups = levels // 2, levels // 32
    quarter = half // 2
    rows = own_rows + TILE
    before_other = jnp.where(t == 0, 1.0, 0.0)
    beta = corner_weight ** 0.5
    clear_ends(K, own_it)
    wl[0] = jnp.zeros((rows, 128), jnp.float32)

    for G in range(groups):
        moving = halo_of(near_lat, far_lat, 0, INNER, OUTER, G, half)

        def assemble(g):
            l = 32 * G + g
            mine, heat = moving(g)
            return cat(it_m[l], mine), cat(part_m[l], heat)

        def store(g, values):
            l = 32 * G + g
            own_it[l + 1], part_n[l] = values

        blocks(32, 8, assemble, store)

    for part_of in range(2):
        start = part_of * quarter
        fixed = halo_of(near_lat, far_lat, half - start, INNER + groups, OUTER + groups, 0, half, upper=part_of == 1)

        def assemble_fixed(i):
            low, high = fixed(start + i)
            return cat(K_m[start + i], low), cat(K_m[start + i + half], high)

        def store_fixed(i, values):
            K[start + i + 1], K[start + i + half + 1] = values

        blocks(quarter, 8, assemble_fixed, store_fixed)

    width = 8

    def weigh(i, carry):
        start = i * width
        ks = [woven(K, start), woven(K, start + 1)]
        its = [woven(own_it, start), woven(own_it, start + 1)]
        low = wl[start]
        for u in range(width):
            l = start + u
            ks = [*ks[-2:], woven(K, l + 2)]
            its = [*its[-2:], woven(own_it, l + 2)]
            here = ks[1]
            high = face(here, ks[2])
            row = face(here, next_row(here))
            before = last_row(row)
            lane = face(here, pltpu.roll(here, 127, 1))
            sums = (low + high) + (row + before) + (lane + pltpu.roll(lane, 1, 1))
            d0 = (1.0 - beta) + sums
            d1 = (1.0 + beta) + sums
            r = reciprocal(d0 * d1)
            left = woven(part_n, l) - ((1.0 + sums) * its[1] - near(its, (low, high, row, before, lane)))
            wl[l + 1] = high
            put(wy, wyp, wx, total, inv0, inv1, part, extra)(
                l, (row, before, lane, sums, d1 * r, d0 * r, left, before_other * its[1])
            )
            low = high
        return carry

    lax.fori_loop(0, levels // width, weigh, 0)


def unpack(xm, initial, it, heat):
    levels = it.shape[0]
    half, groups = levels // 2, levels // 32
    begin = jnp.where(lax.axis_index("tm") == 0, 0.0, 1.0)
    for G in range(groups):
        within = [xm[2 * half + f * groups + G] for f in range(2)]
        read = packed(lambda l: (xm[l], xm[half + l]), within, None, G, half)

        def with_initial(g):
            a, b = read(g)
            return a, b + begin * initial[32 * G + g]

        blocks(32, 8, with_initial, put(it, heat, at=32 * G))


def iterate_block(
    wl, wy, wyp, wx, total, inv0, inv1, part, extra, main_it, main_h, xs, near_diag, far_diag,
    w_own, w_send,
    it, h, s0, s1, x0, x1, y0, y1,
):
    t = lax.axis_index("tm")
    levels, rows = wy.shape[:2]
    own_rows = rows - TILE
    half, groups = levels // 2, levels // 32
    first = t == 0
    beta = corner_weight ** 0.5
    outer_at = 124 * (1 - t)
    outer = lanes_from(ids(own_rows, 1), outer_at)
    clear_ends(it, x0, x1, y0, y1)
    for G in range(groups):
        halo = halo_of(near_diag, far_diag, 0, half + groups, half, G, half)

        def assemble(g):
            l = 32 * G + g
            return [
                cat(jnp.where(outer, strip(xs[f * groups + G], g, outer_at), main[l]), tile)
                for f, (main, tile) in enumerate(zip((main_it, main_h), halo(g)))
            ]

        def store(g, values):
            it[32 * G + g + 1], h[32 * G + g] = values

        blocks(32, 8, assemble, store)

    def faces(l):
        return wl[l], wl[l + 1], wy[l], wyp[l], wx[l]

    def over(width, read, fields, step):
        def body(i, carry):
            start = i * width
            around = [[read(a, start), read(a, start + 1)] for a in fields]
            for u in range(width):
                around = [[*kept[-2:], read(a, start + u + 2)] for a, kept in zip(fields, around)]
                step(start + u, *around)
            return carry

        lax.fori_loop(0, levels // width, body, 0)

    def residual(l, around):
        mid = around[1]
        theirs = woven(h, l) + extra[l] - ((1.0 + total[l]) * mid - near(around, faces(l)))
        mine = part[l] + jnp.where(first, 0.0, 1.0) * mid
        r0 = jnp.where(first, mine, theirs)
        r1 = jnp.where(first, theirs, mine) * beta
        a, b = r0 + r1, r0 - r1
        put(s0, s1)(l, (a, b))
        put(x0, x1, at=1)(l, (a * inv0[l], b * inv1[l]))

    over(16, woven, (it,), residual)

    def sweep(l, around0, around1):
        w = faces(l)
        return (s0[l] + near(around0, w)) * inv0[l], (s1[l] + near(around1, w)) * inv1[l]

    def to(*refs):
        return lambda l, a, b: put(*refs, at=1)(l, sweep(l, a, b))

    def plain(ref, l):
        return ref[l]

    over(16, plain, (x0, x1), to(y0, y1))
    over(16, plain, (y0, y1), to(x0, x1))
    theirs = h

    def last(l, around0, around1):
        a, b = sweep(l, around0, around1)
        w0, w1 = (a + b) * 0.5, (a - b) * (0.5 / beta)
        for ref, value in ((w_own, jnp.where(first, w0, w1)), (theirs, jnp.where(first, w1, w0))):
            for j in range(3):
                ref[l, pl.ds(j, TILE, stride=3), :] = value[j * TILE : (j + 1) * TILE]

    over(16, plain, (x0, x1), last)
    handled = jnp.logical_not(other_half(ids(own_rows, 1), t))

    def pair(l):
        return (jnp.where(handled, theirs[l, :own_rows], pltpu.roll(theirs[l + half, :own_rows], 64, 1)),)

    blocks(half, 16, pair, put(w_send))


def finish(it, w_own, got, out_hbm, out, sems):
    t = lax.axis_index("tm")
    levels, rows = it.shape[:2]
    half = levels // 2
    part = half // CHUNKS
    handled = jnp.logical_not(other_half(ids(rows, 1), t))
    copies = []
    for c in range(CHUNKS):
        def read(i):
            l = c * part + i
            theirs = got[l]
            return (
                it[l] + jnp.where(handled, w_own[l, :rows], theirs),
                it[l + half] + jnp.where(handled, w_own[l + half, :rows], pltpu.roll(theirs, 64, 1)),
            )

        def write(i, values):
            l = c * part + i
            out[l], out[l + half] = values

        blocks(part, 4, read, write)
        for s in range(2):
            span = pl.ds(s * half + c * part, part)
            copy = pltpu.make_async_copy(out.at[span], out_hbm.at[span], sems.at[c, s])
            copy.start()
            copies.append(copy)
    for copy in copies:
        copy.wait()


def two_steps(iterate, heating, initial, region, cond_table):
    it, h = iterate[0], heating[0]
    levels, rows, lanes = it.shape
    half, groups = levels // 2, levels // 32
    lats, lons = lax.axis_size("lat"), lax.axis_size("lon")
    swap = [(0, 1), (1, 0)]
    pairs = [[(i, i + 1) for i in range(start, lats - 1, 2)] for start in (0, 1)]
    pairs = [p + [(j, i) for i, j in p] for p in pairs]
    diagonals = [[(t * lats + i, (1 - t) * lats + j) for t in range(2) for i, j in p] for p in pairs]
    round_lon = [[(i, (i + 1) % lons) for i in range(start, lons, 2)] for start in (0, 1)]
    round_lon = [p + [(j, i) for i, j in p] for p in round_lon]
    full = shape(levels, rows, lanes)
    wide = shape(levels, rows + TILE, lanes)

    def in_hbm(x):
        return pltpu.with_memory_space_constraint(x, pltpu.HBM)

    xm, it, h = call(
        send_first,
        [shape(levels + 2 * groups, rows, lanes), full, full],
        [in_hbm(it), in_hbm(h)],
        scratch=[pltpu.SemaphoreType.DMA((CHUNKS, 2, 2))],
        hbm_ins=(0, 1),
    )
    xm = lax.ppermute(xm, "tm", swap)
    sides = shape(3 * groups, rows, lanes)
    kap, heat, start, near_sides, far_sides = call(
        send_sides,
        [full, full, full, sides, sides],
        [it, h, in_hbm(region), in_hbm(initial), cond_table],
        scratch=[pltpu.VMEM(it.shape, jnp.int32)]
        + [pltpu.VMEM(sides.shape, jnp.float32)] * 2
        + [pltpu.SemaphoreType.DMA((CHUNKS, 2))],
        smem=1,
        hbm_ins=(2, 3),
    )
    near_sides = lax.ppermute(near_sides, "lon", round_lon[0])
    far_sides = lax.ppermute(far_sides, "lon", round_lon[1])
    lat = shape(LAT_TILES, TILE, lanes)
    diag = shape(half + 2 * groups, TILE, lanes)
    messages = call(
        send_rows,
        [lat, lat, diag, diag],
        [it, heat, kap],
        scratch=[pltpu.VMEM((levels, TILE, lanes), jnp.float32)] * 2,
    )
    near_lat, far_lat = call(add_rows, [lat, lat], [near_sides, far_sides, *messages[:2]], aliases={2: 0, 3: 1})
    near_lat = lax.ppermute(near_lat, "lat", pairs[0])
    far_lat = lax.ppermute(far_lat, "lat", pairs[1])
    main = call(assemble_main, [full] * 3, [it, heat, kap, near_sides, far_sides])
    near_diag, far_diag, xs = call(
        add_partner_rows,
        [diag, diag, shape(2 * groups, rows, lanes)],
        [near_sides, far_sides, *messages[2:], main[2]],
        aliases={2: 0, 3: 1},
    )
    near_diag = lax.ppermute(near_diag, ("tm", "lat"), diagonals[0])
    far_diag = lax.ppermute(far_diag, ("tm", "lat"), diagonals[1])
    xs = lax.ppermute(xs, "tm", swap)
    main_it, main_h = call(unpack, [full, full], [xm, start])
    deep = pltpu.VMEM((levels + 2, rows + TILE, lanes), jnp.float32)
    flat = pltpu.VMEM((levels, rows + TILE, lanes), jnp.float32)
    ready = call(
        prepare,
        [shape(levels + 1, rows + TILE, lanes)] + [wide] * 8,
        [*main, near_lat, far_lat, main_it],
        scratch=[deep] * 2 + [flat],
        limit=16,
    )
    w_own, w_send = call(
        iterate_block,
        [wide, shape(half, rows, lanes)],
        [*ready, main_it, main_h, xs, near_diag, far_diag],
        scratch=[deep] + [flat] * 3 + [deep] * 4,
        limit=24,
    )
    got = lax.ppermute(w_send, "tm", swap)
    (out,) = call(
        finish,
        [full],
        [it, w_own, got],
        scratch=[pltpu.VMEM(it.shape, jnp.float32), pltpu.SemaphoreType.DMA((CHUNKS, 2))],
        hbm_outs=(0,),
    )
    return out[None]


def solution(mesh):
    return jax.shard_map(
        two_steps if mesh.shape["tm"] == 2 else on_device,
        mesh=mesh,
        in_specs=(
            P("tm", None, "lat", "lon"),
            P("tm", None, "lat", "lon"),
            P(None, "lat", "lon"),
            P(None, "lat", "lon"),
            P(),
        ),
        out_specs=P("tm", None, "lat", "lon"),
        check_vma=False,
    )
```

```python
import functools

import jax
import jax.numpy as jnp
from jax import lax
from jax.experimental import pallas as pl
from jax.experimental.pallas import tpu as pltpu
from jax.sharding import PartitionSpec as P

SWEEPS = 4


corner_weight = 0.1


def padded(value, sides, width, wrap):
    for axis, dim in sides:
        peers, length = (lax.axis_size(axis), value.shape[dim])
        up = [(i, (i + 1) % peers) for i in range(peers if wrap else peers - 1)]
        down = [(j, i) for i, j in up]
        last = lax.slice_in_dim(value, length - width, length, axis=dim)
        initial = lax.slice_in_dim(value, 0, width, axis=dim)
        before = lax.ppermute(last, axis, up)
        after = lax.ppermute(initial, axis, down)
        value = jnp.concatenate([before, value, after], axis=dim)
    return value


def passed_along(block, axis, distance):
    devices = range(lax.axis_size(axis))
    route = [(i - distance, i) for i in devices if i - distance in devices]
    return lax.ppermute(block, axis, route)


def harmonic(first, second):
    return 2.0 * first * second / (first + second)


def conductivity(region, cond_table):
    classes = jnp.arange(cond_table.shape[0], dtype=jnp.int32)
    onehot = (region[..., None] == classes).astype(jnp.float32)
    return jnp.sum(onehot * cond_table, axis=-1)


def extend(stack):
    lat_ext = padded(stack, (("lat", 2),), 1, False)
    both = padded(lat_ext, (("lon", 3),), 1, True)
    return jnp.pad(both, ((0, 0), (1, 1), (0, 0), (0, 0)))


def face_weights(kext):
    centre = kext[1:-1, 1:-1, 1:-1]
    return (
        harmonic(centre, kext[:-2, 1:-1, 1:-1]),
        harmonic(centre, kext[2:, 1:-1, 1:-1]),
        harmonic(centre, kext[1:-1, :-2, 1:-1]),
        harmonic(centre, kext[1:-1, 2:, 1:-1]),
        harmonic(centre, kext[1:-1, 1:-1, :-2]),
        harmonic(centre, kext[1:-1, 1:-1, 2:]),
    )


def neighbours(weights, ext):
    near = weights[0] * ext[..., :-2, 1:-1, 1:-1] + weights[1] * ext[..., 2:, 1:-1, 1:-1]
    near = near + weights[2] * ext[..., 1:-1, :-2, 1:-1] + weights[3] * ext[..., 1:-1, 2:, 1:-1]
    near = near + weights[4] * ext[..., 1:-1, 1:-1, :-2] + weights[5] * ext[..., 1:-1, 1:-1, 2:]
    return near


def on_device(iterate, heating, initial, region, cond_table):
    steps = lax.axis_size("tm")
    own = lax.axis_index("tm")
    high = lax.Precision.HIGHEST
    kfield = conductivity(region, cond_table)
    ext = extend(jnp.stack([kfield, iterate[0]]))
    weights = face_weights(ext[0])
    total = weights[0] + weights[1] + weights[2] + weights[3] + weights[4] + weights[5]
    shifted = passed_along(iterate, "tm", 1)[0]
    previous = jnp.where(own == 0, initial, shifted)
    residual = heating[0] + previous - ((1.0 + total) * iterate[0] - neighbours(weights, ext[1]))
    scale_own = corner_weight ** (own.astype(jnp.float32) / steps)
    scaled = residual * scale_own
    zeros = jnp.zeros_like(residual)
    piece = lax.all_gather(scaled[None], "tm", axis=0, tiled=True)
    order = jnp.arange(piece.shape[0], dtype=jnp.int32)
    angle = 2.0 * jnp.pi / steps * (own * order % steps).astype(jnp.float32)
    real_part = jnp.einsum("n,nabc->abc", jnp.cos(angle), piece, precision=high)
    imag_part = (zeros, zeros)[1] - jnp.einsum("n,nabc->abc", jnp.sin(angle), piece, precision=high)
    beta = corner_weight ** (1.0 / steps)
    freq_angle = 2.0 * jnp.pi / steps * (own % steps).astype(jnp.float32)
    diag_re = 1.0 - beta * jnp.cos(freq_angle) + total
    diag_im = beta * jnp.sin(freq_angle) + zeros
    denom = diag_re * diag_re + diag_im * diag_im
    inv_re = diag_re / denom
    inv_im = -diag_im / denom
    sol_re = real_part * inv_re - imag_part * inv_im
    sol_im = real_part * inv_im + imag_part * inv_re
    for sweep in range(SWEEPS - 1):
        near = neighbours(weights, extend(jnp.stack([sol_re, sol_im])))
        rhs_re = real_part + near[0]
        rhs_im = imag_part + near[1]
        sol_re = rhs_re * inv_re - rhs_im * inv_im
        sol_im = rhs_re * inv_im + rhs_im * inv_re
    pieces = (
        lax.all_gather(sol_re[None], "tm", axis=0, tiled=True),
        lax.all_gather(sol_im[None], "tm", axis=0, tiled=True),
    )
    order = jnp.arange(pieces[0].shape[0], dtype=jnp.int32)
    angle = 2.0 * jnp.pi / steps * (order * own % steps).astype(jnp.float32)
    summed = jnp.einsum("k,kabc->abc", jnp.cos(angle), pieces[0], precision=high) - jnp.einsum(
        "k,kabc->abc", jnp.sin(angle), pieces[1], precision=high
    )
    back = summed / steps
    return iterate + (back / scale_own)[None]


HALO = 4
TILE = 8


def specs(count, hbm):
    return [pl.BlockSpec(memory_space=pltpu.HBM if i in hbm else pltpu.VMEM) for i in range(count)]


def call(body, outs, ins, scratch=(), limit=8, smem=0, hbm_ins=(), hbm_outs=(), aliases={}):
    moved = sum(x.size * 4 for x in ins) + sum(x.size * 4 for x in outs)
    return pl.pallas_call(
        body,
        out_shape=outs,
        in_specs=specs(len(ins) - smem, hbm_ins) + [pl.BlockSpec(memory_space=pltpu.SMEM)] * smem,
        out_specs=specs(len(outs), hbm_outs),
        scratch_shapes=scratch,
        input_output_aliases=aliases,
        compiler_params=pltpu.CompilerParams(vmem_limit_bytes=limit << 20),
        cost_estimate=pl.CostEstimate(flops=moved * 4, bytes_accessed=moved, transcendentals=0),
    )(*ins)


def shape(*dims):
    return jax.ShapeDtypeStruct(dims, jnp.float32)


def ids(rows, dim, lanes=128):
    return lax.broadcasted_iota(jnp.int32, (rows, lanes), dim)


def other_half(lane, t):
    return ((lane + 64 * t) & 127) >= 64


def cat(*values):
    return jnp.concatenate(values, axis=0)


def blocks(count, width, read, write):
    def body(i, carry):
        for u in range(width):
            write(i * width + u, read(i * width + u))
        return carry

    lax.fori_loop(0, count // width, body, 0)


def put(*refs, at=0):
    def write(l, values):
        for ref, value in zip(refs, values):
            ref[l + at] = value

    return write


def pack_halves(ref, out, base, lo, hi, mask):
    half = ref.shape[0] // 2

    def read(i):
        l = lo + i
        return (jnp.where(mask, ref[l], pltpu.roll(ref[l + half], 64, 1)),)

    blocks(hi - lo, 8, read, put(out, at=base + lo))


def pack_strips(jobs):
    rows = jobs[0][1].shape[1]
    group = ids(rows, 1) // HALO
    accs = [jnp.zeros((rows, 128), jnp.float32) for _ in jobs]
    for g in range(32):
        for i, (read, _, _, first) in enumerate(jobs):
            accs[i] = jnp.where(group == g, pltpu.roll(read(g), (HALO * g + 128 - first) & 127, 1), accs[i])
    for acc, (_, out, place, _) in zip(accs, jobs):
        out[place] = acc


def levels_of(ref, G):
    return lambda g: ref[32 * G + g]


CHUNKS = 4
OUTER = 48
INNER = 51
LAT_TILES = 54


def send_first(it_hbm, h_hbm, xm, it, h, sems):
    t = lax.axis_index("tm")
    levels, rows = it.shape[:2]
    half, groups = levels // 2, levels // 32
    part = half // CHUNKS
    copies = []
    for c in range(CHUNKS):
        for f, (source, target) in enumerate(((it_hbm, it), (h_hbm, h))):
            for s in range(2):
                span = pl.ds(s * half + c * part, part)
                copy = pltpu.make_async_copy(source.at[span], target.at[span], sems.at[c, f, s])
                copy.start()
                copies.append(copy)
    mask = other_half(ids(rows, 1), t)
    for c in range(CHUNKS):
        for f, ref in enumerate((it, h)):
            for s in range(2):
                copies[4 * c + 2 * f + s].wait()
            pack_halves(ref, xm, f * half, c * part, (c + 1) * part, mask)
    pack_strips(
        [
            (levels_of(ref, G), xm, 2 * half + f * groups + G, 60 + 4 * t)
            for f, ref in enumerate((it, h))
            for G in range(groups)
        ]
    )


def even(axis):
    return lax.rem(lax.axis_index(axis), 2) == 0


def send_sides(it, h, region, initial, table, kap, heat, near_sides, far_sides, right, left):
    groups = it.shape[0] // 32
    near_right = even("lon")
    count = near_sides.shape[0]

    def pack(f, ref):
        pack_strips(
            [
                (levels_of(ref, G), out, f * groups + G, first)
                for out, first in ((right, 124), (left, 0))
                for G in range(groups)
            ]
        )

    pack(0, it)
    begin = jnp.where(lax.axis_index("tm") == 0, 1.0, 0.0)
    def read(l):
        classes = region[l]
        value = jnp.full(classes.shape, table[0], jnp.float32)
        for c in range(1, table.shape[0]):
            value = jnp.where(classes == c, table[c], value)
        return value, h[l] + begin * initial[l]

    blocks(region.shape[0], 8, read, put(kap, heat))
    pack(1, heat)
    pack(2, kap)
    for i in range(count):
        near_sides[i] = jnp.where(near_right, right[i], left[i])
        far_sides[i] = jnp.where(near_right, left[i], right[i])


def edge_pair(first, second):
    top = ids(TILE, 0) < HALO
    first_up = even("lat")
    down = jnp.where(top, first[:TILE], pltpu.roll(second[:TILE], HALO, 0))
    up = jnp.where(top, pltpu.roll(first[-TILE:], HALO, 0), second[-TILE:])
    return jnp.where(first_up, up, down), jnp.where(first_up, down, up)


def send_rows(it, heat, kap, near_lat, far_lat, near_diag, far_diag, near_e, far_e):
    t = lax.axis_index("tm")
    levels = it.shape[0]
    half, groups = levels // 2, levels // 32
    other = other_half(ids(TILE, 1), t)
    own = jnp.logical_not(other)

    def read(l):
        found = []
        for low, high in zip(edge_pair(it[l], heat[l]), edge_pair(it[l + half], heat[l + half])):
            high_moved = pltpu.roll(high, 64, 1)
            found += [low, high, jnp.where(own, low, high_moved), jnp.where(other, low, high_moved)]
        return found

    def write(l, values):
        for at, (edges, lat, diag) in enumerate(((near_e, near_lat, near_diag), (far_e, far_lat, far_diag))):
            edges[l], edges[l + half], lat[l], diag[l] = values[4 * at : 4 * at + 4]

    blocks(half, 8, read, write)
    jobs = []
    inner_at = 64 - 4 * t
    for edges, lat, diag in ((near_e, near_lat, near_diag), (far_e, far_lat, far_diag)):
        for G in range(groups):
            jobs.append((levels_of(edges, G), lat, INNER + G, inner_at))
            jobs.append((levels_of(edges, G), diag, half + groups + G, 60 + 4 * t))
    pack_strips(jobs)
    quarter = half // 2

    def read_fixed(l):
        found = []
        for low, high in zip(
            edge_pair(kap[l], kap[l + half]), edge_pair(kap[l + quarter], kap[l + quarter + half])
        ):
            found += [low, high, jnp.where(own, low, pltpu.roll(high, 64, 1))]
        return found

    def write_fixed(l, values):
        for at, (edges, lat) in enumerate(((near_e, near_lat), (far_e, far_lat))):
            edges[l], edges[l + quarter], lat[half + l] = values[3 * at : 3 * at + 3]

    blocks(quarter, 8, read_fixed, write_fixed)
    pack_strips([(levels_of(edges, 0), lat, INNER + groups, inner_at) for edges, lat in ((near_e, near_lat), (far_e, far_lat))])


def side_strips(near_sides, far_sides):
    t = lax.axis_index("tm")
    from_near = (t == 0) != even("lon")
    count = near_sides.shape[0]
    own = [jnp.where(from_near, near_sides[i], far_sides[i]) for i in range(count)]
    partner = [jnp.where(from_near, far_sides[i], near_sides[i]) for i in range(count)]
    return own, partner


def add_rows(near_sides, far_sides, near_lat0, far_lat0, near_lat, far_lat):
    own, _ = side_strips(near_sides, far_sides)
    blocks(LAT_TILES, 9, lambda i: (near_lat0[i], far_lat0[i]), put(near_lat, far_lat))
    for i, (a, b) in enumerate(((0, 2), (1, 3), (4, 5))):
        put(near_lat, far_lat)(OUTER + i, edge_pair(own[a], own[b]))


def add_partner_rows(near_sides, far_sides, near_diag0, far_diag0, _, near_diag, far_diag, xs):
    groups = near_sides.shape[0] // 3
    _, partner = side_strips(near_sides, far_sides)
    blocks(near_diag.shape[0], 9, lambda i: (near_diag0[i], far_diag0[i]), put(near_diag, far_diag))
    for G in range(groups):
        put(near_diag, far_diag)(16 * groups + G, edge_pair(partner[G], partner[groups + G]))
    for i in range(2 * groups):
        xs[i] = partner[i]


def halo_tiles(near_pair, far_pair):
    first_up = even("lat")
    after = jnp.where(first_up, near_pair, far_pair)
    before = jnp.where(first_up, far_pair, near_pair)
    top = ids(TILE, 0) < HALO
    return (
        jnp.where(top, after, pltpu.roll(before, HALO, 0)),
        jnp.where(top, pltpu.roll(after, HALO, 0), before),
    )


def reciprocal(d):
    y = pl.reciprocal(d, approx=True)
    return y * (2.0 - d * y)


def face(a, b):
    return 2.0 * a * b * reciprocal(jnp.maximum(a + b, 1e-30))


def strip(value, g, at):
    return pltpu.roll(value, (at + 256 - HALO * g) & 127, 1)


def lanes_from(lane, at):
    return ((lane + 128 - at) & 127) < HALO


def clear_ends(*refs):
    for ref in refs:
        zero = jnp.zeros(ref.shape[1:], jnp.float32)
        ref[0] = zero
        ref[ref.shape[0] - 1] = zero


def woven(ref, l):
    return cat(*[ref[l, pl.ds(j, TILE, stride=3), :] for j in range(3)])


def next_row(x):
    return cat(x[TILE:], pltpu.roll(x[:TILE], TILE - 1, 0))


def last_row(x):
    return cat(pltpu.roll(x[-TILE:], 1, 0), x[:-TILE])


def near(around, w):
    low, mid, high = around
    wl, wh, wy, wyp, wx = w
    total = wl * low + wh * high
    total = total + (wy * next_row(mid) + wyp * last_row(mid))
    return total + (wx * pltpu.roll(mid, 127, 1) + pltpu.roll(wx * mid, 1, 1))


def packed(read, within, beside, G, half, upper=None):
    t = lax.axis_index("tm")
    lane = ids(within[0].shape[0], 1)
    outer_at = 124 * (1 - t)
    inner_at = 64 - 4 * t
    outer = lanes_from(lane, outer_at)
    inner = lanes_from(lane, inner_at)
    shift_levels = upper is None and 32 * G >= half
    upper = 32 * G >= half if upper is None else upper

    def read_level(g):
        found = []
        for f, value in enumerate(read(32 * G + g - (half if shift_levels else 0))):
            if upper:
                value = pltpu.roll(value, 64, 1)
            value = jnp.where(inner, strip(within[f], g, inner_at), value)
            if beside is not None:
                value = jnp.where(outer, strip(beside[f], g, outer_at), value)
            found.append(value)
        return found

    return read_level


def halo_of(near_pair, far_pair, base, within, beside, G, half, upper=None):
    def tiles(i):
        return halo_tiles(near_pair[i], far_pair[i])

    return packed(lambda l: tiles(base + l), tiles(within + G), tiles(beside + G), G, half, upper)


def assemble_main(it, heat, kap, near_sides, far_sides, own_it, part, K):
    levels, rows = it.shape[:2]
    groups = levels // 32
    outer_at = 124 * (1 - lax.axis_index("tm"))
    outer = lanes_from(ids(rows, 1), outer_at)
    own, _ = side_strips(near_sides, far_sides)
    for G in range(groups):
        def assemble(g):
            return [
                jnp.where(outer, strip(own[f * groups + G], g, outer_at), ref[32 * G + g])
                for f, ref in enumerate((it, heat, kap))
            ]

        blocks(32, 8, assemble, put(own_it, part, K, at=32 * G))


def prepare(
    it_m, part_m, K_m, near_lat, far_lat, _,
    wl, wy, wyp, wx, total, inv0, inv1, part, extra,
    K, own_it, part_n,
):
    t = lax.axis_index("tm")
    levels, own_rows = it_m.shape[:2]
    half, groups = levels // 2, levels // 32
    quarter = half // 2
    rows = own_rows + TILE
    before_other = jnp.where(t == 0, 1.0, 0.0)
    beta = corner_weight ** 0.5
    clear_ends(K, own_it)
    wl[0] = jnp.zeros((rows, 128), jnp.float32)

    for G in range(groups):
        moving = halo_of(near_lat, far_lat, 0, INNER, OUTER, G, half)

        def assemble(g):
            l = 32 * G + g
            mine, heat = moving(g)
            return cat(it_m[l], mine), cat(part_m[l], heat)

        def store(g, values):
            l = 32 * G + g
            own_it[l + 1], part_n[l] = values

        blocks(32, 8, assemble, store)

    for part_of in range(2):
        start = part_of * quarter
        fixed = halo_of(near_lat, far_lat, half - start, INNER + groups, OUTER + groups, 0, half, upper=part_of == 1)

        def assemble_fixed(i):
            low, high = fixed(start + i)
            return cat(K_m[start + i], low), cat(K_m[start + i + half], high)

        def store_fixed(i, values):
            K[start + i + 1], K[start + i + half + 1] = values

        blocks(quarter, 8, assemble_fixed, store_fixed)

    width = 8

    def weigh(i, carry):
        start = i * width
        ks = [woven(K, start), woven(K, start + 1)]
        its = [woven(own_it, start), woven(own_it, start + 1)]
        low = wl[start]
        for u in range(width):
            l = start + u
            ks = [*ks[-2:], woven(K, l + 2)]
            its = [*its[-2:], woven(own_it, l + 2)]
            here = ks[1]
            high = face(here, ks[2])
            row = face(here, next_row(here))
            before = last_row(row)
            lane = face(here, pltpu.roll(here, 127, 1))
            sums = (low + high) + (row + before) + (lane + pltpu.roll(lane, 1, 1))
            d0 = (1.0 - beta) + sums
            d1 = (1.0 + beta) + sums
            r = reciprocal(d0 * d1)
            left = woven(part_n, l) - ((1.0 + sums) * its[1] - near(its, (low, high, row, before, lane)))
            wl[l + 1] = high
            put(wy, wyp, wx, total, inv0, inv1, part, extra)(
                l, (row, before, lane, sums, d1 * r, d0 * r, left, before_other * its[1])
            )
            low = high
        return carry

    lax.fori_loop(0, levels // width, weigh, 0)


def unpack(xm, initial, it, heat):
    levels = it.shape[0]
    half, groups = levels // 2, levels // 32
    begin = jnp.where(lax.axis_index("tm") == 0, 0.0, 1.0)
    for G in range(groups):
        within = [xm[2 * half + f * groups + G] for f in range(2)]
        read = packed(lambda l: (xm[l], xm[half + l]), within, None, G, half)

        def with_initial(g):
            a, b = read(g)
            return a, b + begin * initial[32 * G + g]

        blocks(32, 8, with_initial, put(it, heat, at=32 * G))


ENDS = (38, 36, 34, 32)
EDGE_LEVELS = 35
WIDTHS = ((19, 12, 17, 16), (13, 14, 15, 16))


def iterate_half(upper, wl, wy, wyp, wx, total, inv0, inv1, part, extra, main_it, main_h, xs, near_diag, far_diag, *refs):
    if upper:
        edge, w_own, w_send, *refs = refs
    else:
        w_own, w_send, edge, *refs = refs
    it, h, s0, s1, x0, x1, y0, y1, z0, z1 = refs
    t = lax.axis_index("tm")
    levels, rows = wy.shape[:2]
    own_rows = rows - TILE
    half, groups = levels // 2, levels // 32
    first = t == 0
    beta = corner_weight ** 0.5
    outer_at = 124 * (1 - t)
    outer = lanes_from(ids(own_rows, 1), outer_at)
    clear_ends(it, x0, x1, y0, y1, z0, z1)
    shared = [(it, ENDS[0], 3), (h, ENDS[0], 2)]
    for pair, stage in (((x0, x1), 1), ((y0, y1), 2), ((z0, z1), 3)):
        shared += [(ref, ENDS[stage], 3) for ref in pair]
    shared += [(ref, ENDS[3], ENDS[0] - ENDS[3]) for ref in (s0, s1)]
    shared = [(ref, l) for ref, lo, count in shared for l in range(lo, lo + count)]
    if upper:
        for i, (ref, l) in enumerate(shared):
            ref[l] = edge[i]
    ready = half + TILE
    for G in range(groups):
        lo, hi = max(32 * G, ready if upper else 0), min(32 * (G + 1), levels if upper else ready)
        if lo >= hi:
            continue
        halo = halo_of(near_diag, far_diag, 0, half + groups, half, G, half)

        def assemble(i):
            g = lo - 32 * G + i
            return [
                cat(jnp.where(outer, strip(xs[f * groups + G], g, outer_at), main[lo + i]), tile)
                for f, (main, tile) in enumerate(zip((main_it, main_h), halo(g)))
            ]

        def store(i, values):
            it[lo + i + 1], h[lo + i] = values

        blocks(hi - lo, 8, assemble, store)

    def faces(l):
        return wl[l], wl[l + 1], wy[l], wyp[l], wx[l]

    def over(stage, read, fields, step):
        width = WIDTHS[upper][stage]
        lo, hi = (ENDS[stage], levels) if upper else (0, ENDS[stage])

        def body(i, carry):
            start = lo + i * width
            around = [[read(a, start), read(a, start + 1)] for a in fields]
            for u in range(width):
                around = [[*kept[-2:], read(a, start + u + 2)] for a, kept in zip(fields, around)]
                step(start + u, *around)
            return carry

        lax.fori_loop(0, (hi - lo) // width, body, 0)

    def residual(l, around):
        mid = around[1]
        theirs = woven(h, l) + extra[l] - ((1.0 + total[l]) * mid - near(around, faces(l)))
        mine = part[l] + jnp.where(first, 0.0, 1.0) * mid
        r0 = jnp.where(first, mine, theirs)
        r1 = jnp.where(first, theirs, mine) * beta
        a, b = r0 + r1, r0 - r1
        put(s0, s1)(l, (a, b))
        put(x0, x1, at=1)(l, (a * inv0[l], b * inv1[l]))

    over(0, woven, (it,), residual)

    def sweep(l, around0, around1):
        w = faces(l)
        return (s0[l] + near(around0, w)) * inv0[l], (s1[l] + near(around1, w)) * inv1[l]

    def to(*refs):
        return lambda l, a, b: put(*refs, at=1)(l, sweep(l, a, b))

    def plain(ref, l):
        return ref[l]

    over(1, plain, (x0, x1), to(y0, y1))
    over(2, plain, (y0, y1), to(z0, z1))
    base = half if upper else 0

    def last(l, around0, around1):
        a, b = sweep(l, around0, around1)
        w0, w1 = (a + b) * 0.5, (a - b) * (0.5 / beta)
        for ref, at, value in ((w_own, l - base, jnp.where(first, w0, w1)), (h, l, jnp.where(first, w1, w0))):
            for j in range(3):
                ref[at, pl.ds(j, TILE, stride=3), :] = value[j * TILE : (j + 1) * TILE]

    over(3, plain, (z0, z1), last)
    handled = jnp.logical_not(other_half(ids(own_rows, 1), t))
    quarter = half // 2

    def pair(l):
        high = pltpu.roll(h[base + quarter + l, :own_rows], 64, 1)
        return (jnp.where(handled, h[base + l, :own_rows], high),)

    blocks(quarter, 16, pair, put(w_send))
    if not upper:
        for i, (ref, l) in enumerate(shared):
            edge[i] = ref[l]


def finish(base, it, w_own, got, *refs):
    out_hbm, out, sems = refs[-3:]
    t = lax.axis_index("tm")
    levels, rows = out.shape[:2]
    half = levels // 2
    part = half // CHUNKS
    handled = jnp.logical_not(other_half(ids(rows, 1), t))
    copies = []
    for c in range(CHUNKS):
        def read(i):
            l = c * part + i
            theirs = got[l]
            return (
                it[base + l] + jnp.where(handled, w_own[l, :rows], theirs),
                it[base + l + half] + jnp.where(handled, w_own[l + half, :rows], pltpu.roll(theirs, 64, 1)),
            )

        def write(i, values):
            l = c * part + i
            out[l], out[l + half] = values

        blocks(part, 4, read, write)
        for s in range(2):
            at = s * half + c * part
            copy = pltpu.make_async_copy(out.at[pl.ds(at, part)], out_hbm.at[pl.ds(base + at, part)], sems.at[c, s])
            copy.start()
            copies.append(copy)
    for copy in copies:
        copy.wait()


def two_steps(iterate, heating, initial, region, cond_table):
    it, h = iterate[0], heating[0]
    levels, rows, lanes = it.shape
    half, groups = levels // 2, levels // 32
    lats, lons = lax.axis_size("lat"), lax.axis_size("lon")
    swap = [(0, 1), (1, 0)]
    pairs = [[(i, i + 1) for i in range(start, lats - 1, 2)] for start in (0, 1)]
    pairs = [p + [(j, i) for i, j in p] for p in pairs]
    diagonals = [[(t * lats + i, (1 - t) * lats + j) for t in range(2) for i, j in p] for p in pairs]
    round_lon = [[(i, (i + 1) % lons) for i in range(start, lons, 2)] for start in (0, 1)]
    round_lon = [p + [(j, i) for i, j in p] for p in round_lon]
    full = shape(levels, rows, lanes)
    wide = shape(levels, rows + TILE, lanes)

    def in_hbm(x):
        return pltpu.with_memory_space_constraint(x, pltpu.HBM)

    xm, it, h = call(
        send_first,
        [shape(levels + 2 * groups, rows, lanes), full, full],
        [in_hbm(it), in_hbm(h)],
        scratch=[pltpu.SemaphoreType.DMA((CHUNKS, 2, 2))],
        hbm_ins=(0, 1),
    )
    xm = lax.ppermute(xm, "tm", swap)
    sides = shape(3 * groups, rows, lanes)
    kap, heat, near_sides, far_sides = call(
        send_sides,
        [full, full, sides, sides],
        [it, h, region, initial, cond_table],
        scratch=[pltpu.VMEM(sides.shape, jnp.float32)] * 2,
        smem=1,
    )
    near_sides = lax.ppermute(near_sides, "lon", round_lon[0])
    far_sides = lax.ppermute(far_sides, "lon", round_lon[1])
    lat = shape(LAT_TILES, TILE, lanes)
    diag = shape(half + 2 * groups, TILE, lanes)
    messages = call(
        send_rows,
        [lat, lat, diag, diag],
        [it, heat, kap],
        scratch=[pltpu.VMEM((levels, TILE, lanes), jnp.float32)] * 2,
    )
    near_lat, far_lat = call(add_rows, [lat, lat], [near_sides, far_sides, *messages[:2]])
    near_lat = lax.ppermute(near_lat, "lat", pairs[0])
    far_lat = lax.ppermute(far_lat, "lat", pairs[1])
    main = call(assemble_main, [full] * 3, [it, heat, kap, near_sides, far_sides])
    near_diag, far_diag, xs = call(
        add_partner_rows,
        [diag, diag, shape(2 * groups, rows, lanes)],
        [near_sides, far_sides, *messages[2:], main[2]],
    )
    near_diag = lax.ppermute(near_diag, ("tm", "lat"), diagonals[0])
    far_diag = lax.ppermute(far_diag, ("tm", "lat"), diagonals[1])
    xs = lax.ppermute(xs, "tm", swap)
    main_it, main_h = call(unpack, [full, full], [xm, initial])
    deep = pltpu.VMEM((levels + 2, rows + TILE, lanes), jnp.float32)
    flat = pltpu.VMEM((levels, rows + TILE, lanes), jnp.float32)
    ready = call(
        prepare,
        [shape(levels + 1, rows + TILE, lanes)] + [wide] * 8,
        [*main, near_lat, far_lat, main_it],
        scratch=[deep] * 2 + [flat],
        limit=16,
    )
    given = [*ready, main_it, main_h, xs, near_diag, far_diag]
    corrections = [shape(half, rows + TILE, lanes), shape(half // 2, rows, lanes)]
    fields = [deep, flat, flat, flat] + [deep] * 6
    w_low, send_low, edge = call(
        functools.partial(iterate_half, 0),
        [*corrections, shape(EDGE_LEVELS, rows + TILE, lanes)],
        given,
        scratch=fields,
        limit=24,
    )
    got_low = lax.ppermute(send_low, "tm", swap)
    w_high, send_high = call(
        functools.partial(iterate_half, 1), corrections, [*given, edge], scratch=fields, limit=24
    )
    got_high = lax.ppermute(send_high, "tm", swap)
    last_scratch = [pltpu.VMEM((half, rows, lanes), jnp.float32), pltpu.SemaphoreType.DMA((CHUNKS, 2))]
    (out,) = call(functools.partial(finish, 0), [full], [it, w_low, got_low], scratch=last_scratch, hbm_outs=(0,))
    (out,) = call(
        functools.partial(finish, half),
        [full],
        [it, w_high, got_high, out],
        scratch=last_scratch,
        hbm_ins=(3,),
        hbm_outs=(0,),
        aliases={3: 0},
    )
    return out[None]


def solution(mesh):
    return jax.shard_map(
        two_steps if mesh.shape["tm"] == 2 else on_device,
        mesh=mesh,
        in_specs=(
            P("tm", None, "lat", "lon"),
            P("tm", None, "lat", "lon"),
            P(None, "lat", "lon"),
            P(None, "lat", "lon"),
            P(),
        ),
        out_specs=P("tm", None, "lat", "lon"),
        check_vma=False,
    )
```

```python
import functools

import jax
import jax.numpy as jnp
from jax import lax
from jax.experimental import pallas as pl
from jax.experimental.pallas import tpu as pltpu
from jax.sharding import PartitionSpec as P

SWEEPS = 4


corner_weight = 0.1


def padded(value, sides, width, wrap):
    for axis, dim in sides:
        peers, length = (lax.axis_size(axis), value.shape[dim])
        up = [(i, (i + 1) % peers) for i in range(peers if wrap else peers - 1)]
        down = [(j, i) for i, j in up]
        last = lax.slice_in_dim(value, length - width, length, axis=dim)
        initial = lax.slice_in_dim(value, 0, width, axis=dim)
        before = lax.ppermute(last, axis, up)
        after = lax.ppermute(initial, axis, down)
        value = jnp.concatenate([before, value, after], axis=dim)
    return value


def passed_along(block, axis, distance):
    devices = range(lax.axis_size(axis))
    route = [(i - distance, i) for i in devices if i - distance in devices]
    return lax.ppermute(block, axis, route)


def harmonic(first, second):
    return 2.0 * first * second / (first + second)


def conductivity(region, cond_table):
    classes = jnp.arange(cond_table.shape[0], dtype=jnp.int32)
    onehot = (region[..., None] == classes).astype(jnp.float32)
    return jnp.sum(onehot * cond_table, axis=-1)


def extend(stack):
    lat_ext = padded(stack, (("lat", 2),), 1, False)
    both = padded(lat_ext, (("lon", 3),), 1, True)
    return jnp.pad(both, ((0, 0), (1, 1), (0, 0), (0, 0)))


def face_weights(kext):
    centre = kext[1:-1, 1:-1, 1:-1]
    return (
        harmonic(centre, kext[:-2, 1:-1, 1:-1]),
        harmonic(centre, kext[2:, 1:-1, 1:-1]),
        harmonic(centre, kext[1:-1, :-2, 1:-1]),
        harmonic(centre, kext[1:-1, 2:, 1:-1]),
        harmonic(centre, kext[1:-1, 1:-1, :-2]),
        harmonic(centre, kext[1:-1, 1:-1, 2:]),
    )


def neighbours(weights, ext):
    near = weights[0] * ext[..., :-2, 1:-1, 1:-1] + weights[1] * ext[..., 2:, 1:-1, 1:-1]
    near = near + weights[2] * ext[..., 1:-1, :-2, 1:-1] + weights[3] * ext[..., 1:-1, 2:, 1:-1]
    near = near + weights[4] * ext[..., 1:-1, 1:-1, :-2] + weights[5] * ext[..., 1:-1, 1:-1, 2:]
    return near


def on_device(iterate, heating, initial, region, cond_table):
    steps = lax.axis_size("tm")
    own = lax.axis_index("tm")
    high = lax.Precision.HIGHEST
    kfield = conductivity(region, cond_table)
    ext = extend(jnp.stack([kfield, iterate[0]]))
    weights = face_weights(ext[0])
    total = weights[0] + weights[1] + weights[2] + weights[3] + weights[4] + weights[5]
    shifted = passed_along(iterate, "tm", 1)[0]
    previous = jnp.where(own == 0, initial, shifted)
    residual = heating[0] + previous - ((1.0 + total) * iterate[0] - neighbours(weights, ext[1]))
    scale_own = corner_weight ** (own.astype(jnp.float32) / steps)
    scaled = residual * scale_own
    zeros = jnp.zeros_like(residual)
    piece = lax.all_gather(scaled[None], "tm", axis=0, tiled=True)
    order = jnp.arange(piece.shape[0], dtype=jnp.int32)
    angle = 2.0 * jnp.pi / steps * (own * order % steps).astype(jnp.float32)
    real_part = jnp.einsum("n,nabc->abc", jnp.cos(angle), piece, precision=high)
    imag_part = (zeros, zeros)[1] - jnp.einsum("n,nabc->abc", jnp.sin(angle), piece, precision=high)
    beta = corner_weight ** (1.0 / steps)
    freq_angle = 2.0 * jnp.pi / steps * (own % steps).astype(jnp.float32)
    diag_re = 1.0 - beta * jnp.cos(freq_angle) + total
    diag_im = beta * jnp.sin(freq_angle) + zeros
    denom = diag_re * diag_re + diag_im * diag_im
    inv_re = diag_re / denom
    inv_im = -diag_im / denom
    sol_re = real_part * inv_re - imag_part * inv_im
    sol_im = real_part * inv_im + imag_part * inv_re
    for sweep in range(SWEEPS - 1):
        near = neighbours(weights, extend(jnp.stack([sol_re, sol_im])))
        rhs_re = real_part + near[0]
        rhs_im = imag_part + near[1]
        sol_re = rhs_re * inv_re - rhs_im * inv_im
        sol_im = rhs_re * inv_im + rhs_im * inv_re
    pieces = (
        lax.all_gather(sol_re[None], "tm", axis=0, tiled=True),
        lax.all_gather(sol_im[None], "tm", axis=0, tiled=True),
    )
    order = jnp.arange(pieces[0].shape[0], dtype=jnp.int32)
    angle = 2.0 * jnp.pi / steps * (order * own % steps).astype(jnp.float32)
    summed = jnp.einsum("k,kabc->abc", jnp.cos(angle), pieces[0], precision=high) - jnp.einsum(
        "k,kabc->abc", jnp.sin(angle), pieces[1], precision=high
    )
    back = summed / steps
    return iterate + (back / scale_own)[None]


HALO = 4
TILE = 8


def specs(count, hbm):
    return [pl.BlockSpec(memory_space=pltpu.HBM if i in hbm else pltpu.VMEM) for i in range(count)]


def call(body, outs, ins, scratch=(), limit=8, hbm_ins=(), hbm_outs=(), aliases={}):
    moved = sum(x.size * 4 for x in ins) + sum(x.size * 4 for x in outs)
    return pl.pallas_call(
        body,
        out_shape=outs,
        in_specs=specs(len(ins), hbm_ins),
        out_specs=specs(len(outs), hbm_outs),
        scratch_shapes=scratch,
        input_output_aliases=aliases,
        compiler_params=pltpu.CompilerParams(vmem_limit_bytes=limit << 20),
        cost_estimate=pl.CostEstimate(flops=moved * 4, bytes_accessed=moved, transcendentals=0),
    )(*ins)


def shape(*dims):
    return jax.ShapeDtypeStruct(dims, jnp.float32)


def ids(rows, dim, lanes=128):
    return lax.broadcasted_iota(jnp.int32, (rows, lanes), dim)


def other_half(lane, t):
    return ((lane + 64 * t) & 127) >= 64


def cat(*values):
    return jnp.concatenate(values, axis=0)


def blocks(count, width, read, write):
    def body(i, carry):
        for u in range(width):
            write(i * width + u, read(i * width + u))
        return carry

    lax.fori_loop(0, count // width, body, 0)


def put(*refs, at=0):
    def write(l, values):
        for ref, value in zip(refs, values):
            ref[l + at] = value

    return write


def pack_halves(ref, out, base, lo, hi, mask):
    half = ref.shape[0] // 2

    def read(i):
        l = lo + i
        return (jnp.where(mask, ref[l], pltpu.roll(ref[l + half], 64, 1)),)

    blocks(hi - lo, 8, read, put(out, at=base + lo))


def pack_strips(jobs):
    rows = jobs[0][1].shape[1]
    group = ids(rows, 1) // HALO
    accs = [jnp.zeros((rows, 128), jnp.float32) for _ in jobs]
    for g in range(32):
        for i, (read, _, _, first) in enumerate(jobs):
            accs[i] = jnp.where(group == g, pltpu.roll(read(g), (HALO * g + 128 - first) & 127, 1), accs[i])
    for acc, (_, out, place, _) in zip(accs, jobs):
        out[place] = acc


def levels_of(ref, G):
    return lambda g: ref[32 * G + g]


CHUNKS = 4
OUTER = 48
INNER = 51
LAT_TILES = 54


def send_first(it_hbm, h_hbm, xm, it, h, sems):
    t = lax.axis_index("tm")
    levels, rows = it.shape[:2]
    half, groups = levels // 2, levels // 32
    part = half // CHUNKS
    copies = []
    for f, (source, target) in enumerate(((it_hbm, it), (h_hbm, h))):
        for c in range(CHUNKS):
            for s in range(2):
                span = pl.ds(s * half + c * part, part)
                copy = pltpu.make_async_copy(source.at[span], target.at[span], sems.at[f, c, s])
                copy.start()
                copies.append(copy)
    mask = other_half(ids(rows, 1), t)
    for f, ref in enumerate((it, h)):
        for c in range(CHUNKS):
            for s in range(2):
                copies[2 * CHUNKS * f + 2 * c + s].wait()
            pack_halves(ref, xm, f * half, c * part, (c + 1) * part, mask)
        pack_strips([(levels_of(ref, G), xm, 2 * half + f * groups + G, 60 + 4 * t) for G in range(groups)])


def even(axis):
    return lax.rem(lax.axis_index(axis), 2) == 0


def send_sides(it, h, region, initial, table_hbm, kap, heat, near_sides, far_sides, right, left, table, sem):
    groups = it.shape[0] // 32
    copy = pltpu.make_async_copy(table_hbm, table, sem)
    copy.start()
    near_right = even("lon")
    count = near_sides.shape[0]

    def pack(f, ref):
        pack_strips(
            [
                (levels_of(ref, G), out, f * groups + G, first)
                for out, first in ((right, 124), (left, 0))
                for G in range(groups)
            ]
        )

    pack(0, it)
    copy.wait()
    begin = jnp.where(lax.axis_index("tm") == 0, 1.0, 0.0)
    def read(l):
        classes = region[l]
        value = jnp.full(classes.shape, table[0], jnp.float32)
        for c in range(1, table.shape[0]):
            value = jnp.where(classes == c, table[c], value)
        return value, h[l] + begin * initial[l]

    blocks(region.shape[0], 8, read, put(kap, heat))
    pack(1, heat)
    pack(2, kap)
    for i in range(count):
        near_sides[i] = jnp.where(near_right, right[i], left[i])
        far_sides[i] = jnp.where(near_right, left[i], right[i])


def edge_pair(first, second):
    top = ids(TILE, 0) < HALO
    first_up = even("lat")
    down = jnp.where(top, first[:TILE], pltpu.roll(second[:TILE], HALO, 0))
    up = jnp.where(top, pltpu.roll(first[-TILE:], HALO, 0), second[-TILE:])
    return jnp.where(first_up, up, down), jnp.where(first_up, down, up)


def send_rows(it, heat, kap, near_lat, far_lat, near_diag, far_diag, near_e, far_e):
    t = lax.axis_index("tm")
    levels = it.shape[0]
    half, groups = levels // 2, levels // 32
    other = other_half(ids(TILE, 1), t)
    own = jnp.logical_not(other)

    def read(l):
        found = []
        for low, high in zip(edge_pair(it[l], heat[l]), edge_pair(it[l + half], heat[l + half])):
            high_moved = pltpu.roll(high, 64, 1)
            found += [low, high, jnp.where(own, low, high_moved), jnp.where(other, low, high_moved)]
        return found

    def write(l, values):
        for at, (edges, lat, diag) in enumerate(((near_e, near_lat, near_diag), (far_e, far_lat, far_diag))):
            edges[l], edges[l + half], lat[l], diag[l] = values[4 * at : 4 * at + 4]

    blocks(half, 8, read, write)
    jobs = []
    inner_at = 64 - 4 * t
    for edges, lat, diag in ((near_e, near_lat, near_diag), (far_e, far_lat, far_diag)):
        for G in range(groups):
            jobs.append((levels_of(edges, G), lat, INNER + G, inner_at))
            jobs.append((levels_of(edges, G), diag, half + groups + G, 60 + 4 * t))
    pack_strips(jobs)
    quarter = half // 2

    def read_fixed(l):
        found = []
        for low, high in zip(
            edge_pair(kap[l], kap[l + half]), edge_pair(kap[l + quarter], kap[l + quarter + half])
        ):
            found += [low, high, jnp.where(own, low, pltpu.roll(high, 64, 1))]
        return found

    def write_fixed(l, values):
        for at, (edges, lat) in enumerate(((near_e, near_lat), (far_e, far_lat))):
            edges[l], edges[l + quarter], lat[half + l] = values[3 * at : 3 * at + 3]

    blocks(quarter, 8, read_fixed, write_fixed)
    pack_strips([(levels_of(edges, 0), lat, INNER + groups, inner_at) for edges, lat in ((near_e, near_lat), (far_e, far_lat))])


def side_strips(near_sides, far_sides):
    t = lax.axis_index("tm")
    from_near = (t == 0) != even("lon")
    count = near_sides.shape[0]
    own = [jnp.where(from_near, near_sides[i], far_sides[i]) for i in range(count)]
    partner = [jnp.where(from_near, far_sides[i], near_sides[i]) for i in range(count)]
    return own, partner


def add_rows(near_sides, far_sides, near_lat0, far_lat0, near_lat, far_lat, xs):
    own, partner = side_strips(near_sides, far_sides)
    for i in range(xs.shape[0]):
        xs[i] = partner[i]
    blocks(LAT_TILES, 9, lambda i: (near_lat0[i], far_lat0[i]), put(near_lat, far_lat))
    for i, (a, b) in enumerate(((0, 2), (1, 3), (4, 5))):
        put(near_lat, far_lat)(OUTER + i, edge_pair(own[a], own[b]))


def add_partner_rows(near_sides, far_sides, near_diag0, far_diag0, _, near_diag, far_diag):
    groups = near_sides.shape[0] // 3
    _, partner = side_strips(near_sides, far_sides)
    blocks(near_diag.shape[0], 9, lambda i: (near_diag0[i], far_diag0[i]), put(near_diag, far_diag))
    for G in range(groups):
        put(near_diag, far_diag)(16 * groups + G, edge_pair(partner[G], partner[groups + G]))


def halo_tiles(near_pair, far_pair):
    first_up = even("lat")
    after = jnp.where(first_up, near_pair, far_pair)
    before = jnp.where(first_up, far_pair, near_pair)
    top = ids(TILE, 0) < HALO
    return (
        jnp.where(top, after, pltpu.roll(before, HALO, 0)),
        jnp.where(top, pltpu.roll(after, HALO, 0), before),
    )


def reciprocal(d):
    y = pl.reciprocal(d, approx=True)
    return y * (2.0 - d * y)


def face(a, b):
    return 2.0 * a * b * reciprocal(jnp.maximum(a + b, 1e-30))


def strip(value, g, at):
    return pltpu.roll(value, (at + 256 - HALO * g) & 127, 1)


def lanes_from(lane, at):
    return ((lane + 128 - at) & 127) < HALO


def clear_ends(*refs):
    for ref in refs:
        zero = jnp.zeros(ref.shape[1:], jnp.float32)
        ref[0] = zero
        ref[ref.shape[0] - 1] = zero


def woven(ref, l):
    return cat(*[ref[l, pl.ds(j, TILE, stride=3), :] for j in range(3)])


def next_row(x):
    return cat(x[TILE:], pltpu.roll(x[:TILE], TILE - 1, 0))


def last_row(x):
    return cat(pltpu.roll(x[-TILE:], 1, 0), x[:-TILE])


def near(around, w):
    low, mid, high = around
    wl, wh, wy, wyp, wx = w
    total = wl * low + wh * high
    total = total + (wy * next_row(mid) + wyp * last_row(mid))
    return total + (wx * pltpu.roll(mid, 127, 1) + pltpu.roll(wx * mid, 1, 1))


def packed(read, within, beside, G, half, upper=None):
    t = lax.axis_index("tm")
    lane = ids(within[0].shape[0], 1)
    outer_at = 124 * (1 - t)
    inner_at = 64 - 4 * t
    outer = lanes_from(lane, outer_at)
    inner = lanes_from(lane, inner_at)
    shift_levels = upper is None and 32 * G >= half
    upper = 32 * G >= half if upper is None else upper

    def read_level(g):
        found = []
        for f, value in enumerate(read(32 * G + g - (half if shift_levels else 0))):
            if upper:
                value = pltpu.roll(value, 64, 1)
            value = jnp.where(inner, strip(within[f], g, inner_at), value)
            if beside is not None:
                value = jnp.where(outer, strip(beside[f], g, outer_at), value)
            found.append(value)
        return found

    return read_level


def halo_of(near_pair, far_pair, base, within, beside, G, half, upper=None):
    def tiles(i):
        return halo_tiles(near_pair[i], far_pair[i])

    return packed(lambda l: tiles(base + l), tiles(within + G), tiles(beside + G), G, half, upper)


def assemble_main(it, heat, kap, near_sides, far_sides, own_it, part, K):
    levels, rows = it.shape[:2]
    groups = levels // 32
    outer_at = 124 * (1 - lax.axis_index("tm"))
    outer = lanes_from(ids(rows, 1), outer_at)
    own, _ = side_strips(near_sides, far_sides)
    for G in range(groups):
        def assemble(g):
            return [
                jnp.where(outer, strip(own[f * groups + G], g, outer_at), ref[32 * G + g])
                for f, ref in enumerate((it, heat, kap))
            ]

        blocks(32, 16, assemble, put(own_it, part, K, at=32 * G))


def prepare(
    it_m, part_m, K_m, near_lat, far_lat, _,
    wl, wy, wyp, wx, total, inv0, inv1, part, extra,
    K, own_it, part_n,
):
    t = lax.axis_index("tm")
    levels, own_rows = it_m.shape[:2]
    half, groups = levels // 2, levels // 32
    quarter = half // 2
    rows = own_rows + TILE
    before_other = jnp.where(t == 0, 1.0, 0.0)
    beta = corner_weight ** 0.5
    clear_ends(K, own_it)
    wl[0] = jnp.zeros((rows, 128), jnp.float32)

    for G in range(groups):
        moving = halo_of(near_lat, far_lat, 0, INNER, OUTER, G, half)

        def assemble(g):
            l = 32 * G + g
            mine, heat = moving(g)
            return cat(it_m[l], mine), cat(part_m[l], heat)

        def store(g, values):
            l = 32 * G + g
            own_it[l + 1], part_n[l] = values

        blocks(32, 16, assemble, store)

    for part_of in range(2):
        start = part_of * quarter
        fixed = halo_of(near_lat, far_lat, half - start, INNER + groups, OUTER + groups, 0, half, upper=part_of == 1)

        def assemble_fixed(i):
            low, high = fixed(start + i)
            return cat(K_m[start + i], low), cat(K_m[start + i + half], high)

        def store_fixed(i, values):
            K[start + i + 1], K[start + i + half + 1] = values

        blocks(quarter, 16, assemble_fixed, store_fixed)

    width = 16

    def weigh(i, carry):
        start = i * width
        ks = [woven(K, start), woven(K, start + 1)]
        its = [woven(own_it, start), woven(own_it, start + 1)]
        low = wl[start]
        for u in range(width):
            l = start + u
            ks = [*ks[-2:], woven(K, l + 2)]
            its = [*its[-2:], woven(own_it, l + 2)]
            here = ks[1]
            high = face(here, ks[2])
            row = face(here, next_row(here))
            before = last_row(row)
            lane = face(here, pltpu.roll(here, 127, 1))
            sums = (low + high) + (row + before) + (lane + pltpu.roll(lane, 1, 1))
            d0 = (1.0 - beta) + sums
            d1 = (1.0 + beta) + sums
            r = reciprocal(d0 * d1)
            left = woven(part_n, l) - ((1.0 + sums) * its[1] - near(its, (low, high, row, before, lane)))
            wl[l + 1] = high
            put(wy, wyp, wx, total, inv0, inv1, part, extra)(
                l, (row, before, lane, sums, d1 * r, d0 * r, left, before_other * its[1])
            )
            low = high
        return carry

    lax.fori_loop(0, levels // width, weigh, 0)


def unpack(xm, xs, initial, it, heat):
    levels, rows = it.shape[:2]
    half, groups = levels // 2, levels // 32
    t = lax.axis_index("tm")
    begin = jnp.where(t == 0, 0.0, 1.0)
    outer_at = 124 * (1 - t)
    outer = lanes_from(ids(rows, 1), outer_at)
    for G in range(groups):
        within = [xm[2 * half + f * groups + G] for f in range(2)]
        beside = [xs[f * groups + G] for f in range(2)]
        read = packed(lambda l: (xm[l], xm[half + l]), within, None, G, half)

        def with_initial(g):
            a, b = read(g)
            fields = a, b + begin * initial[32 * G + g]
            return [jnp.where(outer, strip(side, g, outer_at), field) for side, field in zip(beside, fields)]

        blocks(32, 16, with_initial, put(it, heat, at=32 * G))


ENDS = (38, 36, 34, 32)
EDGE_LEVELS = 35
WIDTHS = ((19, 12, 17, 16), (13, 14, 15, 16))


def iterate_half(upper, wl, wy, wyp, wx, total, inv0, inv1, part, extra, main_it, main_h, near_diag, far_diag, *refs):
    if upper:
        edge, w_own, w_send, *refs = refs
    else:
        w_own, w_send, edge, *refs = refs
    it, h, s0, s1, x0, x1, y0, y1, z0, z1 = refs
    t = lax.axis_index("tm")
    levels, rows = wy.shape[:2]
    own_rows = rows - TILE
    half, groups = levels // 2, levels // 32
    first = t == 0
    beta = corner_weight ** 0.5
    clear_ends(it, x0, x1, y0, y1, z0, z1)
    shared = [(it, ENDS[0], 3), (h, ENDS[0], 2)]
    for pair, stage in (((x0, x1), 1), ((y0, y1), 2), ((z0, z1), 3)):
        shared += [(ref, ENDS[stage], 3) for ref in pair]
    shared += [(ref, ENDS[3], ENDS[0] - ENDS[3]) for ref in (s0, s1)]
    shared = [(ref, l) for ref, lo, count in shared for l in range(lo, lo + count)]
    if upper:
        for i, (ref, l) in enumerate(shared):
            ref[l] = edge[i]
    ready = half + TILE
    for G in range(groups):
        lo, hi = max(32 * G, ready if upper else 0), min(32 * (G + 1), levels if upper else ready)
        if lo >= hi:
            continue
        halo = halo_of(near_diag, far_diag, 0, half + groups, half, G, half)

        def assemble(i):
            g = lo - 32 * G + i
            return [
                cat(main[lo + i], tile)
                for main, tile in zip((main_it, main_h), halo(g))
            ]

        def store(i, values):
            it[lo + i + 1], h[lo + i] = values

        blocks(hi - lo, 8, assemble, store)

    def faces(l, low):
        return low, wl[l + 1], wy[l], wyp[l], wx[l]

    def over(stage, read, fields, step):
        width = WIDTHS[upper][stage]
        lo, hi = (ENDS[stage], levels) if upper else (0, ENDS[stage])

        def body(i, carry):
            start = lo + i * width
            around = [[read(a, start), read(a, start + 1)] for a in fields]
            low = wl[start]
            for u in range(width):
                around = [[*kept[-2:], read(a, start + u + 2)] for a, kept in zip(fields, around)]
                w = faces(start + u, low)
                step(start + u, w, *around)
                low = w[1]
            return carry

        lax.fori_loop(0, (hi - lo) // width, body, 0)

    def residual(l, w, around):
        mid = around[1]
        theirs = woven(h, l) + extra[l] - ((1.0 + total[l]) * mid - near(around, w))
        mine = part[l] + jnp.where(first, 0.0, 1.0) * mid
        r0 = jnp.where(first, mine, theirs)
        r1 = jnp.where(first, theirs, mine) * beta
        a, b = r0 + r1, r0 - r1
        put(s0, s1)(l, (a, b))
        put(x0, x1, at=1)(l, (a * inv0[l], b * inv1[l]))

    over(0, woven, (it,), residual)

    def sweep(l, w, around0, around1):
        return (s0[l] + near(around0, w)) * inv0[l], (s1[l] + near(around1, w)) * inv1[l]

    def to(*refs):
        return lambda l, w, a, b: put(*refs, at=1)(l, sweep(l, w, a, b))

    def plain(ref, l):
        return ref[l]

    over(1, plain, (x0, x1), to(y0, y1))
    over(2, plain, (y0, y1), to(z0, z1))
    base = half if upper else 0

    def last(l, w, around0, around1):
        a, b = sweep(l, w, around0, around1)
        w0, w1 = (a + b) * 0.5, (a - b) * (0.5 / beta)
        for ref, at, value in ((w_own, l - base, jnp.where(first, w0, w1)), (h, l, jnp.where(first, w1, w0))):
            for j in range(3):
                ref[at, pl.ds(j, TILE, stride=3), :] = value[j * TILE : (j + 1) * TILE]

    over(3, plain, (z0, z1), last)
    handled = jnp.logical_not(other_half(ids(own_rows, 1), t))
    quarter = half // 2

    def pair(l):
        high = pltpu.roll(h[base + quarter + l, :own_rows], 64, 1)
        return (jnp.where(handled, h[base + l, :own_rows], high),)

    blocks(quarter, 16, pair, put(w_send))
    if not upper:
        for i, (ref, l) in enumerate(shared):
            edge[i] = ref[l]


def finish(base, it, w_own, got, *refs):
    out_hbm, out, sems = refs[-3:]
    t = lax.axis_index("tm")
    levels, rows = out.shape[:2]
    half = levels // 2
    part = half // CHUNKS
    handled = jnp.logical_not(other_half(ids(rows, 1), t))
    copies = []
    for c in range(CHUNKS):
        def read(i):
            l = c * part + i
            theirs = got[l]
            return (
                it[base + l] + jnp.where(handled, w_own[l, :rows], theirs),
                it[base + l + half] + jnp.where(handled, w_own[l + half, :rows], pltpu.roll(theirs, 64, 1)),
            )

        def write(i, values):
            l = c * part + i
            out[l], out[l + half] = values

        blocks(part, 4, read, write)
        for s in range(2):
            at = s * half + c * part
            copy = pltpu.make_async_copy(out.at[pl.ds(at, part)], out_hbm.at[pl.ds(base + at, part)], sems.at[c, s])
            copy.start()
            copies.append(copy)
    for copy in copies:
        copy.wait()


def two_steps(iterate, heating, initial, region, cond_table):
    it, h = iterate[0], heating[0]
    levels, rows, lanes = it.shape
    half, groups = levels // 2, levels // 32
    lats, lons = lax.axis_size("lat"), lax.axis_size("lon")
    swap = [(0, 1), (1, 0)]
    pairs = [[(i, i + 1) for i in range(start, lats - 1, 2)] for start in (0, 1)]
    pairs = [p + [(j, i) for i, j in p] for p in pairs]
    diagonals = [[(t * lats + i, (1 - t) * lats + j) for t in range(2) for i, j in p] for p in pairs]
    round_lon = [[(i, (i + 1) % lons) for i in range(start, lons, 2)] for start in (0, 1)]
    round_lon = [p + [(j, i) for i, j in p] for p in round_lon]
    full = shape(levels, rows, lanes)
    wide = shape(levels, rows + TILE, lanes)

    def in_hbm(x):
        return pltpu.with_memory_space_constraint(x, pltpu.HBM)

    xm, it, h = call(
        send_first,
        [shape(levels + 2 * groups, rows, lanes), full, full],
        [in_hbm(it), in_hbm(h)],
        scratch=[pltpu.SemaphoreType.DMA((2, CHUNKS, 2))],
        hbm_ins=(0, 1),
    )
    xm = lax.ppermute(xm, "tm", swap)
    sides = shape(3 * groups, rows, lanes)
    kap, heat, near_sides, far_sides = call(
        send_sides,
        [full, full, sides, sides],
        [it, h, region, initial, in_hbm(cond_table)],
        scratch=[pltpu.VMEM(sides.shape, jnp.float32)] * 2
        + [pltpu.SMEM(cond_table.shape, jnp.float32), pltpu.SemaphoreType.DMA],
        hbm_ins=(4,),
    )
    near_sides = lax.ppermute(near_sides, "lon", round_lon[0])
    far_sides = lax.ppermute(far_sides, "lon", round_lon[1])
    lat = shape(LAT_TILES, TILE, lanes)
    diag = shape(half + 2 * groups, TILE, lanes)
    messages = call(
        send_rows,
        [lat, lat, diag, diag],
        [it, heat, kap],
        scratch=[pltpu.VMEM((levels, TILE, lanes), jnp.float32)] * 2,
    )
    near_lat, far_lat, xs = call(
        add_rows, [lat, lat, shape(2 * groups, rows, lanes)], [near_sides, far_sides, *messages[:2]]
    )
    near_lat = lax.ppermute(near_lat, "lat", pairs[0])
    far_lat = lax.ppermute(far_lat, "lat", pairs[1])
    xs = lax.ppermute(xs, "tm", swap)
    main = call(assemble_main, [full] * 3, [it, heat, kap, near_sides, far_sides])
    near_diag, far_diag = call(
        add_partner_rows,
        [diag, diag],
        [near_sides, far_sides, *messages[2:], main[2]],
    )
    near_diag = lax.ppermute(near_diag, ("tm", "lat"), diagonals[0])
    far_diag = lax.ppermute(far_diag, ("tm", "lat"), diagonals[1])
    main_it, main_h = call(unpack, [full, full], [xm, xs, initial])
    deep = pltpu.VMEM((levels + 2, rows + TILE, lanes), jnp.float32)
    flat = pltpu.VMEM((levels, rows + TILE, lanes), jnp.float32)
    ready = call(
        prepare,
        [shape(levels + 1, rows + TILE, lanes)] + [wide] * 8,
        [*main, near_lat, far_lat, main_it],
        scratch=[deep] * 2 + [flat],
        limit=16,
    )
    given = [*ready, main_it, main_h, near_diag, far_diag]
    corrections = [shape(half, rows + TILE, lanes), shape(half // 2, rows, lanes)]
    fields = [deep, flat, flat, flat] + [deep] * 6
    w_low, send_low, edge = call(
        functools.partial(iterate_half, 0),
        [*corrections, shape(EDGE_LEVELS, rows + TILE, lanes)],
        given,
        scratch=fields,
        limit=24,
    )
    got_low = lax.ppermute(send_low, "tm", swap)
    w_high, send_high = call(
        functools.partial(iterate_half, 1), corrections, [*given, edge], scratch=fields, limit=24
    )
    got_high = lax.ppermute(send_high, "tm", swap)
    last_scratch = [pltpu.VMEM((half, rows, lanes), jnp.float32), pltpu.SemaphoreType.DMA((CHUNKS, 2))]
    (out,) = call(functools.partial(finish, 0), [full], [it, w_low, got_low], scratch=last_scratch, hbm_outs=(0,))
    (out,) = call(
        functools.partial(finish, half),
        [full],
        [it, w_high, got_high, out],
        scratch=last_scratch,
        hbm_ins=(3,),
        hbm_outs=(0,),
        aliases={3: 0},
    )
    return out[None]


def solution(mesh):
    return jax.shard_map(
        two_steps if mesh.shape["tm"] == 2 else on_device,
        mesh=mesh,
        in_specs=(
            P("tm", None, "lat", "lon"),
            P("tm", None, "lat", "lon"),
            P(None, "lat", "lon"),
            P(None, "lat", "lon"),
            P(),
        ),
        out_specs=P("tm", None, "lat", "lon"),
        check_vma=False,
    )
```

```python
import functools

import jax
import jax.numpy as jnp
from jax import lax
from jax.experimental import pallas as pl
from jax.experimental.pallas import tpu as pltpu
from jax.sharding import PartitionSpec as P

SWEEPS = 4


corner_weight = 0.1


def padded(value, sides, width, wrap):
    for axis, dim in sides:
        peers, length = (lax.axis_size(axis), value.shape[dim])
        up = [(i, (i + 1) % peers) for i in range(peers if wrap else peers - 1)]
        down = [(j, i) for i, j in up]
        last = lax.slice_in_dim(value, length - width, length, axis=dim)
        initial = lax.slice_in_dim(value, 0, width, axis=dim)
        before = lax.ppermute(last, axis, up)
        after = lax.ppermute(initial, axis, down)
        value = jnp.concatenate([before, value, after], axis=dim)
    return value


def passed_along(block, axis, distance):
    devices = range(lax.axis_size(axis))
    route = [(i - distance, i) for i in devices if i - distance in devices]
    return lax.ppermute(block, axis, route)


def harmonic(first, second):
    return 2.0 * first * second / (first + second)


def conductivity(region, cond_table):
    classes = jnp.arange(cond_table.shape[0], dtype=jnp.int32)
    onehot = (region[..., None] == classes).astype(jnp.float32)
    return jnp.sum(onehot * cond_table, axis=-1)


def extend(stack):
    lat_ext = padded(stack, (("lat", 2),), 1, False)
    both = padded(lat_ext, (("lon", 3),), 1, True)
    return jnp.pad(both, ((0, 0), (1, 1), (0, 0), (0, 0)))


def face_weights(kext):
    centre = kext[1:-1, 1:-1, 1:-1]
    return (
        harmonic(centre, kext[:-2, 1:-1, 1:-1]),
        harmonic(centre, kext[2:, 1:-1, 1:-1]),
        harmonic(centre, kext[1:-1, :-2, 1:-1]),
        harmonic(centre, kext[1:-1, 2:, 1:-1]),
        harmonic(centre, kext[1:-1, 1:-1, :-2]),
        harmonic(centre, kext[1:-1, 1:-1, 2:]),
    )


def neighbours(weights, ext):
    near = weights[0] * ext[..., :-2, 1:-1, 1:-1] + weights[1] * ext[..., 2:, 1:-1, 1:-1]
    near = near + weights[2] * ext[..., 1:-1, :-2, 1:-1] + weights[3] * ext[..., 1:-1, 2:, 1:-1]
    near = near + weights[4] * ext[..., 1:-1, 1:-1, :-2] + weights[5] * ext[..., 1:-1, 1:-1, 2:]
    return near


def on_device(iterate, heating, initial, region, cond_table):
    steps = lax.axis_size("tm")
    own = lax.axis_index("tm")
    high = lax.Precision.HIGHEST
    kfield = conductivity(region, cond_table)
    ext = extend(jnp.stack([kfield, iterate[0]]))
    weights = face_weights(ext[0])
    total = weights[0] + weights[1] + weights[2] + weights[3] + weights[4] + weights[5]
    shifted = passed_along(iterate, "tm", 1)[0]
    previous = jnp.where(own == 0, initial, shifted)
    residual = heating[0] + previous - ((1.0 + total) * iterate[0] - neighbours(weights, ext[1]))
    scale_own = corner_weight ** (own.astype(jnp.float32) / steps)
    scaled = residual * scale_own
    zeros = jnp.zeros_like(residual)
    piece = lax.all_gather(scaled[None], "tm", axis=0, tiled=True)
    order = jnp.arange(piece.shape[0], dtype=jnp.int32)
    angle = 2.0 * jnp.pi / steps * (own * order % steps).astype(jnp.float32)
    real_part = jnp.einsum("n,nabc->abc", jnp.cos(angle), piece, precision=high)
    imag_part = (zeros, zeros)[1] - jnp.einsum("n,nabc->abc", jnp.sin(angle), piece, precision=high)
    beta = corner_weight ** (1.0 / steps)
    freq_angle = 2.0 * jnp.pi / steps * (own % steps).astype(jnp.float32)
    diag_re = 1.0 - beta * jnp.cos(freq_angle) + total
    diag_im = beta * jnp.sin(freq_angle) + zeros
    denom = diag_re * diag_re + diag_im * diag_im
    inv_re = diag_re / denom
    inv_im = -diag_im / denom
    sol_re = real_part * inv_re - imag_part * inv_im
    sol_im = real_part * inv_im + imag_part * inv_re
    for sweep in range(SWEEPS - 1):
        near = neighbours(weights, extend(jnp.stack([sol_re, sol_im])))
        rhs_re = real_part + near[0]
        rhs_im = imag_part + near[1]
        sol_re = rhs_re * inv_re - rhs_im * inv_im
        sol_im = rhs_re * inv_im + rhs_im * inv_re
    pieces = (
        lax.all_gather(sol_re[None], "tm", axis=0, tiled=True),
        lax.all_gather(sol_im[None], "tm", axis=0, tiled=True),
    )
    order = jnp.arange(pieces[0].shape[0], dtype=jnp.int32)
    angle = 2.0 * jnp.pi / steps * (order * own % steps).astype(jnp.float32)
    summed = jnp.einsum("k,kabc->abc", jnp.cos(angle), pieces[0], precision=high) - jnp.einsum(
        "k,kabc->abc", jnp.sin(angle), pieces[1], precision=high
    )
    back = summed / steps
    return iterate + (back / scale_own)[None]


HALO = 4
TILE = 8
LEVELS = 64
ROWS = 16
LONS = 128
HALF = 64
SENT = HALF + HALO
PLACES = HALF + 2 * HALO
PAIRS = PLACES // 2
QUADS = PLACES // 4
CHUNKS = 4


def specs(count, hbm):
    return [pl.BlockSpec(memory_space=pltpu.HBM if i in hbm else pltpu.VMEM) for i in range(count)]


def call(body, outs, ins, scratch=(), limit=8, hbm_ins=(), hbm_outs=()):
    moved = sum(x.size * 4 for x in ins) + sum(x.size * 4 for x in outs)
    return pl.pallas_call(
        body,
        out_shape=outs,
        in_specs=specs(len(ins), hbm_ins),
        out_specs=specs(len(outs), hbm_outs),
        scratch_shapes=scratch,
        compiler_params=pltpu.CompilerParams(vmem_limit_bytes=limit << 20),
        cost_estimate=pl.CostEstimate(flops=moved * 4, bytes_accessed=moved, transcendentals=0),
    )(*ins)


def shape(*dims):
    return jax.ShapeDtypeStruct(dims, jnp.float32)


def buffer(*dims):
    return pltpu.VMEM(dims, jnp.float32)


def ids(rows, dim):
    return lax.broadcasted_iota(jnp.int32, (rows, 128), dim)


def in_low(rows):
    return ids(rows, 1) < LEVELS


def swapped(x):
    return pltpu.roll(x, LEVELS, 1)


def cat(*values):
    return jnp.concatenate(values, axis=0)


def even(axis):
    return lax.rem(lax.axis_index(axis), 2) == 0


def blocks(lo, hi, width, step):
    def body(i, carry):
        for u in range(width):
            step(lo + i * width + u)
        return carry

    lax.fori_loop(0, (hi - lo) // width, body, 0)


def send_first(it_hbm, h_hbm, xm, turned, it, h, sems):
    t = lax.axis_index("tm")
    part = it.shape[0] // CHUNKS
    copies = []
    for c in range(CHUNKS):
        for f, (source, target) in enumerate(((it_hbm, it), (h_hbm, h))):
            span = pl.ds(c * part, part)
            copy = pltpu.make_async_copy(source.at[span], target.at[span], sems.at[c, f])
            copy.start()
            copies.append(copy)
    for copy in copies:
        copy.wait()

    def turn(r):
        rows = pl.ds(r, LEVELS, stride=ROWS)
        turned[pl.ds(r, LONS, stride=ROWS), :] = cat(it[rows, :], h[rows, :]).T

    blocks(0, ROWS, 4, turn)
    start = (LONS - SENT) * ROWS * (1 - t)

    def cut(i):
        xm[pl.ds(pl.multiple_of(i * ROWS, ROWS), ROWS), :] = turned[pl.ds(pl.multiple_of(start + i * ROWS, ROWS), ROWS), :]

    blocks(0, SENT, 17, cut)


def send_sides(turned, region, initial, table_hbm, heated, fixed, near_sides, far_sides, table, sem):
    first = lax.axis_index("tm") == 0
    copy = pltpu.make_async_copy(table_hbm, table, sem)
    copy.start()
    copy.wait()
    add = jnp.logical_and(jnp.logical_not(in_low(LONS)), first)

    def turn(r):
        rows = pl.ds(r, LEVELS, stride=ROWS)
        classes = region[rows, :]
        value = jnp.full(classes.shape, table[0], jnp.float32)
        for c in range(1, table.shape[0]):
            value = jnp.where(classes == c, table[c], value)
        both = cat(value, initial[rows, :]).T
        rows = pl.ds(r, LONS, stride=ROWS)
        fixed[rows, :] = both
        heated[rows, :] = turned[rows, :] + jnp.where(add, both, 0.0)

    blocks(0, ROWS, 4, turn)
    near_right = even("lon")
    low = in_low(ROWS)

    def strip(first_lon):
        def at(ref, i):
            return ref[(first_lon + i) * ROWS : (first_lon + i + 1) * ROWS, :]

        return [at(heated, i) for i in range(HALO)] + [
            jnp.where(low, at(fixed, i), swapped(at(fixed, i + 2))) for i in range(2)
        ]

    for i, (right, left) in enumerate(zip(strip(LONS - HALO), strip(0))):
        near_sides[i] = jnp.where(near_right, right, left)
        far_sides[i] = jnp.where(near_right, left, right)


def edge_pair(first, second):
    top = ids(TILE, 0) < HALO
    first_up = even("lat")
    down = jnp.where(top, first[:TILE], pltpu.roll(second[:TILE], HALO, 0))
    up = jnp.where(top, pltpu.roll(first[-TILE:], HALO, 0), second[-TILE:])
    return jnp.where(first_up, up, down), jnp.where(first_up, down, up)


def halo_tiles(near_pair, far_pair):
    first_up = even("lat")
    after = jnp.where(first_up, near_pair, far_pair)
    before = jnp.where(first_up, far_pair, near_pair)
    top = ids(TILE, 0) < HALO
    return (
        jnp.where(top, after, pltpu.roll(before, HALO, 0)),
        jnp.where(top, pltpu.roll(after, HALO, 0), before),
    )


def add_sides(
    heated, fixed, near_sides, far_sides,
    own, own_fixed, near_lat, far_lat, near_diag, far_diag, xs,
    partner,
):
    t = lax.axis_index("tm")
    low = in_low(ROWS)
    from_near = (t == 0) != even("lon")
    count = near_sides.shape[0]
    beside = [jnp.where(from_near, near_sides[i], far_sides[i]) for i in range(count)]
    other = [jnp.where(from_near, far_sides[i], near_sides[i]) for i in range(count)]
    for i in range(HALO):
        own[SENT * t + i] = beside[i]
        partner[SENT * (1 - t) + i] = other[i]
        xs[i] = other[i]
    for i in range(2):
        own_fixed[SENT * t + i] = beside[HALO + i]
        own_fixed[SENT * t + i + 2] = swapped(beside[HALO + i])

    def copy(i):
        at = HALO * (1 - t) + i
        lon = (LONS - SENT) * t + i
        own[at] = heated[lon]
        own_fixed[at] = fixed[lon]
        partner[HALO * t + i] = heated[(LONS - SENT) * (1 - t) + i]

    blocks(0, SENT, 17, copy)

    def rows(i):
        near_lat[i], far_lat[i] = edge_pair(own[i], own[i + PAIRS])
        near_diag[i], far_diag[i] = edge_pair(partner[i], partner[i + PAIRS])

    blocks(0, PAIRS, 12, rows)
    low = in_low(TILE)

    def fixed_rows(i):
        here = edge_pair(own_fixed[i], own_fixed[i + PAIRS])
        there = edge_pair(own_fixed[i + QUADS], own_fixed[i + PAIRS + QUADS])
        near_lat[PAIRS + i], far_lat[PAIRS + i] = [jnp.where(low, a, swapped(b)) for a, b in zip(here, there)]

    blocks(0, QUADS, 9, fixed_rows)


def gather(xm, xs, own_fixed, other):
    t = lax.axis_index("tm")
    add = jnp.logical_and(jnp.logical_not(in_low(ROWS)), t == 1)
    for i in range(HALO):
        other[SENT * t + i] = xs[i]

    def copy(i):
        at = HALO * (1 - t) + i
        other[at] = xm[i] + jnp.where(add, own_fixed[at], 0.0)

    blocks(0, SENT, 17, copy)


def reciprocal(d):
    y = pl.reciprocal(d, approx=True)
    return y * (2.0 - d * y)


def face(a, b):
    return 2.0 * a * b * reciprocal(jnp.maximum(a + b, 1e-30))


def woven(ref, at):
    return cat(*[ref[at, pl.ds(j, TILE, stride=3), :] for j in range(3)])


def next_row(x):
    return cat(x[TILE:], pltpu.roll(x[:TILE], TILE - 1, 0))


def last_row(x):
    return cat(pltpu.roll(x[-TILE:], 1, 0), x[:-TILE])


def near(around, w):
    before, mid, after = around
    wxp, wx, wy, wyp, wl = w
    total = wxp * before + wx * after
    total = total + (wy * next_row(mid) + wyp * last_row(mid))
    return total + (wl * pltpu.roll(mid, 127, 1) + pltpu.roll(wl * mid, 1, 1))


def prepare(own_main, own_fixed, near_lat, far_lat, _, wx, wy, wyp, wl, total, inv, own, K):
    rows = ROWS + TILE
    low = in_low(ROWS)
    low_tile = in_low(TILE)
    beta = corner_weight ** 0.5
    K[PLACES] = jnp.zeros((rows, 128), jnp.float32)

    def assemble(i):
        for at, tile in zip((i, i + PAIRS), halo_tiles(near_lat[i], far_lat[i])):
            own[at] = cat(own_main[at], tile)

    blocks(0, PAIRS, 12, assemble)

    def assemble_fixed(i):
        for at, tile in zip((i, i + PAIRS), halo_tiles(near_lat[PAIRS + i], far_lat[PAIRS + i])):
            moved = swapped(tile)
            for here, value in ((at, jnp.where(low_tile, tile, moved)), (at + QUADS, jnp.where(low_tile, moved, tile))):
                main = own_fixed[here]
                K[here] = cat(jnp.where(low, main, swapped(main)), value)

    blocks(0, QUADS, 9, assemble_fixed)
    lane = ids(rows, 1)
    inside = (lane & (LEVELS - 1)) != LEVELS - 1
    shift = jnp.where(lane < LEVELS, 1.0 - beta, 1.0 + beta)
    width = 18

    def weigh(i, carry):
        start = i * width
        here = woven(K, start)
        before = wx[jnp.maximum(start - 1, 0)]
        for u in range(width):
            at = start + u
            after = woven(K, at + 1)
            side = face(here, after)
            row = face(here, next_row(here))
            previous = last_row(row)
            level = jnp.where(inside, face(here, pltpu.roll(here, 127, 1)), 0.0)
            sums = (before + side) + (row + previous) + (level + pltpu.roll(level, 1, 1))
            wx[at], wy[at], wyp[at], wl[at] = side, row, previous, level
            total[at] = sums
            inv[at] = reciprocal(shift + sums)
            here, before = after, side
        return carry

    wx[0] = jnp.zeros((rows, 128), jnp.float32)
    lax.fori_loop(0, PLACES // width, weigh, 0)


STAGES = ((1, 39, 71), (2, 38, 70), (3, 37, 69), (4, 36, 68))
WIDTHS = ((19, 12, 17, 16), (16, 16, 16, 16))
READY = 40
EDGE = 12


def iterate_half(upper, wx, wy, wyp, wl, total, inv, own, other, near_diag, far_diag, *refs):
    if upper:
        edge, w_own, w_send, *refs = refs
    else:
        w_own, w_send, edge, *refs = refs
    it, source, spec, x, y, z, natural = refs
    rows = ROWS + TILE
    first = lax.axis_index("tm") == 0
    low = in_low(rows)
    beta = corner_weight ** 0.5
    gamma = jnp.where(low, 1.0, beta)
    shared = [(it, 38), (it, 39), (source, 39), (x, 37), (x, 38), (y, 36), (y, 37), (z, 35), (z, 36)]
    shared += [(spec, 36), (spec, 37), (spec, 38)]
    if upper:
        for i, (ref, at) in enumerate(shared):
            ref[at] = edge[i]

    def assemble(second):
        def step(i):
            at = i + (PAIRS if second else 0)
            theirs = cat(other[at], halo_tiles(near_diag[i], far_diag[i])[second])
            mine = own[at]
            step0, step1 = jnp.where(first, mine, theirs), jnp.where(first, theirs, mine)
            moved = swapped(step0)
            it[at] = jnp.where(low, step0, swapped(step1))
            source[at] = jnp.where(low, moved, step1 + moved)

        return step

    if upper:
        blocks(READY - PAIRS, PAIRS, 8, assemble(1))
    else:
        blocks(0, PAIRS, 12, assemble(0))
        blocks(0, READY - PAIRS, 4, assemble(1))

    def over(stage, read, ref, step):
        lo, hi = STAGES[stage][upper : upper + 2]
        width = WIDTHS[upper][stage]

        def body(i, carry):
            start = lo + i * width
            around = [read(ref, start - 1), read(ref, start)]
            before = wx[start - 1]
            for u in range(width):
                at = start + u
                around = [*around[-2:], read(ref, at + 1)]
                side = wx[at]
                step(at, around, (before, side, wy[at], wyp[at], wl[at]))
                before = side
            return carry

        lax.fori_loop(0, (hi - lo) // width, body, 0)

    def residual(at, around, w):
        left = (woven(source, at) - ((1.0 + total[at]) * around[1] - near(around, w))) * gamma
        moved = swapped(left)
        value = jnp.where(low, left + moved, moved - left)
        spec[at] = value
        x[at] = value * inv[at]

    over(0, woven, it, residual)

    def plain(ref, at):
        return ref[at]

    def sweep(at, around, w):
        return (spec[at] + near(around, w)) * inv[at]

    def to(ref):
        def step(at, around, w):
            ref[at] = sweep(at, around, w)

        return step

    over(1, plain, x, to(y))
    over(2, plain, y, to(z))
    base = STAGES[3][upper]
    back = jnp.where(low, 0.5, 0.5 / beta)

    def last(at, around, w):
        value = sweep(at, around, w)
        moved = swapped(value)
        value = jnp.where(low, value + moved, moved - value) * back
        for j in range(3):
            natural[pl.ds((at - base) * rows + j, TILE, stride=3), :] = value[j * TILE : (j + 1) * TILE]

    over(3, plain, z, last)
    count = HALF // 2
    for q in range(4):
        turned = cat(*[natural[pl.ds(q + 4 * j, count, stride=rows), :] for j in range(4)]).T
        step0, step1 = turned[:LEVELS], turned[LEVELS:]
        w_own[q] = jnp.where(first, step0, step1)
        w_send[q] = jnp.where(first, step1, step0)
    if not upper:
        for i, (ref, at) in enumerate(shared):
            edge[i] = ref[at]


def placed(value, j, quarter):
    return pltpu.roll(value, (32 * (quarter - j)) % 128, 1)


def finish_most(it, own_low, own_high, got_low, most):
    first = lax.axis_index("tm") == 0
    group = ids(LEVELS, 1) // 32
    for q in range(4):
        for j in range(4):
            mine = jnp.where(group % 2 == 0, placed(own_low[q], j, 0), placed(own_high[q], j, 1))
            mine = jnp.where(group < 2, mine, 0.0)
            theirs = jnp.where(group == 2, placed(got_low[q], j, 2), 0.0)
            value = mine + theirs
            rows = pl.ds(q + 4 * j, LEVELS, stride=ROWS)
            most[rows, :] = it[rows, :] + jnp.where(first, value, swapped(value))


def finish(most, got_high, out_hbm, out, sems):
    first = lax.axis_index("tm") == 0
    part = LEVELS // CHUNKS
    group = ids(part, 1) // 32
    here = group == jnp.where(first, 3, 1)
    copies = []
    for c in range(CHUNKS):
        for q in range(4):
            for j in range(4):
                value = placed(got_high[q, c * part : (c + 1) * part], j, 3)
                value = jnp.where(here, jnp.where(first, value, swapped(value)), 0.0)
                rows = pl.ds(c * part * ROWS + q + 4 * j, part, stride=ROWS)
                out[rows, :] = most[rows, :] + value
        span = pl.ds(c * part * ROWS, part * ROWS)
        copy = pltpu.make_async_copy(out.at[span], out_hbm.at[span], sems.at[c])
        copy.start()
        copies.append(copy)
    for copy in copies:
        copy.wait()


def two_steps(iterate, heating, initial, region, cond_table):
    lats, lons = lax.axis_size("lat"), lax.axis_size("lon")
    swap = [(0, 1), (1, 0)]
    pairs = [[(i, i + 1) for i in range(start, lats - 1, 2)] for start in (0, 1)]
    pairs = [p + [(j, i) for i, j in p] for p in pairs]
    diagonals = [[(t * lats + i, (1 - t) * lats + j) for t in range(2) for i, j in p] for p in pairs]
    round_lon = [[(i, (i + 1) % lons) for i in range(start, lons, 2)] for start in (0, 1)]
    round_lon = [p + [(j, i) for i, j in p] for p in round_lon]
    flat = (LEVELS * ROWS, LONS)
    turned_flat = (LONS * ROWS, 2 * LEVELS)
    by_lon = (LONS, ROWS, 2 * LEVELS)
    wide = shape(PLACES, ROWS + TILE, 128)

    def in_hbm(x):
        return pltpu.with_memory_space_constraint(x, pltpu.HBM)

    xm, turned, it = call(
        send_first,
        [shape(SENT * ROWS, 128), shape(*turned_flat), shape(*flat)],
        [in_hbm(iterate.reshape(flat)), in_hbm(heating.reshape(flat))],
        scratch=[buffer(*flat), pltpu.SemaphoreType.DMA((CHUNKS, 2))],
        hbm_ins=(0, 1),
    )
    xm = lax.ppermute(xm, "tm", swap)
    sides = shape(HALO + 2, ROWS, 128)
    heated, fixed, near_sides, far_sides = call(
        send_sides,
        [shape(*turned_flat), shape(*turned_flat), sides, sides],
        [turned, region.reshape(flat), initial.reshape(flat), in_hbm(cond_table)],
        scratch=[pltpu.SMEM(cond_table.shape, jnp.float32), pltpu.SemaphoreType.DMA],
        hbm_ins=(3,),
    )
    near_sides = lax.ppermute(near_sides, "lon", round_lon[0])
    far_sides = lax.ppermute(far_sides, "lon", round_lon[1])
    main = shape(PLACES, ROWS, 128)
    lat = shape(PAIRS + QUADS, TILE, 128)
    diag = shape(PAIRS, TILE, 128)
    own_main, own_fixed, near_lat, far_lat, near_diag, far_diag, xs = call(
        add_sides,
        [main, main, lat, lat, diag, diag, shape(HALO, ROWS, 128)],
        [heated.reshape(by_lon), fixed.reshape(by_lon), near_sides, far_sides],
        scratch=[buffer(PLACES, ROWS, 128)],
    )
    near_lat = lax.ppermute(near_lat, "lat", pairs[0])
    far_lat = lax.ppermute(far_lat, "lat", pairs[1])
    xs = lax.ppermute(xs, "tm", swap)
    near_diag = lax.ppermute(near_diag, ("tm", "lat"), diagonals[0])
    far_diag = lax.ppermute(far_diag, ("tm", "lat"), diagonals[1])
    (other,) = call(gather, [main], [xm.reshape(SENT, ROWS, 128), xs, own_fixed])
    *ready, own = call(
        prepare,
        [wide] * 7,
        [own_main, own_fixed, near_lat, far_lat, other],
        scratch=[buffer(PLACES + 1, ROWS + TILE, 128)],
    )
    given = [*ready, own, other, near_diag, far_diag]
    corrections = [shape(4, LEVELS, 128)] * 2
    fields = [buffer(PLACES, ROWS + TILE, 128)] * 6 + [buffer(HALF // 2 * (ROWS + TILE), 128)]
    own_low, send_low, edge = call(
        functools.partial(iterate_half, 0),
        [*corrections, shape(EDGE, ROWS + TILE, 128)],
        given,
        scratch=fields,
        limit=16,
    )
    got_low = lax.ppermute(send_low, "tm", swap)
    own_high, send_high = call(
        functools.partial(iterate_half, 1), corrections, [*given, edge], scratch=fields, limit=16
    )
    got_high = lax.ppermute(send_high, "tm", swap)
    (most,) = call(finish_most, [shape(*flat)], [it, own_low, own_high, got_low])
    (out,) = call(
        finish,
        [shape(*flat)],
        [most, got_high],
        scratch=[buffer(*flat), pltpu.SemaphoreType.DMA((CHUNKS,))],
        hbm_outs=(0,),
    )
    return out.reshape(iterate.shape)


def solution(mesh):
    return jax.shard_map(
        two_steps if mesh.shape["tm"] == 2 else on_device,
        mesh=mesh,
        in_specs=(
            P("tm", None, "lat", "lon"),
            P("tm", None, "lat", "lon"),
            P(None, "lat", "lon"),
            P(None, "lat", "lon"),
            P(),
        ),
        out_specs=P("tm", None, "lat", "lon"),
        check_vma=False,
    )
```

```python
import functools

import jax
import jax.numpy as jnp
from jax import lax
from jax.experimental import pallas as pl
from jax.experimental.pallas import tpu as pltpu
from jax.sharding import PartitionSpec as P

SWEEPS = 4


corner_weight = 0.1


def padded(value, sides, width, wrap):
    for axis, dim in sides:
        peers, length = (lax.axis_size(axis), value.shape[dim])
        up = [(i, (i + 1) % peers) for i in range(peers if wrap else peers - 1)]
        down = [(j, i) for i, j in up]
        last = lax.slice_in_dim(value, length - width, length, axis=dim)
        initial = lax.slice_in_dim(value, 0, width, axis=dim)
        before = lax.ppermute(last, axis, up)
        after = lax.ppermute(initial, axis, down)
        value = jnp.concatenate([before, value, after], axis=dim)
    return value


def passed_along(block, axis, distance):
    devices = range(lax.axis_size(axis))
    route = [(i - distance, i) for i in devices if i - distance in devices]
    return lax.ppermute(block, axis, route)


def harmonic(first, second):
    return 2.0 * first * second / (first + second)


def conductivity(region, cond_table):
    classes = jnp.arange(cond_table.shape[0], dtype=jnp.int32)
    onehot = (region[..., None] == classes).astype(jnp.float32)
    return jnp.sum(onehot * cond_table, axis=-1)


def extend(stack):
    lat_ext = padded(stack, (("lat", 2),), 1, False)
    both = padded(lat_ext, (("lon", 3),), 1, True)
    return jnp.pad(both, ((0, 0), (1, 1), (0, 0), (0, 0)))


def face_weights(kext):
    centre = kext[1:-1, 1:-1, 1:-1]
    return (
        harmonic(centre, kext[:-2, 1:-1, 1:-1]),
        harmonic(centre, kext[2:, 1:-1, 1:-1]),
        harmonic(centre, kext[1:-1, :-2, 1:-1]),
        harmonic(centre, kext[1:-1, 2:, 1:-1]),
        harmonic(centre, kext[1:-1, 1:-1, :-2]),
        harmonic(centre, kext[1:-1, 1:-1, 2:]),
    )


def neighbours(weights, ext):
    near = weights[0] * ext[..., :-2, 1:-1, 1:-1] + weights[1] * ext[..., 2:, 1:-1, 1:-1]
    near = near + weights[2] * ext[..., 1:-1, :-2, 1:-1] + weights[3] * ext[..., 1:-1, 2:, 1:-1]
    near = near + weights[4] * ext[..., 1:-1, 1:-1, :-2] + weights[5] * ext[..., 1:-1, 1:-1, 2:]
    return near


def on_device(iterate, heating, initial, region, cond_table):
    steps = lax.axis_size("tm")
    own = lax.axis_index("tm")
    high = lax.Precision.HIGHEST
    kfield = conductivity(region, cond_table)
    ext = extend(jnp.stack([kfield, iterate[0]]))
    weights = face_weights(ext[0])
    total = weights[0] + weights[1] + weights[2] + weights[3] + weights[4] + weights[5]
    shifted = passed_along(iterate, "tm", 1)[0]
    previous = jnp.where(own == 0, initial, shifted)
    residual = heating[0] + previous - ((1.0 + total) * iterate[0] - neighbours(weights, ext[1]))
    scale_own = corner_weight ** (own.astype(jnp.float32) / steps)
    scaled = residual * scale_own
    zeros = jnp.zeros_like(residual)
    piece = lax.all_gather(scaled[None], "tm", axis=0, tiled=True)
    order = jnp.arange(piece.shape[0], dtype=jnp.int32)
    angle = 2.0 * jnp.pi / steps * (own * order % steps).astype(jnp.float32)
    real_part = jnp.einsum("n,nabc->abc", jnp.cos(angle), piece, precision=high)
    imag_part = (zeros, zeros)[1] - jnp.einsum("n,nabc->abc", jnp.sin(angle), piece, precision=high)
    beta = corner_weight ** (1.0 / steps)
    freq_angle = 2.0 * jnp.pi / steps * (own % steps).astype(jnp.float32)
    diag_re = 1.0 - beta * jnp.cos(freq_angle) + total
    diag_im = beta * jnp.sin(freq_angle) + zeros
    denom = diag_re * diag_re + diag_im * diag_im
    inv_re = diag_re / denom
    inv_im = -diag_im / denom
    sol_re = real_part * inv_re - imag_part * inv_im
    sol_im = real_part * inv_im + imag_part * inv_re
    for sweep in range(SWEEPS - 1):
        near = neighbours(weights, extend(jnp.stack([sol_re, sol_im])))
        rhs_re = real_part + near[0]
        rhs_im = imag_part + near[1]
        sol_re = rhs_re * inv_re - rhs_im * inv_im
        sol_im = rhs_re * inv_im + rhs_im * inv_re
    pieces = (
        lax.all_gather(sol_re[None], "tm", axis=0, tiled=True),
        lax.all_gather(sol_im[None], "tm", axis=0, tiled=True),
    )
    order = jnp.arange(pieces[0].shape[0], dtype=jnp.int32)
    angle = 2.0 * jnp.pi / steps * (order * own % steps).astype(jnp.float32)
    summed = jnp.einsum("k,kabc->abc", jnp.cos(angle), pieces[0], precision=high) - jnp.einsum(
        "k,kabc->abc", jnp.sin(angle), pieces[1], precision=high
    )
    back = summed / steps
    return iterate + (back / scale_own)[None]


HALO = 4
TILE = 8
LEVELS = 64
ROWS = 16
LONS = 128
HALF = 64
SENT = HALF + HALO
PLACES = HALF + 2 * HALO
PAIRS = PLACES // 2
QUADS = PLACES // 4
CHUNKS = 4


def specs(count, hbm):
    return [pl.BlockSpec(memory_space=pltpu.HBM if i in hbm else pltpu.VMEM) for i in range(count)]


def call(body, outs, ins, scratch=(), limit=8, hbm_ins=(), hbm_outs=()):
    moved = sum(x.size * 4 for x in ins) + sum(x.size * 4 for x in outs)
    return pl.pallas_call(
        body,
        out_shape=outs,
        in_specs=specs(len(ins), hbm_ins),
        out_specs=specs(len(outs), hbm_outs),
        scratch_shapes=scratch,
        compiler_params=pltpu.CompilerParams(vmem_limit_bytes=limit << 20),
        cost_estimate=pl.CostEstimate(flops=moved * 4, bytes_accessed=moved, transcendentals=0),
    )(*ins)


def shape(*dims):
    return jax.ShapeDtypeStruct(dims, jnp.float32)


def buffer(*dims):
    return pltpu.VMEM(dims, jnp.float32)


def ids(rows, dim):
    return lax.broadcasted_iota(jnp.int32, (rows, 128), dim)


def in_low(rows):
    return ids(rows, 1) < LEVELS


def swapped(x):
    return pltpu.roll(x, LEVELS, 1)


def cat(*values):
    return jnp.concatenate(values, axis=0)


def even(axis):
    return lax.rem(lax.axis_index(axis), 2) == 0


def blocks(lo, hi, width, step):
    def body(i, carry):
        for u in range(width):
            step(lo + i * width + u)
        return carry

    lax.fori_loop(0, (hi - lo) // width, body, 0)


def send_first(it_hbm, h_hbm, xm, turned, it, h, sems):
    t = lax.axis_index("tm")
    part = it.shape[0] // CHUNKS
    copies = []
    for c in range(CHUNKS):
        for f, (source, target) in enumerate(((it_hbm, it), (h_hbm, h))):
            span = pl.ds(c * part, part)
            copy = pltpu.make_async_copy(source.at[span], target.at[span], sems.at[c, f])
            copy.start()
            copies.append(copy)
    for copy in copies:
        copy.wait()

    def turn(r):
        rows = pl.ds(r, LEVELS, stride=ROWS)
        turned[pl.ds(r, LONS, stride=ROWS), :] = cat(it[rows, :], h[rows, :]).T

    blocks(0, ROWS, 4, turn)
    start = (LONS - SENT) * ROWS * (1 - t)

    def cut(i):
        xm[pl.ds(pl.multiple_of(i * ROWS, ROWS), ROWS), :] = turned[pl.ds(pl.multiple_of(start + i * ROWS, ROWS), ROWS), :]

    blocks(0, SENT, 17, cut)


def heated(turned, fixed):
    add = jnp.logical_and(jnp.logical_not(in_low(ROWS)), lax.axis_index("tm") == 0)
    return turned + jnp.where(add, fixed, 0.0)


def send_sides(turned, region, initial, table_hbm, fixed, near_sides, far_sides, table, sem):
    copy = pltpu.make_async_copy(table_hbm, table, sem)
    copy.start()
    copy.wait()

    def turn(r):
        rows = pl.ds(r, LEVELS, stride=ROWS)
        classes = region[rows, :]
        value = jnp.full(classes.shape, table[0], jnp.float32)
        for c in range(1, table.shape[0]):
            value = jnp.where(classes == c, table[c], value)
        fixed[pl.ds(r, LONS, stride=ROWS), :] = cat(value, initial[rows, :]).T

    blocks(0, ROWS, 4, turn)
    near_right = even("lon")
    low = in_low(ROWS)

    def strip(first_lon):
        def at(ref, i):
            return ref[(first_lon + i) * ROWS : (first_lon + i + 1) * ROWS, :]

        return [heated(at(turned, i), at(fixed, i)) for i in range(HALO)] + [
            jnp.where(low, at(fixed, i), swapped(at(fixed, i + 2))) for i in range(2)
        ]

    for i, (right, left) in enumerate(zip(strip(LONS - HALO), strip(0))):
        near_sides[i] = jnp.where(near_right, right, left)
        far_sides[i] = jnp.where(near_right, left, right)


def edge_pair(first, second):
    top = ids(TILE, 0) < HALO
    first_up = even("lat")
    down = jnp.where(top, first[:TILE], pltpu.roll(second[:TILE], HALO, 0))
    up = jnp.where(top, pltpu.roll(first[-TILE:], HALO, 0), second[-TILE:])
    return jnp.where(first_up, up, down), jnp.where(first_up, down, up)


def halo_tiles(near_pair, far_pair):
    first_up = even("lat")
    after = jnp.where(first_up, near_pair, far_pair)
    before = jnp.where(first_up, far_pair, near_pair)
    top = ids(TILE, 0) < HALO
    return (
        jnp.where(top, after, pltpu.roll(before, HALO, 0)),
        jnp.where(top, pltpu.roll(after, HALO, 0), before),
    )


def add_sides(
    turned, fixed, near_sides, far_sides,
    own, own_fixed, near_lat, far_lat, near_diag, far_diag, xs,
    partner,
):
    t = lax.axis_index("tm")
    low = in_low(ROWS)
    from_near = (t == 0) != even("lon")
    count = near_sides.shape[0]
    beside = [jnp.where(from_near, near_sides[i], far_sides[i]) for i in range(count)]
    other = [jnp.where(from_near, far_sides[i], near_sides[i]) for i in range(count)]
    for i in range(HALO):
        own[SENT * t + i] = beside[i]
        partner[SENT * (1 - t) + i] = other[i]
        xs[i] = other[i]
    for i in range(2):
        own_fixed[SENT * t + i] = beside[HALO + i]
        own_fixed[SENT * t + i + 2] = swapped(beside[HALO + i])

    def copy(i):
        at = HALO * (1 - t) + i
        lon = (LONS - SENT) * t + i
        own[at] = heated(turned[lon], fixed[lon])
        own_fixed[at] = fixed[lon]
        lon = (LONS - SENT) * (1 - t) + i
        partner[HALO * t + i] = heated(turned[lon], fixed[lon])

    blocks(0, SENT, 17, copy)

    def rows(i):
        near_lat[i], far_lat[i] = edge_pair(own[i], own[i + PAIRS])
        near_diag[i], far_diag[i] = edge_pair(partner[i], partner[i + PAIRS])

    blocks(0, PAIRS, 12, rows)
    low = in_low(TILE)

    def fixed_rows(i):
        here = edge_pair(own_fixed[i], own_fixed[i + PAIRS])
        there = edge_pair(own_fixed[i + QUADS], own_fixed[i + PAIRS + QUADS])
        near_lat[PAIRS + i], far_lat[PAIRS + i] = [jnp.where(low, a, swapped(b)) for a, b in zip(here, there)]

    blocks(0, QUADS, 9, fixed_rows)


def gather(xm, own_fixed, other):
    t = lax.axis_index("tm")
    add = jnp.logical_and(jnp.logical_not(in_low(ROWS)), t == 1)

    def step(i):
        other[i] = xm[i] + jnp.where(add, own_fixed[HALO * (1 - t) + i], 0.0)

    blocks(0, SENT, 17, step)


def join(main, xs, _, other):
    t = lax.axis_index("tm")
    for i in range(HALO):
        other[SENT * t + i] = xs[i]

    def step(i):
        other[HALO * (1 - t) + i] = main[i]

    blocks(0, SENT, 17, step)


def reciprocal(d):
    y = pl.reciprocal(d, approx=True)
    return y * (2.0 - d * y)


def face(a, b):
    return 2.0 * a * b * reciprocal(jnp.maximum(a + b, 1e-30))


def woven(ref, at):
    return cat(*[ref[at, pl.ds(j, TILE, stride=3), :] for j in range(3)])


def next_row(x):
    return cat(x[TILE:], pltpu.roll(x[:TILE], TILE - 1, 0))


def last_row(x):
    return cat(pltpu.roll(x[-TILE:], 1, 0), x[:-TILE])


def near(around, w):
    before, mid, after = around
    wxp, wx, wy, wyp, wl = w
    total = wxp * before + wx * after
    total = total + (wy * next_row(mid) + wyp * last_row(mid))
    return total + (wl * pltpu.roll(mid, 127, 1) + pltpu.roll(wl * mid, 1, 1))


def prepare(own_main, own_fixed, near_lat, far_lat, _, wx, wy, wyp, wl, total, inv, own, K):
    rows = ROWS + TILE
    low = in_low(ROWS)
    low_tile = in_low(TILE)
    beta = corner_weight ** 0.5
    K[PLACES] = jnp.zeros((rows, 128), jnp.float32)

    def assemble(i):
        for at, tile in zip((i, i + PAIRS), halo_tiles(near_lat[i], far_lat[i])):
            own[at] = cat(own_main[at], tile)

    blocks(0, PAIRS, 12, assemble)

    def assemble_fixed(i):
        for at, tile in zip((i, i + PAIRS), halo_tiles(near_lat[PAIRS + i], far_lat[PAIRS + i])):
            moved = swapped(tile)
            for here, value in ((at, jnp.where(low_tile, tile, moved)), (at + QUADS, jnp.where(low_tile, moved, tile))):
                main = own_fixed[here]
                K[here] = cat(jnp.where(low, main, swapped(main)), value)

    blocks(0, QUADS, 9, assemble_fixed)
    lane = ids(rows, 1)
    inside = (lane & (LEVELS - 1)) != LEVELS - 1
    shift = jnp.where(lane < LEVELS, 1.0 - beta, 1.0 + beta)
    width = 18

    def weigh(i, carry):
        start = i * width
        here = woven(K, start)
        before = wx[jnp.maximum(start - 1, 0)]
        for u in range(width):
            at = start + u
            after = woven(K, at + 1)
            side = face(here, after)
            row = face(here, next_row(here))
            previous = last_row(row)
            level = jnp.where(inside, face(here, pltpu.roll(here, 127, 1)), 0.0)
            sums = (before + side) + (row + previous) + (level + pltpu.roll(level, 1, 1))
            wx[at], wy[at], wyp[at], wl[at] = side, row, previous, level
            total[at] = sums
            inv[at] = reciprocal(shift + sums)
            here, before = after, side
        return carry

    wx[0] = jnp.zeros((rows, 128), jnp.float32)
    lax.fori_loop(0, PLACES // width, weigh, 0)


STAGES = ((1, 39, 71), (2, 38, 70), (3, 37, 69), (4, 36, 68))
WIDTHS = ((19, 18, 17, 16), (32, 32, 32, 32))
READY = 40
EDGE = 12


def iterate_half(upper, wx, wy, wyp, wl, total, inv, own, other, near_diag, far_diag, *refs):
    if upper:
        edge, w_own, w_send, *refs = refs
    else:
        w_own, w_send, edge, *refs = refs
    it, source, spec, x, y, z, natural = refs
    rows = ROWS + TILE
    first = lax.axis_index("tm") == 0
    low = in_low(rows)
    beta = corner_weight ** 0.5
    gamma = jnp.where(low, 1.0, beta)
    shared = [(it, 38), (it, 39), (source, 39), (x, 37), (x, 38), (y, 36), (y, 37), (z, 35), (z, 36)]
    shared += [(spec, 36), (spec, 37), (spec, 38)]
    if upper:
        for i, (ref, at) in enumerate(shared):
            ref[at] = edge[i]

    def assemble(second):
        def step(i):
            at = i + (PAIRS if second else 0)
            theirs = cat(other[at], halo_tiles(near_diag[i], far_diag[i])[second])
            mine = own[at]
            step0, step1 = jnp.where(first, mine, theirs), jnp.where(first, theirs, mine)
            moved = swapped(step0)
            it[at] = jnp.where(low, step0, swapped(step1))
            source[at] = jnp.where(low, moved, step1 + moved)

        return step

    if upper:
        blocks(READY - PAIRS, PAIRS, 8, assemble(1))
    else:
        blocks(0, PAIRS, 12, assemble(0))
        blocks(0, READY - PAIRS, 4, assemble(1))

    def over(stage, read, ref, step):
        lo, hi = STAGES[stage][upper : upper + 2]
        width = WIDTHS[upper][stage]

        def body(i, carry):
            start = lo + i * width
            around = [read(ref, start - 1), read(ref, start)]
            before = wx[start - 1]
            for u in range(width):
                at = start + u
                around = [*around[-2:], read(ref, at + 1)]
                side = wx[at]
                step(at, around, (before, side, wy[at], wyp[at], wl[at]))
                before = side
            return carry

        lax.fori_loop(0, (hi - lo) // width, body, 0)

    def residual(at, around, w):
        left = (woven(source, at) - ((1.0 + total[at]) * around[1] - near(around, w))) * gamma
        moved = swapped(left)
        value = jnp.where(low, left + moved, moved - left)
        spec[at] = value
        x[at] = value * inv[at]

    over(0, woven, it, residual)

    def plain(ref, at):
        return ref[at]

    def sweep(at, around, w):
        return (spec[at] + near(around, w)) * inv[at]

    def to(ref):
        def step(at, around, w):
            ref[at] = sweep(at, around, w)

        return step

    over(1, plain, x, to(y))
    over(2, plain, y, to(z))
    base = STAGES[3][upper]
    back = jnp.where(low, 0.5, 0.5 / beta)

    def last(at, around, w):
        value = sweep(at, around, w)
        moved = swapped(value)
        value = jnp.where(low, value + moved, moved - value) * back
        for j in range(3):
            natural[pl.ds((at - base) * rows + j, TILE, stride=3), :] = value[j * TILE : (j + 1) * TILE]

    over(3, plain, z, last)
    count = HALF // 2
    for q in range(4):
        turned = cat(*[natural[pl.ds(q + 4 * j, count, stride=rows), :] for j in range(4)]).T
        step0, step1 = turned[:LEVELS], turned[LEVELS:]
        w_own[q] = jnp.where(first, step0, step1)
        w_send[q] = jnp.where(first, step1, step0)
    if not upper:
        for i, (ref, at) in enumerate(shared):
            edge[i] = ref[at]


def placed(value, j, quarter):
    return pltpu.roll(value, (32 * (quarter - j) + 128) & 127, 1)


def finish_most(it, own_low, own_high, got_low, most):
    t = lax.axis_index("tm")
    group = ids(LEVELS, 1) // 32

    def step(q):
        for j in range(4):
            rows = pl.ds(q + 4 * j, LEVELS, stride=ROWS)
            value = it[rows, :]
            for piece, quarter in ((own_low, 2 * t), (own_high, 2 * t + 1), (got_low, 2 - 2 * t)):
                value = jnp.where(group == quarter, value + placed(piece[q], j, quarter), value)
            most[rows, :] = value

    blocks(0, 4, 2, step)


def finish(most, got_high, out_hbm, out, sems):
    quarter = 3 - 2 * lax.axis_index("tm")
    part = LEVELS // CHUNKS
    here = ids(part, 1) // 32 == quarter

    def copy(c):
        span = pl.ds(pl.multiple_of(c * part * ROWS, part * ROWS), part * ROWS)
        return pltpu.make_async_copy(out.at[span], out_hbm.at[span], sems.at[c])

    def step(c):
        for q in range(4):
            value = got_high[q, pl.ds(pl.multiple_of(c * part, part), part), :]
            for j in range(4):
                rows = pl.ds(c * part * ROWS + q + 4 * j, part, stride=ROWS)
                old = most[rows, :]
                out[rows, :] = jnp.where(here, old + placed(value, j, quarter), old)
        copy(c).start()

    blocks(0, CHUNKS, 1, step)
    for c in range(CHUNKS):
        copy(c).wait()


def two_steps(iterate, heating, initial, region, cond_table):
    lats, lons = lax.axis_size("lat"), lax.axis_size("lon")
    swap = [(0, 1), (1, 0)]
    pairs = [[(i, i + 1) for i in range(start, lats - 1, 2)] for start in (0, 1)]
    pairs = [p + [(j, i) for i, j in p] for p in pairs]
    diagonals = [[(t * lats + i, (1 - t) * lats + j) for t in range(2) for i, j in p] for p in pairs]
    round_lon = [[(i, (i + 1) % lons) for i in range(start, lons, 2)] for start in (0, 1)]
    round_lon = [p + [(j, i) for i, j in p] for p in round_lon]
    flat = (LEVELS * ROWS, LONS)
    turned_flat = (LONS * ROWS, 2 * LEVELS)
    by_lon = (LONS, ROWS, 2 * LEVELS)
    wide = shape(PLACES, ROWS + TILE, 128)

    def in_hbm(x):
        return pltpu.with_memory_space_constraint(x, pltpu.HBM)

    xm, turned, it = call(
        send_first,
        [shape(SENT * ROWS, 128), shape(*turned_flat), shape(*flat)],
        [in_hbm(iterate.reshape(flat)), in_hbm(heating.reshape(flat))],
        scratch=[buffer(*flat), pltpu.SemaphoreType.DMA((CHUNKS, 2))],
        hbm_ins=(0, 1),
    )
    xm = lax.ppermute(xm, "tm", swap)
    sides = shape(HALO + 2, ROWS, 128)
    fixed, near_sides, far_sides = call(
        send_sides,
        [shape(*turned_flat), sides, sides],
        [turned, region.reshape(flat), initial.reshape(flat), in_hbm(cond_table)],
        scratch=[pltpu.SMEM(cond_table.shape, jnp.float32), pltpu.SemaphoreType.DMA],
        hbm_ins=(3,),
    )
    near_sides = lax.ppermute(near_sides, "lon", round_lon[0])
    far_sides = lax.ppermute(far_sides, "lon", round_lon[1])
    main = shape(PLACES, ROWS, 128)
    lat = shape(PAIRS + QUADS, TILE, 128)
    diag = shape(PAIRS, TILE, 128)
    own_main, own_fixed, near_lat, far_lat, near_diag, far_diag, xs = call(
        add_sides,
        [main, main, lat, lat, diag, diag, shape(HALO, ROWS, 128)],
        [turned.reshape(by_lon), fixed.reshape(by_lon), near_sides, far_sides],
        scratch=[buffer(PLACES, ROWS, 128)],
    )
    near_lat = lax.ppermute(near_lat, "lat", pairs[0])
    far_lat = lax.ppermute(far_lat, "lat", pairs[1])
    xs = lax.ppermute(xs, "tm", swap)
    near_diag = lax.ppermute(near_diag, ("tm", "lat"), diagonals[0])
    far_diag = lax.ppermute(far_diag, ("tm", "lat"), diagonals[1])
    (other,) = call(gather, [shape(SENT, ROWS, 128)], [xm.reshape(SENT, ROWS, 128), own_fixed])
    *ready, own = call(
        prepare,
        [wide] * 7,
        [own_main, own_fixed, near_lat, far_lat, other],
        scratch=[buffer(PLACES + 1, ROWS + TILE, 128)],
    )
    (other,) = call(join, [main], [other, xs, own])
    given = [*ready, own, other, near_diag, far_diag]
    corrections = [shape(4, LEVELS, 128)] * 2
    fields = [buffer(PLACES, ROWS + TILE, 128)] * 6 + [buffer(HALF // 2 * (ROWS + TILE), 128)]
    own_low, send_low, edge = call(
        functools.partial(iterate_half, 0),
        [*corrections, shape(EDGE, ROWS + TILE, 128)],
        given,
        scratch=fields,
        limit=16,
    )
    got_low = lax.ppermute(send_low, "tm", swap)
    own_high, send_high = call(
        functools.partial(iterate_half, 1), corrections, [*given, edge], scratch=fields, limit=16
    )
    got_high = lax.ppermute(send_high, "tm", swap)
    (most,) = call(finish_most, [shape(*flat)], [it, own_low, own_high, got_low])
    (out,) = call(
        finish,
        [shape(*flat)],
        [most, got_high],
        scratch=[buffer(*flat), pltpu.SemaphoreType.DMA((CHUNKS,))],
        hbm_outs=(0,),
    )
    return out.reshape(iterate.shape)


def solution(mesh):
    return jax.shard_map(
        two_steps if mesh.shape["tm"] == 2 else on_device,
        mesh=mesh,
        in_specs=(
            P("tm", None, "lat", "lon"),
            P("tm", None, "lat", "lon"),
            P(None, "lat", "lon"),
            P(None, "lat", "lon"),
            P(),
        ),
        out_specs=P("tm", None, "lat", "lon"),
        check_vma=False,
    )
```

```python
import functools

import jax
import jax.numpy as jnp
from jax import lax
from jax.experimental import pallas as pl
from jax.experimental.pallas import tpu as pltpu
from jax.sharding import PartitionSpec as P

SWEEPS = 4


corner_weight = 0.1


def padded(value, sides, width, wrap):
    for axis, dim in sides:
        peers, length = (lax.axis_size(axis), value.shape[dim])
        up = [(i, (i + 1) % peers) for i in range(peers if wrap else peers - 1)]
        down = [(j, i) for i, j in up]
        last = lax.slice_in_dim(value, length - width, length, axis=dim)
        initial = lax.slice_in_dim(value, 0, width, axis=dim)
        before = lax.ppermute(last, axis, up)
        after = lax.ppermute(initial, axis, down)
        value = jnp.concatenate([before, value, after], axis=dim)
    return value


def passed_along(block, axis, distance):
    devices = range(lax.axis_size(axis))
    route = [(i - distance, i) for i in devices if i - distance in devices]
    return lax.ppermute(block, axis, route)


def harmonic(first, second):
    return 2.0 * first * second / (first + second)


def conductivity(region, cond_table):
    classes = jnp.arange(cond_table.shape[0], dtype=jnp.int32)
    onehot = (region[..., None] == classes).astype(jnp.float32)
    return jnp.sum(onehot * cond_table, axis=-1)


def extend(stack):
    lat_ext = padded(stack, (("lat", 2),), 1, False)
    both = padded(lat_ext, (("lon", 3),), 1, True)
    return jnp.pad(both, ((0, 0), (1, 1), (0, 0), (0, 0)))


def face_weights(kext):
    centre = kext[1:-1, 1:-1, 1:-1]
    return (
        harmonic(centre, kext[:-2, 1:-1, 1:-1]),
        harmonic(centre, kext[2:, 1:-1, 1:-1]),
        harmonic(centre, kext[1:-1, :-2, 1:-1]),
        harmonic(centre, kext[1:-1, 2:, 1:-1]),
        harmonic(centre, kext[1:-1, 1:-1, :-2]),
        harmonic(centre, kext[1:-1, 1:-1, 2:]),
    )


def neighbours(weights, ext):
    near = weights[0] * ext[..., :-2, 1:-1, 1:-1] + weights[1] * ext[..., 2:, 1:-1, 1:-1]
    near = near + weights[2] * ext[..., 1:-1, :-2, 1:-1] + weights[3] * ext[..., 1:-1, 2:, 1:-1]
    near = near + weights[4] * ext[..., 1:-1, 1:-1, :-2] + weights[5] * ext[..., 1:-1, 1:-1, 2:]
    return near


def on_device(iterate, heating, initial, region, cond_table):
    steps = lax.axis_size("tm")
    own = lax.axis_index("tm")
    high = lax.Precision.HIGHEST
    kfield = conductivity(region, cond_table)
    ext = extend(jnp.stack([kfield, iterate[0]]))
    weights = face_weights(ext[0])
    total = weights[0] + weights[1] + weights[2] + weights[3] + weights[4] + weights[5]
    shifted = passed_along(iterate, "tm", 1)[0]
    previous = jnp.where(own == 0, initial, shifted)
    residual = heating[0] + previous - ((1.0 + total) * iterate[0] - neighbours(weights, ext[1]))
    scale_own = corner_weight ** (own.astype(jnp.float32) / steps)
    scaled = residual * scale_own
    zeros = jnp.zeros_like(residual)
    piece = lax.all_gather(scaled[None], "tm", axis=0, tiled=True)
    order = jnp.arange(piece.shape[0], dtype=jnp.int32)
    angle = 2.0 * jnp.pi / steps * (own * order % steps).astype(jnp.float32)
    real_part = jnp.einsum("n,nabc->abc", jnp.cos(angle), piece, precision=high)
    imag_part = (zeros, zeros)[1] - jnp.einsum("n,nabc->abc", jnp.sin(angle), piece, precision=high)
    beta = corner_weight ** (1.0 / steps)
    freq_angle = 2.0 * jnp.pi / steps * (own % steps).astype(jnp.float32)
    diag_re = 1.0 - beta * jnp.cos(freq_angle) + total
    diag_im = beta * jnp.sin(freq_angle) + zeros
    denom = diag_re * diag_re + diag_im * diag_im
    inv_re = diag_re / denom
    inv_im = -diag_im / denom
    sol_re = real_part * inv_re - imag_part * inv_im
    sol_im = real_part * inv_im + imag_part * inv_re
    for sweep in range(SWEEPS - 1):
        near = neighbours(weights, extend(jnp.stack([sol_re, sol_im])))
        rhs_re = real_part + near[0]
        rhs_im = imag_part + near[1]
        sol_re = rhs_re * inv_re - rhs_im * inv_im
        sol_im = rhs_re * inv_im + rhs_im * inv_re
    pieces = (
        lax.all_gather(sol_re[None], "tm", axis=0, tiled=True),
        lax.all_gather(sol_im[None], "tm", axis=0, tiled=True),
    )
    order = jnp.arange(pieces[0].shape[0], dtype=jnp.int32)
    angle = 2.0 * jnp.pi / steps * (order * own % steps).astype(jnp.float32)
    summed = jnp.einsum("k,kabc->abc", jnp.cos(angle), pieces[0], precision=high) - jnp.einsum(
        "k,kabc->abc", jnp.sin(angle), pieces[1], precision=high
    )
    back = summed / steps
    return iterate + (back / scale_own)[None]


HALO = 4
TILE = 8
LEVELS = 64
ROWS = 16
LONS = 128
HALF = 64
SENT = HALF + HALO
PLACES = HALF + 2 * HALO
PAIRS = PLACES // 2
QUADS = PLACES // 4
CHUNKS = 4


def specs(count, hbm):
    return [pl.BlockSpec(memory_space=pltpu.HBM if i in hbm else pltpu.VMEM) for i in range(count)]


def call(body, outs, ins, scratch=(), limit=8, hbm_ins=(), hbm_outs=()):
    moved = sum(x.size * 4 for x in ins) + sum(x.size * 4 for x in outs)
    return pl.pallas_call(
        body,
        out_shape=outs,
        in_specs=specs(len(ins), hbm_ins),
        out_specs=specs(len(outs), hbm_outs),
        scratch_shapes=scratch,
        compiler_params=pltpu.CompilerParams(vmem_limit_bytes=limit << 20),
        cost_estimate=pl.CostEstimate(flops=moved * 4, bytes_accessed=moved, transcendentals=0),
    )(*ins)


def shape(*dims):
    return jax.ShapeDtypeStruct(dims, jnp.float32)


def buffer(*dims):
    return pltpu.VMEM(dims, jnp.float32)


def ids(rows, dim):
    return lax.broadcasted_iota(jnp.int32, (rows, 128), dim)


def in_low(rows):
    return ids(rows, 1) < LEVELS


def swapped(x):
    return pltpu.roll(x, LEVELS, 1)


def cat(*values):
    return jnp.concatenate(values, axis=0)


def even(axis):
    return lax.rem(lax.axis_index(axis), 2) == 0


def blocks(lo, hi, width, step):
    def body(i, carry):
        for u in range(width):
            step(lo + i * width + u)
        return carry

    lax.fori_loop(0, (hi - lo) // width, body, 0)


def send_first(it_hbm, h_hbm, xm, turned, it, h, sems):
    t = lax.axis_index("tm")
    part = it.shape[0] // CHUNKS
    copies = []
    for c in range(CHUNKS):
        for f, (source, target) in enumerate(((it_hbm, it), (h_hbm, h))):
            span = pl.ds(c * part, part)
            copy = pltpu.make_async_copy(source.at[span], target.at[span], sems.at[c, f])
            copy.start()
            copies.append(copy)
    for copy in copies:
        copy.wait()

    def turn(r):
        rows = pl.ds(r, LEVELS, stride=ROWS)
        turned[pl.ds(r, LONS, stride=ROWS), :] = cat(it[rows, :], h[rows, :]).T

    blocks(0, ROWS, 4, turn)
    start = (LONS - SENT) * ROWS * (1 - t)

    def cut(i):
        xm[pl.ds(pl.multiple_of(i * ROWS, ROWS), ROWS), :] = turned[pl.ds(pl.multiple_of(start + i * ROWS, ROWS), ROWS), :]

    blocks(0, SENT, 17, cut)


def heated(turned, fixed):
    add = jnp.logical_and(jnp.logical_not(in_low(ROWS)), lax.axis_index("tm") == 0)
    return turned + jnp.where(add, fixed, 0.0)


def send_sides(turned, region, initial, table_hbm, fixed, near_sides, far_sides, table, sem):
    copy = pltpu.make_async_copy(table_hbm, table, sem)
    copy.start()
    copy.wait()

    def turn(r):
        rows = pl.ds(r, LEVELS, stride=ROWS)
        classes = region[rows, :]
        value = jnp.full(classes.shape, table[0], jnp.float32)
        for c in range(1, table.shape[0]):
            value = jnp.where(classes == c, table[c], value)
        fixed[pl.ds(r, LONS, stride=ROWS), :] = cat(value, initial[rows, :]).T

    blocks(0, ROWS, 4, turn)
    near_right = even("lon")
    low = in_low(ROWS)

    def strip(first_lon):
        def at(ref, i):
            return ref[(first_lon + i) * ROWS : (first_lon + i + 1) * ROWS, :]

        return [heated(at(turned, i), at(fixed, i)) for i in range(HALO)] + [
            jnp.where(low, at(fixed, i), swapped(at(fixed, i + 2))) for i in range(2)
        ]

    for i, (right, left) in enumerate(zip(strip(LONS - HALO), strip(0))):
        near_sides[i] = jnp.where(near_right, right, left)
        far_sides[i] = jnp.where(near_right, left, right)


def edge_pair(first, second):
    top = ids(TILE, 0) < HALO
    first_up = even("lat")
    down = jnp.where(top, first[:TILE], pltpu.roll(second[:TILE], HALO, 0))
    up = jnp.where(top, pltpu.roll(first[-TILE:], HALO, 0), second[-TILE:])
    return jnp.where(first_up, up, down), jnp.where(first_up, down, up)


def halo_tiles(near_pair, far_pair):
    first_up = even("lat")
    after = jnp.where(first_up, near_pair, far_pair)
    before = jnp.where(first_up, far_pair, near_pair)
    top = ids(TILE, 0) < HALO
    return (
        jnp.where(top, after, pltpu.roll(before, HALO, 0)),
        jnp.where(top, pltpu.roll(after, HALO, 0), before),
    )


def add_sides(turned, fixed, near_sides, far_sides, own, own_fixed, near_lat, far_lat, xs):
    t = lax.axis_index("tm")
    from_near = (t == 0) != even("lon")
    count = near_sides.shape[0]
    beside = [jnp.where(from_near, near_sides[i], far_sides[i]) for i in range(count)]
    for i in range(HALO):
        own[SENT * t + i] = beside[i]
        xs[i] = jnp.where(from_near, far_sides[i], near_sides[i])
    for i in range(2):
        own_fixed[SENT * t + i] = beside[HALO + i]
        own_fixed[SENT * t + i + 2] = swapped(beside[HALO + i])

    def copy(i):
        at = HALO * (1 - t) + i
        lon = (LONS - SENT) * t + i
        own[at] = heated(turned[lon], fixed[lon])
        own_fixed[at] = fixed[lon]

    blocks(0, SENT, 17, copy)

    def rows(i):
        near_lat[i], far_lat[i] = edge_pair(own[i], own[i + PAIRS])

    blocks(0, PAIRS, 12, rows)
    low = in_low(TILE)

    def fixed_rows(i):
        here = edge_pair(own_fixed[i], own_fixed[i + PAIRS])
        there = edge_pair(own_fixed[i + QUADS], own_fixed[i + PAIRS + QUADS])
        near_lat[PAIRS + i], far_lat[PAIRS + i] = [jnp.where(low, a, swapped(b)) for a, b in zip(here, there)]

    blocks(0, QUADS, 9, fixed_rows)


def gather(xm, xs, own_fixed, other, near_rows, far_rows):
    t = lax.axis_index("tm")
    add = jnp.logical_and(jnp.logical_not(in_low(ROWS)), t == 1)
    for i in range(HALO):
        other[SENT * t + i] = xs[i]

    def copy(i):
        at = HALO * (1 - t) + i
        other[at] = xm[i] + jnp.where(add, own_fixed[at], 0.0)

    blocks(0, SENT, 17, copy)

    def rows(i):
        near_rows[i], far_rows[i] = edge_pair(other[i], other[i + PAIRS])

    blocks(0, PAIRS, 12, rows)


def reciprocal(d):
    y = pl.reciprocal(d, approx=True)
    return y * (2.0 - d * y)


def face(a, b):
    return 2.0 * a * b * reciprocal(jnp.maximum(a + b, 1e-30))


def woven(ref, at):
    return cat(*[ref[at, pl.ds(j, TILE, stride=3), :] for j in range(3)])


def next_row(x):
    return cat(x[TILE:], pltpu.roll(x[:TILE], TILE - 1, 0))


def last_row(x):
    return cat(pltpu.roll(x[-TILE:], 1, 0), x[:-TILE])


def near(around, w):
    before, mid, after = around
    wxp, wx, wy, wyp, wl = w
    total = wxp * before + wx * after
    total = total + (wy * next_row(mid) + wyp * last_row(mid))
    return total + (wl * pltpu.roll(mid, 127, 1) + pltpu.roll(wl * mid, 1, 1))


def prepare(own_main, own_fixed, near_lat, far_lat, _, wx, wy, wyp, wl, total, inv, own, K):
    rows = ROWS + TILE
    low = in_low(ROWS)
    low_tile = in_low(TILE)
    beta = corner_weight ** 0.5
    K[PLACES] = jnp.zeros((rows, 128), jnp.float32)

    def assemble(i):
        for at, tile in zip((i, i + PAIRS), halo_tiles(near_lat[i], far_lat[i])):
            own[at] = cat(own_main[at], tile)

    blocks(0, PAIRS, 12, assemble)

    def assemble_fixed(i):
        for at, tile in zip((i, i + PAIRS), halo_tiles(near_lat[PAIRS + i], far_lat[PAIRS + i])):
            moved = swapped(tile)
            for here, value in ((at, jnp.where(low_tile, tile, moved)), (at + QUADS, jnp.where(low_tile, moved, tile))):
                main = own_fixed[here]
                K[here] = cat(jnp.where(low, main, swapped(main)), value)

    blocks(0, QUADS, 9, assemble_fixed)
    lane = ids(rows, 1)
    inside = (lane & (LEVELS - 1)) != LEVELS - 1
    shift = jnp.where(lane < LEVELS, 1.0 - beta, 1.0 + beta)
    width = 18

    def weigh(i, carry):
        start = i * width
        here = woven(K, start)
        before = wx[jnp.maximum(start - 1, 0)]
        for u in range(width):
            at = start + u
            after = woven(K, at + 1)
            side = face(here, after)
            row = face(here, next_row(here))
            previous = last_row(row)
            level = jnp.where(inside, face(here, pltpu.roll(here, 127, 1)), 0.0)
            sums = (before + side) + (row + previous) + (level + pltpu.roll(level, 1, 1))
            wx[at], wy[at], wyp[at], wl[at] = side, row, previous, level
            total[at] = sums
            inv[at] = reciprocal(shift + sums)
            here, before = after, side
        return carry

    wx[0] = jnp.zeros((rows, 128), jnp.float32)
    lax.fori_loop(0, PLACES // width, weigh, 0)


STAGES = ((1, 39, 71), (2, 38, 70), (3, 37, 69), (4, 36, 68))
WIDTHS = ((19, 12, 17, 16), (8, 8, 8, 8))
READY = 40
EDGE = 12


def iterate_half(upper, wx, wy, wyp, wl, total, inv, own, other, near_rows, far_rows, *refs):
    if upper:
        edge, w_own, w_send, *refs = refs
    else:
        w_own, w_send, edge, *refs = refs
    it, source, spec, x, y, z, natural = refs
    rows = ROWS + TILE
    first = lax.axis_index("tm") == 0
    low = in_low(rows)
    beta = corner_weight ** 0.5
    gamma = jnp.where(low, 1.0, beta)
    shared = [(it, 38), (it, 39), (source, 39), (x, 37), (x, 38), (y, 36), (y, 37), (z, 35), (z, 36)]
    shared += [(spec, 36), (spec, 37), (spec, 38)]
    if upper:
        for i, (ref, at) in enumerate(shared):
            ref[at] = edge[i]

    def assemble(second):
        def step(i):
            at = i + (PAIRS if second else 0)
            theirs = cat(other[at], halo_tiles(near_rows[i], far_rows[i])[second])
            mine = own[at]
            step0, step1 = jnp.where(first, mine, theirs), jnp.where(first, theirs, mine)
            moved = swapped(step0)
            it[at] = jnp.where(low, step0, swapped(step1))
            source[at] = jnp.where(low, moved, step1 + moved)

        return step

    if upper:
        blocks(READY - PAIRS, PAIRS, 8, assemble(1))
    else:
        blocks(0, PAIRS, 12, assemble(0))
        blocks(0, READY - PAIRS, 4, assemble(1))

    def over(stage, read, ref, step):
        lo, hi = STAGES[stage][upper : upper + 2]
        width = WIDTHS[upper][stage]

        def body(i, carry):
            start = lo + i * width
            around = [read(ref, start - 1), read(ref, start)]
            before = wx[start - 1]
            for u in range(width):
                at = start + u
                around = [*around[-2:], read(ref, at + 1)]
                side = wx[at]
                step(at, around, (before, side, wy[at], wyp[at], wl[at]))
                before = side
            return carry

        lax.fori_loop(0, (hi - lo) // width, body, 0)

    def residual(at, around, w):
        left = (woven(source, at) - ((1.0 + total[at]) * around[1] - near(around, w))) * gamma
        moved = swapped(left)
        value = jnp.where(low, left + moved, moved - left)
        spec[at] = value
        x[at] = value * inv[at]

    over(0, woven, it, residual)

    def plain(ref, at):
        return ref[at]

    def sweep(at, around, w):
        return (spec[at] + near(around, w)) * inv[at]

    def to(ref):
        def step(at, around, w):
            ref[at] = sweep(at, around, w)

        return step

    over(1, plain, x, to(y))
    over(2, plain, y, to(z))
    base = STAGES[3][upper]
    back = jnp.where(low, 0.5, 0.5 / beta)

    def last(at, around, w):
        value = sweep(at, around, w)
        moved = swapped(value)
        value = jnp.where(low, value + moved, moved - value) * back
        for j in range(3):
            natural[pl.ds((at - base) * rows + j, TILE, stride=3), :] = value[j * TILE : (j + 1) * TILE]

    over(3, plain, z, last)
    count = HALF // 2
    for q in range(4):
        turned = cat(*[natural[pl.ds(q + 4 * j, count, stride=rows), :] for j in range(4)]).T
        step0, step1 = turned[:LEVELS], turned[LEVELS:]
        w_own[q] = jnp.where(first, step0, step1)
        w_send[q] = jnp.where(first, step1, step0)
    if not upper:
        for i, (ref, at) in enumerate(shared):
            edge[i] = ref[at]


def placed(value, j, quarter):
    return pltpu.roll(value, (32 * (quarter - j) + 128) & 127, 1)


def finish_most(it, own_low, own_high, got_low, most):
    t = lax.axis_index("tm")
    group = ids(LEVELS, 1) // 32

    def step(q):
        for j in range(4):
            rows = pl.ds(q + 4 * j, LEVELS, stride=ROWS)
            value = it[rows, :]
            for piece, quarter in ((own_low, 2 * t), (own_high, 2 * t + 1), (got_low, 2 - 2 * t)):
                value = jnp.where(group == quarter, value + placed(piece[q], j, quarter), value)
            most[rows, :] = value

    blocks(0, 4, 2, step)


def finish(most, got_high, out_hbm, out, sems):
    quarter = 3 - 2 * lax.axis_index("tm")
    part = LEVELS // CHUNKS
    here = ids(part, 1) // 32 == quarter

    def copy(c):
        span = pl.ds(pl.multiple_of(c * part * ROWS, part * ROWS), part * ROWS)
        return pltpu.make_async_copy(out.at[span], out_hbm.at[span], sems.at[c])

    def step(c):
        for q in range(4):
            value = got_high[q, pl.ds(pl.multiple_of(c * part, part), part), :]
            for j in range(4):
                rows = pl.ds(c * part * ROWS + q + 4 * j, part, stride=ROWS)
                old = most[rows, :]
                out[rows, :] = jnp.where(here, old + placed(value, j, quarter), old)
        copy(c).start()

    blocks(0, CHUNKS, 1, step)
    for c in range(CHUNKS):
        copy(c).wait()


def two_steps(iterate, heating, initial, region, cond_table):
    lats, lons = lax.axis_size("lat"), lax.axis_size("lon")
    swap = [(0, 1), (1, 0)]
    pairs = [[(i, i + 1) for i in range(start, lats - 1, 2)] for start in (0, 1)]
    pairs = [p + [(j, i) for i, j in p] for p in pairs]
    round_lon = [[(i, (i + 1) % lons) for i in range(start, lons, 2)] for start in (0, 1)]
    round_lon = [p + [(j, i) for i, j in p] for p in round_lon]
    flat = (LEVELS * ROWS, LONS)
    turned_flat = (LONS * ROWS, 2 * LEVELS)
    by_lon = (LONS, ROWS, 2 * LEVELS)
    wide = shape(PLACES, ROWS + TILE, 128)

    def in_hbm(x):
        return pltpu.with_memory_space_constraint(x, pltpu.HBM)

    xm, turned, it = call(
        send_first,
        [shape(SENT * ROWS, 128), shape(*turned_flat), shape(*flat)],
        [in_hbm(iterate.reshape(flat)), in_hbm(heating.reshape(flat))],
        scratch=[buffer(*flat), pltpu.SemaphoreType.DMA((CHUNKS, 2))],
        hbm_ins=(0, 1),
    )
    xm = lax.ppermute(xm, "tm", swap)
    sides = shape(HALO + 2, ROWS, 128)
    fixed, near_sides, far_sides = call(
        send_sides,
        [shape(*turned_flat), sides, sides],
        [turned, region.reshape(flat), initial.reshape(flat), in_hbm(cond_table)],
        scratch=[pltpu.SMEM(cond_table.shape, jnp.float32), pltpu.SemaphoreType.DMA],
        hbm_ins=(3,),
    )
    near_sides = lax.ppermute(near_sides, "lon", round_lon[0])
    far_sides = lax.ppermute(far_sides, "lon", round_lon[1])
    main = shape(PLACES, ROWS, 128)
    lat = shape(PAIRS + QUADS, TILE, 128)
    rows = shape(PAIRS, TILE, 128)
    own_main, own_fixed, near_lat, far_lat, xs = call(
        add_sides,
        [main, main, lat, lat, shape(HALO, ROWS, 128)],
        [turned.reshape(by_lon), fixed.reshape(by_lon), near_sides, far_sides],
    )
    near_lat = lax.ppermute(near_lat, "lat", pairs[0])
    far_lat = lax.ppermute(far_lat, "lat", pairs[1])
    xs = lax.ppermute(xs, "tm", swap)
    other, near_rows, far_rows = call(gather, [main, rows, rows], [xm.reshape(SENT, ROWS, 128), xs, own_fixed])
    near_rows = lax.ppermute(near_rows, "lat", pairs[0])
    far_rows = lax.ppermute(far_rows, "lat", pairs[1])
    *ready, own = call(
        prepare,
        [wide] * 7,
        [own_main, own_fixed, near_lat, far_lat, other],
        scratch=[buffer(PLACES + 1, ROWS + TILE, 128)],
    )
    given = [*ready, own, other, near_rows, far_rows]
    corrections = [shape(4, LEVELS, 128)] * 2
    fields = [buffer(PLACES, ROWS + TILE, 128)] * 6 + [buffer(HALF // 2 * (ROWS + TILE), 128)]
    own_low, send_low, edge = call(
        functools.partial(iterate_half, 0),
        [*corrections, shape(EDGE, ROWS + TILE, 128)],
        given,
        scratch=fields,
        limit=16,
    )
    got_low = lax.ppermute(send_low, "tm", swap)
    own_high, send_high = call(
        functools.partial(iterate_half, 1), corrections, [*given, edge], scratch=fields, limit=16
    )
    got_high = lax.ppermute(send_high, "tm", swap)
    (most,) = call(finish_most, [shape(*flat)], [it, own_low, own_high, got_low])
    (out,) = call(
        finish,
        [shape(*flat)],
        [most, got_high],
        scratch=[buffer(*flat), pltpu.SemaphoreType.DMA((CHUNKS,))],
        hbm_outs=(0,),
    )
    return out.reshape(iterate.shape)


def solution(mesh):
    return jax.shard_map(
        two_steps if mesh.shape["tm"] == 2 else on_device,
        mesh=mesh,
        in_specs=(
            P("tm", None, "lat", "lon"),
            P("tm", None, "lat", "lon"),
            P(None, "lat", "lon"),
            P(None, "lat", "lon"),
            P(),
        ),
        out_specs=P("tm", None, "lat", "lon"),
        check_vma=False,
    )
```

```python
import functools

import jax
import jax.numpy as jnp
from jax import lax
from jax.experimental import pallas as pl
from jax.experimental.pallas import tpu as pltpu
from jax.sharding import PartitionSpec as P

SWEEPS = 4


corner_weight = 0.1


def padded(value, sides, width, wrap):
    for axis, dim in sides:
        peers, length = (lax.axis_size(axis), value.shape[dim])
        up = [(i, (i + 1) % peers) for i in range(peers if wrap else peers - 1)]
        down = [(j, i) for i, j in up]
        last = lax.slice_in_dim(value, length - width, length, axis=dim)
        initial = lax.slice_in_dim(value, 0, width, axis=dim)
        before = lax.ppermute(last, axis, up)
        after = lax.ppermute(initial, axis, down)
        value = jnp.concatenate([before, value, after], axis=dim)
    return value


def passed_along(block, axis, distance):
    devices = range(lax.axis_size(axis))
    route = [(i - distance, i) for i in devices if i - distance in devices]
    return lax.ppermute(block, axis, route)


def harmonic(first, second):
    return 2.0 * first * second / (first + second)


def conductivity(region, cond_table):
    classes = jnp.arange(cond_table.shape[0], dtype=jnp.int32)
    onehot = (region[..., None] == classes).astype(jnp.float32)
    return jnp.sum(onehot * cond_table, axis=-1)


def extend(stack):
    lat_ext = padded(stack, (("lat", 2),), 1, False)
    both = padded(lat_ext, (("lon", 3),), 1, True)
    return jnp.pad(both, ((0, 0), (1, 1), (0, 0), (0, 0)))


def face_weights(kext):
    centre = kext[1:-1, 1:-1, 1:-1]
    return (
        harmonic(centre, kext[:-2, 1:-1, 1:-1]),
        harmonic(centre, kext[2:, 1:-1, 1:-1]),
        harmonic(centre, kext[1:-1, :-2, 1:-1]),
        harmonic(centre, kext[1:-1, 2:, 1:-1]),
        harmonic(centre, kext[1:-1, 1:-1, :-2]),
        harmonic(centre, kext[1:-1, 1:-1, 2:]),
    )


def neighbours(weights, ext):
    near = weights[0] * ext[..., :-2, 1:-1, 1:-1] + weights[1] * ext[..., 2:, 1:-1, 1:-1]
    near = near + weights[2] * ext[..., 1:-1, :-2, 1:-1] + weights[3] * ext[..., 1:-1, 2:, 1:-1]
    near = near + weights[4] * ext[..., 1:-1, 1:-1, :-2] + weights[5] * ext[..., 1:-1, 1:-1, 2:]
    return near


def on_device(iterate, heating, initial, region, cond_table):
    steps = lax.axis_size("tm")
    own = lax.axis_index("tm")
    high = lax.Precision.HIGHEST
    kfield = conductivity(region, cond_table)
    ext = extend(jnp.stack([kfield, iterate[0]]))
    weights = face_weights(ext[0])
    total = weights[0] + weights[1] + weights[2] + weights[3] + weights[4] + weights[5]
    shifted = passed_along(iterate, "tm", 1)[0]
    previous = jnp.where(own == 0, initial, shifted)
    residual = heating[0] + previous - ((1.0 + total) * iterate[0] - neighbours(weights, ext[1]))
    scale_own = corner_weight ** (own.astype(jnp.float32) / steps)
    scaled = residual * scale_own
    zeros = jnp.zeros_like(residual)
    piece = lax.all_gather(scaled[None], "tm", axis=0, tiled=True)
    order = jnp.arange(piece.shape[0], dtype=jnp.int32)
    angle = 2.0 * jnp.pi / steps * (own * order % steps).astype(jnp.float32)
    real_part = jnp.einsum("n,nabc->abc", jnp.cos(angle), piece, precision=high)
    imag_part = (zeros, zeros)[1] - jnp.einsum("n,nabc->abc", jnp.sin(angle), piece, precision=high)
    beta = corner_weight ** (1.0 / steps)
    freq_angle = 2.0 * jnp.pi / steps * (own % steps).astype(jnp.float32)
    diag_re = 1.0 - beta * jnp.cos(freq_angle) + total
    diag_im = beta * jnp.sin(freq_angle) + zeros
    denom = diag_re * diag_re + diag_im * diag_im
    inv_re = diag_re / denom
    inv_im = -diag_im / denom
    sol_re = real_part * inv_re - imag_part * inv_im
    sol_im = real_part * inv_im + imag_part * inv_re
    for sweep in range(SWEEPS - 1):
        near = neighbours(weights, extend(jnp.stack([sol_re, sol_im])))
        rhs_re = real_part + near[0]
        rhs_im = imag_part + near[1]
        sol_re = rhs_re * inv_re - rhs_im * inv_im
        sol_im = rhs_re * inv_im + rhs_im * inv_re
    pieces = (
        lax.all_gather(sol_re[None], "tm", axis=0, tiled=True),
        lax.all_gather(sol_im[None], "tm", axis=0, tiled=True),
    )
    order = jnp.arange(pieces[0].shape[0], dtype=jnp.int32)
    angle = 2.0 * jnp.pi / steps * (order * own % steps).astype(jnp.float32)
    summed = jnp.einsum("k,kabc->abc", jnp.cos(angle), pieces[0], precision=high) - jnp.einsum(
        "k,kabc->abc", jnp.sin(angle), pieces[1], precision=high
    )
    back = summed / steps
    return iterate + (back / scale_own)[None]


HALO = 4
TILE = 8
LEVELS = 64
ROWS = 16
LONS = 128
HALF = 64
SENT = HALF + HALO
PLACES = HALF + 2 * HALO
PAIRS = PLACES // 2
QUADS = PLACES // 4
CHUNKS = 4


def specs(count, hbm):
    return [pl.BlockSpec(memory_space=pltpu.HBM if i in hbm else pltpu.VMEM) for i in range(count)]


def call(body, outs, ins, scratch=(), limit=8, hbm_ins=(), hbm_outs=()):
    moved = sum(x.size * 4 for x in ins) + sum(x.size * 4 for x in outs)
    return pl.pallas_call(
        body,
        out_shape=outs,
        in_specs=specs(len(ins), hbm_ins),
        out_specs=specs(len(outs), hbm_outs),
        scratch_shapes=scratch,
        compiler_params=pltpu.CompilerParams(vmem_limit_bytes=limit << 20),
        cost_estimate=pl.CostEstimate(flops=moved * 4, bytes_accessed=moved, transcendentals=0),
    )(*ins)


def shape(*dims):
    return jax.ShapeDtypeStruct(dims, jnp.float32)


def buffer(*dims):
    return pltpu.VMEM(dims, jnp.float32)


def ids(rows, dim):
    return lax.broadcasted_iota(jnp.int32, (rows, 128), dim)


def in_low(rows):
    return ids(rows, 1) < LEVELS


def swapped(x):
    return pltpu.roll(x, LEVELS, 1)


def cat(*values):
    return jnp.concatenate(values, axis=0)


def even(axis):
    return lax.rem(lax.axis_index(axis), 2) == 0


def blocks(lo, hi, width, step):
    def body(i, carry):
        for u in range(width):
            step(lo + i * width + u)
        return carry

    lax.fori_loop(0, (hi - lo) // width, body, 0)


def send_first(it_hbm, h_hbm, xm, turned, it, h, sems):
    t = lax.axis_index("tm")
    by_level = (LEVELS, ROWS, LONS)
    copies = []
    for k in range(ROWS // TILE):
        for f, (source, target) in enumerate(((it_hbm, it), (h_hbm, h))):
            for c in range(2):
                part = pl.ds(c * LEVELS // 2, LEVELS // 2), pl.ds(k * TILE, TILE)
                copy = pltpu.make_async_copy(source.at[part], target.reshape(by_level).at[part], sems.at[k, f, c])
                copy.start()
                copies.append(copy)

    def turn(r):
        rows = pl.ds(r, LEVELS, stride=ROWS)
        turned[pl.ds(r, LONS, stride=ROWS), :] = cat(it[rows, :], h[rows, :]).T

    for k in range(ROWS // TILE):
        for copy in copies[4 * k : 4 * k + 4]:
            copy.wait()
        blocks(k * TILE, (k + 1) * TILE, 4, turn)
    start = (LONS - SENT) * ROWS * (1 - t)

    def cut(i):
        xm[pl.ds(pl.multiple_of(i * ROWS, ROWS), ROWS), :] = turned[pl.ds(pl.multiple_of(start + i * ROWS, ROWS), ROWS), :]

    blocks(0, SENT, 17, cut)


def heated(turned, fixed):
    add = jnp.logical_and(jnp.logical_not(in_low(ROWS)), lax.axis_index("tm") == 0)
    return turned + jnp.where(add, fixed, 0.0)


def send_sides(turned, region, initial, table_hbm, fixed, near_sides, far_sides, table, sem):
    copy = pltpu.make_async_copy(table_hbm, table, sem)
    copy.start()
    copy.wait()

    def turn(r):
        rows = pl.ds(r, LEVELS, stride=ROWS)
        classes = region[rows, :]
        value = jnp.full(classes.shape, table[0], jnp.float32)
        for c in range(1, table.shape[0]):
            value = jnp.where(classes == c, table[c], value)
        fixed[pl.ds(r, LONS, stride=ROWS), :] = cat(value, initial[rows, :]).T

    blocks(0, ROWS, 4, turn)
    near_right = even("lon")
    low = in_low(ROWS)

    def strip(first_lon):
        def at(ref, i):
            return ref[(first_lon + i) * ROWS : (first_lon + i + 1) * ROWS, :]

        return [heated(at(turned, i), at(fixed, i)) for i in range(HALO)] + [
            jnp.where(low, at(fixed, i), swapped(at(fixed, i + 2))) for i in range(2)
        ]

    for i, (right, left) in enumerate(zip(strip(LONS - HALO), strip(0))):
        near_sides[i] = jnp.where(near_right, right, left)
        far_sides[i] = jnp.where(near_right, left, right)


def edge_pair(first, second):
    top = ids(TILE, 0) < HALO
    first_up = even("lat")
    down = jnp.where(top, first[:TILE], pltpu.roll(second[:TILE], HALO, 0))
    up = jnp.where(top, pltpu.roll(first[-TILE:], HALO, 0), second[-TILE:])
    return jnp.where(first_up, up, down), jnp.where(first_up, down, up)


def halo_tiles(near_pair, far_pair):
    first_up = even("lat")
    after = jnp.where(first_up, near_pair, far_pair)
    before = jnp.where(first_up, far_pair, near_pair)
    top = ids(TILE, 0) < HALO
    return (
        jnp.where(top, after, pltpu.roll(before, HALO, 0)),
        jnp.where(top, pltpu.roll(after, HALO, 0), before),
    )


def add_sides(turned, fixed, near_sides, far_sides, own, own_fixed, near_lat, far_lat, xs):
    t = lax.axis_index("tm")
    from_near = (t == 0) != even("lon")
    count = near_sides.shape[0]
    beside = [jnp.where(from_near, near_sides[i], far_sides[i]) for i in range(count)]
    for i in range(HALO):
        own[SENT * t + i] = beside[i]
        xs[i] = jnp.where(from_near, far_sides[i], near_sides[i])
    for i in range(2):
        own_fixed[SENT * t + i] = beside[HALO + i]
        own_fixed[SENT * t + i + 2] = swapped(beside[HALO + i])

    def copy(i):
        at = HALO * (1 - t) + i
        lon = (LONS - SENT) * t + i
        own[at] = heated(turned[lon], fixed[lon])
        own_fixed[at] = fixed[lon]

    blocks(0, SENT, 17, copy)

    def rows(i):
        near_lat[i], far_lat[i] = edge_pair(own[i], own[i + PAIRS])

    blocks(0, PAIRS, 12, rows)
    low = in_low(TILE)

    def fixed_rows(i):
        here = edge_pair(own_fixed[i], own_fixed[i + PAIRS])
        there = edge_pair(own_fixed[i + QUADS], own_fixed[i + PAIRS + QUADS])
        near_lat[PAIRS + i], far_lat[PAIRS + i] = [jnp.where(low, a, swapped(b)) for a, b in zip(here, there)]

    blocks(0, QUADS, 9, fixed_rows)


def gather(xm, xs, own_fixed, other, near_rows, far_rows):
    t = lax.axis_index("tm")
    add = jnp.logical_and(jnp.logical_not(in_low(ROWS)), t == 1)
    for i in range(HALO):
        other[SENT * t + i] = xs[i]

    def copy(i):
        at = HALO * (1 - t) + i
        other[at] = xm[i] + jnp.where(add, own_fixed[at], 0.0)

    blocks(0, SENT, 17, copy)

    def rows(i):
        near_rows[i], far_rows[i] = edge_pair(other[i], other[i + PAIRS])

    blocks(0, PAIRS, 12, rows)


def reciprocal(d):
    y = pl.reciprocal(d, approx=True)
    return y * (2.0 - d * y)


def face(a, b):
    return 2.0 * a * b * reciprocal(jnp.maximum(a + b, 1e-30))


def woven(ref, at):
    return cat(*[ref[at, pl.ds(j, TILE, stride=3), :] for j in range(3)])


def next_row(x):
    return cat(x[TILE:], pltpu.roll(x[:TILE], TILE - 1, 0))


def last_row(x):
    return cat(pltpu.roll(x[-TILE:], 1, 0), x[:-TILE])


def prepare(own_main, own_fixed, near_lat, far_lat, _, wx, wy, wyp, wl, total, inv, own, K):
    rows = ROWS + TILE
    low = in_low(ROWS)
    low_tile = in_low(TILE)
    beta = corner_weight ** 0.5
    K[PLACES] = jnp.zeros((rows, 128), jnp.float32)

    def assemble(i):
        for at, tile in zip((i, i + PAIRS), halo_tiles(near_lat[i], far_lat[i])):
            own[at] = cat(own_main[at], tile)

    blocks(0, PAIRS, 12, assemble)

    def assemble_fixed(i):
        for at, tile in zip((i, i + PAIRS), halo_tiles(near_lat[PAIRS + i], far_lat[PAIRS + i])):
            moved = swapped(tile)
            for here, value in ((at, jnp.where(low_tile, tile, moved)), (at + QUADS, jnp.where(low_tile, moved, tile))):
                main = own_fixed[here]
                K[here] = cat(jnp.where(low, main, swapped(main)), value)

    blocks(0, QUADS, 9, assemble_fixed)
    lane = ids(rows, 1)
    inside = (lane & (LEVELS - 1)) != LEVELS - 1
    shift = jnp.where(lane < LEVELS, 1.0 - beta, 1.0 + beta)
    width = 18

    def weigh(i, carry):
        start = i * width
        here = woven(K, start)
        before = wx[jnp.maximum(start - 1, 0)]
        for u in range(width):
            at = start + u
            after = woven(K, at + 1)
            side = face(here, after)
            row = face(here, next_row(here))
            previous = last_row(row)
            level = jnp.where(inside, face(here, pltpu.roll(here, 127, 1)), 0.0)
            sums = (before + side) + (row + previous) + (level + pltpu.roll(level, 1, 1))
            wx[at], wy[at], wyp[at], wl[at] = side, row, previous, level
            total[at] = sums
            inv[at] = reciprocal(shift + sums)
            here, before = after, side
        return carry

    wx[0] = jnp.zeros((rows, 128), jnp.float32)
    lax.fori_loop(0, PLACES // width, weigh, 0)


STAGES = ((1, 39, 71), (2, 38, 70), (3, 37, 69), (4, 36, 68))
AHEAD = 2
READY = 40
EDGE = 12


def iterate_half(upper, wx, wy, wyp, wl, total, inv, own, other, near_rows, far_rows, *refs):
    if upper:
        edge, w_own, w_send, *refs = refs
    else:
        w_own, w_send, edge, *refs = refs
    it, source, spec, x, y, z, natural = refs
    rows = ROWS + TILE
    first = lax.axis_index("tm") == 0
    low = in_low(rows)
    beta = corner_weight ** 0.5
    gamma = jnp.where(low, 1.0, beta)
    shared = [(it, 38), (it, 39), (source, 39), (x, 37), (x, 38), (y, 36), (y, 37), (z, 35), (z, 36)]
    shared += [(spec, 36), (spec, 37), (spec, 38)]
    if upper:
        for i, (ref, at) in enumerate(shared):
            ref[at] = edge[i]

    def assemble(second):
        def step(i):
            at = i + (PAIRS if second else 0)
            theirs = cat(other[at], halo_tiles(near_rows[i], far_rows[i])[second])
            mine = own[at]
            step0, step1 = jnp.where(first, mine, theirs), jnp.where(first, theirs, mine)
            moved = swapped(step0)
            it[at] = jnp.where(low, step0, swapped(step1))
            source[at] = jnp.where(low, moved, step1 + moved)

        return step

    if upper:
        blocks(READY - PAIRS, PAIRS, 8, assemble(1))
    else:
        blocks(0, PAIRS, 12, assemble(0))
        blocks(0, READY - PAIRS, 4, assemble(1))

    def over(stage, read, ref, step):
        lo, hi = STAGES[stage][upper : upper + 2]

        def rotated(at):
            at = jnp.minimum(at, PLACES - 1)
            mid = read(ref, at)
            up = pltpu.roll(mid[:TILE], TILE - 1, 0)
            down = pltpu.roll(mid[-TILE:], 1, 0)
            return mid, up, down, pltpu.roll(mid, 127, 1), pltpu.roll(wl[at] * mid, 1, 1)

        def body(i, carry):
            before, last_side, here = carry
            start = lo + i * AHEAD
            ahead = [rotated(start + AHEAD + u) for u in range(AHEAD)]
            both = [*here, *ahead]
            for u in range(AHEAD):
                at = start + u
                mid, up, down, left, right = both[u]
                side = wx[at]
                total = last_side * before + side * both[u + 1][0]
                total = total + (wy[at] * cat(mid[TILE:], up) + wyp[at] * cat(down, mid[:-TILE]))
                step(at, mid, total + (wl[at] * left + right))
                before, last_side = mid, side
            return before, last_side, ahead

        first_carry = read(ref, lo - 1), wx[lo - 1], [rotated(lo + u) for u in range(AHEAD)]
        lax.fori_loop(0, (hi - lo) // AHEAD, body, first_carry)

    def residual(at, mid, around):
        left = (woven(source, at) - ((1.0 + total[at]) * mid - around)) * gamma
        moved = swapped(left)
        value = jnp.where(low, left + moved, moved - left)
        spec[at] = value
        x[at] = value * inv[at]

    over(0, woven, it, residual)

    def plain(ref, at):
        return ref[at]

    def to(ref):
        def step(at, mid, around):
            ref[at] = (spec[at] + around) * inv[at]

        return step

    over(1, plain, x, to(y))
    over(2, plain, y, to(z))
    base = STAGES[3][upper]
    back = jnp.where(low, 0.5, 0.5 / beta)

    def last(at, mid, around):
        value = (spec[at] + around) * inv[at]
        moved = swapped(value)
        value = jnp.where(low, value + moved, moved - value) * back
        for j in range(3):
            natural[pl.ds((at - base) * rows + j, TILE, stride=3), :] = value[j * TILE : (j + 1) * TILE]

    over(3, plain, z, last)
    count = HALF // 2
    for q in range(4):
        turned = cat(*[natural[pl.ds(q + 4 * j, count, stride=rows), :] for j in range(4)]).T
        step0, step1 = turned[:LEVELS], turned[LEVELS:]
        w_own[q] = jnp.where(first, step0, step1)
        w_send[q] = jnp.where(first, step1, step0)
    if not upper:
        for i, (ref, at) in enumerate(shared):
            edge[i] = ref[at]


def placed(value, j, quarter):
    return pltpu.roll(value, (32 * (quarter - j) + 128) & 127, 1)


def finish_most(it, own_low, own_high, got_low, most):
    t = lax.axis_index("tm")
    group = ids(LEVELS, 1) // 32

    def step(q):
        for j in range(4):
            rows = pl.ds(q + 4 * j, LEVELS, stride=ROWS)
            value = it[rows, :]
            for piece, quarter in ((own_low, 2 * t), (own_high, 2 * t + 1), (got_low, 2 - 2 * t)):
                value = jnp.where(group == quarter, value + placed(piece[q], j, quarter), value)
            most[rows, :] = value

    blocks(0, 4, 2, step)


def finish(most, got_high, out_hbm, out, sems):
    quarter = 3 - 2 * lax.axis_index("tm")
    part = LEVELS // CHUNKS
    here = ids(part, 1) // 32 == quarter

    def copy(c):
        span = pl.ds(pl.multiple_of(c * part * ROWS, part * ROWS), part * ROWS)
        return pltpu.make_async_copy(out.at[span], out_hbm.at[span], sems.at[c])

    def step(c):
        for q in range(4):
            value = got_high[q, pl.ds(pl.multiple_of(c * part, part), part), :]
            for j in range(4):
                rows = pl.ds(c * part * ROWS + q + 4 * j, part, stride=ROWS)
                old = most[rows, :]
                out[rows, :] = jnp.where(here, old + placed(value, j, quarter), old)
        copy(c).start()

    blocks(0, CHUNKS, 1, step)
    for c in range(CHUNKS):
        copy(c).wait()


def two_steps(iterate, heating, initial, region, cond_table):
    lats, lons = lax.axis_size("lat"), lax.axis_size("lon")
    swap = [(0, 1), (1, 0)]
    pairs = [[(i, i + 1) for i in range(start, lats - 1, 2)] for start in (0, 1)]
    pairs = [p + [(j, i) for i, j in p] for p in pairs]
    round_lon = [[(i, (i + 1) % lons) for i in range(start, lons, 2)] for start in (0, 1)]
    round_lon = [p + [(j, i) for i, j in p] for p in round_lon]
    flat = (LEVELS * ROWS, LONS)
    turned_flat = (LONS * ROWS, 2 * LEVELS)
    by_lon = (LONS, ROWS, 2 * LEVELS)
    wide = shape(PLACES, ROWS + TILE, 128)

    def in_hbm(x):
        return pltpu.with_memory_space_constraint(x, pltpu.HBM)

    xm, turned, it = call(
        send_first,
        [shape(SENT * ROWS, 128), shape(*turned_flat), shape(*flat)],
        [in_hbm(iterate[0]), in_hbm(heating[0])],
        scratch=[buffer(*flat), pltpu.SemaphoreType.DMA((ROWS // TILE, 2, 2))],
        hbm_ins=(0, 1),
    )
    xm = lax.ppermute(xm, "tm", swap)
    sides = shape(HALO + 2, ROWS, 128)
    fixed, near_sides, far_sides = call(
        send_sides,
        [shape(*turned_flat), sides, sides],
        [turned, region.reshape(flat), initial.reshape(flat), in_hbm(cond_table)],
        scratch=[pltpu.SMEM(cond_table.shape, jnp.float32), pltpu.SemaphoreType.DMA],
        hbm_ins=(3,),
    )
    near_sides = lax.ppermute(near_sides, "lon", round_lon[0])
    far_sides = lax.ppermute(far_sides, "lon", round_lon[1])
    main = shape(PLACES, ROWS, 128)
    lat = shape(PAIRS + QUADS, TILE, 128)
    rows = shape(PAIRS, TILE, 128)
    own_main, own_fixed, near_lat, far_lat, xs = call(
        add_sides,
        [main, main, lat, lat, shape(HALO, ROWS, 128)],
        [turned.reshape(by_lon), fixed.reshape(by_lon), near_sides, far_sides],
    )
    near_lat = lax.ppermute(near_lat, "lat", pairs[0])
    far_lat = lax.ppermute(far_lat, "lat", pairs[1])
    xs = lax.ppermute(xs, "tm", swap)
    other, near_rows, far_rows = call(gather, [main, rows, rows], [xm.reshape(SENT, ROWS, 128), xs, own_fixed])
    near_rows = lax.ppermute(near_rows, "lat", pairs[0])
    far_rows = lax.ppermute(far_rows, "lat", pairs[1])
    *ready, own = call(
        prepare,
        [wide] * 7,
        [own_main, own_fixed, near_lat, far_lat, other],
        scratch=[buffer(PLACES + 1, ROWS + TILE, 128)],
    )
    given = [*ready, own, other, near_rows, far_rows]
    corrections = [shape(4, LEVELS, 128)] * 2
    fields = [buffer(PLACES, ROWS + TILE, 128)] * 6 + [buffer(HALF // 2 * (ROWS + TILE), 128)]
    own_low, send_low, edge = call(
        functools.partial(iterate_half, 0),
        [*corrections, shape(EDGE, ROWS + TILE, 128)],
        given,
        scratch=fields,
        limit=16,
    )
    got_low = lax.ppermute(send_low, "tm", swap)
    own_high, send_high = call(
        functools.partial(iterate_half, 1), corrections, [*given, edge], scratch=fields, limit=16
    )
    got_high = lax.ppermute(send_high, "tm", swap)
    (most,) = call(finish_most, [shape(*flat)], [it, own_low, own_high, got_low])
    (out,) = call(
        finish,
        [shape(*flat)],
        [most, got_high],
        scratch=[buffer(*flat), pltpu.SemaphoreType.DMA((CHUNKS,))],
        hbm_outs=(0,),
    )
    return out.reshape(iterate.shape)


def solution(mesh):
    return jax.shard_map(
        two_steps if mesh.shape["tm"] == 2 else on_device,
        mesh=mesh,
        in_specs=(
            P("tm", None, "lat", "lon"),
            P("tm", None, "lat", "lon"),
            P(None, "lat", "lon"),
            P(None, "lat", "lon"),
            P(),
        ),
        out_specs=P("tm", None, "lat", "lon"),
        check_vma=False,
    )
```

```python
import functools

import jax
import jax.numpy as jnp
from jax import lax
from jax.experimental import pallas as pl
from jax.experimental.pallas import tpu as pltpu
from jax.sharding import PartitionSpec as P

SWEEPS = 4


corner_weight = 0.1


def padded(value, sides, width, wrap):
    for axis, dim in sides:
        peers, length = (lax.axis_size(axis), value.shape[dim])
        up = [(i, (i + 1) % peers) for i in range(peers if wrap else peers - 1)]
        down = [(j, i) for i, j in up]
        last = lax.slice_in_dim(value, length - width, length, axis=dim)
        initial = lax.slice_in_dim(value, 0, width, axis=dim)
        before = lax.ppermute(last, axis, up)
        after = lax.ppermute(initial, axis, down)
        value = jnp.concatenate([before, value, after], axis=dim)
    return value


def passed_along(block, axis, distance):
    devices = range(lax.axis_size(axis))
    route = [(i - distance, i) for i in devices if i - distance in devices]
    return lax.ppermute(block, axis, route)


def harmonic(first, second):
    return 2.0 * first * second / (first + second)


def conductivity(region, cond_table):
    classes = jnp.arange(cond_table.shape[0], dtype=jnp.int32)
    onehot = (region[..., None] == classes).astype(jnp.float32)
    return jnp.sum(onehot * cond_table, axis=-1)


def extend(stack):
    lat_ext = padded(stack, (("lat", 2),), 1, False)
    both = padded(lat_ext, (("lon", 3),), 1, True)
    return jnp.pad(both, ((0, 0), (1, 1), (0, 0), (0, 0)))


def face_weights(kext):
    centre = kext[1:-1, 1:-1, 1:-1]
    return (
        harmonic(centre, kext[:-2, 1:-1, 1:-1]),
        harmonic(centre, kext[2:, 1:-1, 1:-1]),
        harmonic(centre, kext[1:-1, :-2, 1:-1]),
        harmonic(centre, kext[1:-1, 2:, 1:-1]),
        harmonic(centre, kext[1:-1, 1:-1, :-2]),
        harmonic(centre, kext[1:-1, 1:-1, 2:]),
    )


def neighbours(weights, ext):
    near = weights[0] * ext[..., :-2, 1:-1, 1:-1] + weights[1] * ext[..., 2:, 1:-1, 1:-1]
    near = near + weights[2] * ext[..., 1:-1, :-2, 1:-1] + weights[3] * ext[..., 1:-1, 2:, 1:-1]
    near = near + weights[4] * ext[..., 1:-1, 1:-1, :-2] + weights[5] * ext[..., 1:-1, 1:-1, 2:]
    return near


def on_device(iterate, heating, initial, region, cond_table):
    steps = lax.axis_size("tm")
    own = lax.axis_index("tm")
    high = lax.Precision.HIGHEST
    kfield = conductivity(region, cond_table)
    ext = extend(jnp.stack([kfield, iterate[0]]))
    weights = face_weights(ext[0])
    total = weights[0] + weights[1] + weights[2] + weights[3] + weights[4] + weights[5]
    shifted = passed_along(iterate, "tm", 1)[0]
    previous = jnp.where(own == 0, initial, shifted)
    residual = heating[0] + previous - ((1.0 + total) * iterate[0] - neighbours(weights, ext[1]))
    scale_own = corner_weight ** (own.astype(jnp.float32) / steps)
    scaled = residual * scale_own
    zeros = jnp.zeros_like(residual)
    piece = lax.all_gather(scaled[None], "tm", axis=0, tiled=True)
    order = jnp.arange(piece.shape[0], dtype=jnp.int32)
    angle = 2.0 * jnp.pi / steps * (own * order % steps).astype(jnp.float32)
    real_part = jnp.einsum("n,nabc->abc", jnp.cos(angle), piece, precision=high)
    imag_part = (zeros, zeros)[1] - jnp.einsum("n,nabc->abc", jnp.sin(angle), piece, precision=high)
    beta = corner_weight ** (1.0 / steps)
    freq_angle = 2.0 * jnp.pi / steps * (own % steps).astype(jnp.float32)
    diag_re = 1.0 - beta * jnp.cos(freq_angle) + total
    diag_im = beta * jnp.sin(freq_angle) + zeros
    denom = diag_re * diag_re + diag_im * diag_im
    inv_re = diag_re / denom
    inv_im = -diag_im / denom
    sol_re = real_part * inv_re - imag_part * inv_im
    sol_im = real_part * inv_im + imag_part * inv_re
    for sweep in range(SWEEPS - 1):
        near = neighbours(weights, extend(jnp.stack([sol_re, sol_im])))
        rhs_re = real_part + near[0]
        rhs_im = imag_part + near[1]
        sol_re = rhs_re * inv_re - rhs_im * inv_im
        sol_im = rhs_re * inv_im + rhs_im * inv_re
    pieces = (
        lax.all_gather(sol_re[None], "tm", axis=0, tiled=True),
        lax.all_gather(sol_im[None], "tm", axis=0, tiled=True),
    )
    order = jnp.arange(pieces[0].shape[0], dtype=jnp.int32)
    angle = 2.0 * jnp.pi / steps * (order * own % steps).astype(jnp.float32)
    summed = jnp.einsum("k,kabc->abc", jnp.cos(angle), pieces[0], precision=high) - jnp.einsum(
        "k,kabc->abc", jnp.sin(angle), pieces[1], precision=high
    )
    back = summed / steps
    return iterate + (back / scale_own)[None]


HALO = 4
TILE = 8
LEVELS = 64
ROWS = 16
LONS = 128
HALF = 64
SENT = HALF + HALO
PLACES = HALF + 2 * HALO
PAIRS = PLACES // 2
QUADS = PLACES // 4
CHUNKS = 4


def specs(count, hbm):
    return [pl.BlockSpec(memory_space=pltpu.HBM if i in hbm else pltpu.VMEM) for i in range(count)]


def call(body, outs, ins, scratch=(), limit=8, hbm_ins=(), hbm_outs=()):
    moved = sum(x.size * 4 for x in ins) + sum(x.size * 4 for x in outs)
    return pl.pallas_call(
        body,
        out_shape=outs,
        in_specs=specs(len(ins), hbm_ins),
        out_specs=specs(len(outs), hbm_outs),
        scratch_shapes=scratch,
        compiler_params=pltpu.CompilerParams(vmem_limit_bytes=limit << 20),
        cost_estimate=pl.CostEstimate(flops=moved * 4, bytes_accessed=moved, transcendentals=0),
    )(*ins)


def shape(*dims):
    return jax.ShapeDtypeStruct(dims, jnp.float32)


def buffer(*dims):
    return pltpu.VMEM(dims, jnp.float32)


def ids(rows, dim):
    return lax.broadcasted_iota(jnp.int32, (rows, 128), dim)


def in_low(rows):
    return ids(rows, 1) < LEVELS


def swapped(x):
    return pltpu.roll(x, LEVELS, 1)


def cat(*values):
    return jnp.concatenate(values, axis=0)


def even(axis):
    return lax.rem(lax.axis_index(axis), 2) == 0


def blocks(lo, hi, width, step):
    def body(i, carry):
        for u in range(width):
            step(lo + i * width + u)
        return carry

    lax.fori_loop(0, (hi - lo) // width, body, 0)


def send_first(it_hbm, h_hbm, xm, turned, it, h, sems):
    t = lax.axis_index("tm")
    by_level = (LEVELS, ROWS, LONS)
    copies = []
    for k in range(ROWS // TILE):
        for f, (source, target) in enumerate(((it_hbm, it), (h_hbm, h))):
            for c in range(2):
                part = pl.ds(c * LEVELS // 2, LEVELS // 2), pl.ds(k * TILE, TILE)
                copy = pltpu.make_async_copy(source.at[part], target.reshape(by_level).at[part], sems.at[k, f, c])
                copy.start()
                copies.append(copy)

    def turn(r):
        rows = pl.ds(r, LEVELS, stride=ROWS)
        turned[pl.ds(r, LONS, stride=ROWS), :] = cat(it[rows, :], h[rows, :]).T

    for k in range(ROWS // TILE):
        for copy in copies[4 * k : 4 * k + 4]:
            copy.wait()
        blocks(k * TILE, (k + 1) * TILE, 4, turn)
    start = (LONS - SENT) * ROWS * (1 - t)

    def cut(i):
        xm[pl.ds(pl.multiple_of(i * ROWS, ROWS), ROWS), :] = turned[pl.ds(pl.multiple_of(start + i * ROWS, ROWS), ROWS), :]

    blocks(0, SENT, 17, cut)


def heated(turned, fixed):
    add = jnp.logical_and(jnp.logical_not(in_low(ROWS)), lax.axis_index("tm") == 0)
    return turned + jnp.where(add, fixed, 0.0)


def send_sides(turned, region, initial, table_hbm, fixed, near_sides, far_sides, table, sem):
    copy = pltpu.make_async_copy(table_hbm, table, sem)
    copy.start()
    copy.wait()

    def turn(r):
        rows = pl.ds(r, LEVELS, stride=ROWS)
        classes = region[rows, :]
        value = jnp.full(classes.shape, table[0], jnp.float32)
        for c in range(1, table.shape[0]):
            value = jnp.where(classes == c, table[c], value)
        fixed[pl.ds(r, LONS, stride=ROWS), :] = cat(value, initial[rows, :]).T

    blocks(0, ROWS, 4, turn)
    near_right = even("lon")
    low = in_low(ROWS)

    def strip(first_lon):
        def at(ref, i):
            return ref[(first_lon + i) * ROWS : (first_lon + i + 1) * ROWS, :]

        return [heated(at(turned, i), at(fixed, i)) for i in range(HALO)] + [
            jnp.where(low, at(fixed, i), swapped(at(fixed, i + 2))) for i in range(2)
        ]

    for i, (right, left) in enumerate(zip(strip(LONS - HALO), strip(0))):
        near_sides[i] = jnp.where(near_right, right, left)
        far_sides[i] = jnp.where(near_right, left, right)


def edge_pair(first, second):
    top = ids(TILE, 0) < HALO
    first_up = even("lat")
    down = jnp.where(top, first[:TILE], pltpu.roll(second[:TILE], HALO, 0))
    up = jnp.where(top, pltpu.roll(first[-TILE:], HALO, 0), second[-TILE:])
    return jnp.where(first_up, up, down), jnp.where(first_up, down, up)


def halo_tiles(near_pair, far_pair):
    first_up = even("lat")
    after = jnp.where(first_up, near_pair, far_pair)
    before = jnp.where(first_up, far_pair, near_pair)
    top = ids(TILE, 0) < HALO
    return (
        jnp.where(top, after, pltpu.roll(before, HALO, 0)),
        jnp.where(top, pltpu.roll(after, HALO, 0), before),
    )


def add_sides(turned, fixed, near_sides, far_sides, own, own_fixed, near_lat, far_lat, xs):
    t = lax.axis_index("tm")
    from_near = (t == 0) != even("lon")
    count = near_sides.shape[0]
    beside = [jnp.where(from_near, near_sides[i], far_sides[i]) for i in range(count)]
    for i in range(HALO):
        own[SENT * t + i] = beside[i]
        xs[i] = jnp.where(from_near, far_sides[i], near_sides[i])
    for i in range(2):
        own_fixed[SENT * t + i] = beside[HALO + i]
        own_fixed[SENT * t + i + 2] = swapped(beside[HALO + i])

    def copy(i):
        at = HALO * (1 - t) + i
        lon = (LONS - SENT) * t + i
        own[at] = heated(turned[lon], fixed[lon])
        own_fixed[at] = fixed[lon]

    blocks(0, SENT, 17, copy)

    def rows(i):
        near_lat[i], far_lat[i] = edge_pair(own[i], own[i + PAIRS])

    blocks(0, PAIRS, 12, rows)
    low = in_low(TILE)

    def fixed_rows(i):
        here = edge_pair(own_fixed[i], own_fixed[i + PAIRS])
        there = edge_pair(own_fixed[i + QUADS], own_fixed[i + PAIRS + QUADS])
        near_lat[PAIRS + i], far_lat[PAIRS + i] = [jnp.where(low, a, swapped(b)) for a, b in zip(here, there)]

    blocks(0, QUADS, 9, fixed_rows)


def gather(xm, xs, own_fixed, other, near_rows, far_rows):
    t = lax.axis_index("tm")
    add = jnp.logical_and(jnp.logical_not(in_low(ROWS)), t == 1)
    for i in range(HALO):
        other[SENT * t + i] = xs[i]

    def copy(i):
        at = HALO * (1 - t) + i
        other[at] = xm[i] + jnp.where(add, own_fixed[at], 0.0)

    blocks(0, SENT, 17, copy)

    def rows(i):
        near_rows[i], far_rows[i] = edge_pair(other[i], other[i + PAIRS])

    blocks(0, PAIRS, 12, rows)


def reciprocal(d):
    y = pl.reciprocal(d, approx=True)
    return y * (2.0 - d * y)


def face(a, b):
    return 2.0 * a * b * reciprocal(jnp.maximum(a + b, 1e-30))


def woven(ref, at):
    return cat(*[ref[at, pl.ds(j, TILE, stride=3), :] for j in range(3)])


def next_row(x):
    return cat(x[TILE:], pltpu.roll(x[:TILE], TILE - 1, 0))


def last_row(x):
    return cat(pltpu.roll(x[-TILE:], 1, 0), x[:-TILE])


def near(around, w):
    before, mid, after = around
    wxp, wx, wy, wyp, wl = w
    total = wxp * before + wx * after
    total = total + (wy * next_row(mid) + wyp * last_row(mid))
    return total + (wl * pltpu.roll(mid, 127, 1) + pltpu.roll(wl * mid, 1, 1))


def prepare(own_main, own_fixed, near_lat, far_lat, _, wx, wy, wyp, wl, total, inv, own, K):
    rows = ROWS + TILE
    low = in_low(ROWS)
    low_tile = in_low(TILE)
    beta = corner_weight ** 0.5
    K[PLACES] = jnp.zeros((rows, 128), jnp.float32)

    def assemble(i):
        for at, tile in zip((i, i + PAIRS), halo_tiles(near_lat[i], far_lat[i])):
            own[at] = cat(own_main[at], tile)

    blocks(0, PAIRS, 12, assemble)

    def assemble_fixed(i):
        for at, tile in zip((i, i + PAIRS), halo_tiles(near_lat[PAIRS + i], far_lat[PAIRS + i])):
            moved = swapped(tile)
            for here, value in ((at, jnp.where(low_tile, tile, moved)), (at + QUADS, jnp.where(low_tile, moved, tile))):
                main = own_fixed[here]
                K[here] = cat(jnp.where(low, main, swapped(main)), value)

    blocks(0, QUADS, 9, assemble_fixed)
    lane = ids(rows, 1)
    inside = (lane & (LEVELS - 1)) != LEVELS - 1
    shift = jnp.where(lane < LEVELS, 1.0 - beta, 1.0 + beta)
    width = 18

    def weigh(i, carry):
        start = i * width
        here = woven(K, start)
        before = wx[jnp.maximum(start - 1, 0)]
        for u in range(width):
            at = start + u
            after = woven(K, at + 1)
            side = face(here, after)
            row = face(here, next_row(here))
            previous = last_row(row)
            level = jnp.where(inside, face(here, pltpu.roll(here, 127, 1)), 0.0)
            sums = (before + side) + (row + previous) + (level + pltpu.roll(level, 1, 1))
            wx[at], wy[at], wyp[at], wl[at] = side, row, previous, level
            total[at] = sums
            inv[at] = reciprocal(shift + sums)
            here, before = after, side
        return carry

    wx[0] = jnp.zeros((rows, 128), jnp.float32)
    lax.fori_loop(0, PLACES // width, weigh, 0)


RESIDUAL = ((1, 40, 10), (39, 32, 8))
SWEEP = ((2, 1, 36, 12), (38, -1, 32, 16))
FIRST = (4, 36)
COUNT = HALF // 2
READY = 40
EDGE = 12


def iterate_half(upper, wx, wy, wyp, wl, total, inv, own, other, near_rows, far_rows, *refs):
    if upper:
        edge, w_own, w_send, *refs = refs
    else:
        w_own, w_send, edge, *refs = refs
    it, source, spec, x, natural = refs
    rows = ROWS + TILE
    first = lax.axis_index("tm") == 0
    low = in_low(rows)
    beta = corner_weight ** 0.5
    gamma = jnp.where(low, 1.0, beta)
    shared = [(it, 38), (it, 39), (source, 39), (x, 0, 37), (x, 0, 38), (x, 1, 36), (x, 1, 37), (x, 2, 35), (x, 2, 36)]
    shared += [(spec, 36), (spec, 37), (spec, 38)]
    if upper:
        for i, (ref, *at) in enumerate(shared):
            ref[tuple(at)] = edge[i]

    def assemble(second):
        def step(i):
            at = i + (PAIRS if second else 0)
            theirs = cat(other[at], halo_tiles(near_rows[i], far_rows[i])[second])
            mine = own[at]
            step0, step1 = jnp.where(first, mine, theirs), jnp.where(first, theirs, mine)
            moved = swapped(step0)
            it[at] = jnp.where(low, step0, swapped(step1))
            source[at] = jnp.where(low, moved, step1 + moved)

        return step

    if upper:
        blocks(READY - PAIRS, PAIRS, 8, assemble(1))
    else:
        blocks(0, PAIRS, 9, assemble(0))
        blocks(0, READY - PAIRS, 4, assemble(1))

    def over(lo, count, width, read, step):
        def body(i, carry):
            start = lo + i * width
            around = [read(start - 1), read(start)]
            before = wx[start - 1]
            for u in range(width):
                at = start + u
                around = [*around[-2:], read(at + 1)]
                side = wx[at]
                step(at, around[1], near(around, (before, side, wy[at], wyp[at], wl[at])))
                before = side
            return carry

        lax.fori_loop(0, count // width, body, 0)

    def residual(at, mid, around):
        left = (woven(source, at) - ((1.0 + total[at]) * mid - around)) * gamma
        moved = swapped(left)
        value = jnp.where(low, left + moved, moved - left)
        spec[at] = value
        x[0, at] = value * inv[at]

    over(*RESIDUAL[upper], lambda at: woven(it, at), residual)
    lo, shift, places, width = SWEEP[upper]

    def sweep(j, carry):
        def step(at, mid, around):
            x[j + 1, at] = (spec[at] + around) * inv[at]

        over(lo + shift * j, places, width, lambda at: x[j, at], step)
        return carry

    lax.fori_loop(0, SWEEPS - 1, sweep, 0)
    back = jnp.where(low, 0.5, 0.5 / beta)

    def spread(i):
        value = x[SWEEPS - 1, FIRST[upper] + i]
        moved = swapped(value)
        value = jnp.where(low, value + moved, moved - value) * back
        for j in range(3):
            natural[pl.ds(i * rows + j, TILE, stride=3), :] = value[j * TILE : (j + 1) * TILE]

    blocks(0, COUNT, 8, spread)
    for q in range(4):
        turned = cat(*[natural[pl.ds(q + 4 * j, COUNT, stride=rows), :] for j in range(4)]).T
        step0, step1 = turned[:LEVELS], turned[LEVELS:]
        w_own[q] = jnp.where(first, step0, step1)
        w_send[q] = jnp.where(first, step1, step0)
    if not upper:
        for i, (ref, *at) in enumerate(shared):
            edge[i] = ref[tuple(at)]


def placed(value, j, quarter):
    return pltpu.roll(value, (32 * (quarter - j) + 128) & 127, 1)


def finish_most(it, own_low, own_high, got_low, most):
    t = lax.axis_index("tm")
    group = ids(LEVELS, 1) // 32

    def step(q):
        for j in range(4):
            rows = pl.ds(q + 4 * j, LEVELS, stride=ROWS)
            value = it[rows, :]
            for piece, quarter in ((own_low, 2 * t), (own_high, 2 * t + 1), (got_low, 2 - 2 * t)):
                value = jnp.where(group == quarter, value + placed(piece[q], j, quarter), value)
            most[rows, :] = value

    blocks(0, 4, 2, step)


def finish(most, got_high, out_hbm, out, sems):
    quarter = 3 - 2 * lax.axis_index("tm")
    part = LEVELS // CHUNKS
    here = ids(part, 1) // 32 == quarter

    def copy(c):
        span = pl.ds(pl.multiple_of(c * part * ROWS, part * ROWS), part * ROWS)
        return pltpu.make_async_copy(out.at[span], out_hbm.at[span], sems.at[c])

    def step(c):
        for q in range(4):
            value = got_high[q, pl.ds(pl.multiple_of(c * part, part), part), :]
            for j in range(4):
                rows = pl.ds(c * part * ROWS + q + 4 * j, part, stride=ROWS)
                old = most[rows, :]
                out[rows, :] = jnp.where(here, old + placed(value, j, quarter), old)
        copy(c).start()

    blocks(0, CHUNKS, 1, step)
    for c in range(CHUNKS):
        copy(c).wait()


def two_steps(iterate, heating, initial, region, cond_table):
    lats, lons = lax.axis_size("lat"), lax.axis_size("lon")
    swap = [(0, 1), (1, 0)]
    pairs = [[(i, i + 1) for i in range(start, lats - 1, 2)] for start in (0, 1)]
    pairs = [p + [(j, i) for i, j in p] for p in pairs]
    round_lon = [[(i, (i + 1) % lons) for i in range(start, lons, 2)] for start in (0, 1)]
    round_lon = [p + [(j, i) for i, j in p] for p in round_lon]
    flat = (LEVELS * ROWS, LONS)
    turned_flat = (LONS * ROWS, 2 * LEVELS)
    by_lon = (LONS, ROWS, 2 * LEVELS)
    wide = shape(PLACES, ROWS + TILE, 128)

    def in_hbm(x):
        return pltpu.with_memory_space_constraint(x, pltpu.HBM)

    xm, turned, it = call(
        send_first,
        [shape(SENT * ROWS, 128), shape(*turned_flat), shape(*flat)],
        [in_hbm(iterate[0]), in_hbm(heating[0])],
        scratch=[buffer(*flat), pltpu.SemaphoreType.DMA((ROWS // TILE, 2, 2))],
        hbm_ins=(0, 1),
    )
    xm = lax.ppermute(xm, "tm", swap)
    sides = shape(HALO + 2, ROWS, 128)
    fixed, near_sides, far_sides = call(
        send_sides,
        [shape(*turned_flat), sides, sides],
        [turned, region.reshape(flat), initial.reshape(flat), in_hbm(cond_table)],
        scratch=[pltpu.SMEM(cond_table.shape, jnp.float32), pltpu.SemaphoreType.DMA],
        hbm_ins=(3,),
    )
    near_sides = lax.ppermute(near_sides, "lon", round_lon[0])
    far_sides = lax.ppermute(far_sides, "lon", round_lon[1])
    main = shape(PLACES, ROWS, 128)
    lat = shape(PAIRS + QUADS, TILE, 128)
    rows = shape(PAIRS, TILE, 128)
    own_main, own_fixed, near_lat, far_lat, xs = call(
        add_sides,
        [main, main, lat, lat, shape(HALO, ROWS, 128)],
        [turned.reshape(by_lon), fixed.reshape(by_lon), near_sides, far_sides],
    )
    near_lat = lax.ppermute(near_lat, "lat", pairs[0])
    far_lat = lax.ppermute(far_lat, "lat", pairs[1])
    xs = lax.ppermute(xs, "tm", swap)
    other, near_rows, far_rows = call(gather, [main, rows, rows], [xm.reshape(SENT, ROWS, 128), xs, own_fixed])
    near_rows = lax.ppermute(near_rows, "lat", pairs[0])
    far_rows = lax.ppermute(far_rows, "lat", pairs[1])
    *ready, own = call(
        prepare,
        [wide] * 7,
        [own_main, own_fixed, near_lat, far_lat, other],
        scratch=[buffer(PLACES + 1, ROWS + TILE, 128)],
    )
    given = [*ready, own, other, near_rows, far_rows]
    corrections = [shape(4, LEVELS, 128)] * 2
    fields = [buffer(PLACES, ROWS + TILE, 128)] * 3 + [buffer(SWEEPS, PLACES, ROWS + TILE, 128), buffer(COUNT * (ROWS + TILE), 128)]
    own_low, send_low, edge = call(
        functools.partial(iterate_half, 0),
        [*corrections, shape(EDGE, ROWS + TILE, 128)],
        given,
        scratch=fields,
        limit=16,
    )
    got_low = lax.ppermute(send_low, "tm", swap)
    own_high, send_high = call(
        functools.partial(iterate_half, 1), corrections, [*given, edge], scratch=fields, limit=16
    )
    got_high = lax.ppermute(send_high, "tm", swap)
    (most,) = call(finish_most, [shape(*flat)], [it, own_low, own_high, got_low])
    (out,) = call(
        finish,
        [shape(*flat)],
        [most, got_high],
        scratch=[buffer(*flat), pltpu.SemaphoreType.DMA((CHUNKS,))],
        hbm_outs=(0,),
    )
    return out.reshape(iterate.shape)


def solution(mesh):
    return jax.shard_map(
        two_steps if mesh.shape["tm"] == 2 else on_device,
        mesh=mesh,
        in_specs=(
            P("tm", None, "lat", "lon"),
            P("tm", None, "lat", "lon"),
            P(None, "lat", "lon"),
            P(None, "lat", "lon"),
            P(),
        ),
        out_specs=P("tm", None, "lat", "lon"),
        check_vma=False,
    )
```

```python
import functools

import jax
import jax.numpy as jnp
from jax import lax
from jax.experimental import pallas as pl
from jax.experimental.pallas import tpu as pltpu
from jax.sharding import PartitionSpec as P

SWEEPS = 4


corner_weight = 0.1


def padded(value, sides, width, wrap):
    for axis, dim in sides:
        peers, length = (lax.axis_size(axis), value.shape[dim])
        up = [(i, (i + 1) % peers) for i in range(peers if wrap else peers - 1)]
        down = [(j, i) for i, j in up]
        last = lax.slice_in_dim(value, length - width, length, axis=dim)
        initial = lax.slice_in_dim(value, 0, width, axis=dim)
        before = lax.ppermute(last, axis, up)
        after = lax.ppermute(initial, axis, down)
        value = jnp.concatenate([before, value, after], axis=dim)
    return value


def passed_along(block, axis, distance):
    devices = range(lax.axis_size(axis))
    route = [(i - distance, i) for i in devices if i - distance in devices]
    return lax.ppermute(block, axis, route)


def harmonic(first, second):
    return 2.0 * first * second / (first + second)


def conductivity(region, cond_table):
    classes = jnp.arange(cond_table.shape[0], dtype=jnp.int32)
    onehot = (region[..., None] == classes).astype(jnp.float32)
    return jnp.sum(onehot * cond_table, axis=-1)


def extend(stack):
    lat_ext = padded(stack, (("lat", 2),), 1, False)
    both = padded(lat_ext, (("lon", 3),), 1, True)
    return jnp.pad(both, ((0, 0), (1, 1), (0, 0), (0, 0)))


def face_weights(kext):
    centre = kext[1:-1, 1:-1, 1:-1]
    return (
        harmonic(centre, kext[:-2, 1:-1, 1:-1]),
        harmonic(centre, kext[2:, 1:-1, 1:-1]),
        harmonic(centre, kext[1:-1, :-2, 1:-1]),
        harmonic(centre, kext[1:-1, 2:, 1:-1]),
        harmonic(centre, kext[1:-1, 1:-1, :-2]),
        harmonic(centre, kext[1:-1, 1:-1, 2:]),
    )


def neighbours(weights, ext):
    near = weights[0] * ext[..., :-2, 1:-1, 1:-1] + weights[1] * ext[..., 2:, 1:-1, 1:-1]
    near = near + weights[2] * ext[..., 1:-1, :-2, 1:-1] + weights[3] * ext[..., 1:-1, 2:, 1:-1]
    near = near + weights[4] * ext[..., 1:-1, 1:-1, :-2] + weights[5] * ext[..., 1:-1, 1:-1, 2:]
    return near


def on_device(iterate, heating, initial, region, cond_table):
    steps = lax.axis_size("tm")
    own = lax.axis_index("tm")
    high = lax.Precision.HIGHEST
    kfield = conductivity(region, cond_table)
    ext = extend(jnp.stack([kfield, iterate[0]]))
    weights = face_weights(ext[0])
    total = weights[0] + weights[1] + weights[2] + weights[3] + weights[4] + weights[5]
    shifted = passed_along(iterate, "tm", 1)[0]
    previous = jnp.where(own == 0, initial, shifted)
    residual = heating[0] + previous - ((1.0 + total) * iterate[0] - neighbours(weights, ext[1]))
    scale_own = corner_weight ** (own.astype(jnp.float32) / steps)
    scaled = residual * scale_own
    zeros = jnp.zeros_like(residual)
    piece = lax.all_gather(scaled[None], "tm", axis=0, tiled=True)
    order = jnp.arange(piece.shape[0], dtype=jnp.int32)
    angle = 2.0 * jnp.pi / steps * (own * order % steps).astype(jnp.float32)
    real_part = jnp.einsum("n,nabc->abc", jnp.cos(angle), piece, precision=high)
    imag_part = (zeros, zeros)[1] - jnp.einsum("n,nabc->abc", jnp.sin(angle), piece, precision=high)
    beta = corner_weight ** (1.0 / steps)
    freq_angle = 2.0 * jnp.pi / steps * (own % steps).astype(jnp.float32)
    diag_re = 1.0 - beta * jnp.cos(freq_angle) + total
    diag_im = beta * jnp.sin(freq_angle) + zeros
    denom = diag_re * diag_re + diag_im * diag_im
    inv_re = diag_re / denom
    inv_im = -diag_im / denom
    sol_re = real_part * inv_re - imag_part * inv_im
    sol_im = real_part * inv_im + imag_part * inv_re
    for sweep in range(SWEEPS - 1):
        near = neighbours(weights, extend(jnp.stack([sol_re, sol_im])))
        rhs_re = real_part + near[0]
        rhs_im = imag_part + near[1]
        sol_re = rhs_re * inv_re - rhs_im * inv_im
        sol_im = rhs_re * inv_im + rhs_im * inv_re
    pieces = (
        lax.all_gather(sol_re[None], "tm", axis=0, tiled=True),
        lax.all_gather(sol_im[None], "tm", axis=0, tiled=True),
    )
    order = jnp.arange(pieces[0].shape[0], dtype=jnp.int32)
    angle = 2.0 * jnp.pi / steps * (order * own % steps).astype(jnp.float32)
    summed = jnp.einsum("k,kabc->abc", jnp.cos(angle), pieces[0], precision=high) - jnp.einsum(
        "k,kabc->abc", jnp.sin(angle), pieces[1], precision=high
    )
    back = summed / steps
    return iterate + (back / scale_own)[None]


HALO = 4
TILE = 8
LEVELS = 64
ROWS = 16
LONS = 128
HALF = 64
SENT = HALF + HALO
PLACES = HALF + 2 * HALO
PAIRS = PLACES // 2
SENT_PAIRS = SENT // 2
QUADS = PLACES // 4
CHUNKS = 4


def specs(count, hbm):
    return [pl.BlockSpec(memory_space=pltpu.HBM if i in hbm else pltpu.VMEM) for i in range(count)]


def call(body, outs, ins, scratch=(), limit=8, hbm_ins=(), hbm_outs=()):
    moved = sum(x.size * 4 for x in ins) + sum(x.size * 4 for x in outs)
    return pl.pallas_call(
        body,
        out_shape=outs,
        in_specs=specs(len(ins), hbm_ins),
        out_specs=specs(len(outs), hbm_outs),
        scratch_shapes=scratch,
        compiler_params=pltpu.CompilerParams(vmem_limit_bytes=limit << 20),
        cost_estimate=pl.CostEstimate(flops=moved * 4, bytes_accessed=moved, transcendentals=0),
    )(*ins)


def shape(*dims):
    return jax.ShapeDtypeStruct(dims, jnp.float32)


def buffer(*dims):
    return pltpu.VMEM(dims, jnp.float32)


def ids(rows, dim):
    return lax.broadcasted_iota(jnp.int32, (rows, 128), dim)


def in_low(rows):
    return ids(rows, 1) < LEVELS


def swapped(x):
    return pltpu.roll(x, LEVELS, 1)


def cat(*values):
    return jnp.concatenate(values, axis=0)


def even(axis):
    return lax.rem(lax.axis_index(axis), 2) == 0


def blocks(lo, hi, width, step):
    def body(i, carry):
        for u in range(width):
            step(lo + i * width + u)
        return carry

    lax.fori_loop(0, (hi - lo) // width, body, 0)


def send_first(it_hbm, h_hbm, edges, middle, turned, it, h, sems):
    t = lax.axis_index("tm")
    by_level = (LEVELS, ROWS, LONS)
    copies = []
    for k in range(ROWS // TILE):
        for f, (source, target) in enumerate(((it_hbm, it), (h_hbm, h))):
            for c in range(2):
                part = pl.ds(c * LEVELS // 2, LEVELS // 2), pl.ds(k * TILE, TILE)
                copy = pltpu.make_async_copy(source.at[part], target.reshape(by_level).at[part], sems.at[k, f, c])
                copy.start()
                copies.append(copy)

    def turn(r):
        rows = pl.ds(r, LEVELS, stride=ROWS)
        turned[pl.ds(r, LONS, stride=ROWS), :] = cat(it[rows, :], h[rows, :]).T

    for k in range(ROWS // TILE):
        for copy in copies[4 * k : 4 * k + 4]:
            copy.wait()
        blocks(k * TILE, (k + 1) * TILE, 4, turn)
    start = (LONS - SENT) * ROWS * (1 - t)
    top = ids(TILE, 0) < HALO

    def cut(i):
        at = pl.multiple_of(start + i * ROWS, ROWS)
        low, high = turned[pl.ds(at, TILE), :], turned[pl.ds(at + TILE, TILE), :]
        edges[i] = jnp.where(top, low, high)
        middle[i] = jnp.where(top, high, low)

    blocks(0, SENT, 17, cut)


def heated(turned, fixed):
    add = jnp.logical_and(jnp.logical_not(in_low(ROWS)), lax.axis_index("tm") == 0)
    return turned + jnp.where(add, fixed, 0.0)


def send_sides(turned, region, initial, table_hbm, fixed, near_sides, far_sides, table, sem):
    copy = pltpu.make_async_copy(table_hbm, table, sem)
    copy.start()
    copy.wait()

    def turn(r):
        rows = pl.ds(r, LEVELS, stride=ROWS)
        classes = region[rows, :]
        value = jnp.full(classes.shape, table[0], jnp.float32)
        for c in range(1, table.shape[0]):
            value = jnp.where(classes == c, table[c], value)
        fixed[pl.ds(r, LONS, stride=ROWS), :] = cat(value, initial[rows, :]).T

    blocks(0, ROWS, 4, turn)
    near_right = even("lon")
    low = in_low(ROWS)

    def strip(first_lon):
        def at(ref, i):
            return ref[(first_lon + i) * ROWS : (first_lon + i + 1) * ROWS, :]

        return [heated(at(turned, i), at(fixed, i)) for i in range(HALO)] + [
            jnp.where(low, at(fixed, i), swapped(at(fixed, i + 2))) for i in range(2)
        ]

    for i, (right, left) in enumerate(zip(strip(LONS - HALO), strip(0))):
        near_sides[i] = jnp.where(near_right, right, left)
        far_sides[i] = jnp.where(near_right, left, right)


def edge_pair(first, second):
    top = ids(TILE, 0) < HALO
    first_up = even("lat")
    down = jnp.where(top, first[:TILE], pltpu.roll(second[:TILE], HALO, 0))
    up = jnp.where(top, pltpu.roll(first[-TILE:], HALO, 0), second[-TILE:])
    return jnp.where(first_up, up, down), jnp.where(first_up, down, up)


def halo_tiles(near_pair, far_pair):
    first_up = even("lat")
    after = jnp.where(first_up, near_pair, far_pair)
    before = jnp.where(first_up, far_pair, near_pair)
    top = ids(TILE, 0) < HALO
    return (
        jnp.where(top, after, pltpu.roll(before, HALO, 0)),
        jnp.where(top, pltpu.roll(after, HALO, 0), before),
    )


def add_sides(turned, fixed, near_sides, far_sides, own, own_fixed, near_lat, far_lat, partner):
    t = lax.axis_index("tm")
    from_near = (t == 0) != even("lon")
    count = near_sides.shape[0]
    beside = [jnp.where(from_near, near_sides[i], far_sides[i]) for i in range(count)]
    other = [jnp.where(from_near, far_sides[i], near_sides[i]) for i in range(HALO)]
    for i in range(HALO):
        own[SENT * t + i] = beside[i]
        partner[i] = other[i]
    for i in range(2):
        own_fixed[SENT * t + i] = beside[HALO + i]
        own_fixed[SENT * t + i + 2] = swapped(beside[HALO + i])
        at = PAIRS + QUADS + i
        near_lat[at], far_lat[at] = edge_pair(other[i], other[i + 2])

    def copy(i):
        at = HALO * (1 - t) + i
        lon = (LONS - SENT) * t + i
        own[at] = heated(turned[lon], fixed[lon])
        own_fixed[at] = fixed[lon]

    blocks(0, SENT, 17, copy)

    def rows(i):
        near_lat[i], far_lat[i] = edge_pair(own[i], own[i + PAIRS])

    blocks(0, PAIRS, 12, rows)
    low = in_low(TILE)

    def fixed_rows(i):
        here = edge_pair(own_fixed[i], own_fixed[i + PAIRS])
        there = edge_pair(own_fixed[i + QUADS], own_fixed[i + PAIRS + QUADS])
        near_lat[PAIRS + i], far_lat[PAIRS + i] = [jnp.where(low, a, swapped(b)) for a, b in zip(here, there)]

    blocks(0, QUADS, 9, fixed_rows)


def start_of_step(fixed, rows):
    add = jnp.logical_and(jnp.logical_not(in_low(rows)), lax.axis_index("tm") == 1)
    return jnp.where(add, fixed, 0.0)


def pass_rows(edges, own_fixed, heated_edges, near_rows, far_rows):
    base = HALO * (1 - lax.axis_index("tm"))
    top = ids(TILE, 0) < HALO

    def heat(i):
        fixed = own_fixed[base + i]
        heated_edges[i] = edges[i] + start_of_step(jnp.where(top, fixed[:TILE], fixed[TILE:]), TILE)

    blocks(0, SENT, 17, heat)

    def rows(i):
        near_rows[i], far_rows[i] = edge_pair(heated_edges[i], heated_edges[i + SENT_PAIRS])

    blocks(0, SENT_PAIRS, 17, rows)


def gather(edges, middle, own_fixed, _, other):
    base = HALO * (1 - lax.axis_index("tm"))
    top = ids(TILE, 0) < HALO

    def join(i):
        fixed = own_fixed[base + i]
        e = edges[i]
        m = middle[i] + start_of_step(jnp.where(top, fixed[TILE:], fixed[:TILE]), TILE)
        other[i] = cat(jnp.where(top, e, m), jnp.where(top, m, e))

    blocks(0, SENT, 17, join)


def strips(partner, near_lat, far_lat, xs):
    for i in range(2):
        at = PAIRS + QUADS + i
        for place, tile in zip((i, i + 2), halo_tiles(near_lat[at], far_lat[at])):
            xs[place] = cat(partner[place], tile)


def reciprocal(d):
    y = pl.reciprocal(d, approx=True)
    return y * (2.0 - d * y)


def face(a, b):
    return 2.0 * a * b * reciprocal(jnp.maximum(a + b, 1e-30))


def woven(ref, at):
    return cat(*[ref[at, pl.ds(j, TILE, stride=3), :] for j in range(3)])


def next_row(x):
    return cat(x[TILE:], pltpu.roll(x[:TILE], TILE - 1, 0))


def last_row(x):
    return cat(pltpu.roll(x[-TILE:], 1, 0), x[:-TILE])


def near(around, w):
    before, mid, after = around
    wxp, wx, wy, wyp, wl = w
    total = wxp * before + wx * after
    total = total + (wy * next_row(mid) + wyp * last_row(mid))
    return total + (wl * pltpu.roll(mid, 127, 1) + pltpu.roll(wl * mid, 1, 1))


def prepare(own_main, own_fixed, near_lat, far_lat, _, wx, wy, wyp, wl, total, inv, own, K):
    rows = ROWS + TILE
    low = in_low(ROWS)
    low_tile = in_low(TILE)
    beta = corner_weight ** 0.5
    K[PLACES] = jnp.zeros((rows, 128), jnp.float32)

    def assemble(i):
        for at, tile in zip((i, i + PAIRS), halo_tiles(near_lat[i], far_lat[i])):
            own[at] = cat(own_main[at], tile)

    blocks(0, PAIRS, 12, assemble)

    def assemble_fixed(i):
        for at, tile in zip((i, i + PAIRS), halo_tiles(near_lat[PAIRS + i], far_lat[PAIRS + i])):
            moved = swapped(tile)
            for here, value in ((at, jnp.where(low_tile, tile, moved)), (at + QUADS, jnp.where(low_tile, moved, tile))):
                main = own_fixed[here]
                K[here] = cat(jnp.where(low, main, swapped(main)), value)

    blocks(0, QUADS, 9, assemble_fixed)
    lane = ids(rows, 1)
    inside = (lane & (LEVELS - 1)) != LEVELS - 1
    shift = jnp.where(lane < LEVELS, 1.0 - beta, 1.0 + beta)
    width = 18

    def weigh(i, carry):
        start = i * width
        here = woven(K, start)
        before = wx[jnp.maximum(start - 1, 0)]
        for u in range(width):
            at = start + u
            after = woven(K, at + 1)
            side = face(here, after)
            row = face(here, next_row(here))
            previous = last_row(row)
            level = jnp.where(inside, face(here, pltpu.roll(here, 127, 1)), 0.0)
            sums = (before + side) + (row + previous) + (level + pltpu.roll(level, 1, 1))
            wx[at], wy[at], wyp[at], wl[at] = side, row, previous, level
            total[at] = sums
            inv[at] = reciprocal(shift + sums)
            here, before = after, side
        return carry

    wx[0] = jnp.zeros((rows, 128), jnp.float32)
    lax.fori_loop(0, PLACES // width, weigh, 0)


STAGES = ((1, 39, 71), (2, 38, 70), (3, 37, 69), (4, 36, 68))
WIDTHS = ((19, 12, 17, 16), (16, 16, 16, 16))
READY = 40
EDGE = 12


def iterate_half(upper, wx, wy, wyp, wl, total, inv, own, other, near_rows, far_rows, xs, *refs):
    if upper:
        edge, w_own, w_send, *refs = refs
    else:
        w_own, w_send, edge, *refs = refs
    it, source, spec, x, y, z, natural = refs
    rows = ROWS + TILE
    first = lax.axis_index("tm") == 0
    low = in_low(rows)
    beta = corner_weight ** 0.5
    gamma = jnp.where(low, 1.0, beta)
    shared = [(it, 38), (it, 39), (source, 39), (x, 37), (x, 38), (y, 36), (y, 37), (z, 35), (z, 36)]
    shared += [(spec, 36), (spec, 37), (spec, 38)]
    if upper:
        for i, (ref, at) in enumerate(shared):
            ref[at] = edge[i]

    t = lax.axis_index("tm")

    def enter(at, theirs):
        mine = own[at]
        step0, step1 = jnp.where(first, mine, theirs), jnp.where(first, theirs, mine)
        moved = swapped(step0)
        it[at] = jnp.where(low, step0, swapped(step1))
        source[at] = jnp.where(low, moved, step1 + moved)

    def assemble(second):
        def step(i):
            main = i + (SENT_PAIRS if second else 0)
            tile = halo_tiles(near_rows[i], far_rows[i])[second]
            enter(HALO * (1 - t) + main, cat(other[main], tile))

        return step

    if upper:
        blocks(READY - HALO - SENT_PAIRS, SENT_PAIRS, 8, assemble(1))
    else:
        blocks(0, SENT_PAIRS, 17, assemble(0))
        blocks(0, READY - SENT_PAIRS, 6, assemble(1))
    for i in range(HALO):
        enter(SENT * t + i, xs[i])

    def over(stage, read, ref, step):
        lo, hi = STAGES[stage][upper : upper + 2]
        width = WIDTHS[upper][stage]

        def body(i, carry):
            start = lo + i * width
            around = [read(ref, start - 1), read(ref, start)]
            before = wx[start - 1]
            for u in range(width):
                at = start + u
                around = [*around[-2:], read(ref, at + 1)]
                side = wx[at]
                step(at, around, (before, side, wy[at], wyp[at], wl[at]))
                before = side
            return carry

        lax.fori_loop(0, (hi - lo) // width, body, 0)

    def residual(at, around, w):
        left = (woven(source, at) - ((1.0 + total[at]) * around[1] - near(around, w))) * gamma
        moved = swapped(left)
        value = jnp.where(low, left + moved, moved - left)
        spec[at] = value
        x[at] = value * inv[at]

    over(0, woven, it, residual)

    def plain(ref, at):
        return ref[at]

    def sweep(at, around, w):
        return (spec[at] + near(around, w)) * inv[at]

    def to(ref):
        def step(at, around, w):
            ref[at] = sweep(at, around, w)

        return step

    over(1, plain, x, to(y))
    over(2, plain, y, to(z))
    base = STAGES[3][upper]
    back = jnp.where(low, 0.5, 0.5 / beta)

    def last(at, around, w):
        value = sweep(at, around, w)
        moved = swapped(value)
        value = jnp.where(low, value + moved, moved - value) * back
        for j in range(3):
            natural[pl.ds((at - base) * rows + j, TILE, stride=3), :] = value[j * TILE : (j + 1) * TILE]

    over(3, plain, z, last)
    count = HALF // 2
    for q in range(4):
        turned = cat(*[natural[pl.ds(q + 4 * j, count, stride=rows), :] for j in range(4)]).T
        step0, step1 = turned[:LEVELS], turned[LEVELS:]
        w_own[q] = jnp.where(first, step0, step1)
        w_send[q] = jnp.where(first, step1, step0)
    if not upper:
        for i, (ref, at) in enumerate(shared):
            edge[i] = ref[at]


def placed(value, j, quarter):
    return pltpu.roll(value, (32 * (quarter - j) + 128) & 127, 1)


def finish_most(it, own_low, own_high, got_low, most):
    t = lax.axis_index("tm")
    group = ids(LEVELS, 1) // 32

    def step(q):
        for j in range(4):
            rows = pl.ds(q + 4 * j, LEVELS, stride=ROWS)
            value = it[rows, :]
            for piece, quarter in ((own_low, 2 * t), (own_high, 2 * t + 1), (got_low, 2 - 2 * t)):
                value = jnp.where(group == quarter, value + placed(piece[q], j, quarter), value)
            most[rows, :] = value

    blocks(0, 4, 2, step)


def finish(most, got_high, out_hbm, out, sems):
    quarter = 3 - 2 * lax.axis_index("tm")
    part = LEVELS // CHUNKS
    here = ids(part, 1) // 32 == quarter

    def copy(c):
        span = pl.ds(pl.multiple_of(c * part * ROWS, part * ROWS), part * ROWS)
        return pltpu.make_async_copy(out.at[span], out_hbm.at[span], sems.at[c])

    def step(c):
        for q in range(4):
            value = got_high[q, pl.ds(pl.multiple_of(c * part, part), part), :]
            for j in range(4):
                rows = pl.ds(c * part * ROWS + q + 4 * j, part, stride=ROWS)
                old = most[rows, :]
                out[rows, :] = jnp.where(here, old + placed(value, j, quarter), old)
        copy(c).start()

    blocks(0, CHUNKS, 1, step)
    for c in range(CHUNKS):
        copy(c).wait()


def two_steps(iterate, heating, initial, region, cond_table):
    lats, lons = lax.axis_size("lat"), lax.axis_size("lon")
    swap = [(0, 1), (1, 0)]
    pairs = [[(i, i + 1) for i in range(start, lats - 1, 2)] for start in (0, 1)]
    pairs = [p + [(j, i) for i, j in p] for p in pairs]
    round_lon = [[(i, (i + 1) % lons) for i in range(start, lons, 2)] for start in (0, 1)]
    round_lon = [p + [(j, i) for i, j in p] for p in round_lon]
    flat = (LEVELS * ROWS, LONS)
    turned_flat = (LONS * ROWS, 2 * LEVELS)
    by_lon = (LONS, ROWS, 2 * LEVELS)
    wide = shape(PLACES, ROWS + TILE, 128)

    def in_hbm(x):
        return pltpu.with_memory_space_constraint(x, pltpu.HBM)

    half_rows = shape(SENT, TILE, 128)
    edges, middle, turned, it = call(
        send_first,
        [half_rows, half_rows, shape(*turned_flat), shape(*flat)],
        [in_hbm(iterate[0]), in_hbm(heating[0])],
        scratch=[buffer(*flat), pltpu.SemaphoreType.DMA((ROWS // TILE, 2, 2))],
        hbm_ins=(0, 1),
    )
    edges = lax.ppermute(edges, "tm", swap)
    middle = lax.ppermute(middle, "tm", swap)
    sides = shape(HALO + 2, ROWS, 128)
    fixed, near_sides, far_sides = call(
        send_sides,
        [shape(*turned_flat), sides, sides],
        [turned, region.reshape(flat), initial.reshape(flat), in_hbm(cond_table)],
        scratch=[pltpu.SMEM(cond_table.shape, jnp.float32), pltpu.SemaphoreType.DMA],
        hbm_ins=(3,),
    )
    near_sides = lax.ppermute(near_sides, "lon", round_lon[0])
    far_sides = lax.ppermute(far_sides, "lon", round_lon[1])
    main = shape(PLACES, ROWS, 128)
    lat = shape(PAIRS + QUADS + 2, TILE, 128)
    own_main, own_fixed, near_lat, far_lat, partner = call(
        add_sides,
        [main, main, lat, lat, shape(HALO, ROWS, 128)],
        [turned.reshape(by_lon), fixed.reshape(by_lon), near_sides, far_sides],
    )
    near_lat = lax.ppermute(near_lat, "lat", pairs[0])
    far_lat = lax.ppermute(far_lat, "lat", pairs[1])
    rows = shape(SENT_PAIRS, TILE, 128)
    edges, near_rows, far_rows = call(pass_rows, [half_rows, rows, rows], [edges, own_fixed])
    near_rows = lax.ppermute(near_rows, "lat", pairs[0])
    far_rows = lax.ppermute(far_rows, "lat", pairs[1])
    (xs,) = call(strips, [shape(HALO, ROWS + TILE, 128)], [partner, near_lat, far_lat])
    xs = lax.ppermute(xs, "tm", swap)
    *ready, own = call(
        prepare,
        [wide] * 7,
        [own_main, own_fixed, near_lat, far_lat, edges],
        scratch=[buffer(PLACES + 1, ROWS + TILE, 128)],
    )
    (other,) = call(gather, [shape(SENT, ROWS, 128)], [edges, middle, own_fixed, own])
    given = [*ready, own, other, near_rows, far_rows, xs]
    corrections = [shape(4, LEVELS, 128)] * 2
    fields = [buffer(PLACES, ROWS + TILE, 128)] * 6 + [buffer(HALF // 2 * (ROWS + TILE), 128)]
    own_low, send_low, edge = call(
        functools.partial(iterate_half, 0),
        [*corrections, shape(EDGE, ROWS + TILE, 128)],
        given,
        scratch=fields,
        limit=16,
    )
    got_low = lax.ppermute(send_low, "tm", swap)
    own_high, send_high = call(
        functools.partial(iterate_half, 1), corrections, [*given, edge], scratch=fields, limit=16
    )
    got_high = lax.ppermute(send_high, "tm", swap)
    (most,) = call(finish_most, [shape(*flat)], [it, own_low, own_high, got_low])
    (out,) = call(
        finish,
        [shape(*flat)],
        [most, got_high],
        scratch=[buffer(*flat), pltpu.SemaphoreType.DMA((CHUNKS,))],
        hbm_outs=(0,),
    )
    return out.reshape(iterate.shape)


def solution(mesh):
    return jax.shard_map(
        two_steps if mesh.shape["tm"] == 2 else on_device,
        mesh=mesh,
        in_specs=(
            P("tm", None, "lat", "lon"),
            P("tm", None, "lat", "lon"),
            P(None, "lat", "lon"),
            P(None, "lat", "lon"),
            P(),
        ),
        out_specs=P("tm", None, "lat", "lon"),
        check_vma=False,
    )
```

```python
import functools

import jax
import jax.numpy as jnp
from jax import lax
from jax.experimental import pallas as pl
from jax.experimental.pallas import tpu as pltpu
from jax.sharding import PartitionSpec as P

SWEEPS = 4


corner_weight = 0.1


def padded(value, sides, width, wrap):
    for axis, dim in sides:
        peers, length = (lax.axis_size(axis), value.shape[dim])
        up = [(i, (i + 1) % peers) for i in range(peers if wrap else peers - 1)]
        down = [(j, i) for i, j in up]
        last = lax.slice_in_dim(value, length - width, length, axis=dim)
        initial = lax.slice_in_dim(value, 0, width, axis=dim)
        before = lax.ppermute(last, axis, up)
        after = lax.ppermute(initial, axis, down)
        value = jnp.concatenate([before, value, after], axis=dim)
    return value


def passed_along(block, axis, distance):
    devices = range(lax.axis_size(axis))
    route = [(i - distance, i) for i in devices if i - distance in devices]
    return lax.ppermute(block, axis, route)


def harmonic(first, second):
    return 2.0 * first * second / (first + second)


def conductivity(region, cond_table):
    classes = jnp.arange(cond_table.shape[0], dtype=jnp.int32)
    onehot = (region[..., None] == classes).astype(jnp.float32)
    return jnp.sum(onehot * cond_table, axis=-1)


def extend(stack):
    lat_ext = padded(stack, (("lat", 2),), 1, False)
    both = padded(lat_ext, (("lon", 3),), 1, True)
    return jnp.pad(both, ((0, 0), (1, 1), (0, 0), (0, 0)))


def face_weights(kext):
    centre = kext[1:-1, 1:-1, 1:-1]
    return (
        harmonic(centre, kext[:-2, 1:-1, 1:-1]),
        harmonic(centre, kext[2:, 1:-1, 1:-1]),
        harmonic(centre, kext[1:-1, :-2, 1:-1]),
        harmonic(centre, kext[1:-1, 2:, 1:-1]),
        harmonic(centre, kext[1:-1, 1:-1, :-2]),
        harmonic(centre, kext[1:-1, 1:-1, 2:]),
    )


def neighbours(weights, ext):
    near = weights[0] * ext[..., :-2, 1:-1, 1:-1] + weights[1] * ext[..., 2:, 1:-1, 1:-1]
    near = near + weights[2] * ext[..., 1:-1, :-2, 1:-1] + weights[3] * ext[..., 1:-1, 2:, 1:-1]
    near = near + weights[4] * ext[..., 1:-1, 1:-1, :-2] + weights[5] * ext[..., 1:-1, 1:-1, 2:]
    return near


def on_device(iterate, heating, initial, region, cond_table):
    steps = lax.axis_size("tm")
    own = lax.axis_index("tm")
    high = lax.Precision.HIGHEST
    kfield = conductivity(region, cond_table)
    ext = extend(jnp.stack([kfield, iterate[0]]))
    weights = face_weights(ext[0])
    total = weights[0] + weights[1] + weights[2] + weights[3] + weights[4] + weights[5]
    shifted = passed_along(iterate, "tm", 1)[0]
    previous = jnp.where(own == 0, initial, shifted)
    residual = heating[0] + previous - ((1.0 + total) * iterate[0] - neighbours(weights, ext[1]))
    scale_own = corner_weight ** (own.astype(jnp.float32) / steps)
    scaled = residual * scale_own
    zeros = jnp.zeros_like(residual)
    piece = lax.all_gather(scaled[None], "tm", axis=0, tiled=True)
    order = jnp.arange(piece.shape[0], dtype=jnp.int32)
    angle = 2.0 * jnp.pi / steps * (own * order % steps).astype(jnp.float32)
    real_part = jnp.einsum("n,nabc->abc", jnp.cos(angle), piece, precision=high)
    imag_part = (zeros, zeros)[1] - jnp.einsum("n,nabc->abc", jnp.sin(angle), piece, precision=high)
    beta = corner_weight ** (1.0 / steps)
    freq_angle = 2.0 * jnp.pi / steps * (own % steps).astype(jnp.float32)
    diag_re = 1.0 - beta * jnp.cos(freq_angle) + total
    diag_im = beta * jnp.sin(freq_angle) + zeros
    denom = diag_re * diag_re + diag_im * diag_im
    inv_re = diag_re / denom
    inv_im = -diag_im / denom
    sol_re = real_part * inv_re - imag_part * inv_im
    sol_im = real_part * inv_im + imag_part * inv_re
    for sweep in range(SWEEPS - 1):
        near = neighbours(weights, extend(jnp.stack([sol_re, sol_im])))
        rhs_re = real_part + near[0]
        rhs_im = imag_part + near[1]
        sol_re = rhs_re * inv_re - rhs_im * inv_im
        sol_im = rhs_re * inv_im + rhs_im * inv_re
    pieces = (
        lax.all_gather(sol_re[None], "tm", axis=0, tiled=True),
        lax.all_gather(sol_im[None], "tm", axis=0, tiled=True),
    )
    order = jnp.arange(pieces[0].shape[0], dtype=jnp.int32)
    angle = 2.0 * jnp.pi / steps * (order * own % steps).astype(jnp.float32)
    summed = jnp.einsum("k,kabc->abc", jnp.cos(angle), pieces[0], precision=high) - jnp.einsum(
        "k,kabc->abc", jnp.sin(angle), pieces[1], precision=high
    )
    back = summed / steps
    return iterate + (back / scale_own)[None]


HALO = 4
TILE = 8
LEVELS = 64
ROWS = 16
LONS = 128
HALF = 64
SENT = HALF + HALO
PLACES = HALF + 2 * HALO
PAIRS = SENT // 2
QUADS = SENT // 4
CHUNKS = 4


def specs(count, hbm):
    return [pl.BlockSpec(memory_space=pltpu.HBM if i in hbm else pltpu.VMEM) for i in range(count)]


def call(body, outs, ins, scratch=(), limit=8, hbm_ins=(), hbm_outs=()):
    moved = sum(x.size * 4 for x in ins) + sum(x.size * 4 for x in outs)
    return pl.pallas_call(
        body,
        out_shape=outs,
        in_specs=specs(len(ins), hbm_ins),
        out_specs=specs(len(outs), hbm_outs),
        scratch_shapes=scratch,
        compiler_params=pltpu.CompilerParams(vmem_limit_bytes=limit << 20),
        cost_estimate=pl.CostEstimate(flops=moved * 4, bytes_accessed=moved, transcendentals=0),
    )(*ins)


def shape(*dims):
    return jax.ShapeDtypeStruct(dims, jnp.float32)


def buffer(*dims):
    return pltpu.VMEM(dims, jnp.float32)


def ids(rows, dim):
    return lax.broadcasted_iota(jnp.int32, (rows, 128), dim)


def in_low(rows):
    return ids(rows, 1) < LEVELS


def swapped(x):
    return pltpu.roll(x, LEVELS, 1)


def cat(*values):
    return jnp.concatenate(values, axis=0)


def even(axis):
    return lax.rem(lax.axis_index(axis), 2) == 0


def blocks(lo, hi, width, step):
    def body(i, carry):
        for u in range(width):
            step(lo + i * width + u)
        return carry

    lax.fori_loop(0, (hi - lo) // width, body, 0)


def send_first(it_hbm, h_hbm, edges, middle, turned, it, h, sems):
    t = lax.axis_index("tm")
    by_level = (LEVELS, ROWS, LONS)
    copies = []
    for k in range(ROWS // TILE):
        for f, (source, target) in enumerate(((it_hbm, it), (h_hbm, h))):
            for c in range(2):
                part = pl.ds(c * LEVELS // 2, LEVELS // 2), pl.ds(k * TILE, TILE)
                copy = pltpu.make_async_copy(source.at[part], target.reshape(by_level).at[part], sems.at[k, f, c])
                copy.start()
                copies.append(copy)

    def turn(r):
        rows = pl.ds(r, LEVELS, stride=ROWS)
        turned[pl.ds(r, LONS, stride=ROWS), :] = cat(it[rows, :], h[rows, :]).T

    for k in range(ROWS // TILE):
        for copy in copies[4 * k : 4 * k + 4]:
            copy.wait()
        blocks(k * TILE, (k + 1) * TILE, 4, turn)
    start = (LONS - SENT) * ROWS * (1 - t)
    top = ids(TILE, 0) < HALO

    def cut(i):
        at = pl.multiple_of(start + i * ROWS, ROWS)
        low, high = turned[pl.ds(at, TILE), :], turned[pl.ds(at + TILE, TILE), :]
        edges[i] = jnp.where(top, low, high)
        middle[i] = jnp.where(top, high, low)

    blocks(0, SENT, 17, cut)


def heated(turned, fixed):
    add = jnp.logical_and(jnp.logical_not(in_low(ROWS)), lax.axis_index("tm") == 0)
    return turned + jnp.where(add, fixed, 0.0)


def send_sides(turned, region, initial, table_hbm, fixed, near_sides, far_sides, table, sem):
    copy = pltpu.make_async_copy(table_hbm, table, sem)
    copy.start()
    copy.wait()

    def turn(r):
        rows = pl.ds(r, LEVELS, stride=ROWS)
        classes = region[rows, :]
        value = jnp.full(classes.shape, table[0], jnp.float32)
        for c in range(1, table.shape[0]):
            value = jnp.where(classes == c, table[c], value)
        fixed[pl.ds(r, LONS, stride=ROWS), :] = cat(value, initial[rows, :]).T

    blocks(0, ROWS, 4, turn)
    near_right = even("lon")
    low = in_low(ROWS)

    def strip(first_lon):
        def at(ref, i):
            return ref[(first_lon + i) * ROWS : (first_lon + i + 1) * ROWS, :]

        return [heated(at(turned, i), at(fixed, i)) for i in range(HALO)] + [
            jnp.where(low, at(fixed, i), swapped(at(fixed, i + 2))) for i in range(2)
        ]

    for i, (right, left) in enumerate(zip(strip(LONS - HALO), strip(0))):
        near_sides[i] = jnp.where(near_right, right, left)
        far_sides[i] = jnp.where(near_right, left, right)


def edge_pair(first, second):
    top = ids(TILE, 0) < HALO
    first_up = even("lat")
    down = jnp.where(top, first[:TILE], pltpu.roll(second[:TILE], HALO, 0))
    up = jnp.where(top, pltpu.roll(first[-TILE:], HALO, 0), second[-TILE:])
    return jnp.where(first_up, up, down), jnp.where(first_up, down, up)


def halo_tiles(near_pair, far_pair):
    first_up = even("lat")
    after = jnp.where(first_up, near_pair, far_pair)
    before = jnp.where(first_up, far_pair, near_pair)
    top = ids(TILE, 0) < HALO
    return (
        jnp.where(top, after, pltpu.roll(before, HALO, 0)),
        jnp.where(top, pltpu.roll(after, HALO, 0), before),
    )


def own_rows(turned, fixed, main, main_fixed, near_lat, far_lat):
    start = (LONS - SENT) * lax.axis_index("tm")

    def copy(i):
        main[i] = heated(turned[start + i], fixed[start + i])
        main_fixed[i] = fixed[start + i]

    blocks(0, SENT, 17, copy)

    def rows(i):
        near_lat[i], far_lat[i] = edge_pair(main[i], main[i + PAIRS])

    blocks(0, PAIRS, 17, rows)
    low = in_low(TILE)

    def fixed_rows(i):
        here = edge_pair(main_fixed[i], main_fixed[i + PAIRS])
        there = edge_pair(main_fixed[i + QUADS], main_fixed[i + PAIRS + QUADS])
        near_lat[PAIRS + i], far_lat[PAIRS + i] = [jnp.where(low, a, swapped(b)) for a, b in zip(here, there)]

    blocks(0, QUADS, 17, fixed_rows)


def start_of_step(fixed, rows):
    add = jnp.logical_and(jnp.logical_not(in_low(rows)), lax.axis_index("tm") == 1)
    return jnp.where(add, fixed, 0.0)


BESIDE = PAIRS
BESIDE_FIXED = PAIRS + 2
PARTNER = PAIRS + 3


def pass_rows(edges, main_fixed, near_sides, far_sides, heated_edges, near_rows, far_rows, beside, partner):
    top = ids(TILE, 0) < HALO

    def heat(i):
        fixed = main_fixed[i]
        heated_edges[i] = edges[i] + start_of_step(jnp.where(top, fixed[:TILE], fixed[TILE:]), TILE)

    blocks(0, SENT, 17, heat)

    def rows(i):
        near_rows[i], far_rows[i] = edge_pair(heated_edges[i], heated_edges[i + PAIRS])

    blocks(0, PAIRS, 17, rows)
    from_near = (lax.axis_index("tm") == 0) != even("lon")
    for i in range(HALO + 2):
        beside[i] = jnp.where(from_near, near_sides[i], far_sides[i])
    for i in range(HALO):
        partner[i] = jnp.where(from_near, far_sides[i], near_sides[i])
    for i in range(2):
        near_rows[BESIDE + i], far_rows[BESIDE + i] = edge_pair(beside[i], beside[i + 2])
        near_rows[PARTNER + i], far_rows[PARTNER + i] = edge_pair(partner[i], partner[i + 2])
    near_rows[BESIDE_FIXED], far_rows[BESIDE_FIXED] = edge_pair(beside[HALO], beside[HALO + 1])


def gather(edges, middle, main_fixed, _, other):
    top = ids(TILE, 0) < HALO

    def join(i):
        fixed = main_fixed[i]
        e = edges[i]
        m = middle[i] + start_of_step(jnp.where(top, fixed[TILE:], fixed[:TILE]), TILE)
        other[i] = cat(jnp.where(top, e, m), jnp.where(top, m, e))

    blocks(0, SENT, 17, join)


def strips(partner, near_rows, far_rows, xs):
    for i in range(2):
        at = PARTNER + i
        for place, tile in zip((i, i + 2), halo_tiles(near_rows[at], far_rows[at])):
            xs[place] = cat(partner[place], tile)


def reciprocal(d):
    y = pl.reciprocal(d, approx=True)
    return y * (2.0 - d * y)


def face(a, b):
    return 2.0 * a * b * reciprocal(jnp.maximum(a + b, 1e-30))


def woven(ref, at):
    return cat(*[ref[at, pl.ds(j, TILE, stride=3), :] for j in range(3)])


def next_row(x):
    return cat(x[TILE:], pltpu.roll(x[:TILE], TILE - 1, 0))


def last_row(x):
    return cat(pltpu.roll(x[-TILE:], 1, 0), x[:-TILE])


def near(around, w):
    before, mid, after = around
    wxp, wx, wy, wyp, wl = w
    total = wxp * before + wx * after
    total = total + (wy * next_row(mid) + wyp * last_row(mid))
    return total + (wl * pltpu.roll(mid, 127, 1) + pltpu.roll(wl * mid, 1, 1))


def prepare(main, main_fixed, beside, near_lat, far_lat, near_rows, far_rows, wx, wy, wyp, wl, total, inv, own, K):
    t = lax.axis_index("tm")
    base = HALO * (1 - t)
    rows = ROWS + TILE
    low = in_low(ROWS)
    low_tile = in_low(TILE)
    beta = corner_weight ** 0.5
    K[PLACES] = jnp.zeros((rows, 128), jnp.float32)

    def assemble(i):
        for at, tile in zip((i, i + PAIRS), halo_tiles(near_lat[i], far_lat[i])):
            own[base + at] = cat(main[at], tile)

    blocks(0, PAIRS, 17, assemble)

    def assemble_fixed(i):
        for at, tile in zip((i, i + PAIRS), halo_tiles(near_lat[PAIRS + i], far_lat[PAIRS + i])):
            moved = swapped(tile)
            for here, value in ((at, jnp.where(low_tile, tile, moved)), (at + QUADS, jnp.where(low_tile, moved, tile))):
                field = main_fixed[here]
                K[base + here] = cat(jnp.where(low, field, swapped(field)), value)

    blocks(0, QUADS, 17, assemble_fixed)
    for i in range(2):
        at = BESIDE + i
        for place, tile in zip((i, i + 2), halo_tiles(near_rows[at], far_rows[at])):
            own[SENT * t + place] = cat(beside[place], tile)
    for i, tile in enumerate(halo_tiles(near_rows[BESIDE_FIXED], far_rows[BESIDE_FIXED])):
        field = cat(beside[HALO + i], tile)
        moved = swapped(field)
        K[SENT * t + i] = jnp.where(in_low(rows), field, moved)
        K[SENT * t + i + 2] = jnp.where(in_low(rows), moved, field)
    lane = ids(rows, 1)
    inside = (lane & (LEVELS - 1)) != LEVELS - 1
    shift = jnp.where(lane < LEVELS, 1.0 - beta, 1.0 + beta)
    width = 18

    def weigh(i, carry):
        start = i * width
        here = woven(K, start)
        before = wx[jnp.maximum(start - 1, 0)]
        for u in range(width):
            at = start + u
            after = woven(K, at + 1)
            side = face(here, after)
            row = face(here, next_row(here))
            previous = last_row(row)
            level = jnp.where(inside, face(here, pltpu.roll(here, 127, 1)), 0.0)
            sums = (before + side) + (row + previous) + (level + pltpu.roll(level, 1, 1))
            wx[at], wy[at], wyp[at], wl[at] = side, row, previous, level
            total[at] = sums
            inv[at] = reciprocal(shift + sums)
            here, before = after, side
        return carry

    wx[0] = jnp.zeros((rows, 128), jnp.float32)
    lax.fori_loop(0, PLACES // width, weigh, 0)


STAGES = ((1, 39, 71), (2, 38, 70), (3, 37, 69), (4, 36, 68))
WIDTHS = ((19, 12, 17, 16), (16, 16, 16, 16))
READY = 40
EDGE = 12


def iterate_half(upper, wx, wy, wyp, wl, total, inv, own, other, near_rows, far_rows, xs, *refs):
    if upper:
        edge, w_own, w_send, *refs = refs
    else:
        w_own, w_send, edge, *refs = refs
    it, source, spec, x, y, z, natural = refs
    rows = ROWS + TILE
    first = lax.axis_index("tm") == 0
    low = in_low(rows)
    beta = corner_weight ** 0.5
    gamma = jnp.where(low, 1.0, beta)
    shared = [(it, 38), (it, 39), (source, 39), (x, 37), (x, 38), (y, 36), (y, 37), (z, 35), (z, 36)]
    shared += [(spec, 36), (spec, 37), (spec, 38)]
    if upper:
        for i, (ref, at) in enumerate(shared):
            ref[at] = edge[i]

    t = lax.axis_index("tm")

    def enter(at, theirs):
        mine = own[at]
        step0, step1 = jnp.where(first, mine, theirs), jnp.where(first, theirs, mine)
        moved = swapped(step0)
        it[at] = jnp.where(low, step0, swapped(step1))
        source[at] = jnp.where(low, moved, step1 + moved)

    def assemble(second):
        def step(i):
            main = i + (PAIRS if second else 0)
            tile = halo_tiles(near_rows[i], far_rows[i])[second]
            enter(HALO * (1 - t) + main, cat(other[main], tile))

        return step

    if upper:
        blocks(READY - HALO - PAIRS, PAIRS, 8, assemble(1))
    else:
        blocks(0, PAIRS, 17, assemble(0))
        blocks(0, READY - PAIRS, 6, assemble(1))
    for i in range(HALO):
        enter(SENT * t + i, xs[i])

    def over(stage, read, ref, step):
        lo, hi = STAGES[stage][upper : upper + 2]
        width = WIDTHS[upper][stage]

        def body(i, carry):
            start = lo + i * width
            around = [read(ref, start - 1), read(ref, start)]
            before = wx[start - 1]
            for u in range(width):
                at = start + u
                around = [*around[-2:], read(ref, at + 1)]
                side = wx[at]
                step(at, around, (before, side, wy[at], wyp[at], wl[at]))
                before = side
            return carry

        lax.fori_loop(0, (hi - lo) // width, body, 0)

    def residual(at, around, w):
        left = (woven(source, at) - ((1.0 + total[at]) * around[1] - near(around, w))) * gamma
        moved = swapped(left)
        value = jnp.where(low, left + moved, moved - left)
        spec[at] = value
        x[at] = value * inv[at]

    over(0, woven, it, residual)

    def plain(ref, at):
        return ref[at]

    def sweep(at, around, w):
        return (spec[at] + near(around, w)) * inv[at]

    def to(ref):
        def step(at, around, w):
            ref[at] = sweep(at, around, w)

        return step

    over(1, plain, x, to(y))
    over(2, plain, y, to(z))
    base = STAGES[3][upper]
    back = jnp.where(low, 0.5, 0.5 / beta)

    def last(at, around, w):
        value = sweep(at, around, w)
        moved = swapped(value)
        value = jnp.where(low, value + moved, moved - value) * back
        for j in range(3):
            natural[pl.ds((at - base) * rows + j, TILE, stride=3), :] = value[j * TILE : (j + 1) * TILE]

    over(3, plain, z, last)
    count = HALF // 2
    for q in range(4):
        turned = cat(*[natural[pl.ds(q + 4 * j, count, stride=rows), :] for j in range(4)]).T
        step0, step1 = turned[:LEVELS], turned[LEVELS:]
        w_own[q] = jnp.where(first, step0, step1)
        w_send[q] = jnp.where(first, step1, step0)
    if not upper:
        for i, (ref, at) in enumerate(shared):
            edge[i] = ref[at]


def placed(value, j, quarter):
    return pltpu.roll(value, (32 * (quarter - j) + 128) & 127, 1)


def finish_most(it, own_low, own_high, got_low, most):
    t = lax.axis_index("tm")
    group = ids(LEVELS, 1) // 32

    def step(q):
        for j in range(4):
            rows = pl.ds(q + 4 * j, LEVELS, stride=ROWS)
            value = it[rows, :]
            for piece, quarter in ((own_low, 2 * t), (own_high, 2 * t + 1), (got_low, 2 - 2 * t)):
                value = jnp.where(group == quarter, value + placed(piece[q], j, quarter), value)
            most[rows, :] = value

    blocks(0, 4, 2, step)


def finish(most, got_high, out_hbm, out, sems):
    quarter = 3 - 2 * lax.axis_index("tm")
    part = LEVELS // CHUNKS
    here = ids(part, 1) // 32 == quarter

    def copy(c):
        span = pl.ds(pl.multiple_of(c * part * ROWS, part * ROWS), part * ROWS)
        return pltpu.make_async_copy(out.at[span], out_hbm.at[span], sems.at[c])

    def step(c):
        for q in range(4):
            value = got_high[q, pl.ds(pl.multiple_of(c * part, part), part), :]
            for j in range(4):
                rows = pl.ds(c * part * ROWS + q + 4 * j, part, stride=ROWS)
                old = most[rows, :]
                out[rows, :] = jnp.where(here, old + placed(value, j, quarter), old)
        copy(c).start()

    blocks(0, CHUNKS, 1, step)
    for c in range(CHUNKS):
        copy(c).wait()


def two_steps(iterate, heating, initial, region, cond_table):
    lats, lons = lax.axis_size("lat"), lax.axis_size("lon")
    swap = [(0, 1), (1, 0)]
    pairs = [[(i, i + 1) for i in range(start, lats - 1, 2)] for start in (0, 1)]
    pairs = [p + [(j, i) for i, j in p] for p in pairs]
    round_lon = [[(i, (i + 1) % lons) for i in range(start, lons, 2)] for start in (0, 1)]
    round_lon = [p + [(j, i) for i, j in p] for p in round_lon]
    flat = (LEVELS * ROWS, LONS)
    turned_flat = (LONS * ROWS, 2 * LEVELS)
    by_lon = (LONS, ROWS, 2 * LEVELS)
    wide = shape(PLACES, ROWS + TILE, 128)

    def in_hbm(x):
        return pltpu.with_memory_space_constraint(x, pltpu.HBM)

    half_rows = shape(SENT, TILE, 128)
    edges, middle, turned, it = call(
        send_first,
        [half_rows, half_rows, shape(*turned_flat), shape(*flat)],
        [in_hbm(iterate[0]), in_hbm(heating[0])],
        scratch=[buffer(*flat), pltpu.SemaphoreType.DMA((ROWS // TILE, 2, 2))],
        hbm_ins=(0, 1),
    )
    edges = lax.ppermute(edges, "tm", swap)
    middle = lax.ppermute(middle, "tm", swap)
    sides = shape(HALO + 2, ROWS, 128)
    fixed, near_sides, far_sides = call(
        send_sides,
        [shape(*turned_flat), sides, sides],
        [turned, region.reshape(flat), initial.reshape(flat), in_hbm(cond_table)],
        scratch=[pltpu.SMEM(cond_table.shape, jnp.float32), pltpu.SemaphoreType.DMA],
        hbm_ins=(3,),
    )
    near_sides = lax.ppermute(near_sides, "lon", round_lon[0])
    far_sides = lax.ppermute(far_sides, "lon", round_lon[1])
    main = shape(SENT, ROWS, 128)
    lat = shape(PAIRS + QUADS, TILE, 128)
    own_main, main_fixed, near_lat, far_lat = call(
        own_rows, [main, main, lat, lat], [turned.reshape(by_lon), fixed.reshape(by_lon)]
    )
    near_lat = lax.ppermute(near_lat, "lat", pairs[0])
    far_lat = lax.ppermute(far_lat, "lat", pairs[1])
    rows = shape(PARTNER + 2, TILE, 128)
    edges, near_rows, far_rows, beside, partner = call(
        pass_rows,
        [half_rows, rows, rows, sides, shape(HALO, ROWS, 128)],
        [edges, main_fixed, near_sides, far_sides],
    )
    near_rows = lax.ppermute(near_rows, "lat", pairs[0])
    far_rows = lax.ppermute(far_rows, "lat", pairs[1])
    (xs,) = call(strips, [shape(HALO, ROWS + TILE, 128)], [partner, near_rows, far_rows])
    xs = lax.ppermute(xs, "tm", swap)
    *ready, own = call(
        prepare,
        [wide] * 7,
        [own_main, main_fixed, beside, near_lat, far_lat, near_rows, far_rows],
        scratch=[buffer(PLACES + 1, ROWS + TILE, 128)],
    )
    (other,) = call(gather, [main], [edges, middle, main_fixed, own])
    given = [*ready, own, other, near_rows, far_rows, xs]
    corrections = [shape(4, LEVELS, 128)] * 2
    fields = [buffer(PLACES, ROWS + TILE, 128)] * 6 + [buffer(HALF // 2 * (ROWS + TILE), 128)]
    own_low, send_low, edge = call(
        functools.partial(iterate_half, 0),
        [*corrections, shape(EDGE, ROWS + TILE, 128)],
        given,
        scratch=fields,
        limit=16,
    )
    got_low = lax.ppermute(send_low, "tm", swap)
    own_high, send_high = call(
        functools.partial(iterate_half, 1), corrections, [*given, edge], scratch=fields, limit=16
    )
    got_high = lax.ppermute(send_high, "tm", swap)
    (most,) = call(finish_most, [shape(*flat)], [it, own_low, own_high, got_low])
    (out,) = call(
        finish,
        [shape(*flat)],
        [most, got_high],
        scratch=[buffer(*flat), pltpu.SemaphoreType.DMA((CHUNKS,))],
        hbm_outs=(0,),
    )
    return out.reshape(iterate.shape)


def solution(mesh):
    return jax.shard_map(
        two_steps if mesh.shape["tm"] == 2 else on_device,
        mesh=mesh,
        in_specs=(
            P("tm", None, "lat", "lon"),
            P("tm", None, "lat", "lon"),
            P(None, "lat", "lon"),
            P(None, "lat", "lon"),
            P(),
        ),
        out_specs=P("tm", None, "lat", "lon"),
        check_vma=False,
    )
```

```python
import functools

import jax
import jax.numpy as jnp
from jax import lax
from jax.experimental import pallas as pl
from jax.experimental.pallas import tpu as pltpu
from jax.sharding import PartitionSpec as P

SWEEPS = 4


corner_weight = 0.1


def padded(value, sides, width, wrap):
    for axis, dim in sides:
        peers, length = (lax.axis_size(axis), value.shape[dim])
        up = [(i, (i + 1) % peers) for i in range(peers if wrap else peers - 1)]
        down = [(j, i) for i, j in up]
        last = lax.slice_in_dim(value, length - width, length, axis=dim)
        initial = lax.slice_in_dim(value, 0, width, axis=dim)
        before = lax.ppermute(last, axis, up)
        after = lax.ppermute(initial, axis, down)
        value = jnp.concatenate([before, value, after], axis=dim)
    return value


def passed_along(block, axis, distance):
    devices = range(lax.axis_size(axis))
    route = [(i - distance, i) for i in devices if i - distance in devices]
    return lax.ppermute(block, axis, route)


def harmonic(first, second):
    return 2.0 * first * second / (first + second)


def conductivity(region, cond_table):
    classes = jnp.arange(cond_table.shape[0], dtype=jnp.int32)
    onehot = (region[..., None] == classes).astype(jnp.float32)
    return jnp.sum(onehot * cond_table, axis=-1)


def extend(stack):
    lat_ext = padded(stack, (("lat", 2),), 1, False)
    both = padded(lat_ext, (("lon", 3),), 1, True)
    return jnp.pad(both, ((0, 0), (1, 1), (0, 0), (0, 0)))


def face_weights(kext):
    centre = kext[1:-1, 1:-1, 1:-1]
    return (
        harmonic(centre, kext[:-2, 1:-1, 1:-1]),
        harmonic(centre, kext[2:, 1:-1, 1:-1]),
        harmonic(centre, kext[1:-1, :-2, 1:-1]),
        harmonic(centre, kext[1:-1, 2:, 1:-1]),
        harmonic(centre, kext[1:-1, 1:-1, :-2]),
        harmonic(centre, kext[1:-1, 1:-1, 2:]),
    )


def neighbours(weights, ext):
    near = weights[0] * ext[..., :-2, 1:-1, 1:-1] + weights[1] * ext[..., 2:, 1:-1, 1:-1]
    near = near + weights[2] * ext[..., 1:-1, :-2, 1:-1] + weights[3] * ext[..., 1:-1, 2:, 1:-1]
    near = near + weights[4] * ext[..., 1:-1, 1:-1, :-2] + weights[5] * ext[..., 1:-1, 1:-1, 2:]
    return near


def on_device(iterate, heating, initial, region, cond_table):
    steps = lax.axis_size("tm")
    own = lax.axis_index("tm")
    high = lax.Precision.HIGHEST
    kfield = conductivity(region, cond_table)
    ext = extend(jnp.stack([kfield, iterate[0]]))
    weights = face_weights(ext[0])
    total = weights[0] + weights[1] + weights[2] + weights[3] + weights[4] + weights[5]
    shifted = passed_along(iterate, "tm", 1)[0]
    previous = jnp.where(own == 0, initial, shifted)
    residual = heating[0] + previous - ((1.0 + total) * iterate[0] - neighbours(weights, ext[1]))
    scale_own = corner_weight ** (own.astype(jnp.float32) / steps)
    scaled = residual * scale_own
    zeros = jnp.zeros_like(residual)
    piece = lax.all_gather(scaled[None], "tm", axis=0, tiled=True)
    order = jnp.arange(piece.shape[0], dtype=jnp.int32)
    angle = 2.0 * jnp.pi / steps * (own * order % steps).astype(jnp.float32)
    real_part = jnp.einsum("n,nabc->abc", jnp.cos(angle), piece, precision=high)
    imag_part = (zeros, zeros)[1] - jnp.einsum("n,nabc->abc", jnp.sin(angle), piece, precision=high)
    beta = corner_weight ** (1.0 / steps)
    freq_angle = 2.0 * jnp.pi / steps * (own % steps).astype(jnp.float32)
    diag_re = 1.0 - beta * jnp.cos(freq_angle) + total
    diag_im = beta * jnp.sin(freq_angle) + zeros
    denom = diag_re * diag_re + diag_im * diag_im
    inv_re = diag_re / denom
    inv_im = -diag_im / denom
    sol_re = real_part * inv_re - imag_part * inv_im
    sol_im = real_part * inv_im + imag_part * inv_re
    for sweep in range(SWEEPS - 1):
        near = neighbours(weights, extend(jnp.stack([sol_re, sol_im])))
        rhs_re = real_part + near[0]
        rhs_im = imag_part + near[1]
        sol_re = rhs_re * inv_re - rhs_im * inv_im
        sol_im = rhs_re * inv_im + rhs_im * inv_re
    pieces = (
        lax.all_gather(sol_re[None], "tm", axis=0, tiled=True),
        lax.all_gather(sol_im[None], "tm", axis=0, tiled=True),
    )
    order = jnp.arange(pieces[0].shape[0], dtype=jnp.int32)
    angle = 2.0 * jnp.pi / steps * (order * own % steps).astype(jnp.float32)
    summed = jnp.einsum("k,kabc->abc", jnp.cos(angle), pieces[0], precision=high) - jnp.einsum(
        "k,kabc->abc", jnp.sin(angle), pieces[1], precision=high
    )
    back = summed / steps
    return iterate + (back / scale_own)[None]


HALO = 4
TILE = 8
LEVELS = 64
ROWS = 16
LONS = 128
HALF = 64
SENT = HALF + HALO
PLACES = HALF + 2 * HALO
PAIRS = PLACES // 2
SENT_PAIRS = SENT // 2
QUADS = PLACES // 4
SPLIT = 26
FIXED = SPLIT
PARTNER = SPLIT + QUADS
CHUNKS = 4


def specs(count, hbm):
    return [pl.BlockSpec(memory_space=pltpu.HBM if i in hbm else pltpu.VMEM) for i in range(count)]


def call(body, outs, ins, scratch=(), limit=8, hbm_ins=(), hbm_outs=()):
    moved = sum(x.size * 4 for x in ins) + sum(x.size * 4 for x in outs)
    return pl.pallas_call(
        body,
        out_shape=outs,
        in_specs=specs(len(ins), hbm_ins),
        out_specs=specs(len(outs), hbm_outs),
        scratch_shapes=scratch,
        compiler_params=pltpu.CompilerParams(vmem_limit_bytes=limit << 20),
        cost_estimate=pl.CostEstimate(flops=moved * 4, bytes_accessed=moved, transcendentals=0),
    )(*ins)


def shape(*dims):
    return jax.ShapeDtypeStruct(dims, jnp.float32)


def buffer(*dims):
    return pltpu.VMEM(dims, jnp.float32)


def ids(rows, dim):
    return lax.broadcasted_iota(jnp.int32, (rows, 128), dim)


def in_low(rows):
    return ids(rows, 1) < LEVELS


def swapped(x):
    return pltpu.roll(x, LEVELS, 1)


def cat(*values):
    return jnp.concatenate(values, axis=0)


def even(axis):
    return lax.rem(lax.axis_index(axis), 2) == 0


def blocks(lo, hi, width, step):
    def body(i, carry):
        for u in range(width):
            step(lo + i * width + u)
        return carry

    lax.fori_loop(0, (hi - lo) // width, body, 0)


def send_first(it_hbm, h_hbm, edges, middle, turned, it, h, sems):
    t = lax.axis_index("tm")
    by_level = (LEVELS, ROWS, LONS)
    copies = []
    for k in range(ROWS // TILE):
        for f, (source, target) in enumerate(((it_hbm, it), (h_hbm, h))):
            for c in range(2):
                part = pl.ds(c * LEVELS // 2, LEVELS // 2), pl.ds(k * TILE, TILE)
                copy = pltpu.make_async_copy(source.at[part], target.reshape(by_level).at[part], sems.at[k, f, c])
                copy.start()
                copies.append(copy)

    def turn(r):
        rows = pl.ds(r, LEVELS, stride=ROWS)
        turned[pl.ds(r, LONS, stride=ROWS), :] = cat(it[rows, :], h[rows, :]).T

    for k in range(ROWS // TILE):
        for copy in copies[4 * k : 4 * k + 4]:
            copy.wait()
        blocks(k * TILE, (k + 1) * TILE, 4, turn)
    start = (LONS - SENT) * ROWS * (1 - t)
    top = ids(TILE, 0) < HALO

    def cut(i):
        at = pl.multiple_of(start + i * ROWS, ROWS)
        low, high = turned[pl.ds(at, TILE), :], turned[pl.ds(at + TILE, TILE), :]
        edges[i] = jnp.where(top, low, high)
        middle[i] = jnp.where(top, high, low)

    blocks(0, SENT, 17, cut)


def heated(turned, fixed):
    add = jnp.logical_and(jnp.logical_not(in_low(ROWS)), lax.axis_index("tm") == 0)
    return turned + jnp.where(add, fixed, 0.0)


def send_sides(turned, region, initial, table_hbm, fixed, near_sides, far_sides, table, sem):
    copy = pltpu.make_async_copy(table_hbm, table, sem)
    copy.start()
    copy.wait()

    def turn(r):
        rows = pl.ds(r, LEVELS, stride=ROWS)
        classes = region[rows, :]
        value = jnp.full(classes.shape, table[0], jnp.float32)
        for c in range(1, table.shape[0]):
            value = jnp.where(classes == c, table[c], value)
        fixed[pl.ds(r, LONS, stride=ROWS), :] = cat(value, initial[rows, :]).T

    blocks(0, ROWS, 4, turn)
    near_right = even("lon")
    low = in_low(ROWS)

    def strip(first_lon):
        def at(ref, i):
            return ref[(first_lon + i) * ROWS : (first_lon + i + 1) * ROWS, :]

        return [heated(at(turned, i), at(fixed, i)) for i in range(HALO)] + [
            jnp.where(low, at(fixed, i), swapped(at(fixed, i + 2))) for i in range(2)
        ]

    for i, (right, left) in enumerate(zip(strip(LONS - HALO), strip(0))):
        near_sides[i] = jnp.where(near_right, right, left)
        far_sides[i] = jnp.where(near_right, left, right)


def edge_pair(first, second):
    top = ids(TILE, 0) < HALO
    first_up = even("lat")
    down = jnp.where(top, first[:TILE], pltpu.roll(second[:TILE], HALO, 0))
    up = jnp.where(top, pltpu.roll(first[-TILE:], HALO, 0), second[-TILE:])
    return jnp.where(first_up, up, down), jnp.where(first_up, down, up)


def halo_tiles(near_pair, far_pair):
    first_up = even("lat")
    after = jnp.where(first_up, near_pair, far_pair)
    before = jnp.where(first_up, far_pair, near_pair)
    top = ids(TILE, 0) < HALO
    return (
        jnp.where(top, after, pltpu.roll(before, HALO, 0)),
        jnp.where(top, pltpu.roll(after, HALO, 0), before),
    )


def add_sides(turned, fixed, near_sides, far_sides, own, own_fixed, near_lat, far_lat, partner):
    t = lax.axis_index("tm")
    from_near = (t == 0) != even("lon")
    count = near_sides.shape[0]
    beside = [jnp.where(from_near, near_sides[i], far_sides[i]) for i in range(count)]
    other = [jnp.where(from_near, far_sides[i], near_sides[i]) for i in range(HALO)]
    for i in range(HALO):
        own[SENT * t + i] = beside[i]
        partner[i] = other[i]
    for i in range(2):
        own_fixed[SENT * t + i] = beside[HALO + i]
        own_fixed[SENT * t + i + 2] = swapped(beside[HALO + i])
        near_lat[PARTNER + i], far_lat[PARTNER + i] = edge_pair(other[i], other[i + 2])

    def copy(i):
        at = HALO * (1 - t) + i
        lon = (LONS - SENT) * t + i
        own[at] = heated(turned[lon], fixed[lon])
        own_fixed[at] = fixed[lon]

    blocks(0, SENT, 17, copy)

    def rows(i):
        near_lat[i], far_lat[i] = edge_pair(own[i], own[i + PAIRS])

    blocks(0, SPLIT, 13, rows)
    low = in_low(TILE)

    def fixed_rows(i):
        here = edge_pair(own_fixed[i], own_fixed[i + PAIRS])
        there = edge_pair(own_fixed[i + QUADS], own_fixed[i + PAIRS + QUADS])
        near_lat[FIXED + i], far_lat[FIXED + i] = [jnp.where(low, a, swapped(b)) for a, b in zip(here, there)]

    blocks(0, QUADS, 9, fixed_rows)


def start_of_step(fixed, rows):
    add = jnp.logical_and(jnp.logical_not(in_low(rows)), lax.axis_index("tm") == 1)
    return jnp.where(add, fixed, 0.0)


def pass_rows(edges, own, own_fixed, heated_edges, near_rows, far_rows):
    base = HALO * (1 - lax.axis_index("tm"))
    top = ids(TILE, 0) < HALO

    def heat(i):
        fixed = own_fixed[base + i]
        heated_edges[i] = edges[i] + start_of_step(jnp.where(top, fixed[:TILE], fixed[TILE:]), TILE)

    blocks(0, SENT, 17, heat)

    def rows(i):
        near_rows[i], far_rows[i] = edge_pair(heated_edges[i], heated_edges[i + SENT_PAIRS])

    blocks(0, SENT_PAIRS, 17, rows)

    def rest(i):
        near_rows[SENT_PAIRS + i], far_rows[SENT_PAIRS + i] = edge_pair(own[SPLIT + i], own[SPLIT + i + PAIRS])

    blocks(0, PAIRS - SPLIT, 10, rest)


def join(main, near_lat, far_lat, near_rows, far_rows, own):
    def place(i, tiles):
        for at, tile in zip((i, i + PAIRS), tiles):
            own[at] = cat(main[at], tile)

    blocks(0, SPLIT, 13, lambda i: place(i, halo_tiles(near_lat[i], far_lat[i])))

    def rest(i):
        at = SENT_PAIRS + i
        place(SPLIT + i, halo_tiles(near_rows[at], far_rows[at]))

    blocks(0, PAIRS - SPLIT, 10, rest)


def gather(edges, middle, own_fixed, _, other):
    base = HALO * (1 - lax.axis_index("tm"))
    top = ids(TILE, 0) < HALO

    def join(i):
        fixed = own_fixed[base + i]
        e = edges[i]
        m = middle[i] + start_of_step(jnp.where(top, fixed[TILE:], fixed[:TILE]), TILE)
        other[i] = cat(jnp.where(top, e, m), jnp.where(top, m, e))

    blocks(0, SENT, 17, join)


def strips(partner, near_lat, far_lat, xs):
    for i in range(2):
        at = PARTNER + i
        for place, tile in zip((i, i + 2), halo_tiles(near_lat[at], far_lat[at])):
            xs[place] = cat(partner[place], tile)


def reciprocal(d):
    y = pl.reciprocal(d, approx=True)
    return y * (2.0 - d * y)


def face(a, b):
    return 2.0 * a * b * reciprocal(jnp.maximum(a + b, 1e-30))


def woven(ref, at):
    return cat(*[ref[at, pl.ds(j, TILE, stride=3), :] for j in range(3)])


def next_row(x):
    return cat(x[TILE:], pltpu.roll(x[:TILE], TILE - 1, 0))


def last_row(x):
    return cat(pltpu.roll(x[-TILE:], 1, 0), x[:-TILE])


def near(around, w):
    before, mid, after = around
    wxp, wx, wy, wyp, wl = w
    total = wxp * before + wx * after
    total = total + (wy * next_row(mid) + wyp * last_row(mid))
    return total + (wl * pltpu.roll(mid, 127, 1) + pltpu.roll(wl * mid, 1, 1))


def prepare(own_fixed, near_lat, far_lat, _, wx, wy, wyp, wl, total, inv, K):
    rows = ROWS + TILE
    low = in_low(ROWS)
    low_tile = in_low(TILE)
    beta = corner_weight ** 0.5
    K[PLACES] = jnp.zeros((rows, 128), jnp.float32)

    def assemble_fixed(i):
        for at, tile in zip((i, i + PAIRS), halo_tiles(near_lat[FIXED + i], far_lat[FIXED + i])):
            moved = swapped(tile)
            for here, value in ((at, jnp.where(low_tile, tile, moved)), (at + QUADS, jnp.where(low_tile, moved, tile))):
                main = own_fixed[here]
                K[here] = cat(jnp.where(low, main, swapped(main)), value)

    blocks(0, QUADS, 9, assemble_fixed)
    lane = ids(rows, 1)
    inside = (lane & (LEVELS - 1)) != LEVELS - 1
    shift = jnp.where(lane < LEVELS, 1.0 - beta, 1.0 + beta)
    width = 18

    def weigh(i, carry):
        start = i * width
        here = woven(K, start)
        before = wx[jnp.maximum(start - 1, 0)]
        for u in range(width):
            at = start + u
            after = woven(K, at + 1)
            side = face(here, after)
            row = face(here, next_row(here))
            previous = last_row(row)
            level = jnp.where(inside, face(here, pltpu.roll(here, 127, 1)), 0.0)
            sums = (before + side) + (row + previous) + (level + pltpu.roll(level, 1, 1))
            wx[at], wy[at], wyp[at], wl[at] = side, row, previous, level
            total[at] = sums
            inv[at] = reciprocal(shift + sums)
            here, before = after, side
        return carry

    wx[0] = jnp.zeros((rows, 128), jnp.float32)
    lax.fori_loop(0, PLACES // width, weigh, 0)


STAGES = ((1, 39, 71), (2, 38, 70), (3, 37, 69), (4, 36, 68))
WIDTHS = ((19, 12, 17, 16), (16, 16, 16, 16))
READY = 40
EDGE = 12


def iterate_half(upper, wx, wy, wyp, wl, total, inv, own, other, near_rows, far_rows, xs, *refs):
    if upper:
        edge, w_own, w_send, *refs = refs
    else:
        w_own, w_send, edge, *refs = refs
    it, source, spec, x, y, z, natural = refs
    rows = ROWS + TILE
    first = lax.axis_index("tm") == 0
    low = in_low(rows)
    beta = corner_weight ** 0.5
    gamma = jnp.where(low, 1.0, beta)
    shared = [(it, 38), (it, 39), (source, 39), (x, 37), (x, 38), (y, 36), (y, 37), (z, 35), (z, 36)]
    shared += [(spec, 36), (spec, 37), (spec, 38)]
    if upper:
        for i, (ref, at) in enumerate(shared):
            ref[at] = edge[i]

    t = lax.axis_index("tm")

    def enter(at, theirs):
        mine = own[at]
        step0, step1 = jnp.where(first, mine, theirs), jnp.where(first, theirs, mine)
        moved = swapped(step0)
        it[at] = jnp.where(low, step0, swapped(step1))
        source[at] = jnp.where(low, moved, step1 + moved)

    def assemble(second):
        def step(i):
            main = i + (SENT_PAIRS if second else 0)
            tile = halo_tiles(near_rows[i], far_rows[i])[second]
            enter(HALO * (1 - t) + main, cat(other[main], tile))

        return step

    if upper:
        blocks(READY - HALO - SENT_PAIRS, SENT_PAIRS, 8, assemble(1))
    else:
        blocks(0, SENT_PAIRS, 17, assemble(0))
        blocks(0, READY - SENT_PAIRS, 6, assemble(1))
    for i in range(HALO):
        enter(SENT * t + i, xs[i])

    def over(stage, read, ref, step):
        lo, hi = STAGES[stage][upper : upper + 2]
        width = WIDTHS[upper][stage]

        def body(i, carry):
            start = lo + i * width
            around = [read(ref, start - 1), read(ref, start)]
            before = wx[start - 1]
            for u in range(width):
                at = start + u
                around = [*around[-2:], read(ref, at + 1)]
                side = wx[at]
                step(at, around, (before, side, wy[at], wyp[at], wl[at]))
                before = side
            return carry

        lax.fori_loop(0, (hi - lo) // width, body, 0)

    def residual(at, around, w):
        left = (woven(source, at) - ((1.0 + total[at]) * around[1] - near(around, w))) * gamma
        moved = swapped(left)
        value = jnp.where(low, left + moved, moved - left)
        spec[at] = value
        x[at] = value * inv[at]

    over(0, woven, it, residual)

    def plain(ref, at):
        return ref[at]

    def sweep(at, around, w):
        return (spec[at] + near(around, w)) * inv[at]

    def to(ref):
        def step(at, around, w):
            ref[at] = sweep(at, around, w)

        return step

    over(1, plain, x, to(y))
    over(2, plain, y, to(z))
    base = STAGES[3][upper]
    back = jnp.where(low, 0.5, 0.5 / beta)

    def last(at, around, w):
        value = sweep(at, around, w)
        moved = swapped(value)
        value = jnp.where(low, value + moved, moved - value) * back
        for j in range(3):
            natural[pl.ds((at - base) * rows + j, TILE, stride=3), :] = value[j * TILE : (j + 1) * TILE]

    over(3, plain, z, last)
    count = HALF // 2
    for q in range(4):
        turned = cat(*[natural[pl.ds(q + 4 * j, count, stride=rows), :] for j in range(4)]).T
        step0, step1 = turned[:LEVELS], turned[LEVELS:]
        w_own[q] = jnp.where(first, step0, step1)
        w_send[q] = jnp.where(first, step1, step0)
    if not upper:
        for i, (ref, at) in enumerate(shared):
            edge[i] = ref[at]


def placed(value, j, quarter):
    return pltpu.roll(value, (32 * (quarter - j) + 128) & 127, 1)


def finish_most(it, own_low, own_high, got_low, most):
    t = lax.axis_index("tm")
    group = ids(LEVELS, 1) // 32

    def step(q):
        for j in range(4):
            rows = pl.ds(q + 4 * j, LEVELS, stride=ROWS)
            value = it[rows, :]
            for piece, quarter in ((own_low, 2 * t), (own_high, 2 * t + 1), (got_low, 2 - 2 * t)):
                value = jnp.where(group == quarter, value + placed(piece[q], j, quarter), value)
            most[rows, :] = value

    blocks(0, 4, 2, step)


def finish(most, got_high, out_hbm, out, sems):
    quarter = 3 - 2 * lax.axis_index("tm")
    part = LEVELS // CHUNKS
    here = ids(part, 1) // 32 == quarter

    def copy(c):
        span = pl.ds(pl.multiple_of(c * part * ROWS, part * ROWS), part * ROWS)
        return pltpu.make_async_copy(out.at[span], out_hbm.at[span], sems.at[c])

    def step(c):
        for q in range(4):
            value = got_high[q, pl.ds(pl.multiple_of(c * part, part), part), :]
            for j in range(4):
                rows = pl.ds(c * part * ROWS + q + 4 * j, part, stride=ROWS)
                old = most[rows, :]
                out[rows, :] = jnp.where(here, old + placed(value, j, quarter), old)
        copy(c).start()

    blocks(0, CHUNKS, 1, step)
    for c in range(CHUNKS):
        copy(c).wait()


def two_steps(iterate, heating, initial, region, cond_table):
    lats, lons = lax.axis_size("lat"), lax.axis_size("lon")
    swap = [(0, 1), (1, 0)]
    pairs = [[(i, i + 1) for i in range(start, lats - 1, 2)] for start in (0, 1)]
    pairs = [p + [(j, i) for i, j in p] for p in pairs]
    round_lon = [[(i, (i + 1) % lons) for i in range(start, lons, 2)] for start in (0, 1)]
    round_lon = [p + [(j, i) for i, j in p] for p in round_lon]
    flat = (LEVELS * ROWS, LONS)
    turned_flat = (LONS * ROWS, 2 * LEVELS)
    by_lon = (LONS, ROWS, 2 * LEVELS)
    wide = shape(PLACES, ROWS + TILE, 128)

    def in_hbm(x):
        return pltpu.with_memory_space_constraint(x, pltpu.HBM)

    half_rows = shape(SENT, TILE, 128)
    edges, middle, turned, it = call(
        send_first,
        [half_rows, half_rows, shape(*turned_flat), shape(*flat)],
        [in_hbm(iterate[0]), in_hbm(heating[0])],
        scratch=[buffer(*flat), pltpu.SemaphoreType.DMA((ROWS // TILE, 2, 2))],
        hbm_ins=(0, 1),
    )
    edges = lax.ppermute(edges, "tm", swap)
    middle = lax.ppermute(middle, "tm", swap)
    sides = shape(HALO + 2, ROWS, 128)
    fixed, near_sides, far_sides = call(
        send_sides,
        [shape(*turned_flat), sides, sides],
        [turned, region.reshape(flat), initial.reshape(flat), in_hbm(cond_table)],
        scratch=[pltpu.SMEM(cond_table.shape, jnp.float32), pltpu.SemaphoreType.DMA],
        hbm_ins=(3,),
    )
    near_sides = lax.ppermute(near_sides, "lon", round_lon[0])
    far_sides = lax.ppermute(far_sides, "lon", round_lon[1])
    main = shape(PLACES, ROWS, 128)
    lat = shape(PARTNER + 2, TILE, 128)
    own_main, own_fixed, near_lat, far_lat, partner = call(
        add_sides,
        [main, main, lat, lat, shape(HALO, ROWS, 128)],
        [turned.reshape(by_lon), fixed.reshape(by_lon), near_sides, far_sides],
    )
    near_lat = lax.ppermute(near_lat, "lat", pairs[0])
    far_lat = lax.ppermute(far_lat, "lat", pairs[1])
    rows = shape(SENT_PAIRS + PAIRS - SPLIT, TILE, 128)
    edges, near_rows, far_rows = call(pass_rows, [half_rows, rows, rows], [edges, own_main, own_fixed])
    near_rows = lax.ppermute(near_rows, "lat", pairs[0])
    far_rows = lax.ppermute(far_rows, "lat", pairs[1])
    (xs,) = call(strips, [shape(HALO, ROWS + TILE, 128)], [partner, near_lat, far_lat])
    xs = lax.ppermute(xs, "tm", swap)
    ready = call(
        prepare,
        [wide] * 6,
        [own_fixed, near_lat, far_lat, edges],
        scratch=[buffer(PLACES + 1, ROWS + TILE, 128)],
    )
    (other,) = call(gather, [shape(SENT, ROWS, 128)], [edges, middle, own_fixed, ready[0]])
    (own,) = call(join, [wide], [own_main, near_lat, far_lat, near_rows, far_rows])
    given = [*ready, own, other, near_rows, far_rows, xs]
    corrections = [shape(4, LEVELS, 128)] * 2
    fields = [buffer(PLACES, ROWS + TILE, 128)] * 6 + [buffer(HALF // 2 * (ROWS + TILE), 128)]
    own_low, send_low, edge = call(
        functools.partial(iterate_half, 0),
        [*corrections, shape(EDGE, ROWS + TILE, 128)],
        given,
        scratch=fields,
        limit=16,
    )
    got_low = lax.ppermute(send_low, "tm", swap)
    own_high, send_high = call(
        functools.partial(iterate_half, 1), corrections, [*given, edge], scratch=fields, limit=16
    )
    got_high = lax.ppermute(send_high, "tm", swap)
    (most,) = call(finish_most, [shape(*flat)], [it, own_low, own_high, got_low])
    (out,) = call(
        finish,
        [shape(*flat)],
        [most, got_high],
        scratch=[buffer(*flat), pltpu.SemaphoreType.DMA((CHUNKS,))],
        hbm_outs=(0,),
    )
    return out.reshape(iterate.shape)


def solution(mesh):
    return jax.shard_map(
        two_steps if mesh.shape["tm"] == 2 else on_device,
        mesh=mesh,
        in_specs=(
            P("tm", None, "lat", "lon"),
            P("tm", None, "lat", "lon"),
            P(None, "lat", "lon"),
            P(None, "lat", "lon"),
            P(),
        ),
        out_specs=P("tm", None, "lat", "lon"),
        check_vma=False,
    )
```

```python
import functools

import jax
import jax.numpy as jnp
from jax import lax
from jax.experimental import pallas as pl
from jax.experimental.pallas import tpu as pltpu
from jax.sharding import PartitionSpec as P

SWEEPS = 4


corner_weight = 0.1


def padded(value, sides, width, wrap):
    for axis, dim in sides:
        peers, length = (lax.axis_size(axis), value.shape[dim])
        up = [(i, (i + 1) % peers) for i in range(peers if wrap else peers - 1)]
        down = [(j, i) for i, j in up]
        last = lax.slice_in_dim(value, length - width, length, axis=dim)
        initial = lax.slice_in_dim(value, 0, width, axis=dim)
        before = lax.ppermute(last, axis, up)
        after = lax.ppermute(initial, axis, down)
        value = jnp.concatenate([before, value, after], axis=dim)
    return value


def passed_along(block, axis, distance):
    devices = range(lax.axis_size(axis))
    route = [(i - distance, i) for i in devices if i - distance in devices]
    return lax.ppermute(block, axis, route)


def harmonic(first, second):
    return 2.0 * first * second / (first + second)


def conductivity(region, cond_table):
    classes = jnp.arange(cond_table.shape[0], dtype=jnp.int32)
    onehot = (region[..., None] == classes).astype(jnp.float32)
    return jnp.sum(onehot * cond_table, axis=-1)


def extend(stack):
    lat_ext = padded(stack, (("lat", 2),), 1, False)
    both = padded(lat_ext, (("lon", 3),), 1, True)
    return jnp.pad(both, ((0, 0), (1, 1), (0, 0), (0, 0)))


def face_weights(kext):
    centre = kext[1:-1, 1:-1, 1:-1]
    return (
        harmonic(centre, kext[:-2, 1:-1, 1:-1]),
        harmonic(centre, kext[2:, 1:-1, 1:-1]),
        harmonic(centre, kext[1:-1, :-2, 1:-1]),
        harmonic(centre, kext[1:-1, 2:, 1:-1]),
        harmonic(centre, kext[1:-1, 1:-1, :-2]),
        harmonic(centre, kext[1:-1, 1:-1, 2:]),
    )


def neighbours(weights, ext):
    near = weights[0] * ext[..., :-2, 1:-1, 1:-1] + weights[1] * ext[..., 2:, 1:-1, 1:-1]
    near = near + weights[2] * ext[..., 1:-1, :-2, 1:-1] + weights[3] * ext[..., 1:-1, 2:, 1:-1]
    near = near + weights[4] * ext[..., 1:-1, 1:-1, :-2] + weights[5] * ext[..., 1:-1, 1:-1, 2:]
    return near


def on_device(iterate, heating, initial, region, cond_table):
    steps = lax.axis_size("tm")
    own = lax.axis_index("tm")
    high = lax.Precision.HIGHEST
    kfield = conductivity(region, cond_table)
    ext = extend(jnp.stack([kfield, iterate[0]]))
    weights = face_weights(ext[0])
    total = weights[0] + weights[1] + weights[2] + weights[3] + weights[4] + weights[5]
    shifted = passed_along(iterate, "tm", 1)[0]
    previous = jnp.where(own == 0, initial, shifted)
    residual = heating[0] + previous - ((1.0 + total) * iterate[0] - neighbours(weights, ext[1]))
    scale_own = corner_weight ** (own.astype(jnp.float32) / steps)
    scaled = residual * scale_own
    zeros = jnp.zeros_like(residual)
    piece = lax.all_gather(scaled[None], "tm", axis=0, tiled=True)
    order = jnp.arange(piece.shape[0], dtype=jnp.int32)
    angle = 2.0 * jnp.pi / steps * (own * order % steps).astype(jnp.float32)
    real_part = jnp.einsum("n,nabc->abc", jnp.cos(angle), piece, precision=high)
    imag_part = (zeros, zeros)[1] - jnp.einsum("n,nabc->abc", jnp.sin(angle), piece, precision=high)
    beta = corner_weight ** (1.0 / steps)
    freq_angle = 2.0 * jnp.pi / steps * (own % steps).astype(jnp.float32)
    diag_re = 1.0 - beta * jnp.cos(freq_angle) + total
    diag_im = beta * jnp.sin(freq_angle) + zeros
    denom = diag_re * diag_re + diag_im * diag_im
    inv_re = diag_re / denom
    inv_im = -diag_im / denom
    sol_re = real_part * inv_re - imag_part * inv_im
    sol_im = real_part * inv_im + imag_part * inv_re
    for sweep in range(SWEEPS - 1):
        near = neighbours(weights, extend(jnp.stack([sol_re, sol_im])))
        rhs_re = real_part + near[0]
        rhs_im = imag_part + near[1]
        sol_re = rhs_re * inv_re - rhs_im * inv_im
        sol_im = rhs_re * inv_im + rhs_im * inv_re
    pieces = (
        lax.all_gather(sol_re[None], "tm", axis=0, tiled=True),
        lax.all_gather(sol_im[None], "tm", axis=0, tiled=True),
    )
    order = jnp.arange(pieces[0].shape[0], dtype=jnp.int32)
    angle = 2.0 * jnp.pi / steps * (order * own % steps).astype(jnp.float32)
    summed = jnp.einsum("k,kabc->abc", jnp.cos(angle), pieces[0], precision=high) - jnp.einsum(
        "k,kabc->abc", jnp.sin(angle), pieces[1], precision=high
    )
    back = summed / steps
    return iterate + (back / scale_own)[None]


HALO = 4
TILE = 8
LEVELS = 64
ROWS = 16
LONS = 128
HALF = 64
SENT = HALF + HALO
PLACES = HALF + 2 * HALO
PAIRS = PLACES // 2
SENT_PAIRS = SENT // 2
QUADS = PLACES // 4
SPLIT = 26
FIXED = SPLIT
PARTNER = SPLIT + QUADS
CHUNKS = 4


def specs(count, hbm):
    return [pl.BlockSpec(memory_space=pltpu.HBM if i in hbm else pltpu.VMEM) for i in range(count)]


def call(body, outs, ins, scratch=(), limit=8, hbm_ins=(), hbm_outs=()):
    moved = sum(x.size * 4 for x in ins) + sum(x.size * 4 for x in outs)
    return pl.pallas_call(
        body,
        out_shape=outs,
        in_specs=specs(len(ins), hbm_ins),
        out_specs=specs(len(outs), hbm_outs),
        scratch_shapes=scratch,
        compiler_params=pltpu.CompilerParams(vmem_limit_bytes=limit << 20),
        cost_estimate=pl.CostEstimate(flops=moved * 4, bytes_accessed=moved, transcendentals=0),
    )(*ins)


def shape(*dims):
    return jax.ShapeDtypeStruct(dims, jnp.float32)


def buffer(*dims):
    return pltpu.VMEM(dims, jnp.float32)


def ids(rows, dim):
    return lax.broadcasted_iota(jnp.int32, (rows, 128), dim)


def in_low(rows):
    return ids(rows, 1) < LEVELS


def swapped(x):
    return pltpu.roll(x, LEVELS, 1)


def cat(*values):
    return jnp.concatenate(values, axis=0)


def even(axis):
    return lax.rem(lax.axis_index(axis), 2) == 0


def blocks(lo, hi, width, step):
    def body(i, carry):
        for u in range(width):
            step(lo + i * width + u)
        return carry

    lax.fori_loop(0, (hi - lo) // width, body, 0)


def send_first(it_hbm, h_hbm, edges, middle, turned, it, h, sems):
    t = lax.axis_index("tm")
    by_level = (LEVELS, ROWS, LONS)
    copies = []
    for k in range(ROWS // TILE):
        for f, (source, target) in enumerate(((it_hbm, it), (h_hbm, h))):
            for c in range(2):
                part = pl.ds(c * LEVELS // 2, LEVELS // 2), pl.ds(k * TILE, TILE)
                copy = pltpu.make_async_copy(source.at[part], target.reshape(by_level).at[part], sems.at[k, f, c])
                copy.start()
                copies.append(copy)

    def turn(r):
        rows = pl.ds(r, LEVELS, stride=ROWS)
        turned[pl.ds(r, LONS, stride=ROWS), :] = cat(it[rows, :], h[rows, :]).T

    for k in range(ROWS // TILE):
        for copy in copies[4 * k : 4 * k + 4]:
            copy.wait()
        blocks(k * TILE, (k + 1) * TILE, 4, turn)
    start = (LONS - SENT) * ROWS * (1 - t)
    top = ids(TILE, 0) < HALO

    def cut(i):
        at = pl.multiple_of(start + i * ROWS, ROWS)
        low, high = turned[pl.ds(at, TILE), :], turned[pl.ds(at + TILE, TILE), :]
        edges[i] = jnp.where(top, low, high)
        middle[i] = jnp.where(top, high, low)

    blocks(0, SENT, 17, cut)


def heated(turned, fixed):
    add = jnp.logical_and(jnp.logical_not(in_low(ROWS)), lax.axis_index("tm") == 0)
    return turned + jnp.where(add, fixed, 0.0)


def send_sides(turned, region, initial, table_hbm, fixed, near_sides, far_sides, table, sem):
    copy = pltpu.make_async_copy(table_hbm, table, sem)
    copy.start()
    copy.wait()

    def turn(r):
        rows = pl.ds(r, LEVELS, stride=ROWS)
        classes = region[rows, :]
        value = jnp.full(classes.shape, table[0], jnp.float32)
        for c in range(1, table.shape[0]):
            value = jnp.where(classes == c, table[c], value)
        fixed[pl.ds(r, LONS, stride=ROWS), :] = cat(value, initial[rows, :]).T

    blocks(0, ROWS, 4, turn)
    near_right = even("lon")
    low = in_low(ROWS)

    def strip(first_lon):
        def at(ref, i):
            return ref[(first_lon + i) * ROWS : (first_lon + i + 1) * ROWS, :]

        return [heated(at(turned, i), at(fixed, i)) for i in range(HALO)] + [
            jnp.where(low, at(fixed, i), swapped(at(fixed, i + 2))) for i in range(2)
        ]

    for i, (right, left) in enumerate(zip(strip(LONS - HALO), strip(0))):
        near_sides[i] = jnp.where(near_right, right, left)
        far_sides[i] = jnp.where(near_right, left, right)


def edge_pair(first, second):
    top = ids(TILE, 0) < HALO
    first_up = even("lat")
    down = jnp.where(top, first[:TILE], pltpu.roll(second[:TILE], HALO, 0))
    up = jnp.where(top, pltpu.roll(first[-TILE:], HALO, 0), second[-TILE:])
    return jnp.where(first_up, up, down), jnp.where(first_up, down, up)


def halo_tiles(near_pair, far_pair):
    first_up = even("lat")
    after = jnp.where(first_up, near_pair, far_pair)
    before = jnp.where(first_up, far_pair, near_pair)
    top = ids(TILE, 0) < HALO
    return (
        jnp.where(top, after, pltpu.roll(before, HALO, 0)),
        jnp.where(top, pltpu.roll(after, HALO, 0), before),
    )


def add_sides(turned, fixed, near_sides, far_sides, own, own_fixed, near_lat, far_lat, partner):
    t = lax.axis_index("tm")
    from_near = (t == 0) != even("lon")
    count = near_sides.shape[0]
    beside = [jnp.where(from_near, near_sides[i], far_sides[i]) for i in range(count)]
    other = [jnp.where(from_near, far_sides[i], near_sides[i]) for i in range(HALO)]
    for i in range(HALO):
        own[SENT * t + i] = beside[i]
        partner[i] = other[i]
    for i in range(2):
        own_fixed[SENT * t + i] = beside[HALO + i]
        own_fixed[SENT * t + i + 2] = swapped(beside[HALO + i])
        near_lat[PARTNER + i], far_lat[PARTNER + i] = edge_pair(other[i], other[i + 2])

    def copy(i):
        at = HALO * (1 - t) + i
        lon = (LONS - SENT) * t + i
        own[at] = heated(turned[lon], fixed[lon])
        own_fixed[at] = fixed[lon]

    blocks(0, SENT, 17, copy)

    def rows(i):
        near_lat[i], far_lat[i] = edge_pair(own[i], own[i + PAIRS])

    blocks(0, SPLIT, 13, rows)
    low = in_low(TILE)

    def fixed_rows(i):
        here = edge_pair(own_fixed[i], own_fixed[i + PAIRS])
        there = edge_pair(own_fixed[i + QUADS], own_fixed[i + PAIRS + QUADS])
        near_lat[FIXED + i], far_lat[FIXED + i] = [jnp.where(low, a, swapped(b)) for a, b in zip(here, there)]

    blocks(0, QUADS, 9, fixed_rows)


def start_of_step(fixed, rows):
    add = jnp.logical_and(jnp.logical_not(in_low(rows)), lax.axis_index("tm") == 1)
    return jnp.where(add, fixed, 0.0)


def pass_rows(edges, own, own_fixed, heated_edges, near_rows, far_rows):
    base = HALO * (1 - lax.axis_index("tm"))
    top = ids(TILE, 0) < HALO

    def heat(i):
        fixed = own_fixed[base + i]
        heated_edges[i] = edges[i] + start_of_step(jnp.where(top, fixed[:TILE], fixed[TILE:]), TILE)

    blocks(0, SENT, 17, heat)

    def rows(i):
        near_rows[i], far_rows[i] = edge_pair(heated_edges[i], heated_edges[i + SENT_PAIRS])

    blocks(0, SENT_PAIRS, 17, rows)

    def rest(i):
        near_rows[SENT_PAIRS + i], far_rows[SENT_PAIRS + i] = edge_pair(own[SPLIT + i], own[SPLIT + i + PAIRS])

    blocks(0, PAIRS - SPLIT, 10, rest)


def join(near_lat, far_lat, near_rows, far_rows, halo):
    def place(i, tiles):
        halo[i], halo[i + PAIRS] = tiles

    blocks(0, SPLIT, 13, lambda i: place(i, halo_tiles(near_lat[i], far_lat[i])))

    def rest(i):
        at = SENT_PAIRS + i
        place(SPLIT + i, halo_tiles(near_rows[at], far_rows[at]))

    blocks(0, PAIRS - SPLIT, 10, rest)


def both_steps(mine, theirs):
    first = lax.axis_index("tm") == 0
    low = in_low(mine.shape[0])
    step0, step1 = jnp.where(first, mine, theirs), jnp.where(first, theirs, mine)
    moved = swapped(step0)
    return jnp.where(low, step0, swapped(step1)), jnp.where(low, moved, step1 + moved)


def gather(edges, middle, own, own_fixed, it, source):
    base = HALO * (1 - lax.axis_index("tm"))
    top = ids(TILE, 0) < HALO

    def step(i):
        fixed = own_fixed[base + i]
        e = edges[i]
        m = middle[i] + start_of_step(jnp.where(top, fixed[TILE:], fixed[:TILE]), TILE)
        theirs = cat(jnp.where(top, e, m), jnp.where(top, m, e))
        it[base + i], source[base + i] = both_steps(own[base + i], theirs)

    blocks(0, SENT, 17, step)


def strips(partner, near_lat, far_lat, xs):
    for i in range(2):
        at = PARTNER + i
        for place, tile in zip((i, i + 2), halo_tiles(near_lat[at], far_lat[at])):
            xs[place] = cat(partner[place], tile)


def reciprocal(d):
    y = pl.reciprocal(d, approx=True)
    return y * (2.0 - d * y)


def face(a, b):
    return 2.0 * a * b * reciprocal(jnp.maximum(a + b, 1e-30))


def woven(ref, at):
    return cat(*[ref[at, pl.ds(j, TILE, stride=3), :] for j in range(3)])


def next_row(x):
    return cat(x[TILE:], pltpu.roll(x[:TILE], TILE - 1, 0))


def last_row(x):
    return cat(pltpu.roll(x[-TILE:], 1, 0), x[:-TILE])


def near(around, w):
    before, mid, after = around
    wxp, wx, wy, wyp, wl = w
    total = wxp * before + wx * after
    total = total + (wy * next_row(mid) + wyp * last_row(mid))
    return total + (wl * pltpu.roll(mid, 127, 1) + pltpu.roll(wl * mid, 1, 1))


def prepare(own_fixed, near_lat, far_lat, _, wx, wy, wyp, wl, total, inv, K):
    rows = ROWS + TILE
    low = in_low(ROWS)
    low_tile = in_low(TILE)
    beta = corner_weight ** 0.5
    K[PLACES] = jnp.zeros((rows, 128), jnp.float32)

    def assemble_fixed(i):
        for at, tile in zip((i, i + PAIRS), halo_tiles(near_lat[FIXED + i], far_lat[FIXED + i])):
            moved = swapped(tile)
            for here, value in ((at, jnp.where(low_tile, tile, moved)), (at + QUADS, jnp.where(low_tile, moved, tile))):
                main = own_fixed[here]
                K[here] = cat(jnp.where(low, main, swapped(main)), value)

    blocks(0, QUADS, 9, assemble_fixed)
    lane = ids(rows, 1)
    inside = (lane & (LEVELS - 1)) != LEVELS - 1
    shift = jnp.where(lane < LEVELS, 1.0 - beta, 1.0 + beta)
    width = 18

    def weigh(i, carry):
        start = i * width
        here = woven(K, start)
        before = wx[jnp.maximum(start - 1, 0)]
        for u in range(width):
            at = start + u
            after = woven(K, at + 1)
            side = face(here, after)
            row = face(here, next_row(here))
            previous = last_row(row)
            level = jnp.where(inside, face(here, pltpu.roll(here, 127, 1)), 0.0)
            sums = (before + side) + (row + previous) + (level + pltpu.roll(level, 1, 1))
            wx[at], wy[at], wyp[at], wl[at] = side, row, previous, level
            total[at] = sums
            inv[at] = reciprocal(shift + sums)
            here, before = after, side
        return carry

    wx[0] = jnp.zeros((rows, 128), jnp.float32)
    lax.fori_loop(0, PLACES // width, weigh, 0)


STAGES = ((1, 39, 71), (2, 38, 70), (3, 37, 69), (4, 36, 68))
WIDTHS = ((19, 12, 17, 16), (16, 16, 16, 16))
READY = 40
EDGE = 12


def iterate_half(
    upper, wx, wy, wyp, wl, total, inv, own, own_halo, it_main, source_main, near_rows, far_rows, xs, *refs
):
    if upper:
        edge, w_own, w_send, *refs = refs
    else:
        w_own, w_send, edge, *refs = refs
    it, source, spec, x, y, z, natural = refs
    rows = ROWS + TILE
    first = lax.axis_index("tm") == 0
    low = in_low(rows)
    beta = corner_weight ** 0.5
    gamma = jnp.where(low, 1.0, beta)
    shared = [(it, 38), (it, 39), (source, 39), (x, 37), (x, 38), (y, 36), (y, 37), (z, 35), (z, 36)]
    shared += [(spec, 36), (spec, 37), (spec, 38)]
    if upper:
        for i, (ref, at) in enumerate(shared):
            ref[at] = edge[i]

    t = lax.axis_index("tm")

    def assemble(second):
        def step(i):
            at = HALO * (1 - t) + i + (SENT_PAIRS if second else 0)
            a, b = both_steps(own_halo[at], halo_tiles(near_rows[i], far_rows[i])[second])
            it[at], source[at] = cat(it_main[at], a), cat(source_main[at], b)

        return step

    if upper:
        blocks(READY - HALO - SENT_PAIRS, SENT_PAIRS, 8, assemble(1))
    else:
        blocks(0, SENT_PAIRS, 17, assemble(0))
        blocks(0, READY - SENT_PAIRS, 6, assemble(1))
    for i in range(HALO):
        at = SENT * t + i
        it[at], source[at] = both_steps(cat(own[at], own_halo[at]), xs[i])

    def over(stage, read, ref, step):
        lo, hi = STAGES[stage][upper : upper + 2]
        width = WIDTHS[upper][stage]

        def body(i, carry):
            start = lo + i * width
            around = [read(ref, start - 1), read(ref, start)]
            before = wx[start - 1]
            for u in range(width):
                at = start + u
                around = [*around[-2:], read(ref, at + 1)]
                side = wx[at]
                step(at, around, (before, side, wy[at], wyp[at], wl[at]))
                before = side
            return carry

        lax.fori_loop(0, (hi - lo) // width, body, 0)

    def residual(at, around, w):
        left = (woven(source, at) - ((1.0 + total[at]) * around[1] - near(around, w))) * gamma
        moved = swapped(left)
        value = jnp.where(low, left + moved, moved - left)
        spec[at] = value
        x[at] = value * inv[at]

    over(0, woven, it, residual)

    def plain(ref, at):
        return ref[at]

    def sweep(at, around, w):
        return (spec[at] + near(around, w)) * inv[at]

    def to(ref):
        def step(at, around, w):
            ref[at] = sweep(at, around, w)

        return step

    over(1, plain, x, to(y))
    over(2, plain, y, to(z))
    base = STAGES[3][upper]
    back = jnp.where(low, 0.5, 0.5 / beta)

    def last(at, around, w):
        value = sweep(at, around, w)
        moved = swapped(value)
        value = jnp.where(low, value + moved, moved - value) * back
        for j in range(3):
            natural[pl.ds((at - base) * rows + j, TILE, stride=3), :] = value[j * TILE : (j + 1) * TILE]

    over(3, plain, z, last)
    count = HALF // 2
    for q in range(4):
        turned = cat(*[natural[pl.ds(q + 4 * j, count, stride=rows), :] for j in range(4)]).T
        step0, step1 = turned[:LEVELS], turned[LEVELS:]
        w_own[q] = jnp.where(first, step0, step1)
        w_send[q] = jnp.where(first, step1, step0)
    if not upper:
        for i, (ref, at) in enumerate(shared):
            edge[i] = ref[at]


def placed(value, j, quarter):
    return pltpu.roll(value, (32 * (quarter - j) + 128) & 127, 1)


def finish_most(it, own_low, own_high, got_low, most):
    t = lax.axis_index("tm")
    group = ids(LEVELS, 1) // 32

    def step(q):
        for j in range(4):
            rows = pl.ds(q + 4 * j, LEVELS, stride=ROWS)
            value = it[rows, :]
            for piece, quarter in ((own_low, 2 * t), (own_high, 2 * t + 1), (got_low, 2 - 2 * t)):
                value = jnp.where(group == quarter, value + placed(piece[q], j, quarter), value)
            most[rows, :] = value

    blocks(0, 4, 2, step)


def finish(most, got_high, out_hbm, out, sems):
    quarter = 3 - 2 * lax.axis_index("tm")
    part = LEVELS // CHUNKS
    here = ids(part, 1) // 32 == quarter

    def copy(c):
        span = pl.ds(pl.multiple_of(c * part * ROWS, part * ROWS), part * ROWS)
        return pltpu.make_async_copy(out.at[span], out_hbm.at[span], sems.at[c])

    def step(c):
        for q in range(4):
            value = got_high[q, pl.ds(pl.multiple_of(c * part, part), part), :]
            for j in range(4):
                rows = pl.ds(c * part * ROWS + q + 4 * j, part, stride=ROWS)
                old = most[rows, :]
                out[rows, :] = jnp.where(here, old + placed(value, j, quarter), old)
        copy(c).start()

    blocks(0, CHUNKS, 1, step)
    for c in range(CHUNKS):
        copy(c).wait()


def two_steps(iterate, heating, initial, region, cond_table):
    lats, lons = lax.axis_size("lat"), lax.axis_size("lon")
    swap = [(0, 1), (1, 0)]
    pairs = [[(i, i + 1) for i in range(start, lats - 1, 2)] for start in (0, 1)]
    pairs = [p + [(j, i) for i, j in p] for p in pairs]
    round_lon = [[(i, (i + 1) % lons) for i in range(start, lons, 2)] for start in (0, 1)]
    round_lon = [p + [(j, i) for i, j in p] for p in round_lon]
    flat = (LEVELS * ROWS, LONS)
    turned_flat = (LONS * ROWS, 2 * LEVELS)
    by_lon = (LONS, ROWS, 2 * LEVELS)
    wide = shape(PLACES, ROWS + TILE, 128)

    def in_hbm(x):
        return pltpu.with_memory_space_constraint(x, pltpu.HBM)

    half_rows = shape(SENT, TILE, 128)
    edges, middle, turned, it = call(
        send_first,
        [half_rows, half_rows, shape(*turned_flat), shape(*flat)],
        [in_hbm(iterate[0]), in_hbm(heating[0])],
        scratch=[buffer(*flat), pltpu.SemaphoreType.DMA((ROWS // TILE, 2, 2))],
        hbm_ins=(0, 1),
    )
    edges = lax.ppermute(edges, "tm", swap)
    middle = lax.ppermute(middle, "tm", swap)
    sides = shape(HALO + 2, ROWS, 128)
    fixed, near_sides, far_sides = call(
        send_sides,
        [shape(*turned_flat), sides, sides],
        [turned, region.reshape(flat), initial.reshape(flat), in_hbm(cond_table)],
        scratch=[pltpu.SMEM(cond_table.shape, jnp.float32), pltpu.SemaphoreType.DMA],
        hbm_ins=(3,),
    )
    near_sides = lax.ppermute(near_sides, "lon", round_lon[0])
    far_sides = lax.ppermute(far_sides, "lon", round_lon[1])
    main = shape(PLACES, ROWS, 128)
    lat = shape(PARTNER + 2, TILE, 128)
    own_main, own_fixed, near_lat, far_lat, partner = call(
        add_sides,
        [main, main, lat, lat, shape(HALO, ROWS, 128)],
        [turned.reshape(by_lon), fixed.reshape(by_lon), near_sides, far_sides],
    )
    near_lat = lax.ppermute(near_lat, "lat", pairs[0])
    far_lat = lax.ppermute(far_lat, "lat", pairs[1])
    rows = shape(SENT_PAIRS + PAIRS - SPLIT, TILE, 128)
    edges, near_rows, far_rows = call(pass_rows, [half_rows, rows, rows], [edges, own_main, own_fixed])
    near_rows = lax.ppermute(near_rows, "lat", pairs[0])
    far_rows = lax.ppermute(far_rows, "lat", pairs[1])
    (xs,) = call(strips, [shape(HALO, ROWS + TILE, 128)], [partner, near_lat, far_lat])
    xs = lax.ppermute(xs, "tm", swap)
    it_main, source_main = call(gather, [main, main], [edges, middle, own_main, own_fixed])
    ready = call(
        prepare,
        [wide] * 6,
        [own_fixed, near_lat, far_lat, it_main],
        scratch=[buffer(PLACES + 1, ROWS + TILE, 128)],
    )
    (own_halo,) = call(join, [shape(PLACES, TILE, 128)], [near_lat, far_lat, near_rows, far_rows])
    given = [*ready, own_main, own_halo, it_main, source_main, near_rows, far_rows, xs]
    corrections = [shape(4, LEVELS, 128)] * 2
    fields = [buffer(PLACES, ROWS + TILE, 128)] * 6 + [buffer(HALF // 2 * (ROWS + TILE), 128)]
    own_low, send_low, edge = call(
        functools.partial(iterate_half, 0),
        [*corrections, shape(EDGE, ROWS + TILE, 128)],
        given,
        scratch=fields,
        limit=16,
    )
    got_low = lax.ppermute(send_low, "tm", swap)
    own_high, send_high = call(
        functools.partial(iterate_half, 1), corrections, [*given, edge], scratch=fields, limit=16
    )
    got_high = lax.ppermute(send_high, "tm", swap)
    (most,) = call(finish_most, [shape(*flat)], [it, own_low, own_high, got_low])
    (out,) = call(
        finish,
        [shape(*flat)],
        [most, got_high],
        scratch=[buffer(*flat), pltpu.SemaphoreType.DMA((CHUNKS,))],
        hbm_outs=(0,),
    )
    return out.reshape(iterate.shape)


def solution(mesh):
    return jax.shard_map(
        two_steps if mesh.shape["tm"] == 2 else on_device,
        mesh=mesh,
        in_specs=(
            P("tm", None, "lat", "lon"),
            P("tm", None, "lat", "lon"),
            P(None, "lat", "lon"),
            P(None, "lat", "lon"),
            P(),
        ),
        out_specs=P("tm", None, "lat", "lon"),
        check_vma=False,
    )
```

```python
import functools

import jax
import jax.numpy as jnp
from jax import lax
from jax.experimental import pallas as pl
from jax.experimental.pallas import tpu as pltpu
from jax.sharding import PartitionSpec as P

SWEEPS = 4


corner_weight = 0.1


def padded(value, sides, width, wrap):
    for axis, dim in sides:
        peers, length = (lax.axis_size(axis), value.shape[dim])
        up = [(i, (i + 1) % peers) for i in range(peers if wrap else peers - 1)]
        down = [(j, i) for i, j in up]
        last = lax.slice_in_dim(value, length - width, length, axis=dim)
        initial = lax.slice_in_dim(value, 0, width, axis=dim)
        before = lax.ppermute(last, axis, up)
        after = lax.ppermute(initial, axis, down)
        value = jnp.concatenate([before, value, after], axis=dim)
    return value


def passed_along(block, axis, distance):
    devices = range(lax.axis_size(axis))
    route = [(i - distance, i) for i in devices if i - distance in devices]
    return lax.ppermute(block, axis, route)


def harmonic(first, second):
    return 2.0 * first * second / (first + second)


def conductivity(region, cond_table):
    classes = jnp.arange(cond_table.shape[0], dtype=jnp.int32)
    onehot = (region[..., None] == classes).astype(jnp.float32)
    return jnp.sum(onehot * cond_table, axis=-1)


def extend(stack):
    lat_ext = padded(stack, (("lat", 2),), 1, False)
    both = padded(lat_ext, (("lon", 3),), 1, True)
    return jnp.pad(both, ((0, 0), (1, 1), (0, 0), (0, 0)))


def face_weights(kext):
    centre = kext[1:-1, 1:-1, 1:-1]
    return (
        harmonic(centre, kext[:-2, 1:-1, 1:-1]),
        harmonic(centre, kext[2:, 1:-1, 1:-1]),
        harmonic(centre, kext[1:-1, :-2, 1:-1]),
        harmonic(centre, kext[1:-1, 2:, 1:-1]),
        harmonic(centre, kext[1:-1, 1:-1, :-2]),
        harmonic(centre, kext[1:-1, 1:-1, 2:]),
    )


def neighbours(weights, ext):
    near = weights[0] * ext[..., :-2, 1:-1, 1:-1] + weights[1] * ext[..., 2:, 1:-1, 1:-1]
    near = near + weights[2] * ext[..., 1:-1, :-2, 1:-1] + weights[3] * ext[..., 1:-1, 2:, 1:-1]
    near = near + weights[4] * ext[..., 1:-1, 1:-1, :-2] + weights[5] * ext[..., 1:-1, 1:-1, 2:]
    return near


def on_device(iterate, heating, initial, region, cond_table):
    steps = lax.axis_size("tm")
    own = lax.axis_index("tm")
    high = lax.Precision.HIGHEST
    kfield = conductivity(region, cond_table)
    ext = extend(jnp.stack([kfield, iterate[0]]))
    weights = face_weights(ext[0])
    total = weights[0] + weights[1] + weights[2] + weights[3] + weights[4] + weights[5]
    shifted = passed_along(iterate, "tm", 1)[0]
    previous = jnp.where(own == 0, initial, shifted)
    residual = heating[0] + previous - ((1.0 + total) * iterate[0] - neighbours(weights, ext[1]))
    scale_own = corner_weight ** (own.astype(jnp.float32) / steps)
    scaled = residual * scale_own
    zeros = jnp.zeros_like(residual)
    piece = lax.all_gather(scaled[None], "tm", axis=0, tiled=True)
    order = jnp.arange(piece.shape[0], dtype=jnp.int32)
    angle = 2.0 * jnp.pi / steps * (own * order % steps).astype(jnp.float32)
    real_part = jnp.einsum("n,nabc->abc", jnp.cos(angle), piece, precision=high)
    imag_part = (zeros, zeros)[1] - jnp.einsum("n,nabc->abc", jnp.sin(angle), piece, precision=high)
    beta = corner_weight ** (1.0 / steps)
    freq_angle = 2.0 * jnp.pi / steps * (own % steps).astype(jnp.float32)
    diag_re = 1.0 - beta * jnp.cos(freq_angle) + total
    diag_im = beta * jnp.sin(freq_angle) + zeros
    denom = diag_re * diag_re + diag_im * diag_im
    inv_re = diag_re / denom
    inv_im = -diag_im / denom
    sol_re = real_part * inv_re - imag_part * inv_im
    sol_im = real_part * inv_im + imag_part * inv_re
    for sweep in range(SWEEPS - 1):
        near = neighbours(weights, extend(jnp.stack([sol_re, sol_im])))
        rhs_re = real_part + near[0]
        rhs_im = imag_part + near[1]
        sol_re = rhs_re * inv_re - rhs_im * inv_im
        sol_im = rhs_re * inv_im + rhs_im * inv_re
    pieces = (
        lax.all_gather(sol_re[None], "tm", axis=0, tiled=True),
        lax.all_gather(sol_im[None], "tm", axis=0, tiled=True),
    )
    order = jnp.arange(pieces[0].shape[0], dtype=jnp.int32)
    angle = 2.0 * jnp.pi / steps * (order * own % steps).astype(jnp.float32)
    summed = jnp.einsum("k,kabc->abc", jnp.cos(angle), pieces[0], precision=high) - jnp.einsum(
        "k,kabc->abc", jnp.sin(angle), pieces[1], precision=high
    )
    back = summed / steps
    return iterate + (back / scale_own)[None]


HALO = 4
TILE = 8
LEVELS = 64
ROWS = 16
LONS = 128
HALF = 64
SENT = HALF + HALO
PLACES = HALF + 2 * HALO
PAIRS = PLACES // 2
SENT_PAIRS = SENT // 2
QUADS = PLACES // 4
SPLIT = 26
FIXED = SPLIT
PARTNER = SPLIT + QUADS
CHUNKS = 4


def specs(count, hbm):
    return [pl.BlockSpec(memory_space=pltpu.HBM if i in hbm else pltpu.VMEM) for i in range(count)]


def call(body, outs, ins, scratch=(), limit=8, hbm_ins=(), hbm_outs=()):
    moved = sum(x.size * 4 for x in ins) + sum(x.size * 4 for x in outs)
    return pl.pallas_call(
        body,
        out_shape=outs,
        in_specs=specs(len(ins), hbm_ins),
        out_specs=specs(len(outs), hbm_outs),
        scratch_shapes=scratch,
        compiler_params=pltpu.CompilerParams(vmem_limit_bytes=limit << 20),
        cost_estimate=pl.CostEstimate(flops=moved * 4, bytes_accessed=moved, transcendentals=0),
    )(*ins)


def shape(*dims):
    return jax.ShapeDtypeStruct(dims, jnp.float32)


def buffer(*dims):
    return pltpu.VMEM(dims, jnp.float32)


def ids(rows, dim):
    return lax.broadcasted_iota(jnp.int32, (rows, 128), dim)


def in_low(rows):
    return ids(rows, 1) < LEVELS


def swapped(x):
    return pltpu.roll(x, LEVELS, 1)


def main_at(i):
    return jnp.where(lax.axis_index("tm") == 0, SENT - 1 - i, i)


def outer_at(i):
    return jnp.where(lax.axis_index("tm") == 0, PLACES - 1 - i, SENT + i)


def cat(*values):
    return jnp.concatenate(values, axis=0)


def even(axis):
    return lax.rem(lax.axis_index(axis), 2) == 0


def blocks(lo, hi, width, step):
    def body(i, carry):
        for u in range(width):
            step(lo + i * width + u)
        return carry

    lax.fori_loop(0, (hi - lo) // width, body, 0)


def send_first(it_hbm, h_hbm, edges, middle, turned, it, h, sems):
    t = lax.axis_index("tm")
    by_level = (LEVELS, ROWS, LONS)
    copies = []
    for k in range(ROWS // TILE):
        for f, (source, target) in enumerate(((it_hbm, it), (h_hbm, h))):
            for c in range(2):
                part = pl.ds(c * LEVELS // 2, LEVELS // 2), pl.ds(k * TILE, TILE)
                copy = pltpu.make_async_copy(source.at[part], target.reshape(by_level).at[part], sems.at[k, f, c])
                copy.start()
                copies.append(copy)

    def turn(r):
        rows = pl.ds(r, LEVELS, stride=ROWS)
        turned[pl.ds(r, LONS, stride=ROWS), :] = cat(it[rows, :], h[rows, :]).T

    for k in range(ROWS // TILE):
        for copy in copies[4 * k : 4 * k + 4]:
            copy.wait()
        blocks(k * TILE, (k + 1) * TILE, 4, turn)
    start = (LONS - SENT) * ROWS * (1 - t)
    top = ids(TILE, 0) < HALO

    def cut(i):
        at = pl.multiple_of(start + i * ROWS, ROWS)
        low, high = turned[pl.ds(at, TILE), :], turned[pl.ds(at + TILE, TILE), :]
        edges[i] = jnp.where(top, low, high)
        middle[i] = jnp.where(top, high, low)

    blocks(0, SENT, 17, cut)


def heated(turned, fixed):
    add = jnp.logical_and(jnp.logical_not(in_low(ROWS)), lax.axis_index("tm") == 0)
    return turned + jnp.where(add, fixed, 0.0)


def send_sides(turned, region, initial, table_hbm, fixed, near_sides, far_sides, table, sem):
    copy = pltpu.make_async_copy(table_hbm, table, sem)
    copy.start()
    copy.wait()

    def turn(r):
        rows = pl.ds(r, LEVELS, stride=ROWS)
        classes = region[rows, :]
        value = jnp.full(classes.shape, table[0], jnp.float32)
        for c in range(1, table.shape[0]):
            value = jnp.where(classes == c, table[c], value)
        fixed[pl.ds(r, LONS, stride=ROWS), :] = cat(value, initial[rows, :]).T

    blocks(0, ROWS, 4, turn)
    near_right = even("lon")
    low = in_low(ROWS)

    def strip(first_lon):
        def at(ref, i):
            return ref[(first_lon + i) * ROWS : (first_lon + i + 1) * ROWS, :]

        return [heated(at(turned, i), at(fixed, i)) for i in range(HALO)] + [
            jnp.where(low, at(fixed, i), swapped(at(fixed, i + 2))) for i in range(2)
        ]

    for i, (right, left) in enumerate(zip(strip(LONS - HALO), strip(0))):
        near_sides[i] = jnp.where(near_right, right, left)
        far_sides[i] = jnp.where(near_right, left, right)


def edge_pair(first, second):
    top = ids(TILE, 0) < HALO
    first_up = even("lat")
    down = jnp.where(top, first[:TILE], pltpu.roll(second[:TILE], HALO, 0))
    up = jnp.where(top, pltpu.roll(first[-TILE:], HALO, 0), second[-TILE:])
    return jnp.where(first_up, up, down), jnp.where(first_up, down, up)


def halo_tiles(near_pair, far_pair):
    first_up = even("lat")
    after = jnp.where(first_up, near_pair, far_pair)
    before = jnp.where(first_up, far_pair, near_pair)
    top = ids(TILE, 0) < HALO
    return (
        jnp.where(top, after, pltpu.roll(before, HALO, 0)),
        jnp.where(top, pltpu.roll(after, HALO, 0), before),
    )


def add_sides(turned, fixed, near_sides, far_sides, own, own_fixed, near_lat, far_lat, partner):
    t = lax.axis_index("tm")
    from_near = (t == 0) != even("lon")
    count = near_sides.shape[0]
    beside = [jnp.where(from_near, near_sides[i], far_sides[i]) for i in range(count)]
    other = [jnp.where(from_near, far_sides[i], near_sides[i]) for i in range(HALO)]
    for i in range(HALO):
        own[outer_at(i)] = beside[i]
        partner[i] = other[i]
    for i in range(2):
        own_fixed[outer_at(i)] = beside[HALO + i]
        own_fixed[outer_at(i + 2)] = swapped(beside[HALO + i])
        near_lat[PARTNER + i], far_lat[PARTNER + i] = edge_pair(other[i], other[i + 2])

    def copy(i):
        at = main_at(i)
        lon = (LONS - SENT) * t + i
        own[at] = heated(turned[lon], fixed[lon])
        own_fixed[at] = fixed[lon]

    blocks(0, SENT, 17, copy)

    def rows(i):
        near_lat[i], far_lat[i] = edge_pair(own[i], own[i + PAIRS])

    blocks(0, SPLIT, 13, rows)
    low = in_low(TILE)

    def fixed_rows(i):
        here = edge_pair(own_fixed[i], own_fixed[i + PAIRS])
        there = edge_pair(own_fixed[i + QUADS], own_fixed[i + PAIRS + QUADS])
        near_lat[FIXED + i], far_lat[FIXED + i] = [jnp.where(low, a, swapped(b)) for a, b in zip(here, there)]

    blocks(0, QUADS, 9, fixed_rows)


def start_of_step(fixed, rows):
    add = jnp.logical_and(jnp.logical_not(in_low(rows)), lax.axis_index("tm") == 1)
    return jnp.where(add, fixed, 0.0)


def pass_rows(edges, own, own_fixed, heated_edges, near_rows, far_rows):
    top = ids(TILE, 0) < HALO

    def heat(i):
        fixed = own_fixed[main_at(i)]
        heated_edges[i] = edges[i] + start_of_step(jnp.where(top, fixed[:TILE], fixed[TILE:]), TILE)

    blocks(0, SENT, 17, heat)

    def rows(i):
        near_rows[i], far_rows[i] = edge_pair(heated_edges[i], heated_edges[i + SENT_PAIRS])

    blocks(0, SENT_PAIRS, 17, rows)

    def rest(i):
        near_rows[SENT_PAIRS + i], far_rows[SENT_PAIRS + i] = edge_pair(own[SPLIT + i], own[SPLIT + i + PAIRS])

    blocks(0, PAIRS - SPLIT, 10, rest)


def join(near_lat, far_lat, near_rows, far_rows, halo, other):
    def place(i, tiles):
        halo[i], halo[i + PAIRS] = tiles

    blocks(0, SPLIT, 13, lambda i: place(i, halo_tiles(near_lat[i], far_lat[i])))

    def rest(i):
        at = SENT_PAIRS + i
        place(SPLIT + i, halo_tiles(near_rows[at], far_rows[at]))

    blocks(0, PAIRS - SPLIT, 10, rest)

    def theirs(i):
        other[main_at(i)], other[main_at(i + SENT_PAIRS)] = halo_tiles(near_rows[i], far_rows[i])

    blocks(0, SENT_PAIRS, 17, theirs)


def both_steps(mine, theirs):
    first = lax.axis_index("tm") == 0
    low = in_low(mine.shape[0])
    step0, step1 = jnp.where(first, mine, theirs), jnp.where(first, theirs, mine)
    moved = swapped(step0)
    return jnp.where(low, step0, swapped(step1)), jnp.where(low, moved, step1 + moved)


def gather(edges, middle, own, own_fixed, it, source):
    top = ids(TILE, 0) < HALO

    def step(i):
        at = main_at(i)
        fixed = own_fixed[at]
        e = edges[i]
        m = middle[i] + start_of_step(jnp.where(top, fixed[TILE:], fixed[:TILE]), TILE)
        theirs = cat(jnp.where(top, e, m), jnp.where(top, m, e))
        it[at], source[at] = both_steps(own[at], theirs)

    blocks(0, SENT, 17, step)


def strips(partner, near_lat, far_lat, xs):
    for i in range(2):
        at = PARTNER + i
        for place, tile in zip((i, i + 2), halo_tiles(near_lat[at], far_lat[at])):
            xs[place] = cat(partner[place], tile)


def reciprocal(d):
    y = pl.reciprocal(d, approx=True)
    return y * (2.0 - d * y)


def face(a, b):
    return 2.0 * a * b * reciprocal(jnp.maximum(a + b, 1e-30))


def woven(ref, at):
    return cat(*[ref[at, pl.ds(j, TILE, stride=3), :] for j in range(3)])


def next_row(x):
    return cat(x[TILE:], pltpu.roll(x[:TILE], TILE - 1, 0))


def last_row(x):
    return cat(pltpu.roll(x[-TILE:], 1, 0), x[:-TILE])


def near(around, w):
    before, mid, after = around
    wxp, wx, wy, wyp, wl = w
    total = wxp * before + wx * after
    total = total + (wy * next_row(mid) + wyp * last_row(mid))
    return total + (wl * pltpu.roll(mid, 127, 1) + pltpu.roll(wl * mid, 1, 1))


def prepare(own_fixed, near_lat, far_lat, _, wx, wy, wyp, wl, total, inv, K):
    rows = ROWS + TILE
    low = in_low(ROWS)
    low_tile = in_low(TILE)
    beta = corner_weight ** 0.5
    K[PLACES] = jnp.zeros((rows, 128), jnp.float32)

    def assemble_fixed(i):
        for at, tile in zip((i, i + PAIRS), halo_tiles(near_lat[FIXED + i], far_lat[FIXED + i])):
            moved = swapped(tile)
            for here, value in ((at, jnp.where(low_tile, tile, moved)), (at + QUADS, jnp.where(low_tile, moved, tile))):
                main = own_fixed[here]
                K[here] = cat(jnp.where(low, main, swapped(main)), value)

    blocks(0, QUADS, 9, assemble_fixed)
    lane = ids(rows, 1)
    inside = (lane & (LEVELS - 1)) != LEVELS - 1
    shift = jnp.where(lane < LEVELS, 1.0 - beta, 1.0 + beta)
    width = 18

    def weigh(i, carry):
        start = i * width
        here = woven(K, start)
        before = wx[jnp.maximum(start - 1, 0)]
        for u in range(width):
            at = start + u
            after = woven(K, at + 1)
            side = face(here, after)
            row = face(here, next_row(here))
            previous = last_row(row)
            level = jnp.where(inside, face(here, pltpu.roll(here, 127, 1)), 0.0)
            sums = (before + side) + (row + previous) + (level + pltpu.roll(level, 1, 1))
            wx[at], wy[at], wyp[at], wl[at] = side, row, previous, level
            total[at] = sums
            inv[at] = reciprocal(shift + sums)
            here, before = after, side
        return carry

    wx[0] = jnp.zeros((rows, 128), jnp.float32)
    lax.fori_loop(0, PLACES // width, weigh, 0)


STAGES = ((1, 39, 71), (2, 38, 70), (3, 37, 69), (4, 36, 68))
WIDTHS = ((19, 12, 17, 16), (16, 16, 16, 16))
READY = 40
EDGE = 12


def iterate_half(
    upper, wx, wy, wyp, wl, total, inv, own, own_halo, other_halo, it_main, source_main, *refs
):
    if upper:
        xs, edge, w_own, w_send, *refs = refs
    else:
        w_own, w_send, edge, *refs = refs
    it, source, spec, x, y, z, natural = refs
    rows = ROWS + TILE
    first = lax.axis_index("tm") == 0
    low = in_low(rows)
    beta = corner_weight ** 0.5
    gamma = jnp.where(low, 1.0, beta)
    shared = [(it, 38), (it, 39), (source, 39), (x, 37), (x, 38), (y, 36), (y, 37), (z, 35), (z, 36)]
    shared += [(spec, 36), (spec, 37), (spec, 38)]
    if upper:
        for i, (ref, at) in enumerate(shared):
            ref[at] = edge[i]

    def assemble(at):
        a, b = both_steps(own_halo[at], other_halo[at])
        it[at], source[at] = cat(it_main[at], a), cat(source_main[at], b)

    if upper:
        blocks(READY, SENT, 14, assemble)
        for i in range(HALO):
            at = outer_at(i)
            it[at], source[at] = both_steps(cat(own[at], own_halo[at]), xs[i])
    else:
        blocks(0, READY, 10, assemble)

    def over(stage, read, ref, step):
        lo, hi = STAGES[stage][upper : upper + 2]
        width = WIDTHS[upper][stage]

        def body(i, carry):
            start = lo + i * width
            around = [read(ref, start - 1), read(ref, start)]
            before = wx[start - 1]
            for u in range(width):
                at = start + u
                around = [*around[-2:], read(ref, at + 1)]
                side = wx[at]
                step(at, around, (before, side, wy[at], wyp[at], wl[at]))
                before = side
            return carry

        lax.fori_loop(0, (hi - lo) // width, body, 0)

    def residual(at, around, w):
        left = (woven(source, at) - ((1.0 + total[at]) * around[1] - near(around, w))) * gamma
        moved = swapped(left)
        value = jnp.where(low, left + moved, moved - left)
        spec[at] = value
        x[at] = value * inv[at]

    over(0, woven, it, residual)

    def plain(ref, at):
        return ref[at]

    def sweep(at, around, w):
        return (spec[at] + near(around, w)) * inv[at]

    def to(ref):
        def step(at, around, w):
            ref[at] = sweep(at, around, w)

        return step

    over(1, plain, x, to(y))
    over(2, plain, y, to(z))
    base = STAGES[3][upper]
    back = jnp.where(low, 0.5, 0.5 / beta)

    def last(at, around, w):
        value = sweep(at, around, w)
        moved = swapped(value)
        value = jnp.where(low, value + moved, moved - value) * back
        lon = at - base
        lon = jnp.where(first, HALF // 2 - 1 - lon, lon)
        for j in range(3):
            natural[pl.ds(lon * rows + j, TILE, stride=3), :] = value[j * TILE : (j + 1) * TILE]

    over(3, plain, z, last)
    count = HALF // 2
    for q in range(4):
        turned = cat(*[natural[pl.ds(q + 4 * j, count, stride=rows), :] for j in range(4)]).T
        step0, step1 = turned[:LEVELS], turned[LEVELS:]
        w_own[q] = jnp.where(first, step0, step1)
        w_send[q] = jnp.where(first, step1, step0)
    if not upper:
        for i, (ref, at) in enumerate(shared):
            edge[i] = ref[at]


def placed(value, j, quarter):
    return pltpu.roll(value, (32 * (quarter - j) + 128) & 127, 1)


def finish_most(it, own_low, own_high, got_low, most):
    t = lax.axis_index("tm")
    group = ids(LEVELS, 1) // 32

    def step(q):
        for j in range(4):
            rows = pl.ds(q + 4 * j, LEVELS, stride=ROWS)
            value = it[rows, :]
            for piece, quarter in ((own_low, 1 + t), (own_high, 3 * t), (got_low, 2 - t)):
                value = jnp.where(group == quarter, value + placed(piece[q], j, quarter), value)
            most[rows, :] = value

    blocks(0, 4, 2, step)


def finish(most, got_high, out_hbm, out, sems):
    quarter = 3 - 3 * lax.axis_index("tm")
    part = LEVELS // CHUNKS
    here = ids(part, 1) // 32 == quarter

    def copy(c):
        span = pl.ds(pl.multiple_of(c * part * ROWS, part * ROWS), part * ROWS)
        return pltpu.make_async_copy(out.at[span], out_hbm.at[span], sems.at[c])

    def step(c):
        for q in range(4):
            value = got_high[q, pl.ds(pl.multiple_of(c * part, part), part), :]
            for j in range(4):
                rows = pl.ds(c * part * ROWS + q + 4 * j, part, stride=ROWS)
                old = most[rows, :]
                out[rows, :] = jnp.where(here, old + placed(value, j, quarter), old)
        copy(c).start()

    blocks(0, CHUNKS, 1, step)
    for c in range(CHUNKS):
        copy(c).wait()


def two_steps(iterate, heating, initial, region, cond_table):
    lats, lons = lax.axis_size("lat"), lax.axis_size("lon")
    swap = [(0, 1), (1, 0)]
    pairs = [[(i, i + 1) for i in range(start, lats - 1, 2)] for start in (0, 1)]
    pairs = [p + [(j, i) for i, j in p] for p in pairs]
    round_lon = [[(i, (i + 1) % lons) for i in range(start, lons, 2)] for start in (0, 1)]
    round_lon = [p + [(j, i) for i, j in p] for p in round_lon]
    flat = (LEVELS * ROWS, LONS)
    turned_flat = (LONS * ROWS, 2 * LEVELS)
    by_lon = (LONS, ROWS, 2 * LEVELS)
    wide = shape(PLACES, ROWS + TILE, 128)

    def in_hbm(x):
        return pltpu.with_memory_space_constraint(x, pltpu.HBM)

    half_rows = shape(SENT, TILE, 128)
    edges, middle, turned, it = call(
        send_first,
        [half_rows, half_rows, shape(*turned_flat), shape(*flat)],
        [in_hbm(iterate[0]), in_hbm(heating[0])],
        scratch=[buffer(*flat), pltpu.SemaphoreType.DMA((ROWS // TILE, 2, 2))],
        hbm_ins=(0, 1),
    )
    edges = lax.ppermute(edges, "tm", swap)
    middle = lax.ppermute(middle, "tm", swap)
    sides = shape(HALO + 2, ROWS, 128)
    fixed, near_sides, far_sides = call(
        send_sides,
        [shape(*turned_flat), sides, sides],
        [turned, region.reshape(flat), initial.reshape(flat), in_hbm(cond_table)],
        scratch=[pltpu.SMEM(cond_table.shape, jnp.float32), pltpu.SemaphoreType.DMA],
        hbm_ins=(3,),
    )
    near_sides = lax.ppermute(near_sides, "lon", round_lon[0])
    far_sides = lax.ppermute(far_sides, "lon", round_lon[1])
    main = shape(PLACES, ROWS, 128)
    lat = shape(PARTNER + 2, TILE, 128)
    own_main, own_fixed, near_lat, far_lat, partner = call(
        add_sides,
        [main, main, lat, lat, shape(HALO, ROWS, 128)],
        [turned.reshape(by_lon), fixed.reshape(by_lon), near_sides, far_sides],
    )
    near_lat = lax.ppermute(near_lat, "lat", pairs[0])
    far_lat = lax.ppermute(far_lat, "lat", pairs[1])
    rows = shape(SENT_PAIRS + PAIRS - SPLIT, TILE, 128)
    edges, near_rows, far_rows = call(pass_rows, [half_rows, rows, rows], [edges, own_main, own_fixed])
    near_rows = lax.ppermute(near_rows, "lat", pairs[0])
    far_rows = lax.ppermute(far_rows, "lat", pairs[1])
    it_main, source_main = call(gather, [main, main], [edges, middle, own_main, own_fixed])
    (xs,) = call(strips, [shape(HALO, ROWS + TILE, 128)], [partner, near_lat, far_lat])
    xs = lax.ppermute(xs, "tm", swap)
    ready = call(
        prepare,
        [wide] * 6,
        [own_fixed, near_lat, far_lat, it_main],
        scratch=[buffer(PLACES + 1, ROWS + TILE, 128)],
    )
    halos = call(join, [shape(PLACES, TILE, 128)] * 2, [near_lat, far_lat, near_rows, far_rows])
    given = [*ready, own_main, *halos, it_main, source_main]
    corrections = [shape(4, LEVELS, 128)] * 2
    fields = [buffer(PLACES, ROWS + TILE, 128)] * 6 + [buffer(HALF // 2 * (ROWS + TILE), 128)]
    own_low, send_low, edge = call(
        functools.partial(iterate_half, 0),
        [*corrections, shape(EDGE, ROWS + TILE, 128)],
        given,
        scratch=fields,
        limit=16,
    )
    got_low = lax.ppermute(send_low, "tm", swap)
    own_high, send_high = call(
        functools.partial(iterate_half, 1), corrections, [*given, xs, edge], scratch=fields, limit=16
    )
    got_high = lax.ppermute(send_high, "tm", swap)
    (most,) = call(finish_most, [shape(*flat)], [it, own_low, own_high, got_low])
    (out,) = call(
        finish,
        [shape(*flat)],
        [most, got_high],
        scratch=[buffer(*flat), pltpu.SemaphoreType.DMA((CHUNKS,))],
        hbm_outs=(0,),
    )
    return out.reshape(iterate.shape)


def solution(mesh):
    return jax.shard_map(
        two_steps if mesh.shape["tm"] == 2 else on_device,
        mesh=mesh,
        in_specs=(
            P("tm", None, "lat", "lon"),
            P("tm", None, "lat", "lon"),
            P(None, "lat", "lon"),
            P(None, "lat", "lon"),
            P(),
        ),
        out_specs=P("tm", None, "lat", "lon"),
        check_vma=False,
    )
```

```python
import functools

import jax
import jax.numpy as jnp
from jax import lax
from jax.experimental import pallas as pl
from jax.experimental.pallas import tpu as pltpu
from jax.sharding import PartitionSpec as P

SWEEPS = 4


corner_weight = 0.1


def padded(value, sides, width, wrap):
    for axis, dim in sides:
        peers, length = (lax.axis_size(axis), value.shape[dim])
        up = [(i, (i + 1) % peers) for i in range(peers if wrap else peers - 1)]
        down = [(j, i) for i, j in up]
        last = lax.slice_in_dim(value, length - width, length, axis=dim)
        initial = lax.slice_in_dim(value, 0, width, axis=dim)
        before = lax.ppermute(last, axis, up)
        after = lax.ppermute(initial, axis, down)
        value = jnp.concatenate([before, value, after], axis=dim)
    return value


def passed_along(block, axis, distance):
    devices = range(lax.axis_size(axis))
    route = [(i - distance, i) for i in devices if i - distance in devices]
    return lax.ppermute(block, axis, route)


def harmonic(first, second):
    return 2.0 * first * second / (first + second)


def conductivity(region, cond_table):
    classes = jnp.arange(cond_table.shape[0], dtype=jnp.int32)
    onehot = (region[..., None] == classes).astype(jnp.float32)
    return jnp.sum(onehot * cond_table, axis=-1)


def extend(stack):
    lat_ext = padded(stack, (("lat", 2),), 1, False)
    both = padded(lat_ext, (("lon", 3),), 1, True)
    return jnp.pad(both, ((0, 0), (1, 1), (0, 0), (0, 0)))


def face_weights(kext):
    centre = kext[1:-1, 1:-1, 1:-1]
    return (
        harmonic(centre, kext[:-2, 1:-1, 1:-1]),
        harmonic(centre, kext[2:, 1:-1, 1:-1]),
        harmonic(centre, kext[1:-1, :-2, 1:-1]),
        harmonic(centre, kext[1:-1, 2:, 1:-1]),
        harmonic(centre, kext[1:-1, 1:-1, :-2]),
        harmonic(centre, kext[1:-1, 1:-1, 2:]),
    )


def neighbours(weights, ext):
    near = weights[0] * ext[..., :-2, 1:-1, 1:-1] + weights[1] * ext[..., 2:, 1:-1, 1:-1]
    near = near + weights[2] * ext[..., 1:-1, :-2, 1:-1] + weights[3] * ext[..., 1:-1, 2:, 1:-1]
    near = near + weights[4] * ext[..., 1:-1, 1:-1, :-2] + weights[5] * ext[..., 1:-1, 1:-1, 2:]
    return near


def on_device(iterate, heating, initial, region, cond_table):
    steps = lax.axis_size("tm")
    own = lax.axis_index("tm")
    high = lax.Precision.HIGHEST
    kfield = conductivity(region, cond_table)
    ext = extend(jnp.stack([kfield, iterate[0]]))
    weights = face_weights(ext[0])
    total = weights[0] + weights[1] + weights[2] + weights[3] + weights[4] + weights[5]
    shifted = passed_along(iterate, "tm", 1)[0]
    previous = jnp.where(own == 0, initial, shifted)
    residual = heating[0] + previous - ((1.0 + total) * iterate[0] - neighbours(weights, ext[1]))
    scale_own = corner_weight ** (own.astype(jnp.float32) / steps)
    scaled = residual * scale_own
    zeros = jnp.zeros_like(residual)
    piece = lax.all_gather(scaled[None], "tm", axis=0, tiled=True)
    order = jnp.arange(piece.shape[0], dtype=jnp.int32)
    angle = 2.0 * jnp.pi / steps * (own * order % steps).astype(jnp.float32)
    real_part = jnp.einsum("n,nabc->abc", jnp.cos(angle), piece, precision=high)
    imag_part = (zeros, zeros)[1] - jnp.einsum("n,nabc->abc", jnp.sin(angle), piece, precision=high)
    beta = corner_weight ** (1.0 / steps)
    freq_angle = 2.0 * jnp.pi / steps * (own % steps).astype(jnp.float32)
    diag_re = 1.0 - beta * jnp.cos(freq_angle) + total
    diag_im = beta * jnp.sin(freq_angle) + zeros
    denom = diag_re * diag_re + diag_im * diag_im
    inv_re = diag_re / denom
    inv_im = -diag_im / denom
    sol_re = real_part * inv_re - imag_part * inv_im
    sol_im = real_part * inv_im + imag_part * inv_re
    for sweep in range(SWEEPS - 1):
        near = neighbours(weights, extend(jnp.stack([sol_re, sol_im])))
        rhs_re = real_part + near[0]
        rhs_im = imag_part + near[1]
        sol_re = rhs_re * inv_re - rhs_im * inv_im
        sol_im = rhs_re * inv_im + rhs_im * inv_re
    pieces = (
        lax.all_gather(sol_re[None], "tm", axis=0, tiled=True),
        lax.all_gather(sol_im[None], "tm", axis=0, tiled=True),
    )
    order = jnp.arange(pieces[0].shape[0], dtype=jnp.int32)
    angle = 2.0 * jnp.pi / steps * (order * own % steps).astype(jnp.float32)
    summed = jnp.einsum("k,kabc->abc", jnp.cos(angle), pieces[0], precision=high) - jnp.einsum(
        "k,kabc->abc", jnp.sin(angle), pieces[1], precision=high
    )
    back = summed / steps
    return iterate + (back / scale_own)[None]


HALO = 4
TILE = 8
LEVELS = 64
ROWS = 16
LONS = 128
HALF = 64
SENT = HALF + HALO
PLACES = HALF + 2 * HALO
PAIRS = PLACES // 2
SENT_PAIRS = SENT // 2
QUADS = PLACES // 4
SPLIT = 26
FIXED = SPLIT
PARTNER = SPLIT + QUADS
CHUNKS = 4


def specs(count, hbm):
    return [pl.BlockSpec(memory_space=pltpu.HBM if i in hbm else pltpu.VMEM) for i in range(count)]


def call(body, outs, ins, scratch=(), limit=8, hbm_ins=(), hbm_outs=()):
    moved = sum(x.size * 4 for x in ins) + sum(x.size * 4 for x in outs)
    return pl.pallas_call(
        body,
        out_shape=outs,
        in_specs=specs(len(ins), hbm_ins),
        out_specs=specs(len(outs), hbm_outs),
        scratch_shapes=scratch,
        compiler_params=pltpu.CompilerParams(vmem_limit_bytes=limit << 20),
        cost_estimate=pl.CostEstimate(flops=moved * 4, bytes_accessed=moved, transcendentals=0),
    )(*ins)


def shape(*dims):
    return jax.ShapeDtypeStruct(dims, jnp.float32)


def buffer(*dims):
    return pltpu.VMEM(dims, jnp.float32)


def ids(rows, dim):
    return lax.broadcasted_iota(jnp.int32, (rows, 128), dim)


def in_low(rows):
    return ids(rows, 1) < LEVELS


def swapped(x):
    return pltpu.roll(x, LEVELS, 1)


def main_at(i):
    return jnp.where(lax.axis_index("tm") == 0, SENT - 1 - i, i)


def outer_at(i):
    return jnp.where(lax.axis_index("tm") == 0, PLACES - 1 - i, SENT + i)


def cat(*values):
    return jnp.concatenate(values, axis=0)


def even(axis):
    return lax.rem(lax.axis_index(axis), 2) == 0


def blocks(lo, hi, width, step):
    def body(i, carry):
        for u in range(width):
            step(lo + i * width + u)
        return carry

    lax.fori_loop(0, (hi - lo) // width, body, 0)


def send_first(it_hbm, h_hbm, edges, middle, turned, it, h, sems):
    t = lax.axis_index("tm")
    by_level = (LEVELS, ROWS, LONS)
    copies = []
    for k in range(ROWS // TILE):
        for f, (source, target) in enumerate(((it_hbm, it), (h_hbm, h))):
            for c in range(2):
                part = pl.ds(c * LEVELS // 2, LEVELS // 2), pl.ds(k * TILE, TILE)
                copy = pltpu.make_async_copy(source.at[part], target.reshape(by_level).at[part], sems.at[k, f, c])
                copy.start()
                copies.append(copy)

    def turn(r):
        rows = pl.ds(r, LEVELS, stride=ROWS)
        turned[pl.ds(r, LONS, stride=ROWS), :] = cat(it[rows, :], h[rows, :]).T

    for k in range(ROWS // TILE):
        for copy in copies[4 * k : 4 * k + 4]:
            copy.wait()
        blocks(k * TILE, (k + 1) * TILE, 4, turn)
    start = (LONS - SENT) * ROWS * (1 - t)
    top = ids(TILE, 0) < HALO

    def cut(i):
        at = pl.multiple_of(start + i * ROWS, ROWS)
        low, high = turned[pl.ds(at, TILE), :], turned[pl.ds(at + TILE, TILE), :]
        edges[i] = jnp.where(top, low, high)
        middle[i] = jnp.where(top, high, low)

    blocks(0, SENT, 17, cut)


def heated(turned, fixed):
    add = jnp.logical_and(jnp.logical_not(in_low(ROWS)), lax.axis_index("tm") == 0)
    return turned + jnp.where(add, fixed, 0.0)


def send_sides(turned, region, initial, table_hbm, fixed, near_sides, far_sides, table, sem):
    copy = pltpu.make_async_copy(table_hbm, table, sem)
    copy.start()
    copy.wait()

    def turn(r):
        rows = pl.ds(r, LEVELS, stride=ROWS)
        classes = region[rows, :]
        value = jnp.full(classes.shape, table[0], jnp.float32)
        for c in range(1, table.shape[0]):
            value = jnp.where(classes == c, table[c], value)
        fixed[pl.ds(r, LONS, stride=ROWS), :] = cat(value, initial[rows, :]).T

    blocks(0, ROWS, 4, turn)
    near_right = even("lon")
    low = in_low(ROWS)

    def strip(first_lon):
        def at(ref, i):
            return ref[(first_lon + i) * ROWS : (first_lon + i + 1) * ROWS, :]

        return [heated(at(turned, i), at(fixed, i)) for i in range(HALO)] + [
            jnp.where(low, at(fixed, i), swapped(at(fixed, i + 2))) for i in range(2)
        ]

    for i, (right, left) in enumerate(zip(strip(LONS - HALO), strip(0))):
        near_sides[i] = jnp.where(near_right, right, left)
        far_sides[i] = jnp.where(near_right, left, right)


def edge_pair(first, second):
    top = ids(TILE, 0) < HALO
    first_up = even("lat")
    down = jnp.where(top, first[:TILE], pltpu.roll(second[:TILE], HALO, 0))
    up = jnp.where(top, pltpu.roll(first[-TILE:], HALO, 0), second[-TILE:])
    return jnp.where(first_up, up, down), jnp.where(first_up, down, up)


def halo_tiles(near_pair, far_pair):
    first_up = even("lat")
    after = jnp.where(first_up, near_pair, far_pair)
    before = jnp.where(first_up, far_pair, near_pair)
    top = ids(TILE, 0) < HALO
    return (
        jnp.where(top, after, pltpu.roll(before, HALO, 0)),
        jnp.where(top, pltpu.roll(after, HALO, 0), before),
    )


def add_sides(turned, fixed, near_sides, far_sides, own, own_fixed, near_lat, far_lat, partner):
    t = lax.axis_index("tm")
    from_near = (t == 0) != even("lon")
    count = near_sides.shape[0]
    beside = [jnp.where(from_near, near_sides[i], far_sides[i]) for i in range(count)]
    other = [jnp.where(from_near, far_sides[i], near_sides[i]) for i in range(HALO)]
    for i in range(HALO):
        own[outer_at(i)] = beside[i]
        partner[i] = other[i]
    for i in range(2):
        own_fixed[outer_at(i)] = beside[HALO + i]
        own_fixed[outer_at(i + 2)] = swapped(beside[HALO + i])
        near_lat[PARTNER + i], far_lat[PARTNER + i] = edge_pair(other[i], other[i + 2])

    def copy(i):
        at = main_at(i)
        lon = (LONS - SENT) * t + i
        own[at] = heated(turned[lon], fixed[lon])
        own_fixed[at] = fixed[lon]

    blocks(0, SENT, 17, copy)

    def rows(i):
        near_lat[i], far_lat[i] = edge_pair(own[i], own[i + PAIRS])

    blocks(0, SPLIT, 13, rows)
    low = in_low(TILE)

    def fixed_rows(i):
        here = edge_pair(own_fixed[i], own_fixed[i + PAIRS])
        there = edge_pair(own_fixed[i + QUADS], own_fixed[i + PAIRS + QUADS])
        near_lat[FIXED + i], far_lat[FIXED + i] = [jnp.where(low, a, swapped(b)) for a, b in zip(here, there)]

    blocks(0, QUADS, 9, fixed_rows)


def start_of_step(fixed, rows):
    add = jnp.logical_and(jnp.logical_not(in_low(rows)), lax.axis_index("tm") == 1)
    return jnp.where(add, fixed, 0.0)


def pass_rows(edges, own, own_fixed, heated_edges, near_rows, far_rows):
    top = ids(TILE, 0) < HALO

    def heat(i):
        fixed = own_fixed[main_at(i)]
        heated_edges[i] = edges[i] + start_of_step(jnp.where(top, fixed[:TILE], fixed[TILE:]), TILE)

    blocks(0, SENT, 17, heat)

    def rows(i):
        near_rows[i], far_rows[i] = edge_pair(heated_edges[i], heated_edges[i + SENT_PAIRS])

    blocks(0, SENT_PAIRS, 17, rows)

    def rest(i):
        near_rows[SENT_PAIRS + i], far_rows[SENT_PAIRS + i] = edge_pair(own[SPLIT + i], own[SPLIT + i + PAIRS])

    blocks(0, PAIRS - SPLIT, 10, rest)


def join(near_lat, far_lat, near_rows, far_rows, halo, other):
    def place(i, tiles):
        halo[i], halo[i + PAIRS] = tiles

    blocks(0, SPLIT, 13, lambda i: place(i, halo_tiles(near_lat[i], far_lat[i])))

    def rest(i):
        at = SENT_PAIRS + i
        place(SPLIT + i, halo_tiles(near_rows[at], far_rows[at]))

    blocks(0, PAIRS - SPLIT, 10, rest)

    def theirs(i):
        other[main_at(i)], other[main_at(i + SENT_PAIRS)] = halo_tiles(near_rows[i], far_rows[i])

    blocks(0, SENT_PAIRS, 17, theirs)


def both_steps(mine, theirs):
    first = lax.axis_index("tm") == 0
    low = in_low(mine.shape[0])
    step0, step1 = jnp.where(first, mine, theirs), jnp.where(first, theirs, mine)
    moved = swapped(step0)
    return jnp.where(low, step0, swapped(step1)), jnp.where(low, moved, step1 + moved)


def gather(edges, middle, own, own_fixed, it, source):
    top = ids(TILE, 0) < HALO

    def step(i):
        at = main_at(i)
        fixed = own_fixed[at]
        e = edges[i]
        m = middle[i] + start_of_step(jnp.where(top, fixed[TILE:], fixed[:TILE]), TILE)
        theirs = cat(jnp.where(top, e, m), jnp.where(top, m, e))
        it[at], source[at] = both_steps(own[at], theirs)

    blocks(0, SENT, 17, step)


def strips(partner, near_lat, far_lat, xs):
    for i in range(2):
        at = PARTNER + i
        for place, tile in zip((i, i + 2), halo_tiles(near_lat[at], far_lat[at])):
            xs[place] = cat(partner[place], tile)


def reciprocal(d):
    y = pl.reciprocal(d, approx=True)
    return y * (2.0 - d * y)


def face(a, b, twice):
    return twice * b * reciprocal(jnp.maximum(a + b, 1e-30))


def woven(ref, at):
    return cat(*[ref[at, pl.ds(j, TILE, stride=3), :] for j in range(3)])


def next_row(x):
    return cat(x[TILE:], pltpu.roll(x[:TILE], TILE - 1, 0))


def last_row(x):
    return cat(pltpu.roll(x[-TILE:], 1, 0), x[:-TILE])


def near(around, w):
    before, mid, after = around
    wxp, wx, wy, wyp, wl = w
    total = wxp * before + wx * after
    total = total + (wy * next_row(mid) + wyp * last_row(mid))
    return total + (wl * pltpu.roll(mid, 127, 1) + pltpu.roll(wl * mid, 1, 1))


def prepare(own_fixed, near_lat, far_lat, _, wx, wy, wyp, wl, total, inv, K):
    rows = ROWS + TILE
    low = in_low(ROWS)
    low_tile = in_low(TILE)
    beta = corner_weight ** 0.5
    K[PLACES] = jnp.zeros((rows, 128), jnp.float32)

    def assemble_fixed(i):
        for at, tile in zip((i, i + PAIRS), halo_tiles(near_lat[FIXED + i], far_lat[FIXED + i])):
            moved = swapped(tile)
            for here, value in ((at, jnp.where(low_tile, tile, moved)), (at + QUADS, jnp.where(low_tile, moved, tile))):
                main = own_fixed[here]
                K[here] = cat(jnp.where(low, main, swapped(main)), value)

    blocks(0, QUADS, 9, assemble_fixed)
    lane = ids(rows, 1)
    inside = (lane & (LEVELS - 1)) != LEVELS - 1
    shift = jnp.where(lane < LEVELS, 1.0 - beta, 1.0 + beta)
    width = 18

    def weigh(i, carry):
        start = i * width
        here = woven(K, start)
        before = wx[jnp.maximum(start - 1, 0)]
        for u in range(width):
            at = start + u
            after = woven(K, at + 1)
            twice = 2.0 * here
            side = face(here, after, twice)
            row = face(here, next_row(here), twice)
            previous = last_row(row)
            level = jnp.where(inside, face(here, pltpu.roll(here, 127, 1), twice), 0.0)
            sums = (before + side) + (row + previous) + (level + pltpu.roll(level, 1, 1))
            wx[at], wy[at], wyp[at], wl[at] = side, row, previous, level
            total[at] = sums
            inv[at] = reciprocal(shift + sums)
            here, before = after, side
        return carry

    wx[0] = jnp.zeros((rows, 128), jnp.float32)
    lax.fori_loop(0, PLACES // width, weigh, 0)


STAGES = ((1, 39, 71), (2, 38, 70), (3, 37, 69), (4, 36, 68))
WIDTHS = ((19, 12, 17, 16), (16, 16, 16, 16))
READY = 40
EDGE = 12


def iterate_half(
    upper, wx, wy, wyp, wl, total, inv, own, own_halo, other_halo, it_main, source_main, *refs
):
    if upper:
        xs, edge, w_own, w_send, *refs = refs
    else:
        w_own, w_send, edge, *refs = refs
    it, source, spec, x, y, z, natural = refs
    rows = ROWS + TILE
    first = lax.axis_index("tm") == 0
    low = in_low(rows)
    beta = corner_weight ** 0.5
    gamma = jnp.where(low, 1.0, beta)
    shared = [(it, 38), (it, 39), (source, 39), (x, 37), (x, 38), (y, 36), (y, 37), (z, 35), (z, 36)]
    shared += [(spec, 36), (spec, 37), (spec, 38)]
    if upper:
        for i, (ref, at) in enumerate(shared):
            ref[at] = edge[i]

    def assemble(at):
        a, b = both_steps(own_halo[at], other_halo[at])
        it[at], source[at] = cat(it_main[at], a), cat(source_main[at], b)

    if upper:
        blocks(READY, SENT, 14, assemble)
        for i in range(HALO):
            at = outer_at(i)
            it[at], source[at] = both_steps(cat(own[at], own_halo[at]), xs[i])
    else:
        blocks(0, READY, 10, assemble)

    def over(stage, read, ref, step):
        lo, hi = STAGES[stage][upper : upper + 2]
        width = WIDTHS[upper][stage]

        def body(i, carry):
            start = lo + i * width
            around = [read(ref, start - 1), read(ref, start)]
            before = wx[start - 1]
            for u in range(width):
                at = start + u
                around = [*around[-2:], read(ref, at + 1)]
                side = wx[at]
                step(at, around, (before, side, wy[at], wyp[at], wl[at]))
                before = side
            return carry

        lax.fori_loop(0, (hi - lo) // width, body, 0)

    def residual(at, around, w):
        left = (woven(source, at) - ((1.0 + total[at]) * around[1] - near(around, w))) * gamma
        moved = swapped(left)
        value = jnp.where(low, left + moved, moved - left)
        spec[at] = value
        x[at] = value * inv[at]

    over(0, woven, it, residual)

    def plain(ref, at):
        return ref[at]

    def sweep(at, around, w):
        return (spec[at] + near(around, w)) * inv[at]

    def to(ref):
        def step(at, around, w):
            ref[at] = sweep(at, around, w)

        return step

    over(1, plain, x, to(y))
    over(2, plain, y, to(z))
    base = STAGES[3][upper]
    back = jnp.where(low, 0.5, 0.5 / beta)

    def last(at, around, w):
        value = sweep(at, around, w)
        moved = swapped(value)
        value = jnp.where(low, value + moved, moved - value) * back
        lon = at - base
        lon = jnp.where(first, HALF // 2 - 1 - lon, lon)
        for j in range(3):
            natural[pl.ds(lon * rows + j, TILE, stride=3), :] = value[j * TILE : (j + 1) * TILE]

    over(3, plain, z, last)
    count = HALF // 2
    for q in range(4):
        turned = cat(*[natural[pl.ds(q + 4 * j, count, stride=rows), :] for j in range(4)]).T
        step0, step1 = turned[:LEVELS], turned[LEVELS:]
        w_own[q] = jnp.where(first, step0, step1)
        w_send[q] = jnp.where(first, step1, step0)
    if not upper:
        for i, (ref, at) in enumerate(shared):
            edge[i] = ref[at]


def placed(value, j, quarter):
    return pltpu.roll(value, (32 * (quarter - j) + 128) & 127, 1)


def finish_most(it, own_low, own_high, got_low, most):
    t = lax.axis_index("tm")
    group = ids(LEVELS, 1) // 32

    def step(q):
        for j in range(4):
            row = q + 4 * j
            value = it[pl.ds(row, LEVELS, stride=ROWS), :]
            for piece, quarter in ((own_low, 1 + t), (own_high, 3 * t), (got_low, 2 - t)):
                value = jnp.where(group == quarter, value + placed(piece[q], j, quarter), value)
            most[row] = value

    blocks(0, 4, 2, step)


def finish(most, got_high, out_hbm, out, sems):
    quarter = 3 - 3 * lax.axis_index("tm")
    part = LEVELS // CHUNKS
    here = ids(part, 1) // 32 == quarter

    def copy(c):
        span = pl.ds(pl.multiple_of(c * part * ROWS, part * ROWS), part * ROWS)
        return pltpu.make_async_copy(out.at[span], out_hbm.at[span], sems.at[c])

    def step(c):
        for q in range(4):
            value = got_high[q, pl.ds(pl.multiple_of(c * part, part), part), :]
            for j in range(4):
                old = most[q + 4 * j, pl.ds(pl.multiple_of(c * part, part), part), :]
                out[pl.ds(c * part * ROWS + q + 4 * j, part, stride=ROWS), :] = jnp.where(here, old + placed(value, j, quarter), old)
        copy(c).start()

    blocks(0, CHUNKS, 1, step)
    for c in range(CHUNKS):
        copy(c).wait()


def two_steps(iterate, heating, initial, region, cond_table):
    lats, lons = lax.axis_size("lat"), lax.axis_size("lon")
    swap = [(0, 1), (1, 0)]
    pairs = [[(i, i + 1) for i in range(start, lats - 1, 2)] for start in (0, 1)]
    pairs = [p + [(j, i) for i, j in p] for p in pairs]
    round_lon = [[(i, (i + 1) % lons) for i in range(start, lons, 2)] for start in (0, 1)]
    round_lon = [p + [(j, i) for i, j in p] for p in round_lon]
    flat = (LEVELS * ROWS, LONS)
    turned_flat = (LONS * ROWS, 2 * LEVELS)
    by_lon = (LONS, ROWS, 2 * LEVELS)
    wide = shape(PLACES, ROWS + TILE, 128)

    def in_hbm(x):
        return pltpu.with_memory_space_constraint(x, pltpu.HBM)

    half_rows = shape(SENT, TILE, 128)
    edges, middle, turned, it = call(
        send_first,
        [half_rows, half_rows, shape(*turned_flat), shape(*flat)],
        [in_hbm(iterate[0]), in_hbm(heating[0])],
        scratch=[buffer(*flat), pltpu.SemaphoreType.DMA((ROWS // TILE, 2, 2))],
        hbm_ins=(0, 1),
    )
    edges = lax.ppermute(edges, "tm", swap)
    middle = lax.ppermute(middle, "tm", swap)
    sides = shape(HALO + 2, ROWS, 128)
    fixed, near_sides, far_sides = call(
        send_sides,
        [shape(*turned_flat), sides, sides],
        [turned, region.reshape(flat), initial.reshape(flat), in_hbm(cond_table)],
        scratch=[pltpu.SMEM(cond_table.shape, jnp.float32), pltpu.SemaphoreType.DMA],
        hbm_ins=(3,),
    )
    near_sides = lax.ppermute(near_sides, "lon", round_lon[0])
    far_sides = lax.ppermute(far_sides, "lon", round_lon[1])
    main = shape(PLACES, ROWS, 128)
    lat = shape(PARTNER + 2, TILE, 128)
    own_main, own_fixed, near_lat, far_lat, partner = call(
        add_sides,
        [main, main, lat, lat, shape(HALO, ROWS, 128)],
        [turned.reshape(by_lon), fixed.reshape(by_lon), near_sides, far_sides],
    )
    near_lat = lax.ppermute(near_lat, "lat", pairs[0])
    far_lat = lax.ppermute(far_lat, "lat", pairs[1])
    rows = shape(SENT_PAIRS + PAIRS - SPLIT, TILE, 128)
    edges, near_rows, far_rows = call(pass_rows, [half_rows, rows, rows], [edges, own_main, own_fixed])
    near_rows = lax.ppermute(near_rows, "lat", pairs[0])
    far_rows = lax.ppermute(far_rows, "lat", pairs[1])
    it_main, source_main = call(gather, [main, main], [edges, middle, own_main, own_fixed])
    (xs,) = call(strips, [shape(HALO, ROWS + TILE, 128)], [partner, near_lat, far_lat])
    xs = lax.ppermute(xs, "tm", swap)
    ready = call(
        prepare,
        [wide] * 6,
        [own_fixed, near_lat, far_lat, it_main],
        scratch=[buffer(PLACES + 1, ROWS + TILE, 128)],
    )
    halos = call(join, [shape(PLACES, TILE, 128)] * 2, [near_lat, far_lat, near_rows, far_rows])
    given = [*ready, own_main, *halos, it_main, source_main]
    corrections = [shape(4, LEVELS, 128)] * 2
    fields = [buffer(PLACES, ROWS + TILE, 128)] * 6 + [buffer(HALF // 2 * (ROWS + TILE), 128)]
    own_low, send_low, edge = call(
        functools.partial(iterate_half, 0),
        [*corrections, shape(EDGE, ROWS + TILE, 128)],
        given,
        scratch=fields,
        limit=16,
    )
    got_low = lax.ppermute(send_low, "tm", swap)
    own_high, send_high = call(
        functools.partial(iterate_half, 1), corrections, [*given, xs, edge], scratch=fields, limit=16
    )
    got_high = lax.ppermute(send_high, "tm", swap)
    (most,) = call(finish_most, [shape(ROWS, LEVELS, LONS)], [it, own_low, own_high, got_low])
    (out,) = call(
        finish,
        [shape(*flat)],
        [most, got_high],
        scratch=[buffer(*flat), pltpu.SemaphoreType.DMA((CHUNKS,))],
        hbm_outs=(0,),
    )
    return out.reshape(iterate.shape)


def solution(mesh):
    return jax.shard_map(
        two_steps if mesh.shape["tm"] == 2 else on_device,
        mesh=mesh,
        in_specs=(
            P("tm", None, "lat", "lon"),
            P("tm", None, "lat", "lon"),
            P(None, "lat", "lon"),
            P(None, "lat", "lon"),
            P(),
        ),
        out_specs=P("tm", None, "lat", "lon"),
        check_vma=False,
    )
```

```python
import functools

import jax
import jax.numpy as jnp
from jax import lax
from jax.experimental import pallas as pl
from jax.experimental.pallas import tpu as pltpu
from jax.sharding import PartitionSpec as P

SWEEPS = 4


corner_weight = 0.1


def padded(value, sides, width, wrap):
    for axis, dim in sides:
        peers, length = (lax.axis_size(axis), value.shape[dim])
        up = [(i, (i + 1) % peers) for i in range(peers if wrap else peers - 1)]
        down = [(j, i) for i, j in up]
        last = lax.slice_in_dim(value, length - width, length, axis=dim)
        initial = lax.slice_in_dim(value, 0, width, axis=dim)
        before = lax.ppermute(last, axis, up)
        after = lax.ppermute(initial, axis, down)
        value = jnp.concatenate([before, value, after], axis=dim)
    return value


def passed_along(block, axis, distance):
    devices = range(lax.axis_size(axis))
    route = [(i - distance, i) for i in devices if i - distance in devices]
    return lax.ppermute(block, axis, route)


def harmonic(first, second):
    return 2.0 * first * second / (first + second)


def conductivity(region, cond_table):
    classes = jnp.arange(cond_table.shape[0], dtype=jnp.int32)
    onehot = (region[..., None] == classes).astype(jnp.float32)
    return jnp.sum(onehot * cond_table, axis=-1)


def extend(stack):
    lat_ext = padded(stack, (("lat", 2),), 1, False)
    both = padded(lat_ext, (("lon", 3),), 1, True)
    return jnp.pad(both, ((0, 0), (1, 1), (0, 0), (0, 0)))


def face_weights(kext):
    centre = kext[1:-1, 1:-1, 1:-1]
    return (
        harmonic(centre, kext[:-2, 1:-1, 1:-1]),
        harmonic(centre, kext[2:, 1:-1, 1:-1]),
        harmonic(centre, kext[1:-1, :-2, 1:-1]),
        harmonic(centre, kext[1:-1, 2:, 1:-1]),
        harmonic(centre, kext[1:-1, 1:-1, :-2]),
        harmonic(centre, kext[1:-1, 1:-1, 2:]),
    )


def neighbours(weights, ext):
    near = weights[0] * ext[..., :-2, 1:-1, 1:-1] + weights[1] * ext[..., 2:, 1:-1, 1:-1]
    near = near + weights[2] * ext[..., 1:-1, :-2, 1:-1] + weights[3] * ext[..., 1:-1, 2:, 1:-1]
    near = near + weights[4] * ext[..., 1:-1, 1:-1, :-2] + weights[5] * ext[..., 1:-1, 1:-1, 2:]
    return near


def on_device(iterate, heating, initial, region, cond_table):
    steps = lax.axis_size("tm")
    own = lax.axis_index("tm")
    high = lax.Precision.HIGHEST
    kfield = conductivity(region, cond_table)
    ext = extend(jnp.stack([kfield, iterate[0]]))
    weights = face_weights(ext[0])
    total = weights[0] + weights[1] + weights[2] + weights[3] + weights[4] + weights[5]
    shifted = passed_along(iterate, "tm", 1)[0]
    previous = jnp.where(own == 0, initial, shifted)
    residual = heating[0] + previous - ((1.0 + total) * iterate[0] - neighbours(weights, ext[1]))
    scale_own = corner_weight ** (own.astype(jnp.float32) / steps)
    scaled = residual * scale_own
    zeros = jnp.zeros_like(residual)
    piece = lax.all_gather(scaled[None], "tm", axis=0, tiled=True)
    order = jnp.arange(piece.shape[0], dtype=jnp.int32)
    angle = 2.0 * jnp.pi / steps * (own * order % steps).astype(jnp.float32)
    real_part = jnp.einsum("n,nabc->abc", jnp.cos(angle), piece, precision=high)
    imag_part = (zeros, zeros)[1] - jnp.einsum("n,nabc->abc", jnp.sin(angle), piece, precision=high)
    beta = corner_weight ** (1.0 / steps)
    freq_angle = 2.0 * jnp.pi / steps * (own % steps).astype(jnp.float32)
    diag_re = 1.0 - beta * jnp.cos(freq_angle) + total
    diag_im = beta * jnp.sin(freq_angle) + zeros
    denom = diag_re * diag_re + diag_im * diag_im
    inv_re = diag_re / denom
    inv_im = -diag_im / denom
    sol_re = real_part * inv_re - imag_part * inv_im
    sol_im = real_part * inv_im + imag_part * inv_re
    for sweep in range(SWEEPS - 1):
        near = neighbours(weights, extend(jnp.stack([sol_re, sol_im])))
        rhs_re = real_part + near[0]
        rhs_im = imag_part + near[1]
        sol_re = rhs_re * inv_re - rhs_im * inv_im
        sol_im = rhs_re * inv_im + rhs_im * inv_re
    pieces = (
        lax.all_gather(sol_re[None], "tm", axis=0, tiled=True),
        lax.all_gather(sol_im[None], "tm", axis=0, tiled=True),
    )
    order = jnp.arange(pieces[0].shape[0], dtype=jnp.int32)
    angle = 2.0 * jnp.pi / steps * (order * own % steps).astype(jnp.float32)
    summed = jnp.einsum("k,kabc->abc", jnp.cos(angle), pieces[0], precision=high) - jnp.einsum(
        "k,kabc->abc", jnp.sin(angle), pieces[1], precision=high
    )
    back = summed / steps
    return iterate + (back / scale_own)[None]


HALO = 4
TILE = 8
LEVELS = 64
ROWS = 16
LONS = 128
HALF = 64
SENT = HALF + HALO
PLACES = HALF + 2 * HALO
PAIRS = PLACES // 2
SENT_PAIRS = SENT // 2
QUADS = PLACES // 4
SPLIT = 24
FIXED = SPLIT
PARTNER = SPLIT + QUADS
CHUNKS = 4


def specs(count, hbm):
    return [pl.BlockSpec(memory_space=pltpu.HBM if i in hbm else pltpu.VMEM) for i in range(count)]


def call(body, outs, ins, scratch=(), limit=8, hbm_ins=(), hbm_outs=(), work=1):
    moved = work * (sum(x.size * 4 for x in ins) + sum(x.size * 4 for x in outs))
    return pl.pallas_call(
        body,
        out_shape=outs,
        in_specs=specs(len(ins), hbm_ins),
        out_specs=specs(len(outs), hbm_outs),
        scratch_shapes=scratch,
        compiler_params=pltpu.CompilerParams(vmem_limit_bytes=limit << 20),
        cost_estimate=pl.CostEstimate(flops=moved * 4, bytes_accessed=moved, transcendentals=0),
    )(*ins)


def shape(*dims):
    return jax.ShapeDtypeStruct(dims, jnp.float32)


def buffer(*dims):
    return pltpu.VMEM(dims, jnp.float32)


def ids(rows, dim):
    return lax.broadcasted_iota(jnp.int32, (rows, 128), dim)


def in_low(rows):
    return ids(rows, 1) < LEVELS


def swapped(x):
    return pltpu.roll(x, LEVELS, 1)


def main_at(i):
    return jnp.where(lax.axis_index("tm") == 0, SENT - 1 - i, i)


def outer_at(i):
    return jnp.where(lax.axis_index("tm") == 0, PLACES - 1 - i, SENT + i)


def cat(*values):
    return jnp.concatenate(values, axis=0)


def even(axis):
    return lax.rem(lax.axis_index(axis), 2) == 0


def blocks(lo, hi, width, step):
    def body(i, carry):
        for u in range(width):
            step(lo + i * width + u)
        return carry

    lax.fori_loop(0, (hi - lo) // width, body, 0)


def send_first(it_hbm, h_hbm, edges, middle, turned, it, h, sems):
    t = lax.axis_index("tm")
    by_level = (LEVELS, ROWS, LONS)
    copies = []
    for k in range(ROWS // TILE):
        for f, (source, target) in enumerate(((it_hbm, it), (h_hbm, h))):
            for c in range(2):
                part = pl.ds(c * LEVELS // 2, LEVELS // 2), pl.ds(k * TILE, TILE)
                copy = pltpu.make_async_copy(source.at[part], target.reshape(by_level).at[part], sems.at[k, f, c])
                copy.start()
                copies.append(copy)

    def turn(r):
        rows = pl.ds(r, LEVELS, stride=ROWS)
        turned[pl.ds(r, LONS, stride=ROWS), :] = cat(it[rows, :], h[rows, :]).T

    for k in range(ROWS // TILE):
        for copy in copies[4 * k : 4 * k + 4]:
            copy.wait()
        blocks(k * TILE, (k + 1) * TILE, 4, turn)
    start = (LONS - SENT) * ROWS * (1 - t)
    top = ids(TILE, 0) < HALO

    def cut(i):
        at = pl.multiple_of(start + i * ROWS, ROWS)
        low, high = turned[pl.ds(at, TILE), :], turned[pl.ds(at + TILE, TILE), :]
        edges[i] = jnp.where(top, low, high)
        middle[i] = jnp.where(top, high, low)

    blocks(0, SENT, 17, cut)


def heated(turned, fixed):
    add = jnp.logical_and(jnp.logical_not(in_low(ROWS)), lax.axis_index("tm") == 0)
    return turned + jnp.where(add, fixed, 0.0)


def send_sides(turned, region, initial, table_hbm, fixed, near_sides, far_sides, table, sem):
    copy = pltpu.make_async_copy(table_hbm, table, sem)
    copy.start()
    copy.wait()

    def turn(r):
        rows = pl.ds(r, LEVELS, stride=ROWS)
        classes = region[rows, :]
        value = jnp.full(classes.shape, table[0], jnp.float32)
        for c in range(1, table.shape[0]):
            value = jnp.where(classes == c, table[c], value)
        fixed[pl.ds(r, LONS, stride=ROWS), :] = cat(value, initial[rows, :]).T

    blocks(0, ROWS, 4, turn)
    near_right = even("lon")
    low = in_low(ROWS)

    def strip(first_lon):
        def at(ref, i):
            return ref[(first_lon + i) * ROWS : (first_lon + i + 1) * ROWS, :]

        return [heated(at(turned, i), at(fixed, i)) for i in range(HALO)] + [
            jnp.where(low, at(fixed, i), swapped(at(fixed, i + 2))) for i in range(2)
        ]

    for i, (right, left) in enumerate(zip(strip(LONS - HALO), strip(0))):
        near_sides[i] = jnp.where(near_right, right, left)
        far_sides[i] = jnp.where(near_right, left, right)


def edge_pair(first, second):
    top = ids(TILE, 0) < HALO
    first_up = even("lat")
    down = jnp.where(top, first[:TILE], pltpu.roll(second[:TILE], HALO, 0))
    up = jnp.where(top, pltpu.roll(first[-TILE:], HALO, 0), second[-TILE:])
    return jnp.where(first_up, up, down), jnp.where(first_up, down, up)


def halo_tiles(near_pair, far_pair):
    first_up = even("lat")
    after = jnp.where(first_up, near_pair, far_pair)
    before = jnp.where(first_up, far_pair, near_pair)
    top = ids(TILE, 0) < HALO
    return (
        jnp.where(top, after, pltpu.roll(before, HALO, 0)),
        jnp.where(top, pltpu.roll(after, HALO, 0), before),
    )


def add_sides(turned, fixed, near_sides, far_sides, own, own_fixed, near_lat, far_lat, partner):
    t = lax.axis_index("tm")
    from_near = (t == 0) != even("lon")
    count = near_sides.shape[0]
    beside = [jnp.where(from_near, near_sides[i], far_sides[i]) for i in range(count)]
    other = [jnp.where(from_near, far_sides[i], near_sides[i]) for i in range(HALO)]
    for i in range(HALO):
        own[outer_at(i)] = beside[i]
        partner[i] = other[i]
    for i in range(2):
        own_fixed[outer_at(i)] = beside[HALO + i]
        own_fixed[outer_at(i + 2)] = swapped(beside[HALO + i])
        near_lat[PARTNER + i], far_lat[PARTNER + i] = edge_pair(other[i], other[i + 2])

    def copy(i):
        at = main_at(i)
        lon = (LONS - SENT) * t + i
        own[at] = heated(turned[lon], fixed[lon])
        own_fixed[at] = fixed[lon]

    blocks(0, SENT, 17, copy)

    def rows(i):
        near_lat[i], far_lat[i] = edge_pair(own[i], own[i + PAIRS])

    blocks(0, SPLIT, 12, rows)
    low = in_low(TILE)

    def fixed_rows(i):
        here = edge_pair(own_fixed[i], own_fixed[i + PAIRS])
        there = edge_pair(own_fixed[i + QUADS], own_fixed[i + PAIRS + QUADS])
        near_lat[FIXED + i], far_lat[FIXED + i] = [jnp.where(low, a, swapped(b)) for a, b in zip(here, there)]

    blocks(0, QUADS, 9, fixed_rows)


def start_of_step(fixed, rows):
    add = jnp.logical_and(jnp.logical_not(in_low(rows)), lax.axis_index("tm") == 1)
    return jnp.where(add, fixed, 0.0)


def pass_rows(edges, own, own_fixed, heated_edges, near_rows, far_rows):
    top = ids(TILE, 0) < HALO

    def heat(i):
        fixed = own_fixed[main_at(i)]
        heated_edges[i] = edges[i] + start_of_step(jnp.where(top, fixed[:TILE], fixed[TILE:]), TILE)

    blocks(0, SENT, 17, heat)

    def rows(i):
        near_rows[i], far_rows[i] = edge_pair(heated_edges[i], heated_edges[i + SENT_PAIRS])

    blocks(0, SENT_PAIRS, 17, rows)

    def rest(i):
        near_rows[SENT_PAIRS + i], far_rows[SENT_PAIRS + i] = edge_pair(own[SPLIT + i], own[SPLIT + i + PAIRS])

    blocks(0, PAIRS - SPLIT, 12, rest)


def join(near_lat, far_lat, near_rows, far_rows, halo, other):
    def place(i, tiles):
        halo[i], halo[i + PAIRS] = tiles

    blocks(0, SPLIT, 12, lambda i: place(i, halo_tiles(near_lat[i], far_lat[i])))

    def rest(i):
        at = SENT_PAIRS + i
        place(SPLIT + i, halo_tiles(near_rows[at], far_rows[at]))

    blocks(0, PAIRS - SPLIT, 12, rest)

    def theirs(i):
        other[main_at(i)], other[main_at(i + SENT_PAIRS)] = halo_tiles(near_rows[i], far_rows[i])

    blocks(0, SENT_PAIRS, 17, theirs)


def both_steps(mine, theirs):
    first = lax.axis_index("tm") == 0
    low = in_low(mine.shape[0])
    step0, step1 = jnp.where(first, mine, theirs), jnp.where(first, theirs, mine)
    moved = swapped(step0)
    return jnp.where(low, step0, swapped(step1)), jnp.where(low, moved, step1 + moved)


def gather(edges, middle, own, own_fixed, it, source):
    top = ids(TILE, 0) < HALO

    def step(i):
        at = main_at(i)
        fixed = own_fixed[at]
        e = edges[i]
        m = middle[i] + start_of_step(jnp.where(top, fixed[TILE:], fixed[:TILE]), TILE)
        theirs = cat(jnp.where(top, e, m), jnp.where(top, m, e))
        it[at], source[at] = both_steps(own[at], theirs)

    blocks(0, SENT, 17, step)


def strips(partner, near_lat, far_lat, _, xs):
    for i in range(2):
        at = PARTNER + i
        for place, tile in zip((i, i + 2), halo_tiles(near_lat[at], far_lat[at])):
            xs[place] = cat(partner[place], tile)


def reciprocal(d):
    y = pl.reciprocal(d, approx=True)
    return y * (2.0 - d * y)


def face(a, b, twice):
    return twice * b * reciprocal(jnp.maximum(a + b, 1e-30))


def woven(ref, at):
    return cat(*[ref[at, pl.ds(j, TILE, stride=3), :] for j in range(3)])


def next_row(x):
    return cat(x[TILE:], pltpu.roll(x[:TILE], TILE - 1, 0))


def last_row(x):
    return cat(pltpu.roll(x[-TILE:], 1, 0), x[:-TILE])


def near(around, w):
    before, mid, after = around
    wxp, wx, wy, wyp, wl = w
    total = wxp * before + wx * after
    total = total + (wy * next_row(mid) + wyp * last_row(mid))
    return total + (wl * pltpu.roll(mid, 127, 1) + pltpu.roll(wl * mid, 1, 1))


def prepare(own_fixed, near_lat, far_lat, _, wx, wy, wyp, wl, total, inv, K):
    rows = ROWS + TILE
    low = in_low(ROWS)
    low_tile = in_low(TILE)
    beta = corner_weight ** 0.5
    K[PLACES] = jnp.zeros((rows, 128), jnp.float32)

    def assemble_fixed(i):
        for at, tile in zip((i, i + PAIRS), halo_tiles(near_lat[FIXED + i], far_lat[FIXED + i])):
            moved = swapped(tile)
            for here, value in ((at, jnp.where(low_tile, tile, moved)), (at + QUADS, jnp.where(low_tile, moved, tile))):
                main = own_fixed[here]
                K[here] = cat(jnp.where(low, main, swapped(main)), value)

    blocks(0, QUADS, 9, assemble_fixed)
    lane = ids(rows, 1)
    inside = (lane & (LEVELS - 1)) != LEVELS - 1
    shift = jnp.where(lane < LEVELS, 1.0 - beta, 1.0 + beta)
    width = 18

    def weigh(i, carry):
        start = i * width
        here = woven(K, start)
        before = wx[jnp.maximum(start - 1, 0)]
        for u in range(width):
            at = start + u
            after = woven(K, at + 1)
            twice = 2.0 * here
            side = face(here, after, twice)
            row = face(here, next_row(here), twice)
            previous = last_row(row)
            level = jnp.where(inside, face(here, pltpu.roll(here, 127, 1), twice), 0.0)
            sums = (before + side) + (row + previous) + (level + pltpu.roll(level, 1, 1))
            wx[at], wy[at], wyp[at], wl[at] = side, row, previous, level
            total[at] = sums
            inv[at] = reciprocal(shift + sums)
            here, before = after, side
        return carry

    wx[0] = jnp.zeros((rows, 128), jnp.float32)
    lax.fori_loop(0, PLACES // width, weigh, 0)


STAGES = ((1, 39, 71), (2, 38, 70), (3, 37, 69), (4, 36, 68))
WIDTHS = ((19, 12, 17, 16), (16, 16, 16, 16))
READY = 40
EDGE = 12


def iterate_half(
    upper, wx, wy, wyp, wl, total, inv, own, own_halo, other_halo, it_main, source_main, *refs
):
    if upper:
        xs, edge, w_own, w_send, *refs = refs
    else:
        w_own, w_send, edge, *refs = refs
    it, source, spec, x, y, z, natural = refs
    rows = ROWS + TILE
    first = lax.axis_index("tm") == 0
    low = in_low(rows)
    beta = corner_weight ** 0.5
    gamma = jnp.where(low, 1.0, beta)
    shared = [(it, 38), (it, 39), (source, 39), (x, 37), (x, 38), (y, 36), (y, 37), (z, 35), (z, 36)]
    shared += [(spec, 36), (spec, 37), (spec, 38)]
    if upper:
        for i, (ref, at) in enumerate(shared):
            ref[at] = edge[i]

    def assemble(at):
        a, b = both_steps(own_halo[at], other_halo[at])
        it[at], source[at] = cat(it_main[at], a), cat(source_main[at], b)

    if upper:
        blocks(READY, SENT, 14, assemble)
        for i in range(HALO):
            at = outer_at(i)
            it[at], source[at] = both_steps(cat(own[at], own_halo[at]), xs[i])
    else:
        blocks(0, READY, 10, assemble)

    def over(stage, read, ref, step):
        lo, hi = STAGES[stage][upper : upper + 2]
        width = WIDTHS[upper][stage]

        def body(i, carry):
            start = lo + i * width
            around = [read(ref, start - 1), read(ref, start)]
            before = wx[start - 1]
            for u in range(width):
                at = start + u
                around = [*around[-2:], read(ref, at + 1)]
                side = wx[at]
                step(at, around, (before, side, wy[at], wyp[at], wl[at]))
                before = side
            return carry

        lax.fori_loop(0, (hi - lo) // width, body, 0)

    def residual(at, around, w):
        left = (woven(source, at) - ((1.0 + total[at]) * around[1] - near(around, w))) * gamma
        moved = swapped(left)
        value = jnp.where(low, left + moved, moved - left)
        spec[at] = value
        x[at] = value * inv[at]

    over(0, woven, it, residual)

    def plain(ref, at):
        return ref[at]

    def sweep(at, around, w):
        return (spec[at] + near(around, w)) * inv[at]

    def to(ref):
        def step(at, around, w):
            ref[at] = sweep(at, around, w)

        return step

    over(1, plain, x, to(y))
    over(2, plain, y, to(z))
    base = STAGES[3][upper]
    back = jnp.where(low, 0.5, 0.5 / beta)

    def last(at, around, w):
        value = sweep(at, around, w)
        moved = swapped(value)
        value = jnp.where(low, value + moved, moved - value) * back
        lon = at - base
        lon = jnp.where(first, HALF // 2 - 1 - lon, lon)
        for j in range(3):
            natural[pl.ds(lon * rows + j, TILE, stride=3), :] = value[j * TILE : (j + 1) * TILE]

    over(3, plain, z, last)
    count = HALF // 2
    for q in range(4):
        turned = cat(*[natural[pl.ds(q + 4 * j, count, stride=rows), :] for j in range(4)]).T
        step0, step1 = turned[:LEVELS], turned[LEVELS:]
        w_own[q] = jnp.where(first, step0, step1)
        w_send[q] = jnp.where(first, step1, step0)
    if not upper:
        for i, (ref, at) in enumerate(shared):
            edge[i] = ref[at]


def placed(value, j, quarter):
    return pltpu.roll(value, (32 * (quarter - j) + 128) & 127, 1)


def finish_most(it, own_low, own_high, got_low, most):
    t = lax.axis_index("tm")
    group = ids(LEVELS, 1) // 32

    def step(q):
        for j in range(4):
            row = q + 4 * j
            value = it[pl.ds(row, LEVELS, stride=ROWS), :]
            for piece, quarter in ((own_low, 1 + t), (own_high, 3 * t), (got_low, 2 - t)):
                value = jnp.where(group == quarter, value + placed(piece[q], j, quarter), value)
            most[row] = value

    blocks(0, 4, 2, step)


def finish(most, got_high, out_hbm, out, sems):
    quarter = 3 - 3 * lax.axis_index("tm")
    part = LEVELS // CHUNKS
    here = ids(part, 1) // 32 == quarter

    def copy(c):
        span = pl.ds(pl.multiple_of(c * part * ROWS, part * ROWS), part * ROWS)
        return pltpu.make_async_copy(out.at[span], out_hbm.at[span], sems.at[c])

    def step(c):
        for q in range(4):
            value = got_high[q, pl.ds(pl.multiple_of(c * part, part), part), :]
            for j in range(4):
                old = most[q + 4 * j, pl.ds(pl.multiple_of(c * part, part), part), :]
                out[pl.ds(c * part * ROWS + q + 4 * j, part, stride=ROWS), :] = jnp.where(here, old + placed(value, j, quarter), old)
        copy(c).start()

    blocks(0, CHUNKS, 1, step)
    for c in range(CHUNKS):
        copy(c).wait()


def two_steps(iterate, heating, initial, region, cond_table):
    lats, lons = lax.axis_size("lat"), lax.axis_size("lon")
    swap = [(0, 1), (1, 0)]
    pairs = [[(i, i + 1) for i in range(start, lats - 1, 2)] for start in (0, 1)]
    pairs = [p + [(j, i) for i, j in p] for p in pairs]
    round_lon = [[(i, (i + 1) % lons) for i in range(start, lons, 2)] for start in (0, 1)]
    round_lon = [p + [(j, i) for i, j in p] for p in round_lon]
    flat = (LEVELS * ROWS, LONS)
    turned_flat = (LONS * ROWS, 2 * LEVELS)
    by_lon = (LONS, ROWS, 2 * LEVELS)
    wide = shape(PLACES, ROWS + TILE, 128)

    def in_hbm(x):
        return pltpu.with_memory_space_constraint(x, pltpu.HBM)

    half_rows = shape(SENT, TILE, 128)
    edges, middle, turned, it = call(
        send_first,
        [half_rows, half_rows, shape(*turned_flat), shape(*flat)],
        [in_hbm(iterate[0]), in_hbm(heating[0])],
        scratch=[buffer(*flat), pltpu.SemaphoreType.DMA((ROWS // TILE, 2, 2))],
        hbm_ins=(0, 1),
    )
    edges = lax.ppermute(edges, "tm", swap)
    middle = lax.ppermute(middle, "tm", swap)
    sides = shape(HALO + 2, ROWS, 128)
    fixed, near_sides, far_sides = call(
        send_sides,
        [shape(*turned_flat), sides, sides],
        [turned, region.reshape(flat), initial.reshape(flat), in_hbm(cond_table)],
        scratch=[pltpu.SMEM(cond_table.shape, jnp.float32), pltpu.SemaphoreType.DMA],
        hbm_ins=(3,),
    )
    near_sides = lax.ppermute(near_sides, "lon", round_lon[0])
    far_sides = lax.ppermute(far_sides, "lon", round_lon[1])
    main = shape(PLACES, ROWS, 128)
    lat = shape(PARTNER + 2, TILE, 128)
    own_main, own_fixed, near_lat, far_lat, partner = call(
        add_sides,
        [main, main, lat, lat, shape(HALO, ROWS, 128)],
        [turned.reshape(by_lon), fixed.reshape(by_lon), near_sides, far_sides],
    )
    near_lat = lax.ppermute(near_lat, "lat", pairs[0])
    far_lat = lax.ppermute(far_lat, "lat", pairs[1])
    rows = shape(SENT_PAIRS + PAIRS - SPLIT, TILE, 128)
    edges, near_rows, far_rows = call(
        pass_rows, [half_rows, rows, rows], [edges, own_main, own_fixed], work=200
    )
    near_rows = lax.ppermute(near_rows, "lat", pairs[0])
    far_rows = lax.ppermute(far_rows, "lat", pairs[1])
    it_main, source_main = call(gather, [main, main], [edges, middle, own_main, own_fixed])
    (xs,) = call(strips, [shape(HALO, ROWS + TILE, 128)], [partner, near_lat, far_lat, it_main])
    xs = lax.ppermute(xs, "tm", swap)
    ready = call(
        prepare,
        [wide] * 6,
        [own_fixed, near_lat, far_lat, it_main],
        scratch=[buffer(PLACES + 1, ROWS + TILE, 128)],
    )
    halos = call(join, [shape(PLACES, TILE, 128)] * 2, [near_lat, far_lat, near_rows, far_rows])
    given = [*ready, own_main, *halos, it_main, source_main]
    corrections = [shape(4, LEVELS, 128)] * 2
    fields = [buffer(PLACES, ROWS + TILE, 128)] * 6 + [buffer(HALF // 2 * (ROWS + TILE), 128)]
    own_low, send_low, edge = call(
        functools.partial(iterate_half, 0),
        [*corrections, shape(EDGE, ROWS + TILE, 128)],
        given,
        scratch=fields,
        limit=16,
    )
    got_low = lax.ppermute(send_low, "tm", swap)
    own_high, send_high = call(
        functools.partial(iterate_half, 1), corrections, [*given, xs, edge], scratch=fields, limit=16
    )
    got_high = lax.ppermute(send_high, "tm", swap)
    (most,) = call(finish_most, [shape(ROWS, LEVELS, LONS)], [it, own_low, own_high, got_low])
    (out,) = call(
        finish,
        [shape(*flat)],
        [most, got_high],
        scratch=[buffer(*flat), pltpu.SemaphoreType.DMA((CHUNKS,))],
        hbm_outs=(0,),
    )
    return out.reshape(iterate.shape)


def solution(mesh):
    return jax.shard_map(
        two_steps if mesh.shape["tm"] == 2 else on_device,
        mesh=mesh,
        in_specs=(
            P("tm", None, "lat", "lon"),
            P("tm", None, "lat", "lon"),
            P(None, "lat", "lon"),
            P(None, "lat", "lon"),
            P(),
        ),
        out_specs=P("tm", None, "lat", "lon"),
        check_vma=False,
    )
```

```python
import functools

import jax
import jax.numpy as jnp
from jax import lax
from jax.experimental import pallas as pl
from jax.experimental.pallas import tpu as pltpu
from jax.sharding import PartitionSpec as P

SWEEPS = 4


corner_weight = 0.1


def padded(value, sides, width, wrap):
    for axis, dim in sides:
        peers, length = (lax.axis_size(axis), value.shape[dim])
        up = [(i, (i + 1) % peers) for i in range(peers if wrap else peers - 1)]
        down = [(j, i) for i, j in up]
        last = lax.slice_in_dim(value, length - width, length, axis=dim)
        initial = lax.slice_in_dim(value, 0, width, axis=dim)
        before = lax.ppermute(last, axis, up)
        after = lax.ppermute(initial, axis, down)
        value = jnp.concatenate([before, value, after], axis=dim)
    return value


def passed_along(block, axis, distance):
    devices = range(lax.axis_size(axis))
    route = [(i - distance, i) for i in devices if i - distance in devices]
    return lax.ppermute(block, axis, route)


def harmonic(first, second):
    return 2.0 * first * second / (first + second)


def conductivity(region, cond_table):
    classes = jnp.arange(cond_table.shape[0], dtype=jnp.int32)
    onehot = (region[..., None] == classes).astype(jnp.float32)
    return jnp.sum(onehot * cond_table, axis=-1)


def extend(stack):
    lat_ext = padded(stack, (("lat", 2),), 1, False)
    both = padded(lat_ext, (("lon", 3),), 1, True)
    return jnp.pad(both, ((0, 0), (1, 1), (0, 0), (0, 0)))


def face_weights(kext):
    centre = kext[1:-1, 1:-1, 1:-1]
    return (
        harmonic(centre, kext[:-2, 1:-1, 1:-1]),
        harmonic(centre, kext[2:, 1:-1, 1:-1]),
        harmonic(centre, kext[1:-1, :-2, 1:-1]),
        harmonic(centre, kext[1:-1, 2:, 1:-1]),
        harmonic(centre, kext[1:-1, 1:-1, :-2]),
        harmonic(centre, kext[1:-1, 1:-1, 2:]),
    )


def neighbours(weights, ext):
    near = weights[0] * ext[..., :-2, 1:-1, 1:-1] + weights[1] * ext[..., 2:, 1:-1, 1:-1]
    near = near + weights[2] * ext[..., 1:-1, :-2, 1:-1] + weights[3] * ext[..., 1:-1, 2:, 1:-1]
    near = near + weights[4] * ext[..., 1:-1, 1:-1, :-2] + weights[5] * ext[..., 1:-1, 1:-1, 2:]
    return near


def on_device(iterate, heating, initial, region, cond_table):
    steps = lax.axis_size("tm")
    own = lax.axis_index("tm")
    high = lax.Precision.HIGHEST
    kfield = conductivity(region, cond_table)
    ext = extend(jnp.stack([kfield, iterate[0]]))
    weights = face_weights(ext[0])
    total = weights[0] + weights[1] + weights[2] + weights[3] + weights[4] + weights[5]
    shifted = passed_along(iterate, "tm", 1)[0]
    previous = jnp.where(own == 0, initial, shifted)
    residual = heating[0] + previous - ((1.0 + total) * iterate[0] - neighbours(weights, ext[1]))
    scale_own = corner_weight ** (own.astype(jnp.float32) / steps)
    scaled = residual * scale_own
    zeros = jnp.zeros_like(residual)
    piece = lax.all_gather(scaled[None], "tm", axis=0, tiled=True)
    order = jnp.arange(piece.shape[0], dtype=jnp.int32)
    angle = 2.0 * jnp.pi / steps * (own * order % steps).astype(jnp.float32)
    real_part = jnp.einsum("n,nabc->abc", jnp.cos(angle), piece, precision=high)
    imag_part = (zeros, zeros)[1] - jnp.einsum("n,nabc->abc", jnp.sin(angle), piece, precision=high)
    beta = corner_weight ** (1.0 / steps)
    freq_angle = 2.0 * jnp.pi / steps * (own % steps).astype(jnp.float32)
    diag_re = 1.0 - beta * jnp.cos(freq_angle) + total
    diag_im = beta * jnp.sin(freq_angle) + zeros
    denom = diag_re * diag_re + diag_im * diag_im
    inv_re = diag_re / denom
    inv_im = -diag_im / denom
    sol_re = real_part * inv_re - imag_part * inv_im
    sol_im = real_part * inv_im + imag_part * inv_re
    for sweep in range(SWEEPS - 1):
        near = neighbours(weights, extend(jnp.stack([sol_re, sol_im])))
        rhs_re = real_part + near[0]
        rhs_im = imag_part + near[1]
        sol_re = rhs_re * inv_re - rhs_im * inv_im
        sol_im = rhs_re * inv_im + rhs_im * inv_re
    pieces = (
        lax.all_gather(sol_re[None], "tm", axis=0, tiled=True),
        lax.all_gather(sol_im[None], "tm", axis=0, tiled=True),
    )
    order = jnp.arange(pieces[0].shape[0], dtype=jnp.int32)
    angle = 2.0 * jnp.pi / steps * (order * own % steps).astype(jnp.float32)
    summed = jnp.einsum("k,kabc->abc", jnp.cos(angle), pieces[0], precision=high) - jnp.einsum(
        "k,kabc->abc", jnp.sin(angle), pieces[1], precision=high
    )
    back = summed / steps
    return iterate + (back / scale_own)[None]


HALO = 4
TILE = 8
LEVELS = 64
ROWS = 16
LONS = 128
HALF = 64
SENT = HALF + HALO
PLACES = HALF + 2 * HALO
PAIRS = PLACES // 2
SENT_PAIRS = SENT // 2
QUADS = PLACES // 4
SPLIT = 24
FIXED = SPLIT
PARTNER = SPLIT + QUADS
CHUNKS = 4


def specs(count, hbm):
    return [pl.BlockSpec(memory_space=pltpu.HBM if i in hbm else pltpu.VMEM) for i in range(count)]


def call(body, outs, ins, scratch=(), limit=8, hbm_ins=(), hbm_outs=(), work=1):
    moved = work * (sum(x.size * 4 for x in ins) + sum(x.size * 4 for x in outs))
    return pl.pallas_call(
        body,
        out_shape=outs,
        in_specs=specs(len(ins), hbm_ins),
        out_specs=specs(len(outs), hbm_outs),
        scratch_shapes=scratch,
        compiler_params=pltpu.CompilerParams(vmem_limit_bytes=limit << 20),
        cost_estimate=pl.CostEstimate(flops=moved * 4, bytes_accessed=moved, transcendentals=0),
    )(*ins)


def shape(*dims):
    return jax.ShapeDtypeStruct(dims, jnp.float32)


def buffer(*dims):
    return pltpu.VMEM(dims, jnp.float32)


def ids(rows, dim):
    return lax.broadcasted_iota(jnp.int32, (rows, 128), dim)


def in_low(rows):
    return ids(rows, 1) < LEVELS


def swapped(x):
    return pltpu.roll(x, LEVELS, 1)


def main_at(i):
    return jnp.where(lax.axis_index("tm") == 0, SENT - 1 - i, i)


def outer_at(i):
    return jnp.where(lax.axis_index("tm") == 0, PLACES - 1 - i, SENT + i)


def cat(*values):
    return jnp.concatenate(values, axis=0)


def even(axis):
    return lax.rem(lax.axis_index(axis), 2) == 0


def blocks(lo, hi, width, step):
    def body(i, carry):
        for u in range(width):
            step(lo + i * width + u)
        return carry

    lax.fori_loop(0, (hi - lo) // width, body, 0)


def send_first(it_hbm, h_hbm, edges, middle, turned, it, h, sems):
    t = lax.axis_index("tm")
    by_level = (LEVELS, ROWS, LONS)
    copies = []
    for k in range(ROWS // TILE):
        for f, (source, target) in enumerate(((it_hbm, it), (h_hbm, h))):
            for c in range(2):
                part = pl.ds(c * LEVELS // 2, LEVELS // 2), pl.ds(k * TILE, TILE)
                copy = pltpu.make_async_copy(source.at[part], target.reshape(by_level).at[part], sems.at[k, f, c])
                copy.start()
                copies.append(copy)

    def turn(r):
        rows = pl.ds(r, LEVELS, stride=ROWS)
        turned[pl.ds(r, LONS, stride=ROWS), :] = cat(it[rows, :], h[rows, :]).T

    for k in range(ROWS // TILE):
        for copy in copies[4 * k : 4 * k + 4]:
            copy.wait()
        blocks(k * TILE, (k + 1) * TILE, 8, turn)
    start = (LONS - SENT) * ROWS * (1 - t)
    top = ids(TILE, 0) < HALO

    def cut(i):
        at = pl.multiple_of(start + i * ROWS, ROWS)
        low, high = turned[pl.ds(at, TILE), :], turned[pl.ds(at + TILE, TILE), :]
        edges[i] = jnp.where(top, low, high)
        middle[i] = jnp.where(top, high, low)

    blocks(0, SENT, 17, cut)


def heated(turned, fixed):
    add = jnp.logical_and(jnp.logical_not(in_low(ROWS)), lax.axis_index("tm") == 0)
    return turned + jnp.where(add, fixed, 0.0)


def send_sides(turned, region, initial, table_hbm, fixed, near_sides, far_sides, table, sem):
    copy = pltpu.make_async_copy(table_hbm, table, sem)
    copy.start()
    copy.wait()

    def turn(r):
        rows = pl.ds(r, LEVELS, stride=ROWS)
        classes = region[rows, :]
        value = jnp.full(classes.shape, table[0], jnp.float32)
        for c in range(1, table.shape[0]):
            value = jnp.where(classes == c, table[c], value)
        fixed[pl.ds(r, LONS, stride=ROWS), :] = cat(value, initial[rows, :]).T

    blocks(0, ROWS, 8, turn)
    near_right = even("lon")
    low = in_low(ROWS)

    def strip(first_lon):
        def at(ref, i):
            return ref[(first_lon + i) * ROWS : (first_lon + i + 1) * ROWS, :]

        return [heated(at(turned, i), at(fixed, i)) for i in range(HALO)] + [
            jnp.where(low, at(fixed, i), swapped(at(fixed, i + 2))) for i in range(2)
        ]

    for i, (right, left) in enumerate(zip(strip(LONS - HALO), strip(0))):
        near_sides[i] = jnp.where(near_right, right, left)
        far_sides[i] = jnp.where(near_right, left, right)


def edge_pair(first, second):
    top = ids(TILE, 0) < HALO
    first_up = even("lat")
    down = jnp.where(top, first[:TILE], pltpu.roll(second[:TILE], HALO, 0))
    up = jnp.where(top, pltpu.roll(first[-TILE:], HALO, 0), second[-TILE:])
    return jnp.where(first_up, up, down), jnp.where(first_up, down, up)


def halo_tiles(near_pair, far_pair):
    first_up = even("lat")
    after = jnp.where(first_up, near_pair, far_pair)
    before = jnp.where(first_up, far_pair, near_pair)
    top = ids(TILE, 0) < HALO
    return (
        jnp.where(top, after, pltpu.roll(before, HALO, 0)),
        jnp.where(top, pltpu.roll(after, HALO, 0), before),
    )


def add_sides(turned, fixed, near_sides, far_sides, own, own_fixed, near_lat, far_lat, partner):
    t = lax.axis_index("tm")
    from_near = (t == 0) != even("lon")
    count = near_sides.shape[0]
    beside = [jnp.where(from_near, near_sides[i], far_sides[i]) for i in range(count)]
    other = [jnp.where(from_near, far_sides[i], near_sides[i]) for i in range(HALO)]
    for i in range(HALO):
        own[outer_at(i)] = beside[i]
        partner[i] = other[i]
    for i in range(2):
        own_fixed[outer_at(i)] = beside[HALO + i]
        own_fixed[outer_at(i + 2)] = swapped(beside[HALO + i])
        near_lat[PARTNER + i], far_lat[PARTNER + i] = edge_pair(other[i], other[i + 2])

    def copy(i):
        at = main_at(i)
        lon = (LONS - SENT) * t + i
        own[at] = heated(turned[lon], fixed[lon])
        own_fixed[at] = fixed[lon]

    blocks(0, SENT, 17, copy)

    def rows(i):
        near_lat[i], far_lat[i] = edge_pair(own[i], own[i + PAIRS])

    blocks(0, SPLIT, 12, rows)
    low = in_low(TILE)

    def fixed_rows(i):
        here = edge_pair(own_fixed[i], own_fixed[i + PAIRS])
        there = edge_pair(own_fixed[i + QUADS], own_fixed[i + PAIRS + QUADS])
        near_lat[FIXED + i], far_lat[FIXED + i] = [jnp.where(low, a, swapped(b)) for a, b in zip(here, there)]

    blocks(0, QUADS, 9, fixed_rows)


def start_of_step(fixed, rows):
    add = jnp.logical_and(jnp.logical_not(in_low(rows)), lax.axis_index("tm") == 1)
    return jnp.where(add, fixed, 0.0)


def pass_rows(edges, own, own_fixed, heated_edges, near_rows, far_rows):
    top = ids(TILE, 0) < HALO

    def heat(i):
        fixed = own_fixed[main_at(i)]
        heated_edges[i] = edges[i] + start_of_step(jnp.where(top, fixed[:TILE], fixed[TILE:]), TILE)

    blocks(0, SENT, 17, heat)

    def rows(i):
        near_rows[i], far_rows[i] = edge_pair(heated_edges[i], heated_edges[i + SENT_PAIRS])

    blocks(0, SENT_PAIRS, 17, rows)

    def rest(i):
        near_rows[SENT_PAIRS + i], far_rows[SENT_PAIRS + i] = edge_pair(own[SPLIT + i], own[SPLIT + i + PAIRS])

    blocks(0, PAIRS - SPLIT, 12, rest)


def join(near_lat, far_lat, near_rows, far_rows, halo, other):
    def place(i, tiles):
        halo[i], halo[i + PAIRS] = tiles

    blocks(0, SPLIT, 12, lambda i: place(i, halo_tiles(near_lat[i], far_lat[i])))

    def rest(i):
        at = SENT_PAIRS + i
        place(SPLIT + i, halo_tiles(near_rows[at], far_rows[at]))

    blocks(0, PAIRS - SPLIT, 12, rest)

    def theirs(i):
        other[main_at(i)], other[main_at(i + SENT_PAIRS)] = halo_tiles(near_rows[i], far_rows[i])

    blocks(0, SENT_PAIRS, 17, theirs)


def both_steps(mine, theirs):
    first = lax.axis_index("tm") == 0
    low = in_low(mine.shape[0])
    step0, step1 = jnp.where(first, mine, theirs), jnp.where(first, theirs, mine)
    moved = swapped(step0)
    return jnp.where(low, step0, swapped(step1)), jnp.where(low, moved, step1 + moved)


def gather(edges, middle, own, own_fixed, it, source):
    top = ids(TILE, 0) < HALO

    def step(i):
        at = main_at(i)
        fixed = own_fixed[at]
        e = edges[i]
        m = middle[i] + start_of_step(jnp.where(top, fixed[TILE:], fixed[:TILE]), TILE)
        theirs = cat(jnp.where(top, e, m), jnp.where(top, m, e))
        it[at], source[at] = both_steps(own[at], theirs)

    blocks(0, SENT, 17, step)


def strips(partner, near_lat, far_lat, _, xs):
    for i in range(2):
        at = PARTNER + i
        for place, tile in zip((i, i + 2), halo_tiles(near_lat[at], far_lat[at])):
            xs[place] = cat(partner[place], tile)


def reciprocal(d):
    y = pl.reciprocal(d, approx=True)
    return y * (2.0 - d * y)


def face(a, b, twice):
    return twice * b * reciprocal(jnp.maximum(a + b, 1e-30))


def woven(ref, at):
    return cat(*[ref[at, pl.ds(j, TILE, stride=3), :] for j in range(3)])


def next_row(x):
    return cat(x[TILE:], pltpu.roll(x[:TILE], TILE - 1, 0))


def last_row(x):
    return cat(pltpu.roll(x[-TILE:], 1, 0), x[:-TILE])


def near(around, w):
    before, mid, after = around
    wxp, wx, wy, wyp, wl = w
    total = wxp * before + wx * after
    total = total + (wy * next_row(mid) + wyp * last_row(mid))
    return total + (wl * pltpu.roll(mid, 127, 1) + pltpu.roll(wl * mid, 1, 1))


def prepare(own_fixed, near_lat, far_lat, _, wx, wy, wyp, wl, total, inv, K):
    rows = ROWS + TILE
    low = in_low(ROWS)
    low_tile = in_low(TILE)
    beta = corner_weight ** 0.5
    K[PLACES] = jnp.zeros((rows, 128), jnp.float32)

    def assemble_fixed(i):
        for at, tile in zip((i, i + PAIRS), halo_tiles(near_lat[FIXED + i], far_lat[FIXED + i])):
            moved = swapped(tile)
            for here, value in ((at, jnp.where(low_tile, tile, moved)), (at + QUADS, jnp.where(low_tile, moved, tile))):
                main = own_fixed[here]
                K[here] = cat(jnp.where(low, main, swapped(main)), value)

    blocks(0, QUADS, 9, assemble_fixed)
    lane = ids(rows, 1)
    inside = (lane & (LEVELS - 1)) != LEVELS - 1
    shift = jnp.where(lane < LEVELS, 1.0 - beta, 1.0 + beta)
    width = 18

    def weigh(i, carry):
        start = i * width
        here = woven(K, start)
        before = wx[jnp.maximum(start - 1, 0)]
        for u in range(width):
            at = start + u
            after = woven(K, at + 1)
            twice = 2.0 * here
            side = face(here, after, twice)
            row = face(here, next_row(here), twice)
            previous = last_row(row)
            level = jnp.where(inside, face(here, pltpu.roll(here, 127, 1), twice), 0.0)
            sums = (before + side) + (row + previous) + (level + pltpu.roll(level, 1, 1))
            wx[at], wy[at], wyp[at], wl[at] = side, row, previous, level
            total[at] = sums
            inv[at] = reciprocal(shift + sums)
            here, before = after, side
        return carry

    wx[0] = jnp.zeros((rows, 128), jnp.float32)
    lax.fori_loop(0, PLACES // width, weigh, 0)


STAGES = ((1, 39, 71), (2, 38, 70), (3, 37, 69), (4, 36, 68))
WIDTHS = ((19, 12, 17, 16), (16, 16, 16, 16))
READY = 40
EDGE = 12


def iterate_half(
    upper, wx, wy, wyp, wl, total, inv, own, own_halo, other_halo, it_main, source_main, *refs
):
    if upper:
        xs, edge, w_own, w_send, *refs = refs
    else:
        w_own, w_send, edge, *refs = refs
    it, source, spec, x, y, z, natural = refs
    rows = ROWS + TILE
    first = lax.axis_index("tm") == 0
    low = in_low(rows)
    beta = corner_weight ** 0.5
    gamma = jnp.where(low, 1.0, beta)
    shared = [(it, 38), (it, 39), (source, 39), (x, 37), (x, 38), (y, 36), (y, 37), (z, 35), (z, 36)]
    shared += [(spec, 36), (spec, 37), (spec, 38)]
    if upper:
        for i, (ref, at) in enumerate(shared):
            ref[at] = edge[i]

    def assemble(at):
        a, b = both_steps(own_halo[at], other_halo[at])
        it[at], source[at] = cat(it_main[at], a), cat(source_main[at], b)

    if upper:
        blocks(READY, SENT, 14, assemble)
        for i in range(HALO):
            at = outer_at(i)
            it[at], source[at] = both_steps(cat(own[at], own_halo[at]), xs[i])
    else:
        blocks(0, READY, 10, assemble)

    def over(stage, read, ref, step):
        lo, hi = STAGES[stage][upper : upper + 2]
        width = WIDTHS[upper][stage]

        def body(i, carry):
            start = lo + i * width
            around = [read(ref, start - 1), read(ref, start)]
            before = wx[start - 1]
            for u in range(width):
                at = start + u
                around = [*around[-2:], read(ref, at + 1)]
                side = wx[at]
                step(at, around, (before, side, wy[at], wyp[at], wl[at]))
                before = side
            return carry

        lax.fori_loop(0, (hi - lo) // width, body, 0)

    def residual(at, around, w):
        left = (woven(source, at) - ((1.0 + total[at]) * around[1] - near(around, w))) * gamma
        moved = swapped(left)
        value = jnp.where(low, left + moved, moved - left)
        spec[at] = value
        x[at] = value * inv[at]

    over(0, woven, it, residual)

    def plain(ref, at):
        return ref[at]

    def sweep(at, around, w):
        return (spec[at] + near(around, w)) * inv[at]

    def to(ref):
        def step(at, around, w):
            ref[at] = sweep(at, around, w)

        return step

    over(1, plain, x, to(y))
    over(2, plain, y, to(z))
    base = STAGES[3][upper]
    back = jnp.where(low, 0.5, 0.5 / beta)

    def last(at, around, w):
        value = sweep(at, around, w)
        moved = swapped(value)
        value = jnp.where(low, value + moved, moved - value) * back
        lon = at - base
        lon = jnp.where(first, HALF // 2 - 1 - lon, lon)
        for j in range(3):
            natural[pl.ds(lon * rows + j, TILE, stride=3), :] = value[j * TILE : (j + 1) * TILE]

    over(3, plain, z, last)
    count = HALF // 2
    for q in range(4):
        turned = cat(*[natural[pl.ds(q + 4 * j, count, stride=rows), :] for j in range(4)]).T
        step0, step1 = turned[:LEVELS], turned[LEVELS:]
        w_own[q] = jnp.where(first, step0, step1)
        w_send[q] = jnp.where(first, step1, step0)
    if not upper:
        for i, (ref, at) in enumerate(shared):
            edge[i] = ref[at]


def placed(value, j, quarter):
    return pltpu.roll(value, (32 * (quarter - j) + 128) & 127, 1)


def finish_most(it, own_low, own_high, got_low, most):
    t = lax.axis_index("tm")
    group = ids(LEVELS, 1) // 32

    def step(q):
        for j in range(4):
            row = q + 4 * j
            value = it[pl.ds(row, LEVELS, stride=ROWS), :]
            for piece, quarter in ((own_low, 1 + t), (own_high, 3 * t), (got_low, 2 - t)):
                value = jnp.where(group == quarter, value + placed(piece[q], j, quarter), value)
            most[row] = value

    blocks(0, 4, 2, step)


def finish(most, got_high, out_hbm, out, sems):
    quarter = 3 - 3 * lax.axis_index("tm")
    part = LEVELS // CHUNKS
    here = ids(part, 1) // 32 == quarter

    def copy(c):
        span = pl.ds(pl.multiple_of(c * part * ROWS, part * ROWS), part * ROWS)
        return pltpu.make_async_copy(out.at[span], out_hbm.at[span], sems.at[c])

    def step(c):
        for q in range(4):
            value = got_high[q, pl.ds(pl.multiple_of(c * part, part), part), :]
            for j in range(4):
                old = most[q + 4 * j, pl.ds(pl.multiple_of(c * part, part), part), :]
                out[pl.ds(c * part * ROWS + q + 4 * j, part, stride=ROWS), :] = jnp.where(here, old + placed(value, j, quarter), old)
        copy(c).start()

    blocks(0, CHUNKS, 1, step)
    for c in range(CHUNKS):
        copy(c).wait()


def two_steps(iterate, heating, initial, region, cond_table):
    lats, lons = lax.axis_size("lat"), lax.axis_size("lon")
    swap = [(0, 1), (1, 0)]
    pairs = [[(i, i + 1) for i in range(start, lats - 1, 2)] for start in (0, 1)]
    pairs = [p + [(j, i) for i, j in p] for p in pairs]
    round_lon = [[(i, (i + 1) % lons) for i in range(start, lons, 2)] for start in (0, 1)]
    round_lon = [p + [(j, i) for i, j in p] for p in round_lon]
    flat = (LEVELS * ROWS, LONS)
    turned_flat = (LONS * ROWS, 2 * LEVELS)
    by_lon = (LONS, ROWS, 2 * LEVELS)
    wide = shape(PLACES, ROWS + TILE, 128)

    def in_hbm(x):
        return pltpu.with_memory_space_constraint(x, pltpu.HBM)

    half_rows = shape(SENT, TILE, 128)
    edges, middle, turned, it = call(
        send_first,
        [half_rows, half_rows, shape(*turned_flat), shape(*flat)],
        [in_hbm(iterate[0]), in_hbm(heating[0])],
        scratch=[buffer(*flat), pltpu.SemaphoreType.DMA((ROWS // TILE, 2, 2))],
        hbm_ins=(0, 1),
    )
    edges = lax.ppermute(edges, "tm", swap)
    middle = lax.ppermute(middle, "tm", swap)
    sides = shape(HALO + 2, ROWS, 128)
    fixed, near_sides, far_sides = call(
        send_sides,
        [shape(*turned_flat), sides, sides],
        [turned, region.reshape(flat), initial.reshape(flat), in_hbm(cond_table)],
        scratch=[pltpu.SMEM(cond_table.shape, jnp.float32), pltpu.SemaphoreType.DMA],
        hbm_ins=(3,),
    )
    near_sides = lax.ppermute(near_sides, "lon", round_lon[0])
    far_sides = lax.ppermute(far_sides, "lon", round_lon[1])
    main = shape(PLACES, ROWS, 128)
    lat = shape(PARTNER + 2, TILE, 128)
    own_main, own_fixed, near_lat, far_lat, partner = call(
        add_sides,
        [main, main, lat, lat, shape(HALO, ROWS, 128)],
        [turned.reshape(by_lon), fixed.reshape(by_lon), near_sides, far_sides],
    )
    near_lat = lax.ppermute(near_lat, "lat", pairs[0])
    far_lat = lax.ppermute(far_lat, "lat", pairs[1])
    rows = shape(SENT_PAIRS + PAIRS - SPLIT, TILE, 128)
    edges, near_rows, far_rows = call(
        pass_rows, [half_rows, rows, rows], [edges, own_main, own_fixed], work=200
    )
    near_rows = lax.ppermute(near_rows, "lat", pairs[0])
    far_rows = lax.ppermute(far_rows, "lat", pairs[1])
    it_main, source_main = call(gather, [main, main], [edges, middle, own_main, own_fixed])
    (xs,) = call(strips, [shape(HALO, ROWS + TILE, 128)], [partner, near_lat, far_lat, it_main])
    xs = lax.ppermute(xs, "tm", swap)
    ready = call(
        prepare,
        [wide] * 6,
        [own_fixed, near_lat, far_lat, it_main],
        scratch=[buffer(PLACES + 1, ROWS + TILE, 128)],
    )
    halos = call(join, [shape(PLACES, TILE, 128)] * 2, [near_lat, far_lat, near_rows, far_rows])
    given = [*ready, own_main, *halos, it_main, source_main]
    corrections = [shape(4, LEVELS, 128)] * 2
    fields = [buffer(PLACES, ROWS + TILE, 128)] * 6 + [buffer(HALF // 2 * (ROWS + TILE), 128)]
    own_low, send_low, edge = call(
        functools.partial(iterate_half, 0),
        [*corrections, shape(EDGE, ROWS + TILE, 128)],
        given,
        scratch=fields,
        limit=16,
    )
    got_low = lax.ppermute(send_low, "tm", swap)
    own_high, send_high = call(
        functools.partial(iterate_half, 1), corrections, [*given, xs, edge], scratch=fields, limit=16
    )
    got_high = lax.ppermute(send_high, "tm", swap)
    (most,) = call(finish_most, [shape(ROWS, LEVELS, LONS)], [it, own_low, own_high, got_low])
    (out,) = call(
        finish,
        [shape(*flat)],
        [most, got_high],
        scratch=[buffer(*flat), pltpu.SemaphoreType.DMA((CHUNKS,))],
        hbm_outs=(0,),
    )
    return out.reshape(iterate.shape)


def solution(mesh):
    return jax.shard_map(
        two_steps if mesh.shape["tm"] == 2 else on_device,
        mesh=mesh,
        in_specs=(
            P("tm", None, "lat", "lon"),
            P("tm", None, "lat", "lon"),
            P(None, "lat", "lon"),
            P(None, "lat", "lon"),
            P(),
        ),
        out_specs=P("tm", None, "lat", "lon"),
        check_vma=False,
    )
```

```python
import functools

import jax
import jax.numpy as jnp
from jax import lax
from jax.experimental import pallas as pl
from jax.experimental.pallas import tpu as pltpu
from jax.sharding import PartitionSpec as P

SWEEPS = 4


corner_weight = 0.1


def padded(value, sides, width, wrap):
    for axis, dim in sides:
        peers, length = (lax.axis_size(axis), value.shape[dim])
        up = [(i, (i + 1) % peers) for i in range(peers if wrap else peers - 1)]
        down = [(j, i) for i, j in up]
        last = lax.slice_in_dim(value, length - width, length, axis=dim)
        initial = lax.slice_in_dim(value, 0, width, axis=dim)
        before = lax.ppermute(last, axis, up)
        after = lax.ppermute(initial, axis, down)
        value = jnp.concatenate([before, value, after], axis=dim)
    return value


def passed_along(block, axis, distance):
    devices = range(lax.axis_size(axis))
    route = [(i - distance, i) for i in devices if i - distance in devices]
    return lax.ppermute(block, axis, route)


def harmonic(first, second):
    return 2.0 * first * second / (first + second)


def conductivity(region, cond_table):
    classes = jnp.arange(cond_table.shape[0], dtype=jnp.int32)
    onehot = (region[..., None] == classes).astype(jnp.float32)
    return jnp.sum(onehot * cond_table, axis=-1)


def extend(stack):
    lat_ext = padded(stack, (("lat", 2),), 1, False)
    both = padded(lat_ext, (("lon", 3),), 1, True)
    return jnp.pad(both, ((0, 0), (1, 1), (0, 0), (0, 0)))


def face_weights(kext):
    centre = kext[1:-1, 1:-1, 1:-1]
    return (
        harmonic(centre, kext[:-2, 1:-1, 1:-1]),
        harmonic(centre, kext[2:, 1:-1, 1:-1]),
        harmonic(centre, kext[1:-1, :-2, 1:-1]),
        harmonic(centre, kext[1:-1, 2:, 1:-1]),
        harmonic(centre, kext[1:-1, 1:-1, :-2]),
        harmonic(centre, kext[1:-1, 1:-1, 2:]),
    )


def neighbours(weights, ext):
    near = weights[0] * ext[..., :-2, 1:-1, 1:-1] + weights[1] * ext[..., 2:, 1:-1, 1:-1]
    near = near + weights[2] * ext[..., 1:-1, :-2, 1:-1] + weights[3] * ext[..., 1:-1, 2:, 1:-1]
    near = near + weights[4] * ext[..., 1:-1, 1:-1, :-2] + weights[5] * ext[..., 1:-1, 1:-1, 2:]
    return near


def on_device(iterate, heating, initial, region, cond_table):
    steps = lax.axis_size("tm")
    own = lax.axis_index("tm")
    high = lax.Precision.HIGHEST
    kfield = conductivity(region, cond_table)
    ext = extend(jnp.stack([kfield, iterate[0]]))
    weights = face_weights(ext[0])
    total = weights[0] + weights[1] + weights[2] + weights[3] + weights[4] + weights[5]
    shifted = passed_along(iterate, "tm", 1)[0]
    previous = jnp.where(own == 0, initial, shifted)
    residual = heating[0] + previous - ((1.0 + total) * iterate[0] - neighbours(weights, ext[1]))
    scale_own = corner_weight ** (own.astype(jnp.float32) / steps)
    scaled = residual * scale_own
    zeros = jnp.zeros_like(residual)
    piece = lax.all_gather(scaled[None], "tm", axis=0, tiled=True)
    order = jnp.arange(piece.shape[0], dtype=jnp.int32)
    angle = 2.0 * jnp.pi / steps * (own * order % steps).astype(jnp.float32)
    real_part = jnp.einsum("n,nabc->abc", jnp.cos(angle), piece, precision=high)
    imag_part = (zeros, zeros)[1] - jnp.einsum("n,nabc->abc", jnp.sin(angle), piece, precision=high)
    beta = corner_weight ** (1.0 / steps)
    freq_angle = 2.0 * jnp.pi / steps * (own % steps).astype(jnp.float32)
    diag_re = 1.0 - beta * jnp.cos(freq_angle) + total
    diag_im = beta * jnp.sin(freq_angle) + zeros
    denom = diag_re * diag_re + diag_im * diag_im
    inv_re = diag_re / denom
    inv_im = -diag_im / denom
    sol_re = real_part * inv_re - imag_part * inv_im
    sol_im = real_part * inv_im + imag_part * inv_re
    for sweep in range(SWEEPS - 1):
        near = neighbours(weights, extend(jnp.stack([sol_re, sol_im])))
        rhs_re = real_part + near[0]
        rhs_im = imag_part + near[1]
        sol_re = rhs_re * inv_re - rhs_im * inv_im
        sol_im = rhs_re * inv_im + rhs_im * inv_re
    pieces = (
        lax.all_gather(sol_re[None], "tm", axis=0, tiled=True),
        lax.all_gather(sol_im[None], "tm", axis=0, tiled=True),
    )
    order = jnp.arange(pieces[0].shape[0], dtype=jnp.int32)
    angle = 2.0 * jnp.pi / steps * (order * own % steps).astype(jnp.float32)
    summed = jnp.einsum("k,kabc->abc", jnp.cos(angle), pieces[0], precision=high) - jnp.einsum(
        "k,kabc->abc", jnp.sin(angle), pieces[1], precision=high
    )
    back = summed / steps
    return iterate + (back / scale_own)[None]


HALO = 4
TILE = 8
LEVELS = 64
ROWS = 16
LONS = 128
HALF = 64
SENT = HALF + HALO
PLACES = HALF + 2 * HALO
PAIRS = PLACES // 2
SENT_PAIRS = SENT // 2
QUADS = PLACES // 4
SPLIT = 24
FIXED = SPLIT
PARTNER = SPLIT + QUADS
CHUNKS = 4


def specs(count, hbm):
    return [pl.BlockSpec(memory_space=pltpu.HBM if i in hbm else pltpu.VMEM) for i in range(count)]


def call(body, outs, ins, scratch=(), limit=8, hbm_ins=(), hbm_outs=(), work=1):
    moved = work * (sum(x.size * 4 for x in ins) + sum(x.size * 4 for x in outs))
    return pl.pallas_call(
        body,
        out_shape=outs,
        in_specs=specs(len(ins), hbm_ins),
        out_specs=specs(len(outs), hbm_outs),
        scratch_shapes=scratch,
        compiler_params=pltpu.CompilerParams(vmem_limit_bytes=limit << 20),
        cost_estimate=pl.CostEstimate(flops=moved * 4, bytes_accessed=moved, transcendentals=0),
    )(*ins)


def shape(*dims):
    return jax.ShapeDtypeStruct(dims, jnp.float32)


def buffer(*dims):
    return pltpu.VMEM(dims, jnp.float32)


def ids(rows, dim):
    return lax.broadcasted_iota(jnp.int32, (rows, 128), dim)


def in_low(rows):
    return ids(rows, 1) < LEVELS


def swapped(x):
    return pltpu.roll(x, LEVELS, 1)


def main_at(i):
    return jnp.where(lax.axis_index("tm") == 0, SENT - 1 - i, i)


def outer_at(i):
    return jnp.where(lax.axis_index("tm") == 0, PLACES - 1 - i, SENT + i)


def cat(*values):
    return jnp.concatenate(values, axis=0)


def even(axis):
    return lax.rem(lax.axis_index(axis), 2) == 0


def blocks(lo, hi, width, step):
    def body(i, carry):
        for u in range(width):
            step(lo + i * width + u)
        return carry

    lax.fori_loop(0, (hi - lo) // width, body, 0)


def send_first(it_hbm, h_hbm, edges, middle, turned, it, h, sems):
    t = lax.axis_index("tm")
    by_level = (LEVELS, ROWS, LONS)
    copies = []
    for k in range(ROWS // TILE):
        for f, (source, target) in enumerate(((it_hbm, it), (h_hbm, h))):
            for c in range(2):
                part = pl.ds(c * LEVELS // 2, LEVELS // 2), pl.ds(k * TILE, TILE)
                copy = pltpu.make_async_copy(source.at[part], target.reshape(by_level).at[part], sems.at[k, f, c])
                copy.start()
                copies.append(copy)

    def turn(r):
        rows = pl.ds(r, LEVELS, stride=ROWS)
        turned[pl.ds(r, LONS, stride=ROWS), :] = cat(it[rows, :], h[rows, :]).T

    for k in range(ROWS // TILE):
        for copy in copies[4 * k : 4 * k + 4]:
            copy.wait()
        blocks(k * TILE, (k + 1) * TILE, 8, turn)
    start = (LONS - SENT) * ROWS * (1 - t)
    top = ids(TILE, 0) < HALO

    def cut(i):
        at = pl.multiple_of(start + i * ROWS, ROWS)
        low, high = turned[pl.ds(at, TILE), :], turned[pl.ds(at + TILE, TILE), :]
        edges[i] = jnp.where(top, low, high)
        middle[i] = jnp.where(top, high, low)

    blocks(0, SENT, 17, cut)


def heated(turned, fixed):
    add = jnp.logical_and(jnp.logical_not(in_low(ROWS)), lax.axis_index("tm") == 0)
    return turned + jnp.where(add, fixed, 0.0)


def send_sides(turned, region, initial, table_hbm, fixed, near_sides, far_sides, table, sem):
    copy = pltpu.make_async_copy(table_hbm, table, sem)
    copy.start()
    copy.wait()

    def turn(r):
        rows = pl.ds(r, LEVELS, stride=ROWS)
        classes = region[rows, :]
        value = jnp.full(classes.shape, table[0], jnp.float32)
        for c in range(1, table.shape[0]):
            value = jnp.where(classes == c, table[c], value)
        fixed[pl.ds(r, LONS, stride=ROWS), :] = cat(value, initial[rows, :]).T

    blocks(0, ROWS, 8, turn)
    near_right = even("lon")
    low = in_low(ROWS)

    def strip(first_lon):
        def at(ref, i):
            return ref[(first_lon + i) * ROWS : (first_lon + i + 1) * ROWS, :]

        return [heated(at(turned, i), at(fixed, i)) for i in range(HALO)] + [
            jnp.where(low, at(fixed, i), swapped(at(fixed, i + 2))) for i in range(2)
        ]

    for i, (right, left) in enumerate(zip(strip(LONS - HALO), strip(0))):
        near_sides[i] = jnp.where(near_right, right, left)
        far_sides[i] = jnp.where(near_right, left, right)


def edge_pair(first, second):
    top = ids(TILE, 0) < HALO
    first_up = even("lat")
    down = jnp.where(top, first[:TILE], pltpu.roll(second[:TILE], HALO, 0))
    up = jnp.where(top, pltpu.roll(first[-TILE:], HALO, 0), second[-TILE:])
    return jnp.where(first_up, up, down), jnp.where(first_up, down, up)


def halo_tiles(near_pair, far_pair):
    first_up = even("lat")
    after = jnp.where(first_up, near_pair, far_pair)
    before = jnp.where(first_up, far_pair, near_pair)
    top = ids(TILE, 0) < HALO
    return (
        jnp.where(top, after, pltpu.roll(before, HALO, 0)),
        jnp.where(top, pltpu.roll(after, HALO, 0), before),
    )


def add_sides(turned, fixed, near_sides, far_sides, own, own_fixed, near_lat, far_lat, partner):
    t = lax.axis_index("tm")
    from_near = (t == 0) != even("lon")
    count = near_sides.shape[0]
    beside = [jnp.where(from_near, near_sides[i], far_sides[i]) for i in range(count)]
    other = [jnp.where(from_near, far_sides[i], near_sides[i]) for i in range(HALO)]
    for i in range(HALO):
        own[outer_at(i)] = beside[i]
        partner[i] = other[i]
    for i in range(2):
        own_fixed[outer_at(i)] = beside[HALO + i]
        own_fixed[outer_at(i + 2)] = swapped(beside[HALO + i])
        near_lat[PARTNER + i], far_lat[PARTNER + i] = edge_pair(other[i], other[i + 2])

    def copy(i):
        at = main_at(i)
        lon = (LONS - SENT) * t + i
        own[at] = heated(turned[lon], fixed[lon])
        own_fixed[at] = fixed[lon]

    blocks(0, SENT, 34, copy)

    def rows(i):
        near_lat[i], far_lat[i] = edge_pair(own[i], own[i + PAIRS])

    blocks(0, SPLIT, 12, rows)
    low = in_low(TILE)

    def fixed_rows(i):
        here = edge_pair(own_fixed[i], own_fixed[i + PAIRS])
        there = edge_pair(own_fixed[i + QUADS], own_fixed[i + PAIRS + QUADS])
        near_lat[FIXED + i], far_lat[FIXED + i] = [jnp.where(low, a, swapped(b)) for a, b in zip(here, there)]

    blocks(0, QUADS, 9, fixed_rows)


def start_of_step(fixed, rows):
    add = jnp.logical_and(jnp.logical_not(in_low(rows)), lax.axis_index("tm") == 1)
    return jnp.where(add, fixed, 0.0)


def pass_rows(edges, own, own_fixed, heated_edges, near_rows, far_rows):
    top = ids(TILE, 0) < HALO

    def heat(i):
        fixed = own_fixed[main_at(i)]
        heated_edges[i] = edges[i] + start_of_step(jnp.where(top, fixed[:TILE], fixed[TILE:]), TILE)

    blocks(0, SENT, 17, heat)

    def rows(i):
        near_rows[i], far_rows[i] = edge_pair(heated_edges[i], heated_edges[i + SENT_PAIRS])

    blocks(0, SENT_PAIRS, 17, rows)

    def rest(i):
        near_rows[SENT_PAIRS + i], far_rows[SENT_PAIRS + i] = edge_pair(own[SPLIT + i], own[SPLIT + i + PAIRS])

    blocks(0, PAIRS - SPLIT, 12, rest)


def join(near_lat, far_lat, near_rows, far_rows, halo, other):
    def place(i, tiles):
        halo[i], halo[i + PAIRS] = tiles

    blocks(0, SPLIT, 12, lambda i: place(i, halo_tiles(near_lat[i], far_lat[i])))

    def rest(i):
        at = SENT_PAIRS + i
        place(SPLIT + i, halo_tiles(near_rows[at], far_rows[at]))

    blocks(0, PAIRS - SPLIT, 12, rest)

    def theirs(i):
        other[main_at(i)], other[main_at(i + SENT_PAIRS)] = halo_tiles(near_rows[i], far_rows[i])

    blocks(0, SENT_PAIRS, 17, theirs)


def both_steps(mine, theirs):
    first = lax.axis_index("tm") == 0
    low = in_low(mine.shape[0])
    step0, step1 = jnp.where(first, mine, theirs), jnp.where(first, theirs, mine)
    moved = swapped(step0)
    return jnp.where(low, step0, swapped(step1)), jnp.where(low, moved, step1 + moved)


def gather(edges, middle, own, own_fixed, it, source):
    top = ids(TILE, 0) < HALO

    def step(i):
        at = main_at(i)
        fixed = own_fixed[at]
        e = edges[i]
        m = middle[i] + start_of_step(jnp.where(top, fixed[TILE:], fixed[:TILE]), TILE)
        theirs = cat(jnp.where(top, e, m), jnp.where(top, m, e))
        it[at], source[at] = both_steps(own[at], theirs)

    blocks(0, SENT, 17, step)


def strips(partner, near_lat, far_lat, _, xs):
    for i in range(2):
        at = PARTNER + i
        for place, tile in zip((i, i + 2), halo_tiles(near_lat[at], far_lat[at])):
            xs[place] = cat(partner[place], tile)


def reciprocal(d):
    y = pl.reciprocal(d, approx=True)
    return y * (2.0 - d * y)


def face(a, b, twice):
    return twice * b * reciprocal(jnp.maximum(a + b, 1e-30))


def woven(ref, at):
    return cat(*[ref[at, pl.ds(j, TILE, stride=3), :] for j in range(3)])


def next_row(x):
    return cat(x[TILE:], pltpu.roll(x[:TILE], TILE - 1, 0))


def last_row(x):
    return cat(pltpu.roll(x[-TILE:], 1, 0), x[:-TILE])


def near(around, w):
    before, mid, after = around
    wxp, wx, wy, wyp, wl = w
    total = wxp * before + wx * after
    total = total + (wy * next_row(mid) + wyp * last_row(mid))
    return total + (wl * pltpu.roll(mid, 127, 1) + pltpu.roll(wl * mid, 1, 1))


def prepare(own_fixed, near_lat, far_lat, _, wx, wy, wyp, wl, total, inv, K):
    rows = ROWS + TILE
    low = in_low(ROWS)
    low_tile = in_low(TILE)
    beta = corner_weight ** 0.5
    K[PLACES] = jnp.zeros((rows, 128), jnp.float32)

    def assemble_fixed(i):
        for at, tile in zip((i, i + PAIRS), halo_tiles(near_lat[FIXED + i], far_lat[FIXED + i])):
            moved = swapped(tile)
            for here, value in ((at, jnp.where(low_tile, tile, moved)), (at + QUADS, jnp.where(low_tile, moved, tile))):
                main = own_fixed[here]
                K[here] = cat(jnp.where(low, main, swapped(main)), value)

    blocks(0, QUADS, 9, assemble_fixed)
    lane = ids(rows, 1)
    inside = (lane & (LEVELS - 1)) != LEVELS - 1
    shift = jnp.where(lane < LEVELS, 1.0 - beta, 1.0 + beta)
    width = 18

    def weigh(i, carry):
        start = i * width
        here = woven(K, start)
        before = wx[jnp.maximum(start - 1, 0)]
        for u in range(width):
            at = start + u
            after = woven(K, at + 1)
            twice = 2.0 * here
            side = face(here, after, twice)
            row = face(here, next_row(here), twice)
            previous = last_row(row)
            level = jnp.where(inside, face(here, pltpu.roll(here, 127, 1), twice), 0.0)
            sums = (before + side) + (row + previous) + (level + pltpu.roll(level, 1, 1))
            wx[at], wy[at], wyp[at], wl[at] = side, row, previous, level
            total[at] = sums
            inv[at] = reciprocal(shift + sums)
            here, before = after, side
        return carry

    wx[0] = jnp.zeros((rows, 128), jnp.float32)
    lax.fori_loop(0, PLACES // width, weigh, 0)


STAGES = ((1, 39, 71), (2, 38, 70), (3, 37, 69), (4, 36, 68))
WIDTHS = ((19, 12, 17, 16), (16, 16, 16, 16))
READY = 40
EDGE = 12


def iterate_half(
    upper, wx, wy, wyp, wl, total, inv, own, own_halo, other_halo, it_main, source_main, *refs
):
    if upper:
        xs, edge, w_own, w_send, *refs = refs
    else:
        w_own, w_send, edge, *refs = refs
    it, source, spec, x, y, z, natural = refs
    rows = ROWS + TILE
    first = lax.axis_index("tm") == 0
    low = in_low(rows)
    beta = corner_weight ** 0.5
    gamma = jnp.where(low, 1.0, beta)
    shared = [(it, 38), (it, 39), (source, 39), (x, 37), (x, 38), (y, 36), (y, 37), (z, 35), (z, 36)]
    shared += [(spec, 36), (spec, 37), (spec, 38)]
    if upper:
        for i, (ref, at) in enumerate(shared):
            ref[at] = edge[i]

    def assemble(at):
        a, b = both_steps(own_halo[at], other_halo[at])
        it[at], source[at] = cat(it_main[at], a), cat(source_main[at], b)

    if upper:
        blocks(READY, SENT, 14, assemble)
        for i in range(HALO):
            at = outer_at(i)
            it[at], source[at] = both_steps(cat(own[at], own_halo[at]), xs[i])
    else:
        blocks(0, READY, 10, assemble)

    def over(stage, read, ref, step):
        lo, hi = STAGES[stage][upper : upper + 2]
        width = WIDTHS[upper][stage]

        def body(i, carry):
            start = lo + i * width
            around = [read(ref, start - 1), read(ref, start)]
            before = wx[start - 1]
            for u in range(width):
                at = start + u
                around = [*around[-2:], read(ref, at + 1)]
                side = wx[at]
                step(at, around, (before, side, wy[at], wyp[at], wl[at]))
                before = side
            return carry

        lax.fori_loop(0, (hi - lo) // width, body, 0)

    def residual(at, around, w):
        left = (woven(source, at) - ((1.0 + total[at]) * around[1] - near(around, w))) * gamma
        moved = swapped(left)
        value = jnp.where(low, left + moved, moved - left)
        spec[at] = value
        x[at] = value * inv[at]

    over(0, woven, it, residual)

    def plain(ref, at):
        return ref[at]

    def sweep(at, around, w):
        return (spec[at] + near(around, w)) * inv[at]

    def to(ref):
        def step(at, around, w):
            ref[at] = sweep(at, around, w)

        return step

    over(1, plain, x, to(y))
    over(2, plain, y, to(z))
    base = STAGES[3][upper]
    back = jnp.where(low, 0.5, 0.5 / beta)

    def last(at, around, w):
        value = sweep(at, around, w)
        moved = swapped(value)
        value = jnp.where(low, value + moved, moved - value) * back
        lon = at - base
        lon = jnp.where(first, HALF // 2 - 1 - lon, lon)
        for j in range(3):
            natural[pl.ds(lon * rows + j, TILE, stride=3), :] = value[j * TILE : (j + 1) * TILE]

    over(3, plain, z, last)
    count = HALF // 2
    for q in range(4):
        turned = cat(*[natural[pl.ds(q + 4 * j, count, stride=rows), :] for j in range(4)]).T
        step0, step1 = turned[:LEVELS], turned[LEVELS:]
        w_own[q] = jnp.where(first, step0, step1)
        w_send[q] = jnp.where(first, step1, step0)
    if not upper:
        for i, (ref, at) in enumerate(shared):
            edge[i] = ref[at]


def placed(value, j, quarter):
    return pltpu.roll(value, (32 * (quarter - j) + 128) & 127, 1)


def finish_most(it, own_low, own_high, got_low, most):
    t = lax.axis_index("tm")
    group = ids(LEVELS, 1) // 32

    def step(q):
        for j in range(4):
            row = q + 4 * j
            value = it[pl.ds(row, LEVELS, stride=ROWS), :]
            for piece, quarter in ((own_low, 1 + t), (own_high, 3 * t), (got_low, 2 - t)):
                value = jnp.where(group == quarter, value + placed(piece[q], j, quarter), value)
            most[row] = value

    blocks(0, 4, 2, step)


def finish(most, got_high, out_hbm, out, sems):
    quarter = 3 - 3 * lax.axis_index("tm")
    part = LEVELS // CHUNKS
    here = ids(part, 1) // 32 == quarter

    def copy(c):
        span = pl.ds(pl.multiple_of(c * part * ROWS, part * ROWS), part * ROWS)
        return pltpu.make_async_copy(out.at[span], out_hbm.at[span], sems.at[c])

    def step(c):
        for q in range(4):
            value = got_high[q, pl.ds(pl.multiple_of(c * part, part), part), :]
            for j in range(4):
                old = most[q + 4 * j, pl.ds(pl.multiple_of(c * part, part), part), :]
                out[pl.ds(c * part * ROWS + q + 4 * j, part, stride=ROWS), :] = jnp.where(here, old + placed(value, j, quarter), old)
        copy(c).start()

    blocks(0, CHUNKS, 2, step)
    for c in range(CHUNKS):
        copy(c).wait()


def two_steps(iterate, heating, initial, region, cond_table):
    lats, lons = lax.axis_size("lat"), lax.axis_size("lon")
    swap = [(0, 1), (1, 0)]
    pairs = [[(i, i + 1) for i in range(start, lats - 1, 2)] for start in (0, 1)]
    pairs = [p + [(j, i) for i, j in p] for p in pairs]
    round_lon = [[(i, (i + 1) % lons) for i in range(start, lons, 2)] for start in (0, 1)]
    round_lon = [p + [(j, i) for i, j in p] for p in round_lon]
    flat = (LEVELS * ROWS, LONS)
    turned_flat = (LONS * ROWS, 2 * LEVELS)
    by_lon = (LONS, ROWS, 2 * LEVELS)
    wide = shape(PLACES, ROWS + TILE, 128)

    def in_hbm(x):
        return pltpu.with_memory_space_constraint(x, pltpu.HBM)

    half_rows = shape(SENT, TILE, 128)
    edges, middle, turned, it = call(
        send_first,
        [half_rows, half_rows, shape(*turned_flat), shape(*flat)],
        [in_hbm(iterate[0]), in_hbm(heating[0])],
        scratch=[buffer(*flat), pltpu.SemaphoreType.DMA((ROWS // TILE, 2, 2))],
        hbm_ins=(0, 1),
    )
    edges = lax.ppermute(edges, "tm", swap)
    middle = lax.ppermute(middle, "tm", swap)
    sides = shape(HALO + 2, ROWS, 128)
    fixed, near_sides, far_sides = call(
        send_sides,
        [shape(*turned_flat), sides, sides],
        [turned, region.reshape(flat), initial.reshape(flat), in_hbm(cond_table)],
        scratch=[pltpu.SMEM(cond_table.shape, jnp.float32), pltpu.SemaphoreType.DMA],
        hbm_ins=(3,),
    )
    near_sides = lax.ppermute(near_sides, "lon", round_lon[0])
    far_sides = lax.ppermute(far_sides, "lon", round_lon[1])
    main = shape(PLACES, ROWS, 128)
    lat = shape(PARTNER + 2, TILE, 128)
    own_main, own_fixed, near_lat, far_lat, partner = call(
        add_sides,
        [main, main, lat, lat, shape(HALO, ROWS, 128)],
        [turned.reshape(by_lon), fixed.reshape(by_lon), near_sides, far_sides],
    )
    near_lat = lax.ppermute(near_lat, "lat", pairs[0])
    far_lat = lax.ppermute(far_lat, "lat", pairs[1])
    rows = shape(SENT_PAIRS + PAIRS - SPLIT, TILE, 128)
    edges, near_rows, far_rows = call(
        pass_rows, [half_rows, rows, rows], [edges, own_main, own_fixed], work=200
    )
    near_rows = lax.ppermute(near_rows, "lat", pairs[0])
    far_rows = lax.ppermute(far_rows, "lat", pairs[1])
    it_main, source_main = call(gather, [main, main], [edges, middle, own_main, own_fixed])
    (xs,) = call(strips, [shape(HALO, ROWS + TILE, 128)], [partner, near_lat, far_lat, it_main])
    xs = lax.ppermute(xs, "tm", swap)
    ready = call(
        prepare,
        [wide] * 6,
        [own_fixed, near_lat, far_lat, it_main],
        scratch=[buffer(PLACES + 1, ROWS + TILE, 128)],
    )
    halos = call(join, [shape(PLACES, TILE, 128)] * 2, [near_lat, far_lat, near_rows, far_rows])
    given = [*ready, own_main, *halos, it_main, source_main]
    corrections = [shape(4, LEVELS, 128)] * 2
    fields = [buffer(PLACES, ROWS + TILE, 128)] * 6 + [buffer(HALF // 2 * (ROWS + TILE), 128)]
    own_low, send_low, edge = call(
        functools.partial(iterate_half, 0),
        [*corrections, shape(EDGE, ROWS + TILE, 128)],
        given,
        scratch=fields,
        limit=16,
    )
    got_low = lax.ppermute(send_low, "tm", swap)
    own_high, send_high = call(
        functools.partial(iterate_half, 1), corrections, [*given, xs, edge], scratch=fields, limit=16
    )
    got_high = lax.ppermute(send_high, "tm", swap)
    (most,) = call(finish_most, [shape(ROWS, LEVELS, LONS)], [it, own_low, own_high, got_low])
    (out,) = call(
        finish,
        [shape(*flat)],
        [most, got_high],
        scratch=[buffer(*flat), pltpu.SemaphoreType.DMA((CHUNKS,))],
        hbm_outs=(0,),
    )
    return out.reshape(iterate.shape)


def solution(mesh):
    return jax.shard_map(
        two_steps if mesh.shape["tm"] == 2 else on_device,
        mesh=mesh,
        in_specs=(
            P("tm", None, "lat", "lon"),
            P("tm", None, "lat", "lon"),
            P(None, "lat", "lon"),
            P(None, "lat", "lon"),
            P(),
        ),
        out_specs=P("tm", None, "lat", "lon"),
        check_vma=False,
    )
```

```python
import functools

import jax
import jax.numpy as jnp
from jax import lax
from jax.experimental import pallas as pl
from jax.experimental.pallas import tpu as pltpu
from jax.sharding import PartitionSpec as P

SWEEPS = 4


corner_weight = 0.1


def padded(value, sides, width, wrap):
    for axis, dim in sides:
        peers, length = (lax.axis_size(axis), value.shape[dim])
        up = [(i, (i + 1) % peers) for i in range(peers if wrap else peers - 1)]
        down = [(j, i) for i, j in up]
        last = lax.slice_in_dim(value, length - width, length, axis=dim)
        initial = lax.slice_in_dim(value, 0, width, axis=dim)
        before = lax.ppermute(last, axis, up)
        after = lax.ppermute(initial, axis, down)
        value = jnp.concatenate([before, value, after], axis=dim)
    return value


def passed_along(block, axis, distance):
    devices = range(lax.axis_size(axis))
    route = [(i - distance, i) for i in devices if i - distance in devices]
    return lax.ppermute(block, axis, route)


def harmonic(first, second):
    return 2.0 * first * second / (first + second)


def conductivity(region, cond_table):
    classes = jnp.arange(cond_table.shape[0], dtype=jnp.int32)
    onehot = (region[..., None] == classes).astype(jnp.float32)
    return jnp.sum(onehot * cond_table, axis=-1)


def extend(stack):
    lat_ext = padded(stack, (("lat", 2),), 1, False)
    both = padded(lat_ext, (("lon", 3),), 1, True)
    return jnp.pad(both, ((0, 0), (1, 1), (0, 0), (0, 0)))


def face_weights(kext):
    centre = kext[1:-1, 1:-1, 1:-1]
    return (
        harmonic(centre, kext[:-2, 1:-1, 1:-1]),
        harmonic(centre, kext[2:, 1:-1, 1:-1]),
        harmonic(centre, kext[1:-1, :-2, 1:-1]),
        harmonic(centre, kext[1:-1, 2:, 1:-1]),
        harmonic(centre, kext[1:-1, 1:-1, :-2]),
        harmonic(centre, kext[1:-1, 1:-1, 2:]),
    )


def neighbours(weights, ext):
    near = weights[0] * ext[..., :-2, 1:-1, 1:-1] + weights[1] * ext[..., 2:, 1:-1, 1:-1]
    near = near + weights[2] * ext[..., 1:-1, :-2, 1:-1] + weights[3] * ext[..., 1:-1, 2:, 1:-1]
    near = near + weights[4] * ext[..., 1:-1, 1:-1, :-2] + weights[5] * ext[..., 1:-1, 1:-1, 2:]
    return near


def on_device(iterate, heating, initial, region, cond_table):
    steps = lax.axis_size("tm")
    own = lax.axis_index("tm")
    high = lax.Precision.HIGHEST
    kfield = conductivity(region, cond_table)
    ext = extend(jnp.stack([kfield, iterate[0]]))
    weights = face_weights(ext[0])
    total = weights[0] + weights[1] + weights[2] + weights[3] + weights[4] + weights[5]
    shifted = passed_along(iterate, "tm", 1)[0]
    previous = jnp.where(own == 0, initial, shifted)
    residual = heating[0] + previous - ((1.0 + total) * iterate[0] - neighbours(weights, ext[1]))
    scale_own = corner_weight ** (own.astype(jnp.float32) / steps)
    scaled = residual * scale_own
    zeros = jnp.zeros_like(residual)
    piece = lax.all_gather(scaled[None], "tm", axis=0, tiled=True)
    order = jnp.arange(piece.shape[0], dtype=jnp.int32)
    angle = 2.0 * jnp.pi / steps * (own * order % steps).astype(jnp.float32)
    real_part = jnp.einsum("n,nabc->abc", jnp.cos(angle), piece, precision=high)
    imag_part = (zeros, zeros)[1] - jnp.einsum("n,nabc->abc", jnp.sin(angle), piece, precision=high)
    beta = corner_weight ** (1.0 / steps)
    freq_angle = 2.0 * jnp.pi / steps * (own % steps).astype(jnp.float32)
    diag_re = 1.0 - beta * jnp.cos(freq_angle) + total
    diag_im = beta * jnp.sin(freq_angle) + zeros
    denom = diag_re * diag_re + diag_im * diag_im
    inv_re = diag_re / denom
    inv_im = -diag_im / denom
    sol_re = real_part * inv_re - imag_part * inv_im
    sol_im = real_part * inv_im + imag_part * inv_re
    for sweep in range(SWEEPS - 1):
        near = neighbours(weights, extend(jnp.stack([sol_re, sol_im])))
        rhs_re = real_part + near[0]
        rhs_im = imag_part + near[1]
        sol_re = rhs_re * inv_re - rhs_im * inv_im
        sol_im = rhs_re * inv_im + rhs_im * inv_re
    pieces = (
        lax.all_gather(sol_re[None], "tm", axis=0, tiled=True),
        lax.all_gather(sol_im[None], "tm", axis=0, tiled=True),
    )
    order = jnp.arange(pieces[0].shape[0], dtype=jnp.int32)
    angle = 2.0 * jnp.pi / steps * (order * own % steps).astype(jnp.float32)
    summed = jnp.einsum("k,kabc->abc", jnp.cos(angle), pieces[0], precision=high) - jnp.einsum(
        "k,kabc->abc", jnp.sin(angle), pieces[1], precision=high
    )
    back = summed / steps
    return iterate + (back / scale_own)[None]


HALO = 4
TILE = 8
LEVELS = 64
ROWS = 16
LONS = 128
HALF = 64
SENT = HALF + HALO
PLACES = HALF + 2 * HALO
PAIRS = PLACES // 2
SENT_PAIRS = SENT // 2
QUADS = PLACES // 4
SPLIT = 24
FIXED = SPLIT
PARTNER = SPLIT + QUADS
CHUNKS = 4


def specs(count, hbm):
    return [pl.BlockSpec(memory_space=pltpu.HBM if i in hbm else pltpu.VMEM) for i in range(count)]


def call(body, outs, ins, scratch=(), limit=8, hbm_ins=(), hbm_outs=(), work=1):
    moved = work * (sum(x.size * 4 for x in ins) + sum(x.size * 4 for x in outs))
    return pl.pallas_call(
        body,
        out_shape=outs,
        in_specs=specs(len(ins), hbm_ins),
        out_specs=specs(len(outs), hbm_outs),
        scratch_shapes=scratch,
        compiler_params=pltpu.CompilerParams(vmem_limit_bytes=limit << 20),
        cost_estimate=pl.CostEstimate(flops=moved * 4, bytes_accessed=moved, transcendentals=0),
    )(*ins)


def shape(*dims):
    return jax.ShapeDtypeStruct(dims, jnp.float32)


def buffer(*dims):
    return pltpu.VMEM(dims, jnp.float32)


def ids(rows, dim):
    return lax.broadcasted_iota(jnp.int32, (rows, 128), dim)


def in_low(rows):
    return ids(rows, 1) < LEVELS


def swapped(x):
    return pltpu.roll(x, LEVELS, 1)


def main_at(i):
    return jnp.where(lax.axis_index("tm") == 0, SENT - 1 - i, i)


def outer_at(i):
    return jnp.where(lax.axis_index("tm") == 0, PLACES - 1 - i, SENT + i)


def cat(*values):
    return jnp.concatenate(values, axis=0)


def even(axis):
    return lax.rem(lax.axis_index(axis), 2) == 0


def blocks(lo, hi, width, step):
    def body(i, carry):
        for u in range(width):
            step(lo + i * width + u)
        return carry

    lax.fori_loop(0, (hi - lo) // width, body, 0)


def send_first(it_hbm, h_hbm, edges, middle, turned, it, h, sems):
    t = lax.axis_index("tm")
    by_level = (LEVELS, ROWS, LONS)
    copies = []
    for k in range(ROWS // TILE):
        for f, (source, target) in enumerate(((it_hbm, it), (h_hbm, h))):
            for c in range(2):
                part = pl.ds(c * LEVELS // 2, LEVELS // 2), pl.ds(k * TILE, TILE)
                copy = pltpu.make_async_copy(source.at[part], target.reshape(by_level).at[part], sems.at[k, f, c])
                copy.start()
                copies.append(copy)

    def turn(r):
        rows = pl.ds(r, LEVELS, stride=ROWS)
        turned[pl.ds(r, LONS, stride=ROWS), :] = cat(it[rows, :], h[rows, :]).T

    for k in range(ROWS // TILE):
        for copy in copies[4 * k : 4 * k + 4]:
            copy.wait()
        blocks(k * TILE, (k + 1) * TILE, 8, turn)
    start = (LONS - SENT) * ROWS * (1 - t)
    top = ids(TILE, 0) < HALO

    def cut(i):
        at = pl.multiple_of(start + i * ROWS, ROWS)
        low, high = turned[pl.ds(at, TILE), :], turned[pl.ds(at + TILE, TILE), :]
        edges[i] = jnp.where(top, low, high)
        middle[i] = jnp.where(top, high, low)

    blocks(0, SENT, 17, cut)


def heated(turned, fixed):
    add = jnp.logical_and(jnp.logical_not(in_low(ROWS)), lax.axis_index("tm") == 0)
    return turned + jnp.where(add, fixed, 0.0)


def send_sides(turned, region, initial, table_hbm, fixed, near_sides, far_sides, table, sem):
    copy = pltpu.make_async_copy(table_hbm, table, sem)
    copy.start()
    copy.wait()

    def turn(r):
        rows = pl.ds(r, LEVELS, stride=ROWS)
        classes = region[rows, :]
        value = jnp.full(classes.shape, table[0], jnp.float32)
        for c in range(1, table.shape[0]):
            value = jnp.where(classes == c, table[c], value)
        fixed[pl.ds(r, LONS, stride=ROWS), :] = cat(value, initial[rows, :]).T

    blocks(0, ROWS, 8, turn)
    near_right = even("lon")
    low = in_low(ROWS)

    def strip(first_lon):
        def at(ref, i):
            return ref[(first_lon + i) * ROWS : (first_lon + i + 1) * ROWS, :]

        return [heated(at(turned, i), at(fixed, i)) for i in range(HALO)] + [
            jnp.where(low, at(fixed, i), swapped(at(fixed, i + 2))) for i in range(2)
        ]

    for i, (right, left) in enumerate(zip(strip(LONS - HALO), strip(0))):
        near_sides[i] = jnp.where(near_right, right, left)
        far_sides[i] = jnp.where(near_right, left, right)


def edge_pair(first, second):
    top = ids(TILE, 0) < HALO
    first_up = even("lat")
    down = jnp.where(top, first[:TILE], pltpu.roll(second[:TILE], HALO, 0))
    up = jnp.where(top, pltpu.roll(first[-TILE:], HALO, 0), second[-TILE:])
    return jnp.where(first_up, up, down), jnp.where(first_up, down, up)


def halo_tiles(near_pair, far_pair):
    first_up = even("lat")
    after = jnp.where(first_up, near_pair, far_pair)
    before = jnp.where(first_up, far_pair, near_pair)
    top = ids(TILE, 0) < HALO
    return (
        jnp.where(top, after, pltpu.roll(before, HALO, 0)),
        jnp.where(top, pltpu.roll(after, HALO, 0), before),
    )


def add_sides(turned, fixed, near_sides, far_sides, own, own_fixed, near_lat, far_lat, partner):
    t = lax.axis_index("tm")
    from_near = (t == 0) != even("lon")
    count = near_sides.shape[0]
    beside = [jnp.where(from_near, near_sides[i], far_sides[i]) for i in range(count)]
    other = [jnp.where(from_near, far_sides[i], near_sides[i]) for i in range(HALO)]
    for i in range(HALO):
        own[outer_at(i)] = beside[i]
        partner[i] = other[i]
    for i in range(2):
        own_fixed[outer_at(i)] = beside[HALO + i]
        own_fixed[outer_at(i + 2)] = swapped(beside[HALO + i])
        near_lat[PARTNER + i], far_lat[PARTNER + i] = edge_pair(other[i], other[i + 2])

    def copy(i):
        at = main_at(i)
        lon = (LONS - SENT) * t + i
        own[at] = heated(turned[lon], fixed[lon])
        own_fixed[at] = fixed[lon]

    blocks(0, SENT, 17, copy)

    def rows(i):
        near_lat[i], far_lat[i] = edge_pair(own[i], own[i + PAIRS])

    blocks(0, SPLIT, 12, rows)
    low = in_low(TILE)

    def fixed_rows(i):
        here = edge_pair(own_fixed[i], own_fixed[i + PAIRS])
        there = edge_pair(own_fixed[i + QUADS], own_fixed[i + PAIRS + QUADS])
        near_lat[FIXED + i], far_lat[FIXED + i] = [jnp.where(low, a, swapped(b)) for a, b in zip(here, there)]

    blocks(0, QUADS, 9, fixed_rows)


def start_of_step(fixed, rows):
    add = jnp.logical_and(jnp.logical_not(in_low(rows)), lax.axis_index("tm") == 1)
    return jnp.where(add, fixed, 0.0)


def pass_rows(edges, own, own_fixed, heated_edges, near_rows, far_rows):
    top = ids(TILE, 0) < HALO

    def heat(i):
        fixed = own_fixed[main_at(i)]
        heated_edges[i] = edges[i] + start_of_step(jnp.where(top, fixed[:TILE], fixed[TILE:]), TILE)

    blocks(0, SENT, 17, heat)

    def rows(i):
        near_rows[i], far_rows[i] = edge_pair(heated_edges[i], heated_edges[i + SENT_PAIRS])

    blocks(0, SENT_PAIRS, 17, rows)

    def rest(i):
        near_rows[SENT_PAIRS + i], far_rows[SENT_PAIRS + i] = edge_pair(own[SPLIT + i], own[SPLIT + i + PAIRS])

    blocks(0, PAIRS - SPLIT, 12, rest)


def join(near_lat, far_lat, near_rows, far_rows, halo, other):
    def place(i, tiles):
        halo[i], halo[i + PAIRS] = tiles

    blocks(0, SPLIT, 12, lambda i: place(i, halo_tiles(near_lat[i], far_lat[i])))

    def rest(i):
        at = SENT_PAIRS + i
        place(SPLIT + i, halo_tiles(near_rows[at], far_rows[at]))

    blocks(0, PAIRS - SPLIT, 12, rest)

    def theirs(i):
        other[main_at(i)], other[main_at(i + SENT_PAIRS)] = halo_tiles(near_rows[i], far_rows[i])

    blocks(0, SENT_PAIRS, 17, theirs)


def both_steps(mine, theirs):
    first = lax.axis_index("tm") == 0
    low = in_low(mine.shape[0])
    step0, step1 = jnp.where(first, mine, theirs), jnp.where(first, theirs, mine)
    moved = swapped(step0)
    return jnp.where(low, step0, swapped(step1)), jnp.where(low, moved, step1 + moved)


def gather(edges, middle, own, own_fixed, it, source):
    top = ids(TILE, 0) < HALO

    def step(i):
        at = main_at(i)
        fixed = own_fixed[at]
        e = edges[i]
        m = middle[i] + start_of_step(jnp.where(top, fixed[TILE:], fixed[:TILE]), TILE)
        theirs = cat(jnp.where(top, e, m), jnp.where(top, m, e))
        it[at], source[at] = both_steps(own[at], theirs)

    blocks(0, SENT, 17, step)


def strips(partner, near_lat, far_lat, _, xs):
    for i in range(2):
        at = PARTNER + i
        for place, tile in zip((i, i + 2), halo_tiles(near_lat[at], far_lat[at])):
            xs[place] = cat(partner[place], tile)


def reciprocal(d):
    y = pl.reciprocal(d, approx=True)
    return y * (2.0 - d * y)


def face(a, b, twice):
    return twice * b * reciprocal(jnp.maximum(a + b, 1e-30))


def woven(ref, at):
    return cat(*[ref[at, pl.ds(j, TILE, stride=3), :] for j in range(3)])


def woven_at(row):
    return row % 3 * TILE + row // 3


def next_row(x):
    return cat(x[TILE:], pltpu.roll(x[:TILE], TILE - 1, 0))


def last_row(x):
    return cat(pltpu.roll(x[-TILE:], 1, 0), x[:-TILE])


def near(around, w):
    before, mid, after = around
    wxp, wx, wy, wyp, wl = w
    total = wxp * before + wx * after
    total = total + (wy * next_row(mid) + wyp * last_row(mid))
    return total + (wl * pltpu.roll(mid, 127, 1) + pltpu.roll(wl * mid, 1, 1))


def prepare(own_fixed, near_lat, far_lat, _, wx, wy, wyp, wl, total, inv, K):
    rows = ROWS + TILE
    low = in_low(ROWS)
    low_tile = in_low(TILE)
    beta = corner_weight ** 0.5
    K[PLACES] = jnp.zeros((rows, 128), jnp.float32)

    def assemble_fixed(i):
        for at, tile in zip((i, i + PAIRS), halo_tiles(near_lat[FIXED + i], far_lat[FIXED + i])):
            moved = swapped(tile)
            for here, value in ((at, jnp.where(low_tile, tile, moved)), (at + QUADS, jnp.where(low_tile, moved, tile))):
                main = own_fixed[here]
                K[here] = cat(jnp.where(low, main, swapped(main)), value)

    blocks(0, QUADS, 9, assemble_fixed)
    lane = ids(rows, 1)
    inside = (lane & (LEVELS - 1)) != LEVELS - 1
    shift = jnp.where(lane < LEVELS, 1.0 - beta, 1.0 + beta)
    width = 18

    def weigh(i, carry):
        start = i * width
        here = woven(K, start)
        before = wx[jnp.maximum(start - 1, 0)]
        for u in range(width):
            at = start + u
            after = woven(K, at + 1)
            twice = 2.0 * here
            side = face(here, after, twice)
            row = face(here, next_row(here), twice)
            previous = last_row(row)
            level = jnp.where(inside, face(here, pltpu.roll(here, 127, 1), twice), 0.0)
            sums = (before + side) + (row + previous) + (level + pltpu.roll(level, 1, 1))
            wx[at], wy[at], wyp[at], wl[at] = side, row, previous, level
            total[at] = sums
            inv[at] = reciprocal(shift + sums)
            here, before = after, side
        return carry

    wx[0] = jnp.zeros((rows, 128), jnp.float32)
    lax.fori_loop(0, PLACES // width, weigh, 0)


STAGES = ((1, 39, 71), (2, 38, 70), (3, 37, 69), (4, 36, 68))
WIDTHS = ((19, 12, 17, 16), (16, 16, 16, 16))
READY = 40
EDGE = 12


def iterate_half(
    upper, wx, wy, wyp, wl, total, inv, own, own_halo, other_halo, it_main, source_main, *refs
):
    if upper:
        xs, edge, w_own, w_send, *refs = refs
    else:
        w_own, w_send, edge, *refs = refs
    it, source, spec, x, y, z, natural = refs
    rows = ROWS + TILE
    first = lax.axis_index("tm") == 0
    low = in_low(rows)
    beta = corner_weight ** 0.5
    gamma = jnp.where(low, 1.0, beta)
    shared = [(it, 38), (it, 39), (source, 39), (x, 37), (x, 38), (y, 36), (y, 37), (z, 35), (z, 36)]
    shared += [(spec, 36), (spec, 37), (spec, 38)]
    if upper:
        for i, (ref, at) in enumerate(shared):
            ref[at] = edge[i]

    def assemble(at):
        a, b = both_steps(own_halo[at], other_halo[at])
        it[at], source[at] = cat(it_main[at], a), cat(source_main[at], b)

    if upper:
        blocks(READY, SENT, 14, assemble)
        for i in range(HALO):
            at = outer_at(i)
            it[at], source[at] = both_steps(cat(own[at], own_halo[at]), xs[i])
    else:
        blocks(0, READY, 10, assemble)

    def over(stage, read, ref, step):
        lo, hi = STAGES[stage][upper : upper + 2]
        width = WIDTHS[upper][stage]

        def body(i, carry):
            start = lo + i * width
            around = [read(ref, start - 1), read(ref, start)]
            before = wx[start - 1]
            for u in range(width):
                at = start + u
                around = [*around[-2:], read(ref, at + 1)]
                side = wx[at]
                step(at, around, (before, side, wy[at], wyp[at], wl[at]))
                before = side
            return carry

        lax.fori_loop(0, (hi - lo) // width, body, 0)

    def residual(at, around, w):
        left = (woven(source, at) - ((1.0 + total[at]) * around[1] - near(around, w))) * gamma
        moved = swapped(left)
        value = jnp.where(low, left + moved, moved - left)
        spec[at] = value
        x[at] = value * inv[at]

    over(0, woven, it, residual)

    def plain(ref, at):
        return ref[at]

    def sweep(at, around, w):
        return (spec[at] + near(around, w)) * inv[at]

    def to(ref):
        def step(at, around, w):
            ref[at] = sweep(at, around, w)

        return step

    over(1, plain, x, to(y))
    over(2, plain, y, to(z))
    base = STAGES[3][upper]
    back = jnp.where(low, 0.5, 0.5 / beta)

    def last(at, around, w):
        value = sweep(at, around, w)
        moved = swapped(value)
        value = jnp.where(low, value + moved, moved - value) * back
        lon = at - base
        lon = jnp.where(first, HALF // 2 - 1 - lon, lon)
        natural[pl.ds(pl.multiple_of(lon * rows, TILE), rows), :] = value

    over(3, plain, z, last)
    count = HALF // 2
    for q in range(4):
        turned = cat(*[natural[pl.ds(woven_at(q + 4 * j), count, stride=rows), :] for j in range(4)]).T
        step0, step1 = turned[:LEVELS], turned[LEVELS:]
        w_own[q] = jnp.where(first, step0, step1)
        w_send[q] = jnp.where(first, step1, step0)
    if not upper:
        for i, (ref, at) in enumerate(shared):
            edge[i] = ref[at]


def placed(value, j, quarter):
    return pltpu.roll(value, (32 * (quarter - j) + 128) & 127, 1)


def finish_most(it, own_low, own_high, got_low, most):
    t = lax.axis_index("tm")
    group = ids(LEVELS, 1) // 32

    def step(q):
        for j in range(4):
            row = q + 4 * j
            value = it[pl.ds(row, LEVELS, stride=ROWS), :]
            for piece, quarter in ((own_low, 1 + t), (own_high, 3 * t), (got_low, 2 - t)):
                value = jnp.where(group == quarter, value + placed(piece[q], j, quarter), value)
            most[row] = value

    blocks(0, 4, 2, step)


def finish(most, got_high, out_hbm, out, sems):
    quarter = 3 - 3 * lax.axis_index("tm")
    part = LEVELS // CHUNKS
    here = ids(part, 1) // 32 == quarter

    def copy(c):
        span = pl.ds(pl.multiple_of(c * part * ROWS, part * ROWS), part * ROWS)
        return pltpu.make_async_copy(out.at[span], out_hbm.at[span], sems.at[c])

    def step(c):
        for q in range(4):
            value = got_high[q, pl.ds(pl.multiple_of(c * part, part), part), :]
            for j in range(4):
                old = most[q + 4 * j, pl.ds(pl.multiple_of(c * part, part), part), :]
                out[pl.ds(c * part * ROWS + q + 4 * j, part, stride=ROWS), :] = jnp.where(here, old + placed(value, j, quarter), old)
        copy(c).start()

    blocks(0, CHUNKS, 1, step)
    for c in range(CHUNKS):
        copy(c).wait()


def two_steps(iterate, heating, initial, region, cond_table):
    lats, lons = lax.axis_size("lat"), lax.axis_size("lon")
    swap = [(0, 1), (1, 0)]
    pairs = [[(i, i + 1) for i in range(start, lats - 1, 2)] for start in (0, 1)]
    pairs = [p + [(j, i) for i, j in p] for p in pairs]
    round_lon = [[(i, (i + 1) % lons) for i in range(start, lons, 2)] for start in (0, 1)]
    round_lon = [p + [(j, i) for i, j in p] for p in round_lon]
    flat = (LEVELS * ROWS, LONS)
    turned_flat = (LONS * ROWS, 2 * LEVELS)
    by_lon = (LONS, ROWS, 2 * LEVELS)
    wide = shape(PLACES, ROWS + TILE, 128)

    def in_hbm(x):
        return pltpu.with_memory_space_constraint(x, pltpu.HBM)

    half_rows = shape(SENT, TILE, 128)
    edges, middle, turned, it = call(
        send_first,
        [half_rows, half_rows, shape(*turned_flat), shape(*flat)],
        [in_hbm(iterate[0]), in_hbm(heating[0])],
        scratch=[buffer(*flat), pltpu.SemaphoreType.DMA((ROWS // TILE, 2, 2))],
        hbm_ins=(0, 1),
    )
    edges = lax.ppermute(edges, "tm", swap)
    middle = lax.ppermute(middle, "tm", swap)
    sides = shape(HALO + 2, ROWS, 128)
    fixed, near_sides, far_sides = call(
        send_sides,
        [shape(*turned_flat), sides, sides],
        [turned, region.reshape(flat), initial.reshape(flat), in_hbm(cond_table)],
        scratch=[pltpu.SMEM(cond_table.shape, jnp.float32), pltpu.SemaphoreType.DMA],
        hbm_ins=(3,),
    )
    near_sides = lax.ppermute(near_sides, "lon", round_lon[0])
    far_sides = lax.ppermute(far_sides, "lon", round_lon[1])
    main = shape(PLACES, ROWS, 128)
    lat = shape(PARTNER + 2, TILE, 128)
    own_main, own_fixed, near_lat, far_lat, partner = call(
        add_sides,
        [main, main, lat, lat, shape(HALO, ROWS, 128)],
        [turned.reshape(by_lon), fixed.reshape(by_lon), near_sides, far_sides],
    )
    near_lat = lax.ppermute(near_lat, "lat", pairs[0])
    far_lat = lax.ppermute(far_lat, "lat", pairs[1])
    rows = shape(SENT_PAIRS + PAIRS - SPLIT, TILE, 128)
    edges, near_rows, far_rows = call(
        pass_rows, [half_rows, rows, rows], [edges, own_main, own_fixed], work=200
    )
    near_rows = lax.ppermute(near_rows, "lat", pairs[0])
    far_rows = lax.ppermute(far_rows, "lat", pairs[1])
    it_main, source_main = call(gather, [main, main], [edges, middle, own_main, own_fixed])
    (xs,) = call(strips, [shape(HALO, ROWS + TILE, 128)], [partner, near_lat, far_lat, it_main])
    xs = lax.ppermute(xs, "tm", swap)
    ready = call(
        prepare,
        [wide] * 6,
        [own_fixed, near_lat, far_lat, it_main],
        scratch=[buffer(PLACES + 1, ROWS + TILE, 128)],
    )
    halos = call(join, [shape(PLACES, TILE, 128)] * 2, [near_lat, far_lat, near_rows, far_rows])
    given = [*ready, own_main, *halos, it_main, source_main]
    corrections = [shape(4, LEVELS, 128)] * 2
    fields = [buffer(PLACES, ROWS + TILE, 128)] * 6 + [buffer(HALF // 2 * (ROWS + TILE), 128)]
    own_low, send_low, edge = call(
        functools.partial(iterate_half, 0),
        [*corrections, shape(EDGE, ROWS + TILE, 128)],
        given,
        scratch=fields,
        limit=16,
    )
    got_low = lax.ppermute(send_low, "tm", swap)
    own_high, send_high = call(
        functools.partial(iterate_half, 1), corrections, [*given, xs, edge], scratch=fields, limit=16
    )
    got_high = lax.ppermute(send_high, "tm", swap)
    (most,) = call(finish_most, [shape(ROWS, LEVELS, LONS)], [it, own_low, own_high, got_low])
    (out,) = call(
        finish,
        [shape(*flat)],
        [most, got_high],
        scratch=[buffer(*flat), pltpu.SemaphoreType.DMA((CHUNKS,))],
        hbm_outs=(0,),
    )
    return out.reshape(iterate.shape)


def solution(mesh):
    return jax.shard_map(
        two_steps if mesh.shape["tm"] == 2 else on_device,
        mesh=mesh,
        in_specs=(
            P("tm", None, "lat", "lon"),
            P("tm", None, "lat", "lon"),
            P(None, "lat", "lon"),
            P(None, "lat", "lon"),
            P(),
        ),
        out_specs=P("tm", None, "lat", "lon"),
        check_vma=False,
    )
```
